32 devices in a mesh: fsdp: 8 (over y, x, core), tp: 4 (over z).
Axes of the slice: x: 2, y: 2, z: 4, core: 2. Of those that a mesh axis runs over, the one named last changes fastest.
Arguments:
- tokens: bfloat16 [8192, 2048], P(('fsdp', 'tp')), may hold values from -6 to 6
- attn_gain: bfloat16 [2048], P('fsdp'), may hold values from 0.5 to 1.5
- query_weight: bfloat16 [2048, 2048], P('fsdp', 'tp'), may hold values from -0.125 to 0.125
- key_weight: bfloat16 [2048, 256], P('fsdp', 'tp'), may hold values from -0.125 to 0.125
- value_weight: bfloat16 [2048, 256], P('fsdp', 'tp'), may hold values from -0.125 to 0.125
- output_weight: bfloat16 [2048, 2048], P('tp', 'fsdp'), may hold values from -3 to 3
- mlp_gain: bfloat16 [2048], P('fsdp'), may hold values from 0.5 to 1.5
- gate_weight: bfloat16 [2048, 5632], P('fsdp', 'tp'), may hold values from -0.125 to 0.125
- up_weight: bfloat16 [2048, 5632], P('fsdp', 'tp'), may hold values from -0.125 to 0.125
- down_weight: bfloat16 [5632, 2048], P('tp', 'fsdp'), may hold values from -0.078125 to 0.078125
- out_grad: bfloat16 [8192, 2048], P(('fsdp', 'tp')), may hold values from -6 to 6
- lengths: int32 [2], replicated, may hold values from 1024 to 4096, as said below
Outputs:
- layer_out: bfloat16 [8192, 2048], P(('fsdp', 'tp'))
- tokens_grad: float32 [8192, 2048], P(('fsdp', 'tp'))
- grad_attn_gain: float32 [2048], P('fsdp')
- grad_query: float32 [2048, 2048], P('fsdp', 'tp')
- grad_key: float32 [2048, 256], P('fsdp', 'tp')
- grad_value: float32 [2048, 256], P('fsdp', 'tp')
- grad_output: float32 [2048, 2048], P('tp', 'fsdp')
- grad_mlp_gain: float32 [2048], P('fsdp')
- grad_gate: float32 [2048, 5632], P('fsdp', 'tp')
- grad_up: float32 [2048, 5632], P('fsdp', 'tp')
- grad_down: float32 [5632, 2048], P('tp', 'fsdp')
The draws below stay inside these ranges and needn't reach their ends.
Inputs may be any that keep to these rules, and one draw needn't show every extreme that they name: `lengths`: one sequence, which one drawn from the seed, is exactly 4096 long, the others at least 1024 and shorter than 4096; their sum is less than 8192.
All inputs are finite; a program needn't handle non-finite values.
Results may differ from the reference program's by a relative error of at most 0.025.
Values may be sent and summed in bfloat16 or wider, within the bound.
A program may use at most 256 MiB of HBM per device.

```python
import jax
import jax.numpy as jnp
from jax import lax

D = 2048
HEADS = 32
KV_HEADS = 4
HEAD_DIM = 64
FF = 5632
STRETCH = 1024
STREAM = 8192
MAX_LEN = 4096
MIN_LEN = 1024
SEQS = 2
REACH = 4


def draw_lengths(key, part):
    base = jax.random.fold_in(key, 17)
    key_pad = jax.random.fold_in(base, 1)
    key_weights = jax.random.fold_in(base, 2)
    key_place = jax.random.fold_in(base, 3)
    others = SEQS - 1
    padding = jax.random.randint(key_pad, (), 1, STRETCH // 2 + 1).astype(jnp.int32)
    slack = (STREAM - MAX_LEN - others * MIN_LEN - padding).astype(jnp.int32)
    weights = jax.random.randint(key_weights, (others,), 100, 121).astype(jnp.int32)
    extra = slack * weights // jnp.sum(weights)
    rest = (MIN_LEN + extra).astype(jnp.int32)
    place = jax.random.randint(key_place, (), 0, SEQS).astype(jnp.int32)
    index = jnp.arange(SEQS).astype(jnp.int32)
    source = jnp.clip(index - (index > place).astype(jnp.int32), 0, others - 1).astype(jnp.int32)
    return jnp.where(index == place, MAX_LEN, rest[source]).astype(jnp.int32)


def block_scale(own_key, dims, split, low, high):
    def one(dim, blocks):
        draws = jax.random.uniform(jax.random.fold_in(jax.random.fold_in(own_key, 6), dim), (blocks,), jnp.float32, low / len(split), high / len(split))
        return jnp.repeat(jnp.exp(draws), dims[dim] // blocks).reshape((-1,) + (1,) * (len(dims) - dim - 1))

    factor_of = one(*split[0])
    for cut in split[1:]:
        factor_of = factor_of * one(*cut)
    return factor_of


def normal_values(rng, shape, deviation, most, shards=(), dtype=jnp.bfloat16):
    entries = jax.random.normal(rng, shape, jnp.float32) * deviation
    if len(shards) > 0:
        entries = block_scale(rng, shape, shards, -0.22, 0.18) * entries
    return jnp.clip(entries, min=-most, max=most).astype(dtype)


def setup_inputs(seed: int = 0) -> dict:
    arg_keys = jax.random.split(jax.random.key(seed), 13)
    tokens = normal_values(arg_keys[0], (STREAM, D), 1.0, 6.0, ((0, 32),))
    attn_gain = jnp.clip(1.0 + 0.1 * jax.random.normal(arg_keys[1], (D,), jnp.float32), 0.5, 1.5).astype(jnp.bfloat16)
    query_weight = normal_values(arg_keys[2], (D, D), D ** -0.5, 0.125, ((0, 8), (1, 4)))
    key_weight = normal_values(arg_keys[3], (D, KV_HEADS * HEAD_DIM), D ** -0.5, 0.125, ((0, 8), (1, 4)))
    value_weight = normal_values(arg_keys[4], (D, KV_HEADS * HEAD_DIM), D ** -0.5, 0.125, ((0, 8), (1, 4)))
    output_weight = normal_values(arg_keys[5], (D, D), (max(D // 512, 1)) ** -0.5, 3.0, ((0, 4), (1, 8)))
    mlp_gain = jnp.clip(1.0 + 0.1 * jax.random.normal(arg_keys[6], (D,), jnp.float32), 0.5, 1.5).astype(jnp.bfloat16)
    gate_weight = normal_values(arg_keys[7], (D, FF), D ** -0.5, 0.125, ((0, 8), (1, 4)))
    up_weight = normal_values(arg_keys[8], (D, FF), D ** -0.5, 0.125, ((0, 8), (1, 4)))
    down_weight = normal_values(arg_keys[9], (FF, D), FF ** -0.5, 0.078125, ((0, 4), (1, 8)))
    out_grad = normal_values(arg_keys[10], (STREAM, D), 1.0, 6.0, ((0, 32),))
    lengths = draw_lengths(jax.random.fold_in(arg_keys[12], 71), 0)
    return dict(tokens=tokens, attn_gain=attn_gain, query_weight=query_weight, key_weight=key_weight, value_weight=value_weight, output_weight=output_weight, mlp_gain=mlp_gain, gate_weight=gate_weight, up_weight=up_weight, down_weight=down_weight, out_grad=out_grad, lengths=lengths)


@jax.custom_vjp
def low(v):
    return lax.optimization_barrier(v.astype(jnp.bfloat16)).astype(jnp.float32)

@jax.custom_vjp
def low_back(v):
    return v

def low_keep(v):
    return (low(v), None)

def low_pass(kept, grad):
    return (grad,)

def back_keep(v):
    return (v, None)

def back_low(kept, grad):
    return (low(grad),)
low.defvjp(low_keep, low_pass)
low_back.defvjp(back_keep, back_low)
epsilon = 1e-05
highest = lax.Precision.HIGHEST

def stream_layout(slots, lengths):
    seq_count = lengths.shape[0]
    seq_index = jnp.arange(seq_count).astype(jnp.int32)
    ends = jnp.cumsum(lengths).astype(jnp.int32)
    starts = (ends - lengths).astype(jnp.int32)
    segment = lax.optimization_barrier(jnp.sum((slots[:, None] >= ends[None, :]).astype(jnp.int32), axis=1)).astype(jnp.int32)
    start_of = lax.optimization_barrier(jnp.sum(jnp.where(segment[:, None] == seq_index[None, :], starts[None, :], 0), axis=1)).astype(jnp.int32)
    position = jnp.where((segment < seq_count) & (slots >= 0), slots - start_of, 0).astype(jnp.int32)
    segment = jnp.where(slots < 0, -1, segment).astype(jnp.int32)
    return (segment, position)

def rms_rows(values, gain):
    inverse = lax.rsqrt(lax.optimization_barrier(jnp.mean(values * values, axis=-1, keepdims=True)) + epsilon)
    return values * inverse * gain

def rotary_tables(positions):
    ladder = jnp.arange(HEAD_DIM // 2).astype(jnp.float32)
    frequency = 10000.0 ** (-2.0 * ladder / HEAD_DIM)
    angle_half = positions.astype(jnp.float32)[:, None] * frequency[None, :]
    angles = jnp.concatenate([angle_half, angle_half], axis=1)
    return (jnp.cos(angles)[:, None, :], jnp.sin(angles)[:, None, :])

def rotate(values, cosine, sine_table):
    middle = values.shape[-1] // 2
    turned = jnp.concatenate([-values[..., middle:], values[..., :middle]], axis=-1)
    return values * cosine + turned * sine_table

def head_group(query_group, key_head, value_head, key_seen):
    scores = jnp.einsum('qgd,wd->gqw', query_group, key_head, precision=highest) * HEAD_DIM ** (-0.5)
    scores = jnp.where(key_seen[None], low_back(scores), -1e+30)
    largest = lax.optimization_barrier(jnp.max(scores, axis=-1, keepdims=True))
    raised = jnp.exp(scores - largest)
    attn_probs = raised / lax.optimization_barrier(jnp.sum(raised, axis=-1, keepdims=True))
    return jnp.einsum('gqw,wd->qgd', low(attn_probs), value_head, precision=highest)
head_group_saved = jax.checkpoint(head_group)

def attend_block(block_index, queries, keys_padded, values_padded, segment_padded, position_padded):
    window = (REACH + 1) * STRETCH
    offset = block_index.astype(jnp.int32) * STRETCH
    front_rows = REACH * STRETCH
    query_block = lax.dynamic_slice_in_dim(queries, offset, STRETCH, 0)
    key_block = lax.dynamic_slice_in_dim(keys_padded, offset, window, 0)
    value_block = lax.dynamic_slice_in_dim(values_padded, offset, window, 0)
    query_segments = lax.dynamic_slice_in_dim(segment_padded, offset + front_rows, STRETCH, 0)
    query_positions = lax.dynamic_slice_in_dim(position_padded, offset + front_rows, STRETCH, 0)
    key_segments = lax.dynamic_slice_in_dim(segment_padded, offset, window, 0)
    key_positions = lax.dynamic_slice_in_dim(position_padded, offset, window, 0)
    key_seen = (key_segments[None, :] == query_segments[:, None]) & (key_positions[None, :] <= query_positions[:, None])

    def one_head(packed):
        return head_group_saved(packed[0], packed[1], packed[2], key_seen)
    outputs = lax.map(one_head, (jnp.moveaxis(query_block, 1, 0), jnp.moveaxis(key_block, 1, 0), jnp.moveaxis(value_block, 1, 0)))
    return jnp.moveaxis(outputs, 0, 1).reshape(STRETCH, HEADS * HEAD_DIM)

def reference(tokens, attn_gain, query_weight, key_weight, value_weight, output_weight, mlp_gain, gate_weight, up_weight, down_weight, out_grad, lengths):
    front_rows = REACH * STRETCH
    padded_slots = (jnp.arange(STREAM + front_rows) - front_rows).astype(jnp.int32)
    segment_padded, position_padded = stream_layout(padded_slots, lengths.astype(jnp.int32))
    segment_ids = segment_padded[front_rows:]
    positions = position_padded[front_rows:]
    valid_rows = (segment_ids < SEQS)[:, None]
    cosine, sine_table = rotary_tables(positions)
    group_size = HEADS // KV_HEADS

    def forward(tokens, attn_gain, query_weight, key_weight, value_weight, output_weight, mlp_gain, gate_weight, up_weight, down_weight):
        normed = low(rms_rows(tokens, attn_gain))
        queries = jnp.dot(normed, query_weight, precision=highest).reshape(STREAM, HEADS, HEAD_DIM)
        queries = low(rotate(low_back(queries), cosine, sine_table))
        key_vectors = jnp.dot(normed, key_weight, precision=highest).reshape(STREAM, KV_HEADS, HEAD_DIM)
        key_vectors = low(rotate(low_back(key_vectors), cosine, sine_table))
        values = low(low_back(jnp.dot(normed, value_weight, precision=highest))).reshape(STREAM, KV_HEADS, HEAD_DIM)
        keys_padded = jnp.concatenate([jnp.zeros((front_rows, KV_HEADS, HEAD_DIM), jnp.float32), key_vectors])
        values_padded = jnp.concatenate([jnp.zeros((front_rows, KV_HEADS, HEAD_DIM), jnp.float32), values])
        grouped = queries.reshape(STREAM, KV_HEADS, group_size, HEAD_DIM)

        def block_step(block_index):
            return attend_block(block_index, grouped, keys_padded, values_padded, segment_padded, position_padded)
        attended = lax.map(block_step, jnp.arange(STREAM // STRETCH).astype(jnp.int32)).reshape(STREAM, D)
        attended = low(low_back(attended))
        middle = tokens + low_back(jnp.dot(attended, output_weight, precision=highest))
        normed_mid = low(rms_rows(middle, mlp_gain))
        gate_proj = low_back(jnp.dot(normed_mid, gate_weight, precision=highest))
        up_proj = low_back(jnp.dot(normed_mid, up_weight, precision=highest))
        hidden = low(jax.nn.silu(gate_proj) * up_proj)
        down_proj = low_back(jnp.dot(hidden, down_weight, precision=highest))
        return jnp.where(valid_rows, middle + down_proj, 0.0)
    floats = [a.astype(jnp.float32) for a in (tokens, attn_gain, query_weight, key_weight, value_weight, output_weight, mlp_gain, gate_weight, up_weight, down_weight)]
    primal, pullback = jax.vjp(forward, *floats)
    gradients = pullback(out_grad.astype(jnp.float32))
    return (primal.astype(jnp.bfloat16), gradients[0], gradients[1], gradients[2], gradients[3], gradients[4], gradients[5], gradients[6], gradients[7], gradients[8], gradients[9])
```

```python
import jax
import jax.numpy as jnp
from jax import lax
from jax.experimental import pallas as pl
from jax.experimental.pallas import tpu as pltpu
from jax.sharding import PartitionSpec as P

HEAD_DIM = 64
MAX_SPAN = 4096


epsilon = 1e-05


def passed_along(block, axis, distance):
    devices = range(lax.axis_size(axis))
    route = [(i - distance, i) for i in devices if i - distance in devices]
    return lax.ppermute(block, axis, route)


def stream_layout(slots, lengths):
    seq_count = lengths.shape[0]
    seq_index = jnp.arange(seq_count, dtype=jnp.int32)
    ends = jnp.sum(jnp.where(seq_index[:, None] >= seq_index[None, :], lengths[None, :], 0), axis=1)
    starts = ends - lengths
    segment = jnp.sum((slots[:, None] >= ends[None, :]).astype(jnp.int32), axis=1)
    start_of = jnp.sum(
        jnp.where(segment[:, None] == seq_index[None, :], starts[None, :], 0), axis=1
    )
    position = jnp.where((segment < seq_count) & (slots >= 0), slots - start_of, 0)
    segment = jnp.where(slots < 0, -1, segment)
    return (segment, position)


def rotary_tables(positions, head_width):
    ladder = jnp.arange(head_width // 2).astype(jnp.float32)
    frequency = 10000.0 ** (-2.0 * ladder / head_width)
    angle_half = positions.astype(jnp.float32)[:, None] * frequency[None, :]
    angles = jnp.concatenate([angle_half, angle_half], axis=1)
    return (jnp.cos(angles)[:, None, :], jnp.sin(angles)[:, None, :])


def rotate(values, cosine, sine_table):
    middle = values.shape[-1] // 2
    turned = jnp.concatenate([-values[..., middle:], values[..., :middle]], axis=-1)
    return values * cosine + turned * sine_table


def rotate_back(values, cosine, sine_table):
    middle = values.shape[-1] // 2
    scaled = values * sine_table
    turned = jnp.concatenate([scaled[..., middle:], -scaled[..., :middle]], axis=-1)
    return values * cosine + turned


def inner_rows(left, right):
    return lax.dot_general(
        left, right, (((0,), (0,)), ((), ())), preferred_element_type=jnp.float32
    )


def outer_cols(left, right):
    return lax.dot_general(
        left, right, (((1,), (1,)), ((), ())), preferred_element_type=jnp.float32
    )


def norm_back(grad_normed, gain_wide, normed, inverse):
    scaled_grad = grad_normed * gain_wide
    return inverse * (scaled_grad - normed * jnp.mean(scaled_grad * normed, axis=1, keepdims=True))


def local(
    tokens,
    attn_gain,
    query_weight,
    key_weight,
    value_weight,
    output_weight,
    mlp_gain,
    gate_weight,
    up_weight,
    down_weight,
    out_grad,
    lengths,
):
    row_count = tokens.shape[0]
    tp_count = lax.axis_size("tp")
    block_rows = row_count * tp_count
    slot_total = block_rows * lax.axis_size("fsdp")
    longest = min(MAX_SPAN, slot_total // 2)
    reach_count = (longest - 2) // block_rows + 1
    window = (reach_count + 1) * block_rows
    front_rows = reach_count * block_rows
    block_index = lax.axis_index("fsdp")
    tp_index = lax.axis_index("tp")
    head_width = HEAD_DIM
    query_width = query_weight.shape[1]
    key_width = key_weight.shape[1]
    heads_here = query_width // head_width
    score_scale = head_width ** (-0.5)
    seq_count = lengths.shape[0]
    row_base = (block_index * tp_count + tp_index) * row_count
    my_slots = row_base + jnp.arange(row_count, dtype=jnp.int32)
    my_segments, my_positions = stream_layout(my_slots, lengths)
    valid_rows = (my_segments < seq_count)[:, None]
    gathered = (
        lax.all_gather(query_weight, "fsdp", axis=0, tiled=True),
        lax.all_gather(key_weight, "fsdp", axis=0, tiled=True),
        lax.all_gather(value_weight, "fsdp", axis=0, tiled=True),
        lax.all_gather(output_weight, "fsdp", axis=1, tiled=True),
        lax.all_gather(gate_weight, "fsdp", axis=0, tiled=True),
        lax.all_gather(up_weight, "fsdp", axis=0, tiled=True),
        lax.all_gather(down_weight, "fsdp", axis=1, tiled=True),
        lax.all_gather(attn_gain, "fsdp", axis=0, tiled=True),
        lax.all_gather(mlp_gain, "fsdp", axis=0, tiled=True),
    )
    (
        full_query,
        full_key,
        full_value,
        full_output,
        full_gate,
        full_up,
        full_down,
        gain_first,
        gain_second,
    ) = gathered
    w_inner = jnp.concatenate([full_query, full_key, full_value], axis=1)
    gain_first_wide = gain_first.astype(jnp.float32)
    gain_second_wide = gain_second.astype(jnp.float32)
    tokens_wide = tokens.astype(jnp.float32)
    inverse_first = lax.rsqrt(jnp.mean(tokens_wide * tokens_wide, axis=1, keepdims=True) + epsilon)
    normed_first = tokens_wide * inverse_first
    scaled_first = (normed_first * gain_first_wide).astype(jnp.bfloat16)
    rows_first = lax.all_gather(scaled_first, "tp", axis=0, tiled=True)
    projected = jnp.dot(rows_first, w_inner, preferred_element_type=jnp.float32)
    block_base = block_index * block_rows
    key_slots = block_base - front_rows + jnp.arange(window, dtype=jnp.int32)
    key_segments, key_positions = stream_layout(key_slots, lengths)
    query_segments = key_segments[front_rows:]
    block_positions = key_positions[front_rows:]
    cosine, sine_table = rotary_tables(block_positions, head_width)
    queries = rotate(
        projected[:, :query_width].reshape(block_rows, heads_here, head_width), cosine, sine_table
    ).astype(jnp.bfloat16)
    keys_local = rotate(
        projected[:, query_width : query_width + key_width].reshape(block_rows, 1, head_width),
        cosine,
        sine_table,
    )
    keys_local = keys_local.reshape(block_rows, head_width).astype(jnp.bfloat16)
    values_local = projected[:, query_width + key_width :].astype(jnp.bfloat16)
    pair_local = jnp.concatenate([keys_local, values_local], axis=1)
    pieces = []
    for offset in range(reach_count, 0, -1):
        pieces.append(passed_along(pair_local, "fsdp", offset))
    pair_window = jnp.concatenate(pieces + [pair_local], axis=0)
    key_window = pair_window[:, :head_width]
    value_window = pair_window[:, head_width:]
    key_seen = (key_segments[None, :] == query_segments[:, None]) & (
        key_positions[None, :] <= block_positions[:, None]
    )

    def head_scores(query_head):
        scores = outer_cols(query_head, key_window) * score_scale
        return jnp.where(key_seen, scores, -1e30)

    def head_forward(query_head):
        scores = head_scores(query_head)
        largest = jnp.max(scores, axis=1, keepdims=True)
        raised = jnp.exp(scores - largest)
        row_total = jnp.sum(raised, axis=1, keepdims=True)
        attn_probs = (raised / row_total).astype(jnp.bfloat16)
        head_out = jnp.dot(attn_probs, value_window, preferred_element_type=jnp.float32)
        return (head_out, (largest + jnp.log(row_total))[:, 0])

    query_heads = jnp.moveaxis(queries, 1, 0)
    head_outs, log_totals = lax.map(head_forward, query_heads)
    attended = jnp.moveaxis(head_outs, 0, 1).reshape(block_rows, query_width).astype(jnp.bfloat16)
    attn_share = lax.psum_scatter(
        jnp.dot(attended, full_output, preferred_element_type=jnp.float32).astype(jnp.bfloat16),
        "tp",
        scatter_dimension=0,
        tiled=True,
    ).astype(jnp.float32)
    middle = tokens_wide + attn_share
    inverse_second = lax.rsqrt(jnp.mean(middle * middle, axis=1, keepdims=True) + epsilon)
    normed_second = middle * inverse_second
    scaled_second = (normed_second * gain_second_wide).astype(jnp.bfloat16)
    rows_second = lax.all_gather(scaled_second, "tp", axis=0, tiled=True)
    gate_proj = jnp.dot(rows_second, full_gate, preferred_element_type=jnp.float32)
    up_proj = jnp.dot(rows_second, full_up, preferred_element_type=jnp.float32)
    gate_sigmoid = jax.nn.sigmoid(gate_proj)
    gate_active = gate_proj * gate_sigmoid
    hidden = (gate_active * up_proj).astype(jnp.bfloat16)
    mlp_share = lax.psum_scatter(
        jnp.dot(hidden, full_down, preferred_element_type=jnp.float32).astype(jnp.bfloat16),
        "tp",
        scatter_dimension=0,
        tiled=True,
    ).astype(jnp.float32)
    layer_out = jnp.where(valid_rows, middle + mlp_share, 0.0).astype(jnp.bfloat16)
    grad_rows = jnp.where(valid_rows, out_grad.astype(jnp.float32), 0.0)
    grad_low = grad_rows.astype(jnp.bfloat16)
    regathered = (
        lax.all_gather(query_weight, "fsdp", axis=0, tiled=True),
        lax.all_gather(key_weight, "fsdp", axis=0, tiled=True),
        lax.all_gather(value_weight, "fsdp", axis=0, tiled=True),
        lax.all_gather(output_weight, "fsdp", axis=1, tiled=True),
        lax.all_gather(gate_weight, "fsdp", axis=0, tiled=True),
        lax.all_gather(up_weight, "fsdp", axis=0, tiled=True),
        lax.all_gather(down_weight, "fsdp", axis=1, tiled=True),
        lax.all_gather(attn_gain, "fsdp", axis=0, tiled=True),
        lax.all_gather(mlp_gain, "fsdp", axis=0, tiled=True),
    )
    (
        full_query,
        full_key,
        full_value,
        full_output,
        full_gate,
        full_up,
        full_down,
        gain_first,
        gain_second,
    ) = regathered
    w_inner = jnp.concatenate([full_query, full_key, full_value], axis=1)
    grad_down_rows = lax.all_gather(grad_low, "tp", axis=0, tiled=True)
    grad_down_w = inner_rows(hidden, grad_down_rows)
    grad_hidden = outer_cols(grad_down_rows, full_down)
    grad_up_low = (grad_hidden * gate_active).astype(jnp.bfloat16)
    grad_gate_low = (
        grad_hidden * up_proj * gate_sigmoid * (1.0 + gate_proj * (1.0 - gate_sigmoid))
    ).astype(jnp.bfloat16)
    grad_gate_w = inner_rows(rows_second, grad_gate_low)
    grad_up_w = inner_rows(rows_second, grad_up_low)
    grad_second = lax.psum_scatter(
        (outer_cols(grad_gate_low, full_gate) + outer_cols(grad_up_low, full_up)).astype(
            jnp.bfloat16
        ),
        "tp",
        scatter_dimension=0,
        tiled=True,
    ).astype(jnp.float32)
    gain_second_part = jnp.sum(grad_second * normed_second, axis=0)
    grad_middle = grad_rows + norm_back(
        grad_second, gain_second_wide, normed_second, inverse_second
    )
    middle_low = grad_middle.astype(jnp.bfloat16)
    grad_attn_rows = lax.all_gather(middle_low, "tp", axis=0, tiled=True)
    grad_output_w = inner_rows(attended, grad_attn_rows)
    grad_attended = outer_cols(grad_attn_rows, full_output).astype(jnp.bfloat16)
    grad_heads = jnp.moveaxis(grad_attended.reshape(block_rows, heads_here, head_width), 1, 0)

    def head_backward(packed):
        query_head, grad_head, log_total = packed
        attn_probs = jnp.exp(head_scores(query_head) - log_total[:, None])
        probs_low = attn_probs.astype(jnp.bfloat16)
        grad_value_head = inner_rows(probs_low, grad_head)
        grad_probs = outer_cols(grad_head, value_window)
        grad_scores = (
            attn_probs * (grad_probs - jnp.sum(attn_probs * grad_probs, axis=1, keepdims=True))
        ).astype(jnp.bfloat16)
        grad_query_head = (
            jnp.dot(grad_scores, key_window, preferred_element_type=jnp.float32) * score_scale
        )
        grad_key_head = inner_rows(grad_scores, query_head) * score_scale
        return (grad_query_head, grad_key_head, grad_value_head)

    grad_query_heads, grad_key_heads, grad_value_heads = lax.map(
        head_backward, (query_heads, grad_heads, log_totals)
    )
    grad_pair = jnp.concatenate(
        [jnp.sum(grad_key_heads, axis=0), jnp.sum(grad_value_heads, axis=0)], axis=1
    )
    own_grad = grad_pair[front_rows:]
    for offset in range(1, reach_count + 1):
        piece_start = (reach_count - offset) * block_rows
        own_grad = own_grad + passed_along(
            grad_pair[piece_start : piece_start + block_rows].astype(jnp.bfloat16), "fsdp", -offset
        ).astype(jnp.float32)
    grad_key_lin = rotate_back(
        own_grad[:, :head_width].reshape(block_rows, 1, head_width), cosine, sine_table
    )
    grad_key_low = grad_key_lin.reshape(block_rows, head_width).astype(jnp.bfloat16)
    grad_value_low = own_grad[:, head_width:].astype(jnp.bfloat16)
    grad_query_lin = rotate_back(jnp.moveaxis(grad_query_heads, 0, 1), cosine, sine_table)
    grad_query_low = grad_query_lin.reshape(block_rows, query_width).astype(jnp.bfloat16)
    grad_inner = jnp.concatenate([grad_query_low, grad_key_low, grad_value_low], axis=1)
    grad_inner_w = inner_rows(rows_first, grad_inner)
    grad_first = lax.psum_scatter(
        outer_cols(grad_inner, w_inner).astype(jnp.bfloat16), "tp", scatter_dimension=0, tiled=True
    ).astype(jnp.float32)
    gain_first_part = jnp.sum(grad_first * normed_first, axis=0)
    tokens_grad = grad_middle + norm_back(grad_first, gain_first_wide, normed_first, inverse_first)
    reduced = (
        lax.psum_scatter(
            grad_inner_w[:, :query_width].astype(jnp.bfloat16),
            "fsdp",
            scatter_dimension=0,
            tiled=True,
        ).astype(jnp.float32),
        lax.psum_scatter(
            grad_inner_w[:, query_width : query_width + key_width].astype(jnp.bfloat16),
            "fsdp",
            scatter_dimension=0,
            tiled=True,
        ).astype(jnp.float32),
        lax.psum_scatter(
            grad_inner_w[:, query_width + key_width :].astype(jnp.bfloat16),
            "fsdp",
            scatter_dimension=0,
            tiled=True,
        ).astype(jnp.float32),
        lax.psum_scatter(
            grad_output_w.astype(jnp.bfloat16), "fsdp", scatter_dimension=1, tiled=True
        ).astype(jnp.float32),
        lax.psum_scatter(
            grad_gate_w.astype(jnp.bfloat16), "fsdp", scatter_dimension=0, tiled=True
        ).astype(jnp.float32),
        lax.psum_scatter(
            grad_up_w.astype(jnp.bfloat16), "fsdp", scatter_dimension=0, tiled=True
        ).astype(jnp.float32),
        lax.psum_scatter(
            grad_down_w.astype(jnp.bfloat16), "fsdp", scatter_dimension=1, tiled=True
        ).astype(jnp.float32),
        lax.psum_scatter(
            gain_first_part.astype(jnp.bfloat16), "fsdp", scatter_dimension=0, tiled=True
        ).astype(jnp.float32),
        lax.psum_scatter(
            gain_second_part.astype(jnp.bfloat16), "fsdp", scatter_dimension=0, tiled=True
        ).astype(jnp.float32),
    )
    gain_sums = lax.psum((reduced[7], reduced[8]), "tp")
    return (
        layer_out,
        tokens_grad,
        gain_sums[0],
        reduced[0],
        reduced[1],
        reduced[2],
        reduced[3],
        gain_sums[1],
        reduced[4],
        reduced[5],
        reduced[6],
    )


MESH = pl.DeviceIdType.MESH
CORE, ALONG_X, ALONG_Y = 1, 2, 4
PARTS = 4


def greet(partners):
    barrier = pltpu.get_barrier_semaphore()
    for partner in partners:
        pl.semaphore_signal(barrier, inc=1, device_id=partner, device_id_type=MESH)
    pl.semaphore_wait(barrier, len(partners))


def remote(source, target, sent, arrived, partner):
    return pltpu.make_async_remote_copy(
        src_ref=source,
        dst_ref=target,
        send_sem=sent,
        recv_sem=arrived,
        device_id=partner,
        device_id_type=MESH,
    )


def comm_params(number, vmem=None):
    return pltpu.CompilerParams(
        collective_id=number, has_side_effects=True, vmem_limit_bytes=vmem
    )


ANYWHERE = pl.BlockSpec(memory_space=pl.ANY)
IN_VMEM = pl.BlockSpec(memory_space=pltpu.VMEM)


def plane_gather(rows, number):
    height, width = rows.shape
    piece = height // PARTS

    def kernel(x_ref, o_ref, local_sem, sent, arrived):
        f = lax.axis_index("fsdp")
        t = lax.axis_index("tp")
        near = [(f ^ k, t) for k in (CORE, ALONG_X, ALONG_Y)]
        greet(near)
        keep = pltpu.make_async_copy(
            x_ref, o_ref.at[pl.ds(pl.multiple_of(f * height, height), height)], local_sem
        )
        keep.start()
        copies = []

        def send(owner, j, way, slot, first=False):
            place = o_ref.at[pl.ds(pl.multiple_of(owner * height + j * piece, piece), piece)]
            source = x_ref.at[pl.ds(j * piece, piece)] if first else place
            c = remote(source, place, sent.at[slot, j], arrived.at[slot, j], near[way])
            c.start()
            copies.append(c)
            return c

        along = {}
        for k in range(PARTS):
            jx, jy = k, (k + PARTS // 2) % PARTS
            along[1, jx] = send(f, jx, 1, 1, True)
            along[2, jy] = send(f, jy, 2, 2, True)
        own = [send(f, j, 0, 0, True) for j in range(PARTS)]
        passed = {}
        for k in range(PARTS):
            jx, jy = k, (k + PARTS // 2) % PARTS
            along[1, jx].wait_recv()
            if jx < PARTS // 2:
                passed[jx] = send(f ^ ALONG_X, jx, 2, 6)
            passed["x", jx] = send(f ^ ALONG_X, jx, 0, 3)
            along[2, jy].wait_recv()
            if jy >= PARTS // 2:
                passed[jy] = send(f ^ ALONG_Y, jy, 1, 6)
            passed["y", jy] = send(f ^ ALONG_Y, jy, 0, 4)
        for k in range(PARTS // 2):
            for j in (k, k + PARTS // 2):
                passed[j].wait_recv()
                passed["d", j] = send(f ^ ALONG_X ^ ALONG_Y, j, 0, 5)
        for j in range(PARTS):
            own[j].wait_recv()
            for kind in "xyd":
                passed[kind, j].wait_recv()
        for c in copies:
            c.wait_send()
        keep.wait()

    return pl.pallas_call(
        kernel,
        out_shape=jax.ShapeDtypeStruct((8 * height, width), rows.dtype),
        in_specs=[ANYWHERE],
        out_specs=ANYWHERE,
        scratch_shapes=[
            pltpu.SemaphoreType.DMA,
            pltpu.SemaphoreType.DMA((7, PARTS)),
            pltpu.SemaphoreType.DMA((7, PARTS)),
        ],
        compiler_params=comm_params(number),
        name=f"plane_gather_{number}",
    )(rows)


def plane_sum(parts, number):
    total, width = parts.shape
    height = total // 8
    half = height // 2

    def kernel(p_ref, o_ref, ra, s, rx, ry, rlast, sent, arrived):
        f = lax.axis_index("fsdp")
        t = lax.axis_index("tp")
        core, along_x, along_y = [(f ^ k, t) for k in (CORE, ALONG_X, ALONG_Y)]
        greet((core, along_x, along_y))
        masks = (ALONG_X ^ ALONG_Y, ALONG_X, ALONG_Y, 0)

        def chunk(owner):
            return p_ref.at[pl.ds(pl.multiple_of(owner * height, height), height)]

        copies = []

        def send(source, target, slot, partner):
            c = remote(source, target, sent.at[slot], arrived.at[slot], partner)
            c.start()
            copies.append(c)
            return c

        first = [send(chunk(f ^ CORE ^ m), ra.at[i], i, core) for i, m in enumerate(masks)]
        top, low = pl.ds(0, half), pl.ds(half, half)

        def gather_own(i):
            first[i].wait_recv()
            s[i] = (
                chunk(f ^ masks[i])[...].astype(jnp.float32) + ra[i].astype(jnp.float32)
            ).astype(jnp.bfloat16)

        gather_own(0)
        x0 = send(s.at[0, top], rx.at[0], 4, along_x)
        y0 = send(s.at[0, low], ry.at[0], 5, along_y)
        gather_own(1)
        x1 = send(s.at[1, top], rx.at[1], 6, along_x)
        gather_own(2)
        y1 = send(s.at[2, low], ry.at[1], 7, along_y)
        gather_own(3)
        x0.wait_recv()
        s[2, top] = (s[2, top].astype(jnp.float32) + rx[0].astype(jnp.float32)).astype(jnp.bfloat16)
        y2 = send(s.at[2, top], rlast.at[0], 8, along_y)
        y0.wait_recv()
        s[1, low] = (s[1, low].astype(jnp.float32) + ry[0].astype(jnp.float32)).astype(jnp.bfloat16)
        x2 = send(s.at[1, low], rlast.at[1], 9, along_x)
        x1.wait_recv()
        o_ref[top] = s[3, top].astype(jnp.float32) + rx[1].astype(jnp.float32)
        y1.wait_recv()
        o_ref[low] = s[3, low].astype(jnp.float32) + ry[1].astype(jnp.float32)
        y2.wait_recv()
        o_ref[top] += rlast[0].astype(jnp.float32)
        x2.wait_recv()
        o_ref[low] += rlast[1].astype(jnp.float32)
        for c in copies:
            c.wait_send()

    return pl.pallas_call(
        kernel,
        out_shape=jax.ShapeDtypeStruct((height, width), jnp.float32),
        in_specs=[IN_VMEM],
        out_specs=IN_VMEM,
        scratch_shapes=[
            pltpu.VMEM((4, height, width), jnp.bfloat16),
            pltpu.VMEM((4, height, width), jnp.bfloat16),
            pltpu.VMEM((2, half, width), jnp.bfloat16),
            pltpu.VMEM((2, half, width), jnp.bfloat16),
            pltpu.VMEM((2, half, width), jnp.bfloat16),
            pltpu.SemaphoreType.DMA((10,)),
            pltpu.SemaphoreType.DMA((10,)),
        ],
        compiler_params=comm_params(number, 48 << 20),
        name=f"plane_sum_{number}",
    )(parts)


def plane_exchange(arrays, out_shapes, slices, number):
    count = len(arrays)
    pairs = len(slices(0, 0, None, None))

    def kernel(*refs):
        sources, targets = refs[:count], refs[count : count + len(out_shapes)]
        local_sem, sent, arrived = refs[-3:]
        f = lax.axis_index("fsdp")
        t = lax.axis_index("tp")
        greet([(f ^ k, t) for k in range(1, 8)])
        copies = []
        for k in (6, 7, 2, 4, 3, 5, 1):
            j = f ^ k
            for i, (source, target) in enumerate(slices(j, f, sources, targets)):
                c = remote(source, target, sent.at[k, i], arrived.at[k, i], (j, t))
                c.start()
                copies.append(c)
        kept = []
        for i, (source, target) in enumerate(slices(f, f, sources, targets)):
            c = pltpu.make_async_copy(source, target, local_sem.at[i])
            c.start()
            kept.append(c)
        for c in kept + copies:
            c.wait()

    return pl.pallas_call(
        kernel,
        out_shape=[jax.ShapeDtypeStruct(shape, jnp.bfloat16) for shape in out_shapes],
        in_specs=[ANYWHERE] * count,
        out_specs=[ANYWHERE] * len(out_shapes),
        scratch_shapes=[
            pltpu.SemaphoreType.DMA((pairs,)),
            pltpu.SemaphoreType.DMA((8, pairs)),
            pltpu.SemaphoreType.DMA((8, pairs)),
        ],
        compiler_params=comm_params(number),
        name=f"plane_exchange_{number}",
    )(*arrays)


def columns(index, width):
    return pl.ds(pl.multiple_of(index * width, width), width)


def pair_gather(pair, number):
    rows, width = pair.shape
    half = rows // 2

    def kernel(x_ref, o_ref, local_sem, sent, arrived):
        f = lax.axis_index("fsdp")
        t = lax.axis_index("tp")
        mine = pl.ds(pl.multiple_of(lax.rem(f, 2) * half, half), half)
        others = [(f, lax.rem(t + k, 4)) for k in (1, 2, 3)]
        greet(others + [(f ^ CORE, t)])
        keep = pltpu.make_async_copy(x_ref, o_ref.at[t], local_sem)
        keep.start()
        out = []
        for k in (2, 1, 3):
            c = remote(
                x_ref.at[mine], o_ref.at[t, mine], sent.at[k], arrived.at[k], (f, lax.rem(t + k, 4))
            )
            c.start()
            out.append((k, c))
        on = []
        for k, c in sorted(out, key=lambda item: item[0]):
            c.wait_recv()
            place = o_ref.at[lax.rem(t + 4 - k, 4), mine]
            d = remote(place, place, sent.at[3 + k], arrived.at[3 + k], (f ^ CORE, t))
            d.start()
            on.append(d)
        for d in on:
            d.wait()
        for k, c in out:
            c.wait_send()
        keep.wait()

    return pl.pallas_call(
        kernel,
        out_shape=jax.ShapeDtypeStruct((4, rows, width), pair.dtype),
        in_specs=[ANYWHERE],
        out_specs=ANYWHERE,
        scratch_shapes=[
            pltpu.SemaphoreType.DMA,
            pltpu.SemaphoreType.DMA((7,)),
            pltpu.SemaphoreType.DMA((7,)),
        ],
        compiler_params=comm_params(number),
        name=f"pair_gather_{number}",
    )(pair)


def pair_sum(parts, number):
    _, chunks, height, width = parts.shape
    half = chunks // 2

    def kernel(p_ref, o_ref, ra, s, rz, sent, arrived):
        f = lax.axis_index("fsdp")
        t = lax.axis_index("tp")
        side = lax.rem(f, 2)
        mine, other = pl.ds(side * half, half), pl.ds((1 - side) * half, half)
        core = (f ^ CORE, t)
        greet([(f, lax.rem(t + k, 4)) for k in (1, 2, 3)] + [core])
        first = []
        for k in (2, 1, 3, 0):
            plane = lax.rem(t + k, 4)
            c = remote(p_ref.at[plane, other], ra.at[k], sent.at[k], arrived.at[k], core)
            c.start()
            first.append((k, c))
        out = []
        for k, c in first:
            c.wait_recv()
            plane = lax.rem(t + k, 4)
            total = p_ref[plane, mine].astype(jnp.float32) + ra[k].astype(jnp.float32)
            if k:
                s[k] = total.astype(jnp.bfloat16)
                d = remote(s.at[k], rz.at[k], sent.at[3 + k], arrived.at[3 + k], (f, plane))
                d.start()
                out.append((k, d))
            else:
                o_ref[mine] = total
        for k, d in out:
            d.wait_recv()
            o_ref[mine] += rz[k].astype(jnp.float32)
        back = remote(o_ref.at[mine], o_ref.at[mine], sent.at[7], arrived.at[7], core)
        back.start()
        back.wait()
        for k, c in first + out:
            c.wait_send()

    return pl.pallas_call(
        kernel,
        out_shape=jax.ShapeDtypeStruct((chunks, height, width), jnp.float32),
        in_specs=[IN_VMEM],
        out_specs=IN_VMEM,
        scratch_shapes=[
            pltpu.VMEM((4, half, height, width), jnp.bfloat16),
            pltpu.VMEM((4, half, height, width), jnp.bfloat16),
            pltpu.VMEM((4, half, height, width), jnp.bfloat16),
            pltpu.SemaphoreType.DMA((8,)),
            pltpu.SemaphoreType.DMA((8,)),
        ],
        compiler_params=comm_params(number, 32 << 20),
        name=f"pair_sum_{number}",
    )(parts)


def dot_nn(left, right):
    return jnp.dot(left, right, preferred_element_type=jnp.float32)


def seen_keys(begin_row, first_key, first_query, shape):
    key_slot = first_key + lax.broadcasted_iota(jnp.int32, shape, 0)
    query_slot = first_query + lax.broadcasted_iota(jnp.int32, (1, shape[1]), 1)
    return (key_slot <= query_slot) & (key_slot >= begin_row)


def head_lanes(block, heads):
    return jnp.concatenate([block[h * HEAD_DIM : (h + 1) * HEAD_DIM] for h in range(heads)], axis=1)


def attend(info, begins, queries, pair):
    depth, slots = queries.shape
    heads = depth // HEAD_DIM
    size = slots // 8
    span = heads * size

    def kernel(info_ref, begin_ref, q_ref, kv_ref, o_ref, l_ref, q_s, m_s, t_s, a_s):
        f = pl.program_id(0)
        low, middle, own = info_ref[f, 0], info_ref[f, 1], info_ref[f, 2]
        q_s[...] = head_lanes(q_ref[...], heads)
        m_s[...] = jnp.full_like(m_s, -1e30)
        t_s[...] = jnp.zeros_like(t_s)
        a_s[...] = jnp.zeros_like(a_s)

        def step(g, masked):
            block = kv_ref[lax.rem(g, 4), pl.ds(pl.multiple_of(lax.div(g, 4) * size, size), size)]
            keys, values = block[:, :HEAD_DIM], block[:, HEAD_DIM:]
            value_cols = values.astype(jnp.float32).T.astype(jnp.bfloat16)
            if masked:
                seen = seen_keys(begin_ref[0], g * size, own * size, (size, size))
            for h in range(heads):
                lanes = pl.ds(h * size, size)
                scores = dot_nn(keys, q_s[:, lanes])
                if masked:
                    scores = jnp.where(seen, scores, -1e30)
                largest = m_s[:, lanes]
                higher = jnp.maximum(largest, jnp.max(scores, axis=0, keepdims=True))
                raised = jnp.exp(scores - higher)
                fade = jnp.exp(largest - higher)
                m_s[:, lanes] = higher
                t_s[:, lanes] = t_s[:, lanes] * fade + jnp.sum(raised, axis=0, keepdims=True)
                a_s[:, lanes] = a_s[:, lanes] * fade + dot_nn(
                    value_cols, raised.astype(jnp.bfloat16)
                )

        def masked_step(g, carry):
            step(g, True)
            return carry

        def plain_step(g, carry):
            step(g, False)
            return carry

        step(own, True)
        lax.fori_loop(low, middle, masked_step, 0)
        lax.fori_loop(middle, own, plain_step, 0)
        result = a_s[...] / t_s[...]
        for h in range(heads):
            o_ref[h * HEAD_DIM : (h + 1) * HEAD_DIM] = result[:, h * size : (h + 1) * size].astype(
                jnp.bfloat16
            )
        l_ref[0] = m_s[...] + jnp.log(t_s[...])

    return pl.pallas_call(
        kernel,
        grid_spec=pltpu.PrefetchScalarGridSpec(
            num_scalar_prefetch=1,
            grid=(8,),
            in_specs=[
                pl.BlockSpec((1, 1, size), lambda f, info: (f, 0, 0)),
                pl.BlockSpec((depth, size), lambda f, info: (0, f)),
                pl.BlockSpec((4, slots, 2 * HEAD_DIM), lambda f, info: (0, 0, 0)),
            ],
            out_specs=[
                pl.BlockSpec((depth, size), lambda f, info: (0, f)),
                pl.BlockSpec((1, 1, span), lambda f, info: (f, 0, 0)),
            ],
            scratch_shapes=[
                pltpu.VMEM((HEAD_DIM, span), jnp.bfloat16),
                pltpu.VMEM((1, span), jnp.float32),
                pltpu.VMEM((1, span), jnp.float32),
                pltpu.VMEM((HEAD_DIM, span), jnp.float32),
            ],
        ),
        out_shape=[
            jax.ShapeDtypeStruct((depth, slots), jnp.bfloat16),
            jax.ShapeDtypeStruct((8, 1, span), jnp.float32),
        ],
        compiler_params=pltpu.CompilerParams(vmem_limit_bytes=40 << 20),
        cost_estimate=pl.CostEstimate(
            flops=30_000_000_000, bytes_accessed=6_000_000, transcendentals=16_000_000
        ),
        name="attend",
    )(info, begins, queries, pair)


def attend_back(info, begins, queries, pair, outputs, grads, totals):
    depth, slots = queries.shape
    heads = depth // HEAD_DIM
    size = slots // 8
    span = heads * size

    def kernel(
        info_ref, begin_ref, q_ref, kv_ref, o_ref, g_ref, l_ref, dq_ref, dkv_ref, q_s, g_s, d_s, a_s, w_s
    ):
        f = pl.program_id(0)
        low, middle, own = info_ref[f, 0], info_ref[f, 1], info_ref[f, 2]

        @pl.when(f == 0)
        def _():
            w_s[...] = jnp.zeros_like(w_s)

        q_s[...] = head_lanes(q_ref[...], heads)
        g_s[...] = head_lanes(g_ref[...], heads)
        out_lanes = head_lanes(o_ref[...], heads).astype(jnp.float32)
        d_s[...] = jnp.sum(out_lanes * g_s[...].astype(jnp.float32), axis=0, keepdims=True)
        a_s[...] = jnp.zeros_like(a_s)

        def step(g, masked):
            block = kv_ref[lax.rem(g, 4), pl.ds(pl.multiple_of(lax.div(g, 4) * size, size), size)]
            keys, values = block[:, :HEAD_DIM], block[:, HEAD_DIM:]
            key_cols = keys.astype(jnp.float32).T.astype(jnp.bfloat16)
            if masked:
                seen = seen_keys(begin_ref[0], g * size, own * size, (size, size))
            grad_keys = jnp.zeros((HEAD_DIM, size), jnp.float32)
            grad_values = jnp.zeros((HEAD_DIM, size), jnp.float32)
            for h in range(heads):
                lanes = pl.ds(h * size, size)
                query, grad = q_s[:, lanes], g_s[:, lanes]
                raised = jnp.exp(dot_nn(keys, query) - l_ref[0, :, lanes])
                if masked:
                    raised = jnp.where(seen, raised, 0.0)
                grad_probs = dot_nn(values, grad)
                scores = (raised * (grad_probs - d_s[:, lanes])).astype(jnp.bfloat16)
                grad_values += outer_cols(grad, raised.astype(jnp.bfloat16))
                grad_keys += outer_cols(query, scores)
                a_s[:, lanes] += dot_nn(key_cols, scores)
            w_s[lax.rem(g, 4), lax.div(g, 4), :HEAD_DIM] += grad_keys
            w_s[lax.rem(g, 4), lax.div(g, 4), HEAD_DIM:] += grad_values

        def masked_step(g, carry):
            step(g, True)
            return carry

        def plain_step(g, carry):
            step(g, False)
            return carry

        step(own, True)
        lax.fori_loop(low, middle, masked_step, 0)
        lax.fori_loop(middle, own, plain_step, 0)
        result = a_s[...] * HEAD_DIM ** (-0.5)
        for h in range(heads):
            dq_ref[h * HEAD_DIM : (h + 1) * HEAD_DIM] = result[:, h * size : (h + 1) * size]

        @pl.when(f == 7)
        def _():
            dkv_ref[...] = w_s[...].astype(jnp.bfloat16)

    return pl.pallas_call(
        kernel,
        grid_spec=pltpu.PrefetchScalarGridSpec(
            num_scalar_prefetch=1,
            grid=(8,),
            in_specs=[
                pl.BlockSpec((1, 1, size), lambda f, info: (f, 0, 0)),
                pl.BlockSpec((depth, size), lambda f, info: (0, f)),
                pl.BlockSpec((4, slots, 2 * HEAD_DIM), lambda f, info: (0, 0, 0)),
                pl.BlockSpec((depth, size), lambda f, info: (0, f)),
                pl.BlockSpec((depth, size), lambda f, info: (0, f)),
                pl.BlockSpec((1, 1, span), lambda f, info: (f, 0, 0)),
            ],
            out_specs=[
                pl.BlockSpec((depth, size), lambda f, info: (0, f)),
                pl.BlockSpec((4, 8, 2 * HEAD_DIM, size), lambda f, info: (0, 0, 0, 0)),
            ],
            scratch_shapes=[
                pltpu.VMEM((HEAD_DIM, span), jnp.bfloat16),
                pltpu.VMEM((HEAD_DIM, span), jnp.bfloat16),
                pltpu.VMEM((1, span), jnp.float32),
                pltpu.VMEM((HEAD_DIM, span), jnp.float32),
                pltpu.VMEM((4, 8, 2 * HEAD_DIM, size), jnp.float32),
            ],
        ),
        out_shape=[
            jax.ShapeDtypeStruct((depth, slots), jnp.float32),
            jax.ShapeDtypeStruct((4, 8, 2 * HEAD_DIM, size), jnp.bfloat16),
        ],
        compiler_params=pltpu.CompilerParams(vmem_limit_bytes=40 << 20),
        cost_estimate=pl.CostEstimate(
            flops=70_000_000_000, bytes_accessed=10_000_000, transcendentals=16_000_000
        ),
        name="attend_back",
    )(info, begins, queries, pair, outputs, grads, totals)


def turn(values, cosine, sine_table):
    heads = values.shape[0] // HEAD_DIM
    split = values.reshape(heads, 2, HEAD_DIM // 2, values.shape[1])
    first, second = split[:, 0], split[:, 1]
    turned = jnp.stack(
        [first * cosine - second * sine_table, second * cosine + first * sine_table], axis=1
    )
    return turned.reshape(values.shape)


def turn_back(values, cosine, sine_table):
    return turn(values, cosine, -sine_table)


def segment_begins(slots, lengths):
    seq_index = jnp.arange(lengths.shape[0], dtype=jnp.int32)
    ends = jnp.sum(jnp.where(seq_index[:, None] >= seq_index[None, :], lengths[None, :], 0), axis=1)
    passed = slots[:, None] >= ends[None, :]
    begins = jnp.sum(jnp.where(passed, lengths[None, :], 0), axis=1)
    return begins, slots < ends[-1]


def local_plane(
    tokens,
    attn_gain,
    query_weight,
    key_weight,
    value_weight,
    output_weight,
    mlp_gain,
    gate_weight,
    up_weight,
    down_weight,
    out_grad,
    lengths,
):
    size, width = tokens.shape
    f = lax.axis_index("fsdp")
    t = lax.axis_index("tp")
    block = query_weight.shape[0]
    head_rows = query_weight.shape[1] // 2
    units = gate_weight.shape[1] // 8
    bf16, f32 = jnp.bfloat16, jnp.float32

    attn_stack = jnp.concatenate(
        [query_weight.T, key_weight.T, value_weight.T, output_weight], axis=0
    )
    attn_all = lax.all_gather(attn_stack, "tp", axis=0, tiled=False)
    hidden_parts = [w.reshape(8, units, block) for w in (gate_weight.T, up_weight.T, down_weight)]

    def hidden_slices(j, f, sources, targets):
        if sources is None:
            return [None] * 3
        return [(s.at[j], o.at[:, columns(f, block)]) for s, o in zip(sources, targets)]

    gate_part, up_part, down_part = plane_exchange(
        hidden_parts, [(units, width)] * 3, hidden_slices, 1
    )
    gate_rows = lax.all_gather(gate_part, "tp", axis=0, tiled=True)
    up_rows = lax.all_gather(up_part, "tp", axis=0, tiled=True)
    down_rows = lax.all_gather(down_part, "tp", axis=0, tiled=True)

    gains = lax.all_gather(jnp.stack([attn_gain, mlp_gain]), "fsdp", axis=0, tiled=False)
    gains = jnp.moveaxis(gains, 0, 1).reshape(2, width).astype(f32)
    gain_first, gain_second = gains[0:1], gains[1:2]

    my_slots = (f * 4 + t) * size + jnp.arange(size, dtype=jnp.int32)
    _, my_valid = segment_begins(my_slots, lengths)
    valid_rows = my_valid[:, None]
    chunk_index = jnp.arange(8, dtype=jnp.int32) * 4 + t
    plane_slots = (chunk_index[:, None] * size + jnp.arange(size, dtype=jnp.int32)[None, :]).reshape(-1)
    begins, plane_valid = segment_begins(plane_slots, lengths)
    positions = jnp.where(plane_valid, plane_slots - begins, 0)
    begins = begins.reshape(8, 1, size)
    info = jnp.stack(
        [
            begins[:, 0, 0] // size,
            jnp.minimum((begins[:, 0, size - 1] + size - 1) // size, chunk_index),
            chunk_index,
        ],
        axis=1,
    ).astype(jnp.int32)
    ladder = jnp.arange(HEAD_DIM // 2).astype(f32)
    frequency = 10000.0 ** (-2.0 * ladder / HEAD_DIM)
    angles = positions.astype(f32)[None, :] * frequency[:, None]
    cosine, sine_table = jnp.cos(angles), jnp.sin(angles)

    tokens_wide = tokens.astype(f32)
    inverse_first = lax.rsqrt(jnp.mean(tokens_wide * tokens_wide, axis=1, keepdims=True) + epsilon)
    normed_first = tokens_wide * inverse_first
    scaled_first = (normed_first * gain_first).astype(bf16)
    rows_first = plane_gather(scaled_first, 2)

    def attn_slices(j, f, sources, targets):
        if sources is None:
            return [None] * 3
        quarter, side = lax.div(j, 2), lax.rem(j, 2)
        (source,), (target,) = sources, targets
        place = columns(f, block)
        pair_rows = 2 * HEAD_DIM
        return [
            (
                source.at[quarter, pl.ds(pl.multiple_of(side * head_rows, head_rows), head_rows)],
                target.at[pl.ds(0, head_rows), place],
            ),
            (
                source.at[quarter, pl.ds(2 * head_rows, pair_rows)],
                target.at[pl.ds(head_rows, pair_rows), place],
            ),
            (
                source.at[
                    quarter,
                    pl.ds(
                        pl.multiple_of(2 * head_rows + pair_rows + side * head_rows, 2 * HEAD_DIM),
                        head_rows,
                    ),
                ],
                target.at[pl.ds(head_rows + pair_rows, head_rows), place],
            ),
        ]

    (attn_rows,) = plane_exchange(
        [attn_all], [(2 * head_rows + 2 * HEAD_DIM, width)], attn_slices, 3
    )
    inner_end = head_rows + 2 * HEAD_DIM
    inner_rows_w, output_rows = attn_rows[:inner_end], attn_rows[inner_end:]
    projected = outer_cols(inner_rows_w, rows_first)
    queries = (turn(projected[:head_rows], cosine, sine_table).astype(bf16) * 0.125).astype(bf16)
    keys = turn(projected[head_rows : head_rows + HEAD_DIM], cosine, sine_table)
    pair_local = jnp.concatenate([keys, projected[head_rows + HEAD_DIM :]], axis=0).astype(bf16).T
    pair = pair_gather(pair_local, 4)
    attended, totals = attend(info, begins, queries, pair)
    attn_share = plane_sum(inner_rows(attended, output_rows).astype(bf16), 5)
    middle = tokens_wide + attn_share
    inverse_second = lax.rsqrt(jnp.mean(middle * middle, axis=1, keepdims=True) + epsilon)
    normed_second = middle * inverse_second
    scaled_second = (normed_second * gain_second).astype(bf16)
    rows_second = plane_gather(scaled_second, 6)

    gate_proj = outer_cols(gate_rows, rows_second)
    up_proj = outer_cols(up_rows, rows_second)
    gate_sigmoid = jax.nn.sigmoid(gate_proj)
    gate_active = gate_proj * gate_sigmoid
    hidden = (gate_active * up_proj).astype(bf16)
    mlp_share = plane_sum(inner_rows(hidden, down_rows).astype(bf16), 7)
    layer_out = jnp.where(valid_rows, middle + mlp_share, 0.0).astype(bf16)

    grad_rows_own = jnp.where(valid_rows, out_grad.astype(f32), 0.0)
    grad_rows = plane_gather(grad_rows_own.astype(bf16), 8)
    grad_down_w = dot_nn(hidden, grad_rows).astype(bf16)
    grad_hidden = outer_cols(down_rows, grad_rows)
    grad_up_low = (grad_hidden * gate_active).astype(bf16)
    grad_gate_low = (
        grad_hidden * up_proj * gate_sigmoid * (1.0 + gate_proj * (1.0 - gate_sigmoid))
    ).astype(bf16)
    grad_gate_w = dot_nn(grad_gate_low, rows_second).astype(bf16)
    grad_up_w = dot_nn(grad_up_low, rows_second).astype(bf16)
    grad_second = plane_sum(
        (inner_rows(grad_gate_low, gate_rows) + inner_rows(grad_up_low, up_rows)).astype(bf16), 9
    )
    hidden_grads = [
        lax.psum_scatter(g, "tp", scatter_dimension=0, tiled=True)
        for g in (grad_down_w, grad_gate_w, grad_up_w)
    ]
    gain_second_part = jnp.sum(grad_second * normed_second, axis=0)
    grad_middle = grad_rows_own + norm_back(grad_second, gain_second, normed_second, inverse_second)
    middle_rows = plane_gather(grad_middle.astype(bf16), 10)
    grad_output_w = dot_nn(attended, middle_rows).astype(bf16)
    grad_attended = outer_cols(output_rows, middle_rows).astype(bf16)
    grad_queries, grad_pair_parts = attend_back(
        info, begins, queries, pair, attended, grad_attended, totals
    )
    grad_pair = pair_sum(grad_pair_parts, 11)
    grad_pair = jnp.moveaxis(grad_pair, 0, 1).reshape(2 * HEAD_DIM, 8 * size)
    grad_query_low = turn_back(grad_queries, cosine, sine_table).astype(bf16)
    grad_key_low = turn_back(grad_pair[:HEAD_DIM], cosine, sine_table)
    first_core = lax.rem(f, 2) == 0
    grad_single = jnp.where(first_core, grad_key_low, grad_pair[HEAD_DIM:]).astype(bf16)
    grad_inner = jnp.concatenate([grad_query_low, grad_single], axis=0)
    single_rows = jnp.where(
        first_core,
        attn_rows[head_rows : head_rows + HEAD_DIM],
        attn_rows[head_rows + HEAD_DIM : inner_end],
    )
    single_weights = jnp.concatenate([attn_rows[:head_rows], single_rows], axis=0)
    grad_first = plane_sum(inner_rows(grad_inner, single_weights).astype(bf16), 12)
    grad_inner_w = dot_nn(grad_inner, rows_first).astype(bf16)
    gain_first_part = jnp.sum(grad_first * normed_first, axis=0)
    tokens_grad = grad_middle + norm_back(grad_first, gain_first, normed_first, inverse_first)

    single_end = head_rows + HEAD_DIM
    attn_grads = jnp.concatenate([grad_inner_w, grad_output_w], axis=0)

    def attn_back(j, f, sources, targets):
        if sources is None:
            return [None]
        return [(sources[0].at[:, columns(j, block)], targets[0].at[f])]

    (attn_parts,) = plane_exchange(
        [attn_grads], [(8, single_end + head_rows, block)], attn_back, 13
    )
    attn_own = lax.psum_scatter(
        attn_parts.reshape(4 * 2 * (single_end + head_rows), block),
        "tp",
        scatter_dimension=0,
        tiled=True,
    ).reshape(2, single_end + head_rows, block)

    def hidden_back(j, f, sources, targets):
        if sources is None:
            return [None] * 3
        return [(s.at[:, columns(j, block)], o.at[f]) for s, o in zip(sources, targets)]

    own_down, own_gate, own_up = plane_exchange(
        hidden_grads, [(8, units, block)] * 3, hidden_back, 14
    )
    gain_sums = lax.psum(jnp.stack([gain_first_part, gain_second_part]), ("fsdp", "tp"))
    gain_sums = lax.dynamic_slice_in_dim(gain_sums, f * block, block, 1)
    return (
        layer_out,
        tokens_grad,
        gain_sums[0],
        attn_own[:, :head_rows].reshape(2 * head_rows, block).T.astype(f32),
        attn_own[0, head_rows:single_end].T.astype(f32),
        attn_own[1, head_rows:single_end].T.astype(f32),
        attn_own[:, single_end:].reshape(2 * head_rows, block).astype(f32),
        gain_sums[1],
        own_gate.reshape(8 * units, block).T.astype(f32),
        own_up.reshape(8 * units, block).T.astype(f32),
        own_down.reshape(8 * units, block).astype(f32),
    )


def solution(mesh):
    plane = dict(mesh.shape) == {"fsdp": 8, "tp": 4}
    body = local_plane if plane else local
    in_specs = (
        P(("fsdp", "tp"), None),
        P("fsdp"),
        P("fsdp", "tp"),
        P("fsdp", "tp"),
        P("fsdp", "tp"),
        P("tp", "fsdp"),
        P("fsdp"),
        P("fsdp", "tp"),
        P("fsdp", "tp"),
        P("tp", "fsdp"),
        P(("fsdp", "tp"), None),
        P(),
    )
    out_specs = (
        P(("fsdp", "tp"), None),
        P(("fsdp", "tp"), None),
        P("fsdp"),
        P("fsdp", "tp"),
        P("fsdp", "tp"),
        P("fsdp", "tp"),
        P("tp", "fsdp"),
        P("fsdp"),
        P("fsdp", "tp"),
        P("fsdp", "tp"),
        P("tp", "fsdp"),
    )
    return jax.shard_map(body, mesh=mesh, in_specs=in_specs, out_specs=out_specs, check_vma=False)
```

```python
import jax
import jax.numpy as jnp
from jax import lax
from jax.experimental import pallas as pl
from jax.experimental.pallas import tpu as pltpu
from jax.sharding import PartitionSpec as P

HEAD_DIM = 64
MAX_SPAN = 4096


epsilon = 1e-05


def passed_along(block, axis, distance):
    devices = range(lax.axis_size(axis))
    route = [(i - distance, i) for i in devices if i - distance in devices]
    return lax.ppermute(block, axis, route)


def stream_layout(slots, lengths):
    seq_count = lengths.shape[0]
    seq_index = jnp.arange(seq_count, dtype=jnp.int32)
    ends = jnp.sum(jnp.where(seq_index[:, None] >= seq_index[None, :], lengths[None, :], 0), axis=1)
    starts = ends - lengths
    segment = jnp.sum((slots[:, None] >= ends[None, :]).astype(jnp.int32), axis=1)
    start_of = jnp.sum(
        jnp.where(segment[:, None] == seq_index[None, :], starts[None, :], 0), axis=1
    )
    position = jnp.where((segment < seq_count) & (slots >= 0), slots - start_of, 0)
    segment = jnp.where(slots < 0, -1, segment)
    return (segment, position)


def rotary_tables(positions, head_width):
    ladder = jnp.arange(head_width // 2).astype(jnp.float32)
    frequency = 10000.0 ** (-2.0 * ladder / head_width)
    angle_half = positions.astype(jnp.float32)[:, None] * frequency[None, :]
    angles = jnp.concatenate([angle_half, angle_half], axis=1)
    return (jnp.cos(angles)[:, None, :], jnp.sin(angles)[:, None, :])


def rotate(values, cosine, sine_table):
    middle = values.shape[-1] // 2
    turned = jnp.concatenate([-values[..., middle:], values[..., :middle]], axis=-1)
    return values * cosine + turned * sine_table


def rotate_back(values, cosine, sine_table):
    middle = values.shape[-1] // 2
    scaled = values * sine_table
    turned = jnp.concatenate([scaled[..., middle:], -scaled[..., :middle]], axis=-1)
    return values * cosine + turned


def inner_rows(left, right):
    return lax.dot_general(
        left, right, (((0,), (0,)), ((), ())), preferred_element_type=jnp.float32
    )


def outer_cols(left, right):
    return lax.dot_general(
        left, right, (((1,), (1,)), ((), ())), preferred_element_type=jnp.float32
    )


def norm_back(grad_normed, gain_wide, normed, inverse):
    scaled_grad = grad_normed * gain_wide
    return inverse * (scaled_grad - normed * jnp.mean(scaled_grad * normed, axis=1, keepdims=True))


def local(
    tokens,
    attn_gain,
    query_weight,
    key_weight,
    value_weight,
    output_weight,
    mlp_gain,
    gate_weight,
    up_weight,
    down_weight,
    out_grad,
    lengths,
):
    row_count = tokens.shape[0]
    tp_count = lax.axis_size("tp")
    block_rows = row_count * tp_count
    slot_total = block_rows * lax.axis_size("fsdp")
    longest = min(MAX_SPAN, slot_total // 2)
    reach_count = (longest - 2) // block_rows + 1
    window = (reach_count + 1) * block_rows
    front_rows = reach_count * block_rows
    block_index = lax.axis_index("fsdp")
    tp_index = lax.axis_index("tp")
    head_width = HEAD_DIM
    query_width = query_weight.shape[1]
    key_width = key_weight.shape[1]
    heads_here = query_width // head_width
    score_scale = head_width ** (-0.5)
    seq_count = lengths.shape[0]
    row_base = (block_index * tp_count + tp_index) * row_count
    my_slots = row_base + jnp.arange(row_count, dtype=jnp.int32)
    my_segments, my_positions = stream_layout(my_slots, lengths)
    valid_rows = (my_segments < seq_count)[:, None]
    gathered = (
        lax.all_gather(query_weight, "fsdp", axis=0, tiled=True),
        lax.all_gather(key_weight, "fsdp", axis=0, tiled=True),
        lax.all_gather(value_weight, "fsdp", axis=0, tiled=True),
        lax.all_gather(output_weight, "fsdp", axis=1, tiled=True),
        lax.all_gather(gate_weight, "fsdp", axis=0, tiled=True),
        lax.all_gather(up_weight, "fsdp", axis=0, tiled=True),
        lax.all_gather(down_weight, "fsdp", axis=1, tiled=True),
        lax.all_gather(attn_gain, "fsdp", axis=0, tiled=True),
        lax.all_gather(mlp_gain, "fsdp", axis=0, tiled=True),
    )
    (
        full_query,
        full_key,
        full_value,
        full_output,
        full_gate,
        full_up,
        full_down,
        gain_first,
        gain_second,
    ) = gathered
    w_inner = jnp.concatenate([full_query, full_key, full_value], axis=1)
    gain_first_wide = gain_first.astype(jnp.float32)
    gain_second_wide = gain_second.astype(jnp.float32)
    tokens_wide = tokens.astype(jnp.float32)
    inverse_first = lax.rsqrt(jnp.mean(tokens_wide * tokens_wide, axis=1, keepdims=True) + epsilon)
    normed_first = tokens_wide * inverse_first
    scaled_first = (normed_first * gain_first_wide).astype(jnp.bfloat16)
    rows_first = lax.all_gather(scaled_first, "tp", axis=0, tiled=True)
    projected = jnp.dot(rows_first, w_inner, preferred_element_type=jnp.float32)
    block_base = block_index * block_rows
    key_slots = block_base - front_rows + jnp.arange(window, dtype=jnp.int32)
    key_segments, key_positions = stream_layout(key_slots, lengths)
    query_segments = key_segments[front_rows:]
    block_positions = key_positions[front_rows:]
    cosine, sine_table = rotary_tables(block_positions, head_width)
    queries = rotate(
        projected[:, :query_width].reshape(block_rows, heads_here, head_width), cosine, sine_table
    ).astype(jnp.bfloat16)
    keys_local = rotate(
        projected[:, query_width : query_width + key_width].reshape(block_rows, 1, head_width),
        cosine,
        sine_table,
    )
    keys_local = keys_local.reshape(block_rows, head_width).astype(jnp.bfloat16)
    values_local = projected[:, query_width + key_width :].astype(jnp.bfloat16)
    pair_local = jnp.concatenate([keys_local, values_local], axis=1)
    pieces = []
    for offset in range(reach_count, 0, -1):
        pieces.append(passed_along(pair_local, "fsdp", offset))
    pair_window = jnp.concatenate(pieces + [pair_local], axis=0)
    key_window = pair_window[:, :head_width]
    value_window = pair_window[:, head_width:]
    key_seen = (key_segments[None, :] == query_segments[:, None]) & (
        key_positions[None, :] <= block_positions[:, None]
    )

    def head_scores(query_head):
        scores = outer_cols(query_head, key_window) * score_scale
        return jnp.where(key_seen, scores, -1e30)

    def head_forward(query_head):
        scores = head_scores(query_head)
        largest = jnp.max(scores, axis=1, keepdims=True)
        raised = jnp.exp(scores - largest)
        row_total = jnp.sum(raised, axis=1, keepdims=True)
        attn_probs = (raised / row_total).astype(jnp.bfloat16)
        head_out = jnp.dot(attn_probs, value_window, preferred_element_type=jnp.float32)
        return (head_out, (largest + jnp.log(row_total))[:, 0])

    query_heads = jnp.moveaxis(queries, 1, 0)
    head_outs, log_totals = lax.map(head_forward, query_heads)
    attended = jnp.moveaxis(head_outs, 0, 1).reshape(block_rows, query_width).astype(jnp.bfloat16)
    attn_share = lax.psum_scatter(
        jnp.dot(attended, full_output, preferred_element_type=jnp.float32).astype(jnp.bfloat16),
        "tp",
        scatter_dimension=0,
        tiled=True,
    ).astype(jnp.float32)
    middle = tokens_wide + attn_share
    inverse_second = lax.rsqrt(jnp.mean(middle * middle, axis=1, keepdims=True) + epsilon)
    normed_second = middle * inverse_second
    scaled_second = (normed_second * gain_second_wide).astype(jnp.bfloat16)
    rows_second = lax.all_gather(scaled_second, "tp", axis=0, tiled=True)
    gate_proj = jnp.dot(rows_second, full_gate, preferred_element_type=jnp.float32)
    up_proj = jnp.dot(rows_second, full_up, preferred_element_type=jnp.float32)
    gate_sigmoid = jax.nn.sigmoid(gate_proj)
    gate_active = gate_proj * gate_sigmoid
    hidden = (gate_active * up_proj).astype(jnp.bfloat16)
    mlp_share = lax.psum_scatter(
        jnp.dot(hidden, full_down, preferred_element_type=jnp.float32).astype(jnp.bfloat16),
        "tp",
        scatter_dimension=0,
        tiled=True,
    ).astype(jnp.float32)
    layer_out = jnp.where(valid_rows, middle + mlp_share, 0.0).astype(jnp.bfloat16)
    grad_rows = jnp.where(valid_rows, out_grad.astype(jnp.float32), 0.0)
    grad_low = grad_rows.astype(jnp.bfloat16)
    regathered = (
        lax.all_gather(query_weight, "fsdp", axis=0, tiled=True),
        lax.all_gather(key_weight, "fsdp", axis=0, tiled=True),
        lax.all_gather(value_weight, "fsdp", axis=0, tiled=True),
        lax.all_gather(output_weight, "fsdp", axis=1, tiled=True),
        lax.all_gather(gate_weight, "fsdp", axis=0, tiled=True),
        lax.all_gather(up_weight, "fsdp", axis=0, tiled=True),
        lax.all_gather(down_weight, "fsdp", axis=1, tiled=True),
        lax.all_gather(attn_gain, "fsdp", axis=0, tiled=True),
        lax.all_gather(mlp_gain, "fsdp", axis=0, tiled=True),
    )
    (
        full_query,
        full_key,
        full_value,
        full_output,
        full_gate,
        full_up,
        full_down,
        gain_first,
        gain_second,
    ) = regathered
    w_inner = jnp.concatenate([full_query, full_key, full_value], axis=1)
    grad_down_rows = lax.all_gather(grad_low, "tp", axis=0, tiled=True)
    grad_down_w = inner_rows(hidden, grad_down_rows)
    grad_hidden = outer_cols(grad_down_rows, full_down)
    grad_up_low = (grad_hidden * gate_active).astype(jnp.bfloat16)
    grad_gate_low = (
        grad_hidden * up_proj * gate_sigmoid * (1.0 + gate_proj * (1.0 - gate_sigmoid))
    ).astype(jnp.bfloat16)
    grad_gate_w = inner_rows(rows_second, grad_gate_low)
    grad_up_w = inner_rows(rows_second, grad_up_low)
    grad_second = lax.psum_scatter(
        (outer_cols(grad_gate_low, full_gate) + outer_cols(grad_up_low, full_up)).astype(
            jnp.bfloat16
        ),
        "tp",
        scatter_dimension=0,
        tiled=True,
    ).astype(jnp.float32)
    gain_second_part = jnp.sum(grad_second * normed_second, axis=0)
    grad_middle = grad_rows + norm_back(
        grad_second, gain_second_wide, normed_second, inverse_second
    )
    middle_low = grad_middle.astype(jnp.bfloat16)
    grad_attn_rows = lax.all_gather(middle_low, "tp", axis=0, tiled=True)
    grad_output_w = inner_rows(attended, grad_attn_rows)
    grad_attended = outer_cols(grad_attn_rows, full_output).astype(jnp.bfloat16)
    grad_heads = jnp.moveaxis(grad_attended.reshape(block_rows, heads_here, head_width), 1, 0)

    def head_backward(packed):
        query_head, grad_head, log_total = packed
        attn_probs = jnp.exp(head_scores(query_head) - log_total[:, None])
        probs_low = attn_probs.astype(jnp.bfloat16)
        grad_value_head = inner_rows(probs_low, grad_head)
        grad_probs = outer_cols(grad_head, value_window)
        grad_scores = (
            attn_probs * (grad_probs - jnp.sum(attn_probs * grad_probs, axis=1, keepdims=True))
        ).astype(jnp.bfloat16)
        grad_query_head = (
            jnp.dot(grad_scores, key_window, preferred_element_type=jnp.float32) * score_scale
        )
        grad_key_head = inner_rows(grad_scores, query_head) * score_scale
        return (grad_query_head, grad_key_head, grad_value_head)

    grad_query_heads, grad_key_heads, grad_value_heads = lax.map(
        head_backward, (query_heads, grad_heads, log_totals)
    )
    grad_pair = jnp.concatenate(
        [jnp.sum(grad_key_heads, axis=0), jnp.sum(grad_value_heads, axis=0)], axis=1
    )
    own_grad = grad_pair[front_rows:]
    for offset in range(1, reach_count + 1):
        piece_start = (reach_count - offset) * block_rows
        own_grad = own_grad + passed_along(
            grad_pair[piece_start : piece_start + block_rows].astype(jnp.bfloat16), "fsdp", -offset
        ).astype(jnp.float32)
    grad_key_lin = rotate_back(
        own_grad[:, :head_width].reshape(block_rows, 1, head_width), cosine, sine_table
    )
    grad_key_low = grad_key_lin.reshape(block_rows, head_width).astype(jnp.bfloat16)
    grad_value_low = own_grad[:, head_width:].astype(jnp.bfloat16)
    grad_query_lin = rotate_back(jnp.moveaxis(grad_query_heads, 0, 1), cosine, sine_table)
    grad_query_low = grad_query_lin.reshape(block_rows, query_width).astype(jnp.bfloat16)
    grad_inner = jnp.concatenate([grad_query_low, grad_key_low, grad_value_low], axis=1)
    grad_inner_w = inner_rows(rows_first, grad_inner)
    grad_first = lax.psum_scatter(
        outer_cols(grad_inner, w_inner).astype(jnp.bfloat16), "tp", scatter_dimension=0, tiled=True
    ).astype(jnp.float32)
    gain_first_part = jnp.sum(grad_first * normed_first, axis=0)
    tokens_grad = grad_middle + norm_back(grad_first, gain_first_wide, normed_first, inverse_first)
    reduced = (
        lax.psum_scatter(
            grad_inner_w[:, :query_width].astype(jnp.bfloat16),
            "fsdp",
            scatter_dimension=0,
            tiled=True,
        ).astype(jnp.float32),
        lax.psum_scatter(
            grad_inner_w[:, query_width : query_width + key_width].astype(jnp.bfloat16),
            "fsdp",
            scatter_dimension=0,
            tiled=True,
        ).astype(jnp.float32),
        lax.psum_scatter(
            grad_inner_w[:, query_width + key_width :].astype(jnp.bfloat16),
            "fsdp",
            scatter_dimension=0,
            tiled=True,
        ).astype(jnp.float32),
        lax.psum_scatter(
            grad_output_w.astype(jnp.bfloat16), "fsdp", scatter_dimension=1, tiled=True
        ).astype(jnp.float32),
        lax.psum_scatter(
            grad_gate_w.astype(jnp.bfloat16), "fsdp", scatter_dimension=0, tiled=True
        ).astype(jnp.float32),
        lax.psum_scatter(
            grad_up_w.astype(jnp.bfloat16), "fsdp", scatter_dimension=0, tiled=True
        ).astype(jnp.float32),
        lax.psum_scatter(
            grad_down_w.astype(jnp.bfloat16), "fsdp", scatter_dimension=1, tiled=True
        ).astype(jnp.float32),
        lax.psum_scatter(
            gain_first_part.astype(jnp.bfloat16), "fsdp", scatter_dimension=0, tiled=True
        ).astype(jnp.float32),
        lax.psum_scatter(
            gain_second_part.astype(jnp.bfloat16), "fsdp", scatter_dimension=0, tiled=True
        ).astype(jnp.float32),
    )
    gain_sums = lax.psum((reduced[7], reduced[8]), "tp")
    return (
        layer_out,
        tokens_grad,
        gain_sums[0],
        reduced[0],
        reduced[1],
        reduced[2],
        reduced[3],
        gain_sums[1],
        reduced[4],
        reduced[5],
        reduced[6],
    )


MESH = pl.DeviceIdType.MESH
CORE, ALONG_X, ALONG_Y = 1, 2, 4
PARTS = 4
VMEM_MOST = 60 << 20


def greet(partners):
    barrier = pltpu.get_barrier_semaphore()
    for partner in partners:
        pl.semaphore_signal(barrier, inc=1, device_id=partner, device_id_type=MESH)
    pl.semaphore_wait(barrier, len(partners))


def remote(source, target, sent, arrived, partner):
    return pltpu.make_async_remote_copy(
        src_ref=source,
        dst_ref=target,
        send_sem=sent,
        recv_sem=arrived,
        device_id=partner,
        device_id_type=MESH,
    )


def comm_params(number, vmem=None):
    return pltpu.CompilerParams(
        collective_id=number, has_side_effects=True, vmem_limit_bytes=vmem
    )


def lasting(microseconds):
    return pl.CostEstimate(
        flops=int(microseconds * 1.1e9), bytes_accessed=1_000_000, transcendentals=0
    )


ANYWHERE = pl.BlockSpec(memory_space=pl.ANY)
IN_VMEM = pl.BlockSpec(memory_space=pltpu.VMEM)


def columns(index, width):
    return pl.ds(pl.multiple_of(index * width, width), width)


class PlaneGather:
    def __init__(self, store, sent, arrived):
        self.f, self.t = lax.axis_index("fsdp"), lax.axis_index("tp")
        self.store, self.sent, self.arrived = store, sent, arrived
        self.piece = store.shape[1] // PARTS
        self.near = [(self.f ^ k, self.t) for k in (CORE, ALONG_X, ALONG_Y)]
        self.copies, self.on = [], {}

    def send(self, owner, j, way, slot):
        place = self.store.at[owner, pl.ds(j * self.piece, self.piece)]
        c = remote(
            place, place, self.sent.at[slot, j], self.arrived.at[slot, j], self.near[way]
        )
        c.start()
        self.copies.append(c)
        self.on[slot, j] = c

    def begin(self):
        for k in range(PARTS):
            self.send(self.f, k, 1, 1)
            self.send(self.f, (k + PARTS // 2) % PARTS, 2, 2)
        for k in range(PARTS):
            self.send(self.f, k, 0, 0)

    def arrive(self, slot, j):
        self.on[slot, j].wait_recv()

    def advance(self, k):
        jx, jy = k, (k + PARTS // 2) % PARTS
        self.arrive(1, jx)
        if jx < PARTS // 2:
            self.send(self.f ^ ALONG_X, jx, 2, 6)
        self.send(self.f ^ ALONG_X, jx, 0, 3)
        self.arrive(2, jy)
        if jy >= PARTS // 2:
            self.send(self.f ^ ALONG_Y, jy, 1, 6)
        self.send(self.f ^ ALONG_Y, jy, 0, 4)

    def far(self):
        for k in range(PARTS // 2):
            for j in (k, k + PARTS // 2):
                self.arrive(6, j)
                self.send(self.f ^ ALONG_X ^ ALONG_Y, j, 0, 5)

    def wait_core(self, *slots):
        for slot in slots:
            for j in range(PARTS):
                self.arrive(slot, j)

    def finish(self):
        for c in self.copies:
            c.wait_send()


GATHER_SEMAPHORES = [pltpu.SemaphoreType.DMA((7, PARTS)), pltpu.SemaphoreType.DMA((7, PARTS))]


class PlaneSum:
    masks = (ALONG_X ^ ALONG_Y, ALONG_X, ALONG_Y, 0)

    def __init__(self, stage, other, held, from_x, from_y, last, sent, arrived):
        self.f, self.t = lax.axis_index("fsdp"), lax.axis_index("tp")
        self.stage, self.other, self.held = stage, other, held
        self.from_x, self.from_y, self.last = from_x, from_y, last
        self.sent, self.arrived = sent, arrived
        self.near = [(self.f ^ k, self.t) for k in (CORE, ALONG_X, ALONG_Y)]
        self.copies, self.on = [], {}
        half = held.shape[1] // 2
        self.top, self.low = pl.ds(0, half), pl.ds(half, half)

    def send(self, source, target, slot, way):
        c = remote(source, target, self.sent.at[slot], self.arrived.at[slot], self.near[way])
        c.start()
        self.copies.append(c)
        self.on[slot] = c

    def begin(self, write_part, after=None):
        for i, mask in enumerate(self.masks):
            if i >= 2:
                self.on[i - 2].wait_send()
                self.copies = [c for c in self.copies if c is not self.on[i - 2]]
            write_part(self.f ^ CORE ^ mask, self.stage.at[i % 2])
            self.send(self.stage.at[i % 2], self.other.at[i], i, 0)
            write_part(self.f ^ mask, self.held.at[i])
            if after is not None:
                after(i)
            self.on[i].wait_recv()
            self.held[i] = (
                self.held[i].astype(jnp.float32) + self.other[i].astype(jnp.float32)
            ).astype(jnp.bfloat16)
            if i == 0:
                self.send(self.held.at[0, self.top], self.from_x.at[0], 4, 1)
                self.send(self.held.at[0, self.low], self.from_y.at[0], 5, 2)
            if i == 1:
                self.send(self.held.at[1, self.top], self.from_x.at[1], 6, 1)
            if i == 2:
                self.send(self.held.at[2, self.low], self.from_y.at[1], 7, 2)

    def turn(self):
        self.on[4].wait_recv()
        self.held[2, self.top] = (
            self.held[2, self.top].astype(jnp.float32) + self.from_x[0].astype(jnp.float32)
        ).astype(jnp.bfloat16)
        self.send(self.held.at[2, self.top], self.last.at[0], 8, 2)
        self.on[5].wait_recv()
        self.held[1, self.low] = (
            self.held[1, self.low].astype(jnp.float32) + self.from_y[0].astype(jnp.float32)
        ).astype(jnp.bfloat16)
        self.send(self.held.at[1, self.low], self.last.at[1], 9, 1)

    def end(self, total):
        for rows, first, second, take in (
            (self.top, 6, 8, lambda: self.from_x[1]),
            (self.low, 7, 9, lambda: self.from_y[1]),
        ):
            self.on[first].wait_recv()
            part = self.held[3, rows].astype(jnp.float32) + take().astype(jnp.float32)
            self.on[second].wait_recv()
            total[rows] = part + self.last[second - 8].astype(jnp.float32)

    def finish(self):
        for c in self.copies:
            c.wait_send()


def sum_scratch(height, width):
    chunks = [pltpu.VMEM((n, height, width), jnp.bfloat16) for n in (2, 4, 4)]
    return chunks + [pltpu.VMEM((2, height // 2, width), jnp.bfloat16)] * 3 + [pltpu.SemaphoreType.DMA((10,)), pltpu.SemaphoreType.DMA((10,))]


NARROW = 512


def chunk_part(pairs, size):
    def write_part(owner, ref):
        lanes = columns(owner, size)
        lefts = [left[:, lanes] for left, _ in pairs]

        def step(n, carry):
            wide = columns(n, NARROW)
            total = inner_rows(lefts[0], pairs[0][1][:, wide])
            for left, (_, right) in zip(lefts[1:], pairs[1:]):
                total += inner_rows(left, right[:, wide])
            ref[:, wide] = total.astype(jnp.bfloat16)
            return carry

        lax.fori_loop(0, ref.shape[1] // NARROW, step, 0)

    return write_part


def plane_greet():
    f, t = lax.axis_index("fsdp"), lax.axis_index("tp")
    greet([(f ^ k, t) for k in (CORE, ALONG_X, ALONG_Y)])


def forward_output(attended, output_rows, tokens, gain, grads, number):
    size, width = tokens.shape
    f32, bf16 = jnp.float32, jnp.bfloat16

    def kernel(
        o_ref, w_ref, x_ref, gain_ref, dy_ref,
        middle_ref, row_ref, dys_ref,
        stage, other, held, from_x, from_y, last, sum_sent, sum_arrived,
        dys, dys_sent, dys_arrived, keep_sem,
    ):
        f = lax.axis_index("fsdp")
        dys[f] = dy_ref[...]
        plane_greet()
        gather_dys = PlaneGather(dys, dys_sent, dys_arrived)
        total = PlaneSum(stage, other, held, from_x, from_y, last, sum_sent, sum_arrived)
        total.begin(chunk_part([(o_ref, w_ref)], size))
        gather_dys.begin()
        total.turn()
        for k in range(PARTS):
            gather_dys.advance(k)
        total.end(middle_ref)
        middle = x_ref[...].astype(f32) + middle_ref[...]
        middle_ref[...] = middle
        inverse = lax.rsqrt(jnp.mean(middle * middle, axis=1, keepdims=True) + epsilon)
        row_ref[...] = (middle * inverse * gain_ref[...]).astype(bf16)
        gather_dys.wait_core(0, 3, 4)
        gather_dys.far()
        gather_dys.wait_core(5)
        keep = pltpu.make_async_copy(dys, dys_ref, keep_sem)
        keep.start()
        keep.wait()
        total.finish()
        gather_dys.finish()

    return pl.pallas_call(
        kernel,
        out_shape=[
            jax.ShapeDtypeStruct((size, width), f32),
            jax.ShapeDtypeStruct((size, width), bf16),
            jax.ShapeDtypeStruct((8, size, width), bf16),
        ],
        in_specs=[IN_VMEM] * 5,
        out_specs=[IN_VMEM, IN_VMEM, ANYWHERE],
        scratch_shapes=sum_scratch(size, width)
        + [pltpu.VMEM((8, size, width), bf16)]
        + GATHER_SEMAPHORES
        + [pltpu.SemaphoreType.DMA],
        compiler_params=comm_params(number, 50 << 20),
        cost_estimate=lasting(75),
        name="forward_output",
    )(attended, output_rows, tokens, gain, grads)


def forward_hidden(row, dys, gate_rows, up_rows, down_rows, number):
    size, width = row.shape
    units = gate_rows.shape[0]
    f32, bf16 = jnp.float32, jnp.bfloat16

    def kernel(
        row_ref, dys_hbm, gate_hbm, up_hbm, down_hbm,
        rows_ref, hidden_ref, dgate_ref, dup_ref,
        rows, rows_sent, rows_arrived, dys, gate_w, up_w, down_w, load_sem, dh, out, out_sem, keep_sem,
    ):
        f = lax.axis_index("fsdp")
        loads = [
            pltpu.make_async_copy(source, target, load_sem.at[i])
            for i, (source, target) in enumerate(
                ((down_hbm, down_w), (dys_hbm, dys), (gate_hbm, gate_w), (up_hbm, up_w))
            )
        ]
        for load in loads:
            load.start()
        rows[f] = row_ref[...]
        plane_greet()
        gather_rows = PlaneGather(rows, rows_sent, rows_arrived)
        gather_rows.begin()
        loads[0].wait()
        loads[1].wait()

        def grad_chunk(i, carry):
            dh[i] = outer_cols(down_w[...], dys[i])
            return carry

        for k in range(PARTS):
            lax.fori_loop(2 * k, 2 * k + 2, grad_chunk, 0)
            gather_rows.advance(k)
        loads[2].wait()
        loads[3].wait()

        def out_copies(slot, owner):
            return [
                pltpu.make_async_copy(
                    out.at[slot, n], target.at[:, columns(owner, size)], out_sem.at[slot, n]
                )
                for n, target in enumerate((hidden_ref, dgate_ref, dup_ref))
            ]

        def chunk(i, carry):
            owner = f ^ i
            slot = lax.rem(i, 2)

            @pl.when(i >= 2)
            def _():
                for c in out_copies(slot, owner):
                    c.wait()

            gate = outer_cols(gate_w[...], rows[owner])
            up = outer_cols(up_w[...], rows[owner])
            sigmoid = jax.nn.sigmoid(gate)
            active = gate * sigmoid
            grad = dh[owner]
            out[slot, 0] = (active * up).astype(bf16)
            out[slot, 1] = (grad * up * sigmoid * (1.0 + gate * (1.0 - sigmoid))).astype(bf16)
            out[slot, 2] = (grad * active).astype(bf16)
            for c in out_copies(slot, owner):
                c.start()
            return carry

        gather_rows.wait_core(0)
        lax.fori_loop(0, 2, chunk, 0)
        gather_rows.wait_core(3, 4)
        lax.fori_loop(2, 4, chunk, 0)
        gather_rows.far()
        lax.fori_loop(4, 6, chunk, 0)
        gather_rows.wait_core(5)
        keep = pltpu.make_async_copy(rows, rows_ref, keep_sem)
        keep.start()
        lax.fori_loop(6, 8, chunk, 0)
        for i in (6, 7):
            for c in out_copies(i % 2, f ^ i):
                c.wait()
        keep.wait()
        gather_rows.finish()

    store = pltpu.VMEM((8, size, width), bf16)
    weights = pltpu.VMEM((units, width), bf16)
    return pl.pallas_call(
        kernel,
        out_shape=[jax.ShapeDtypeStruct((8, size, width), bf16)]
        + [jax.ShapeDtypeStruct((units, 8 * size), bf16)] * 3,
        in_specs=[IN_VMEM] + [ANYWHERE] * 4,
        out_specs=[ANYWHERE] * 4,
        scratch_shapes=[store]
        + GATHER_SEMAPHORES
        + [store]
        + [weights] * 3
        + [
            pltpu.SemaphoreType.DMA((4,)),
            pltpu.VMEM((8, units, size), f32),
            pltpu.VMEM((2, 3, units, size), bf16),
            pltpu.SemaphoreType.DMA((2, 3)),
            pltpu.SemaphoreType.DMA,
        ],
        compiler_params=comm_params(number, 50 << 20),
        cost_estimate=lasting(55),
        name="forward_hidden",
    )(row, dys, gate_rows, up_rows, down_rows)


def backward_middle(
    dgate, dup, hidden, gate_rows, up_rows, rows, dys, output_rows, attended, middle, grads, gain, number
):
    size, width = middle.shape
    units = gate_rows.shape[0]
    depth = output_rows.shape[0]
    blocks = width // size
    f32, bf16 = jnp.float32, jnp.bfloat16
    early = 5

    def kernel(
        dgate_hbm, dup_hbm, hidden_hbm, gate_hbm, up_hbm, rows_hbm, dys_hbm,
        w_ref, o_ref, middle_ref, dy_ref, gain_ref,
        grad_ref, gain_grad_ref, grad_o_ref, do_ref, units_ref,
        stage, other, held, from_x, from_y, last, sum_sent, sum_arrived,
        store, store_sent, store_arrived,
        dgate_v, dup_v, hidden_v, gate_w, up_w, load_sem,
        tall, tall_sem, out, out_sem, o_sum,
    ):
        f = lax.axis_index("fsdp")
        loads = [
            pltpu.make_async_copy(source, target, load_sem.at[i])
            for i, (source, target) in enumerate(
                (
                    (dgate_hbm, dgate_v),
                    (gate_hbm, gate_w),
                    (dup_hbm, dup_v),
                    (up_hbm, up_w),
                    (hidden_hbm, hidden_v),
                )
            )
        ]
        for load in loads:
            load.start()

        def tall_loads(n, slot):
            place = columns(n, size)
            return [
                pltpu.make_async_copy(
                    source.at[:, :, place], tall.at[slot, i], tall_sem.at[slot, i]
                )
                for i, source in enumerate((dys_hbm, rows_hbm))
            ]

        for c in tall_loads(0, 0):
            c.start()
        plane_greet()
        total = PlaneSum(stage, other, held, from_x, from_y, last, sum_sent, sum_arrived)
        gather = PlaneGather(store, store_sent, store_arrived)
        for load in loads[:4]:
            load.wait()
        total.begin(chunk_part([(dgate_v, gate_w), (dup_v, up_w)], size))
        total.turn()
        loads[4].wait()

        def out_copies(n, slot):
            return [
                pltpu.make_async_copy(
                    out.at[slot, i], units_ref.at[:, i, :, columns(n, size)], out_sem.at[slot, i]
                )
                for i in range(3)
            ]

        def block(n, carry):
            slot = lax.rem(n, 2)

            @pl.when(n + 1 < blocks)
            def _():
                for c in tall_loads(n + 1, 1 - slot):
                    c.start()

            for c in tall_loads(n, slot):
                c.wait()

            @pl.when(n >= 2)
            def _():
                for c in out_copies(n, slot):
                    c.wait()

            dy_cols = tall[slot, 0].reshape(8 * size, size)
            row_cols = tall[slot, 1].reshape(8 * size, size)
            out[slot, 0] = dot_nn(hidden_v[...], dy_cols).astype(bf16).reshape(4, units // 4, size)
            out[slot, 1] = dot_nn(dgate_v[...], row_cols).astype(bf16).reshape(4, units // 4, size)
            out[slot, 2] = dot_nn(dup_v[...], row_cols).astype(bf16).reshape(4, units // 4, size)
            for c in out_copies(n, slot):
                c.start()
            return carry

        lax.fori_loop(0, early, block, 0)
        total.end(grad_ref)
        middle = middle_ref[...]
        inverse = lax.rsqrt(jnp.mean(middle * middle, axis=1, keepdims=True) + epsilon)
        normed = middle * inverse
        grad = grad_ref[...]
        gain_grad_ref[...] = jnp.sum(grad * normed, axis=0, keepdims=True)
        grad = dy_ref[...].astype(f32) + norm_back(grad, gain_ref[...], normed, inverse)
        grad_ref[...] = grad
        store[f] = grad.astype(bf16)
        gather.begin()
        gather.advance(0)
        lax.fori_loop(early, early + 1, block, 0)
        gather.advance(1)
        lax.fori_loop(early + 1, early + 2, block, 0)
        gather.advance(2)
        lax.fori_loop(early + 2, blocks, block, 0)
        gather.advance(3)

        def chunk(i, carry):
            owner = f ^ i
            lanes = columns(owner, size)
            do_ref[:, lanes] = outer_cols(w_ref[...], store[owner]).astype(bf16)
            o_sum[...] += dot_nn(o_ref[:, lanes], store[owner])
            return carry

        o_sum[...] = jnp.zeros_like(o_sum)
        gather.wait_core(0)
        lax.fori_loop(0, 2, chunk, 0)
        gather.wait_core(3, 4)
        lax.fori_loop(2, 6, chunk, 0)
        gather.far()
        gather.wait_core(5)
        lax.fori_loop(6, 8, chunk, 0)
        grad_o_ref[...] = o_sum[...].astype(bf16)
        for n in (blocks - 2, blocks - 1):
            for c in out_copies(n, n % 2):
                c.wait()
        total.finish()
        gather.finish()

    weights = pltpu.VMEM((units, width), bf16)
    return pl.pallas_call(
        kernel,
        out_shape=[
            jax.ShapeDtypeStruct((size, width), f32),
            jax.ShapeDtypeStruct((1, width), f32),
            jax.ShapeDtypeStruct((depth, width), bf16),
            jax.ShapeDtypeStruct((depth, 8 * size), bf16),
        ]
        + [jax.ShapeDtypeStruct((4, 3, units // 4, width), bf16)],
        in_specs=[ANYWHERE] * 7 + [IN_VMEM] * 5,
        out_specs=[IN_VMEM] * 4 + [ANYWHERE],
        scratch_shapes=sum_scratch(size, width)
        + [pltpu.VMEM((8, size, width), bf16)]
        + GATHER_SEMAPHORES
        + [weights] * 5
        + [
            pltpu.SemaphoreType.DMA((5,)),
            pltpu.VMEM((2, 2, 8, size, size), bf16),
            pltpu.SemaphoreType.DMA((2, 2)),
            pltpu.VMEM((2, 3, 4, units // 4, size), bf16),
            pltpu.SemaphoreType.DMA((2, 3)),
            pltpu.VMEM((depth, width), f32),
        ],
        compiler_params=comm_params(number, VMEM_MOST),
        cost_estimate=lasting(92),
        name="backward_middle",
    )(dgate, dup, hidden, gate_rows, up_rows, rows, dys, output_rows, attended, middle, grads, gain)


def everyone(f, t):
    return [(f ^ k, t) for k in range(1, 8)] + [(f, lax.rem(t + k, 4)) for k in (1, 2, 3)]


def first_exchange(parts, inner, gains, number):
    _, units, block = parts[0].shape
    count = len(parts)
    far_first = (6, 7, 2, 4, 3, 5, 1)

    def kernel(*refs):
        sources, (inner_ref, gains_ref) = refs[:count], refs[count : count + 2]
        targets, (inner_all, gains_all) = refs[count + 2 : 2 * count + 2], refs[2 * count + 2 : 2 * count + 4]
        sent, arrived, z_sent, z_arrived, kept_sem = refs[2 * count + 4 :]
        f, t = lax.axis_index("fsdp"), lax.axis_index("tp")
        place = columns(f, block)
        kept = [
            pltpu.make_async_copy(s.at[f], o.at[:, place], kept_sem.at[i])
            for i, (s, o) in enumerate(zip(sources, targets))
        ] + [pltpu.make_async_copy(inner_ref, inner_all.at[t], kept_sem.at[count])]
        for c in kept:
            c.start()
        gains_all[f] = gains_ref[...]
        greet(everyone(f, t))
        copies = []
        for k in (2, 1, 3):
            copies.append(
                remote(inner_ref, inner_all.at[t], z_sent.at[k], z_arrived.at[k], (f, lax.rem(t + k, 4)))
            )
        for k in far_first:
            copies.append(
                remote(gains_ref, gains_all.at[f], sent.at[k, count], arrived.at[k, count], (f ^ k, t))
            )
        for i, (s, o) in enumerate(zip(sources, targets)):
            for k in far_first:
                copies.append(
                    remote(s.at[f ^ k], o.at[:, place], sent.at[k, i], arrived.at[k, i], (f ^ k, t))
                )
        for c in copies:
            c.start()
        for c in kept + copies:
            c.wait()

    return pl.pallas_call(
        kernel,
        out_shape=[jax.ShapeDtypeStruct((units, 8 * block), jnp.bfloat16)] * count
        + [
            jax.ShapeDtypeStruct((4, *inner.shape), inner.dtype),
            jax.ShapeDtypeStruct((8, *gains.shape), gains.dtype),
        ],
        in_specs=[ANYWHERE] * (count + 1) + [IN_VMEM],
        out_specs=[ANYWHERE] * (count + 1) + [IN_VMEM],
        scratch_shapes=[
            pltpu.SemaphoreType.DMA((8, count + 1)),
            pltpu.SemaphoreType.DMA((8, count + 1)),
            pltpu.SemaphoreType.DMA((4,)),
            pltpu.SemaphoreType.DMA((4,)),
            pltpu.SemaphoreType.DMA((count + 1,)),
        ],
        compiler_params=comm_params(number),
        cost_estimate=lasting(32),
        name="first_exchange",
    )(*parts, inner, gains)


def turn_heads(values, cosine, sine_table):
    half = HEAD_DIM // 2
    turned = []
    for h in range(values.shape[0] // HEAD_DIM):
        first = values[h * HEAD_DIM : h * HEAD_DIM + half]
        second = values[h * HEAD_DIM + half : (h + 1) * HEAD_DIM]
        turned.append(first * cosine - second * sine_table)
        turned.append(second * cosine + first * sine_table)
    return jnp.concatenate(turned, axis=0)


def first_rows(tokens, gains, inner_all, output_own, cosine, sine_table, number):
    size, width = tokens.shape
    block = width // 8
    quarter_rows = output_own.shape[0]
    depth = quarter_rows // 2
    pair_rows = 2 * HEAD_DIM
    f32, bf16 = jnp.float32, jnp.bfloat16

    def kernel(
        x_ref, gains_ref, inner_ref, own_ref, cos_ref, sin_ref,
        rows_ref, q_ref, pair_ref, w_ref, wo_ref, wo_all,
        rows, rows_sent, rows_arrived, pair_v,
        w_sent, w_arrived, o_sent, o_arrived, z_sent, z_arrived, p_sent, p_arrived, on_sent, on_arrived, kept_sem,
    ):
        f, t = lax.axis_index("fsdp"), lax.axis_index("tp")
        place = columns(f, block)
        far_first = (6, 7, 2, 4, 3, 5, 1)

        def inner_slices(j):
            quarter, side = lax.div(j, 2), lax.rem(j, 2)
            return [
                (
                    inner_ref.at[quarter, pl.ds(pl.multiple_of(side * depth, depth), depth)],
                    w_ref.at[pl.ds(0, depth), place],
                ),
                (
                    inner_ref.at[quarter, pl.ds(2 * depth, pair_rows)],
                    w_ref.at[pl.ds(depth, pair_rows), place],
                ),
            ]

        def output_slice(j):
            quarter, side = lax.div(j, 2), lax.rem(j, 2)
            return (
                wo_all.at[quarter, pl.ds(pl.multiple_of(side * depth, depth), depth)],
                wo_ref.at[:, place],
            )

        kept = [
            pltpu.make_async_copy(s, o, kept_sem.at[i]) for i, (s, o) in enumerate(inner_slices(f))
        ]
        kept.append(pltpu.make_async_copy(own_ref, wo_all.at[t], kept_sem.at[2]))
        for c in kept:
            c.start()
        greet(everyone(f, t))
        copies, along_z = [], []
        for k in (2, 1, 3):
            c = remote(own_ref, wo_all.at[t], z_sent.at[k], z_arrived.at[k], (f, lax.rem(t + k, 4)))
            c.start()
            along_z.append(c)
        weights = []
        for k in far_first:
            for i, (s, o) in enumerate(inner_slices(f ^ k)):
                c = remote(s, o, w_sent.at[k, i], w_arrived.at[k, i], (f ^ k, t))
                c.start()
                weights.append(c)
        gain = jnp.concatenate([gains_ref[j, 0:1] for j in range(8)], axis=1)
        wide = x_ref[...].astype(f32)
        inverse = lax.rsqrt(jnp.mean(wide * wide, axis=1, keepdims=True) + epsilon)
        rows[f] = (wide * inverse * gain).astype(bf16)
        gather = PlaneGather(rows, rows_sent, rows_arrived)
        gather.begin()
        for k in range(PARTS):
            gather.advance(k)
        for c in kept[:2]:
            c.wait()
        for c in weights:
            c.wait_recv()

        def chunk(i, carry):
            owner = f ^ i
            lanes = columns(owner, size)
            projected = outer_cols(w_ref[...], rows[owner])
            cosine, sine = cos_ref[:, lanes], sin_ref[:, lanes]
            queries = turn_heads(projected[:depth], cosine, sine).astype(bf16)
            q_ref[:, lanes] = (queries.astype(f32) * HEAD_DIM ** (-0.5)).astype(bf16)
            keys = turn_heads(projected[depth : depth + HEAD_DIM], cosine, sine)
            pair = jnp.concatenate([keys, projected[depth + HEAD_DIM :]], axis=0)
            pair_v[owner] = pair.T.astype(bf16)
            return carry

        spread = []

        def spread_pair(i):
            for k in (2, 1, 3):
                c = remote(
                    pair_v.at[f ^ i],
                    pair_ref.at[t, f ^ i],
                    p_sent.at[i // 2, k],
                    p_arrived.at[i // 2, k],
                    (f, lax.rem(t + k, 4)),
                )
                c.start()
                spread.append((i, k, c))

        gather.wait_core(0)
        lax.fori_loop(0, 2, chunk, 0)
        spread_pair(0)
        gather.wait_core(3, 4)
        lax.fori_loop(2, 6, chunk, 0)
        spread_pair(2)
        spread_pair(4)
        gather.far()
        gather.wait_core(5)
        lax.fori_loop(6, 8, chunk, 0)
        spread_pair(6)
        own_pair = pltpu.make_async_copy(pair_v, pair_ref.at[t], kept_sem.at[3])
        own_pair.start()
        keep_rows = pltpu.make_async_copy(rows, rows_ref, kept_sem.at[4])
        keep_rows.start()
        kept[2].wait()
        for c in along_z:
            c.wait_recv()
        for k in far_first:
            s, o = output_slice(f ^ k)
            c = remote(s, o, o_sent.at[k], o_arrived.at[k], (f ^ k, t))
            c.start()
            copies.append(c)
        s, o = output_slice(f)
        keep_output = pltpu.make_async_copy(s, o, kept_sem.at[5])
        keep_output.start()
        passed = []
        for i, k, c in spread:
            c.wait_recv()
            spot = pair_ref.at[lax.rem(t + 4 - k, 4), f ^ i]
            d = remote(spot, spot, on_sent.at[i // 2, k], on_arrived.at[i // 2, k], (f ^ CORE, t))
            d.start()
            passed.append(d)
        for c in passed + copies:
            c.wait()
        for c in weights + along_z + [c for _, _, c in spread]:
            c.wait_send()
        gather.finish()
        own_pair.wait()
        keep_rows.wait()
        keep_output.wait()

    dma = pltpu.SemaphoreType.DMA
    return pl.pallas_call(
        kernel,
        out_shape=[
            jax.ShapeDtypeStruct((8, size, width), bf16),
            jax.ShapeDtypeStruct((depth, 8 * size), bf16),
            jax.ShapeDtypeStruct((4, 8, size, pair_rows), bf16),
            jax.ShapeDtypeStruct((depth + pair_rows, width), bf16),
            jax.ShapeDtypeStruct((depth, width), bf16),
            jax.ShapeDtypeStruct((4, quarter_rows, block), bf16),
        ],
        in_specs=[IN_VMEM, IN_VMEM, ANYWHERE, ANYWHERE, IN_VMEM, IN_VMEM],
        out_specs=[ANYWHERE, IN_VMEM, ANYWHERE, IN_VMEM, ANYWHERE, ANYWHERE],
        scratch_shapes=[pltpu.VMEM((8, size, width), bf16)]
        + GATHER_SEMAPHORES
        + [
            pltpu.VMEM((8, size, pair_rows), bf16),
            dma((8, 2)),
            dma((8, 2)),
            dma((8,)),
            dma((8,)),
            dma((4,)),
            dma((4,)),
            dma((4, 4)),
            dma((4, 4)),
            dma((4, 4)),
            dma((4, 4)),
            dma((6,)),
        ],
        compiler_params=comm_params(number, 40 << 20),
        cost_estimate=lasting(85),
        name="first_rows",
    )(tokens, gains, inner_all, output_own, cosine, sine_table)[:5]


def backward_pairs(pair_parts, hidden, down_rows, middle, valid, grad_output, number):
    size, width = middle.shape
    units = hidden.shape[0]
    depth = grad_output.shape[0]
    _, chunks, height, _ = pair_parts.shape
    half = chunks // 2
    f32, bf16 = jnp.float32, jnp.bfloat16

    def kernel(
        p_ref, hidden_hbm, down_hbm, middle_ref, valid_ref, g_ref,
        pair_ref, out_ref, spread_ref,
        stage, other, held, from_x, from_y, last, sum_sent, sum_arrived,
        hidden_v, down_w, load_sem, ra, s, rz, sent, arrived, g_sent, g_arrived, share,
    ):
        f, t = lax.axis_index("fsdp"), lax.axis_index("tp")
        loads = [
            pltpu.make_async_copy(hidden_hbm, hidden_v, load_sem.at[0]),
            pltpu.make_async_copy(down_hbm, down_w, load_sem.at[1]),
            pltpu.make_async_copy(g_ref.at[:, columns(f, size)], spread_ref.at[f], load_sem.at[2]),
        ]
        for c in loads:
            c.start()
        side = lax.rem(f, 2)
        mine, theirs = pl.ds(side * half, half), pl.ds((1 - side) * half, half)
        core = (f ^ CORE, t)
        greet(everyone(f, t))
        first = []
        for k in (2, 1, 3, 0):
            plane = lax.rem(t + k, 4)
            c = remote(p_ref.at[plane, theirs], ra.at[k], sent.at[k], arrived.at[k], core)
            c.start()
            first.append((k, c))
        out = []
        for k, c in first:
            c.wait_recv()
            plane = lax.rem(t + k, 4)
            both = p_ref[plane, mine].astype(f32) + ra[k].astype(f32)
            if k:
                s[k] = both.astype(bf16)
                d = remote(s.at[k], rz.at[k], sent.at[3 + k], arrived.at[3 + k], (f, plane))
                d.start()
                out.append((k, d))
            else:
                pair_ref[mine] = both
        for c in loads[:2]:
            c.wait()
        total = PlaneSum(stage, other, held, from_x, from_y, last, sum_sent, sum_arrived)
        total.begin(chunk_part([(hidden_v, down_w)], size))
        spread = []
        for k in (6, 7, 2, 4, 3, 5, 1):
            c = remote(
                g_ref.at[:, columns(f ^ k, size)],
                spread_ref.at[f],
                g_sent.at[k],
                g_arrived.at[k],
                (f ^ k, t),
            )
            c.start()
            spread.append(c)
        total.turn()
        for k, d in out:
            d.wait_recv()
            pair_ref[mine] += rz[k].astype(f32)
        back = remote(pair_ref.at[mine], pair_ref.at[mine], sent.at[7], arrived.at[7], core)
        back.start()
        total.end(share)
        out_ref[...] = jnp.where(valid_ref[...] > 0, middle_ref[...] + share[...], 0.0).astype(bf16)
        back.wait()
        for c in spread:
            c.wait()
        loads[2].wait()
        for k, c in first + out:
            c.wait_send()
        total.finish()

    dma = pltpu.SemaphoreType.DMA
    return pl.pallas_call(
        kernel,
        out_shape=[
            jax.ShapeDtypeStruct((chunks, height, size), f32),
            jax.ShapeDtypeStruct((size, width), bf16),
            jax.ShapeDtypeStruct((8, depth, size), bf16),
        ],
        in_specs=[IN_VMEM, ANYWHERE, ANYWHERE, IN_VMEM, IN_VMEM, ANYWHERE],
        out_specs=[IN_VMEM, IN_VMEM, ANYWHERE],
        scratch_shapes=sum_scratch(size, width)
        + [pltpu.VMEM((units, 8 * size), bf16), pltpu.VMEM((units, width), bf16), dma((3,))]
        + [pltpu.VMEM((4, half, height, size), bf16)] * 3
        + [dma((8,)), dma((8,)), dma((8,)), dma((8,)), pltpu.VMEM((size, width), f32)],
        compiler_params=comm_params(number, VMEM_MOST),
        cost_estimate=lasting(50),
        name="backward_pairs",
    )(pair_parts, hidden, down_rows, middle, valid, grad_output)


def backward_first(grad_inner, weights, rows, tokens, grad_middle, gain, number):
    size, width = tokens.shape
    depth = grad_inner.shape[0]
    block = width // 8
    f32, bf16 = jnp.float32, jnp.bfloat16

    def kernel(
        g_ref, w_ref, rows_hbm, x_ref, middle_ref, gain_ref,
        tokens_grad_ref, gain_grad_ref, spread_ref,
        stage, other, held, from_x, from_y, last, sum_sent, sum_arrived,
        rows_v, load_sem, w_grad, sent, arrived,
    ):
        f, t = lax.axis_index("fsdp"), lax.axis_index("tp")
        load = pltpu.make_async_copy(rows_hbm, rows_v, load_sem.at[0])
        load.start()
        greet([(f ^ k, t) for k in range(1, 8)])
        total = PlaneSum(stage, other, held, from_x, from_y, last, sum_sent, sum_arrived)
        total.begin(chunk_part([(g_ref, w_ref)], size))
        load.wait()
        spread = []

        def weight_grad(k):
            j = f ^ k
            right = rows_v[:, :, columns(j, block)].reshape(8 * size, block)
            w_grad[k] = dot_nn(g_ref[...], right).astype(bf16)
            if k:
                c = remote(w_grad.at[k], spread_ref.at[f], sent.at[k], arrived.at[k], (j, t))
                c.start()
                spread.append(c)

        for k in (6, 7, 2, 4):
            weight_grad(k)
        total.turn()
        for k in (3, 5, 1, 0):
            weight_grad(k)
        keep = pltpu.make_async_copy(w_grad.at[0], spread_ref.at[f], load_sem.at[1])
        keep.start()
        wide = x_ref[...].astype(f32)
        inverse = lax.rsqrt(jnp.mean(wide * wide, axis=1, keepdims=True) + epsilon)
        normed = wide * inverse
        total.end(tokens_grad_ref)
        grad = tokens_grad_ref[...]
        gain_grad_ref[...] = jnp.sum(grad * normed, axis=0, keepdims=True)
        tokens_grad_ref[...] = middle_ref[...] + norm_back(grad, gain_ref[...], normed, inverse)
        for c in spread:
            c.wait()
        keep.wait()
        total.finish()

    dma = pltpu.SemaphoreType.DMA
    return pl.pallas_call(
        kernel,
        out_shape=[
            jax.ShapeDtypeStruct((size, width), f32),
            jax.ShapeDtypeStruct((1, width), f32),
            jax.ShapeDtypeStruct((8, depth, block), bf16),
        ],
        in_specs=[IN_VMEM, IN_VMEM, ANYWHERE, IN_VMEM, IN_VMEM, IN_VMEM],
        out_specs=[IN_VMEM, IN_VMEM, ANYWHERE],
        scratch_shapes=sum_scratch(size, width)
        + [
            pltpu.VMEM((8, size, width), bf16),
            dma((2,)),
            pltpu.VMEM((8, depth, block), bf16),
            dma((8,)),
            dma((8,)),
        ],
        compiler_params=comm_params(number, VMEM_MOST),
        cost_estimate=lasting(60),
        name="backward_first",
    )(grad_inner, weights, rows, tokens, grad_middle, gain)


def last_exchange(hidden_grads, gain_parts, number):
    count, units, width = hidden_grads.shape
    block = width // 8
    f32, bf16 = jnp.float32, jnp.bfloat16
    far_first = (6, 7, 2, 4, 3, 5, 1)

    def kernel(
        source, gains_ref, target, sums_ref, taken, planes, sent, arrived, z_sent, z_arrived, kept_sem
    ):
        f, t = lax.axis_index("fsdp"), lax.axis_index("tp")
        keep = pltpu.make_async_copy(source.at[:, :, columns(f, block)], target.at[f], kept_sem)
        keep.start()
        greet(everyone(f, t))
        gains = []
        for k in far_first:
            c = remote(
                gains_ref.at[f ^ k], taken.at[k], sent.at[k, 0], arrived.at[k, 0], (f ^ k, t)
            )
            c.start()
            gains.append(c)
        copies = []
        for k in far_first:
            c = remote(
                source.at[:, :, columns(f ^ k, block)],
                target.at[f],
                sent.at[k, 1],
                arrived.at[k, 1],
                (f ^ k, t),
            )
            c.start()
            copies.append(c)
        total = gains_ref[f]
        for k, c in zip(far_first, gains):
            c.wait_recv()
            total += taken[k]
        planes[0] = total
        along_z = []
        for k in (1, 2, 3):
            c = remote(planes.at[0], planes.at[k], z_sent.at[k], z_arrived.at[k], (f, lax.rem(t + k, 4)))
            c.start()
            along_z.append(c)
        for c in along_z:
            c.wait_recv()
        sums = planes[lax.rem(t, 4)]
        for plane in (1, 2, 3):
            sums += planes[lax.rem(t + 4 - plane, 4)]
        sums_ref[...] = sums
        for c in [keep] + copies:
            c.wait()
        for c in gains + along_z:
            c.wait_send()

    dma = pltpu.SemaphoreType.DMA
    return pl.pallas_call(
        kernel,
        out_shape=[
            jax.ShapeDtypeStruct((8, count, units, block), bf16),
            jax.ShapeDtypeStruct(gain_parts.shape[1:], f32),
        ],
        in_specs=[ANYWHERE, IN_VMEM],
        out_specs=[ANYWHERE, IN_VMEM],
        scratch_shapes=[
            pltpu.VMEM(gain_parts.shape, f32),
            pltpu.VMEM((4, *gain_parts.shape[1:]), f32),
            dma((8, 2)),
            dma((8, 2)),
            dma((4,)),
            dma((4,)),
            dma,
        ],
        compiler_params=comm_params(number),
        cost_estimate=lasting(28),
        name="last_exchange",
    )(hidden_grads, gain_parts)


def dot_nn(left, right):
    return jnp.dot(left, right, preferred_element_type=jnp.float32)


def seen_keys(begin_row, first_key, first_query, shape):
    key_slot = first_key + lax.broadcasted_iota(jnp.int32, shape, 0)
    query_slot = first_query + lax.broadcasted_iota(jnp.int32, (1, shape[1]), 1)
    return (key_slot <= query_slot) & (key_slot >= begin_row)


def head_lanes(block, heads):
    return jnp.concatenate([block[h * HEAD_DIM : (h + 1) * HEAD_DIM] for h in range(heads)], axis=1)


def attend(info, begins, queries, pair):
    depth, slots = queries.shape
    heads = depth // HEAD_DIM
    size = slots // 8
    span = heads * size

    def kernel(info_ref, begin_ref, q_ref, kv_ref, o_ref, l_ref, q_s, m_s, t_s, a_s):
        f = pl.program_id(0)
        low, middle, own = info_ref[f, 0], info_ref[f, 1], info_ref[f, 2]
        q_s[...] = head_lanes(q_ref[...], heads)
        m_s[...] = jnp.full_like(m_s, -1e30)
        t_s[...] = jnp.zeros_like(t_s)
        a_s[...] = jnp.zeros_like(a_s)

        def step(g, masked):
            block = kv_ref[lax.rem(g, 4), lax.div(g, 4)]
            keys, values = block[:, :HEAD_DIM], block[:, HEAD_DIM:]
            value_cols = values.astype(jnp.float32).T.astype(jnp.bfloat16)
            if masked:
                seen = seen_keys(begin_ref[0], g * size, own * size, (size, size))
            for h in range(heads):
                lanes = pl.ds(h * size, size)
                scores = dot_nn(keys, q_s[:, lanes])
                if masked:
                    scores = jnp.where(seen, scores, -1e30)
                largest = m_s[:, lanes]
                higher = jnp.maximum(largest, jnp.max(scores, axis=0, keepdims=True))
                raised = jnp.exp(scores - higher)
                fade = jnp.exp(largest - higher)
                m_s[:, lanes] = higher
                t_s[:, lanes] = t_s[:, lanes] * fade + jnp.sum(raised, axis=0, keepdims=True)
                a_s[:, lanes] = a_s[:, lanes] * fade + dot_nn(
                    value_cols, raised.astype(jnp.bfloat16)
                )

        def masked_step(g, carry):
            step(g, True)
            return carry

        def plain_step(g, carry):
            step(g, False)
            return carry

        step(own, True)
        lax.fori_loop(low, middle, masked_step, 0)
        lax.fori_loop(middle, own, plain_step, 0)
        result = a_s[...] / t_s[...]
        for h in range(heads):
            o_ref[h * HEAD_DIM : (h + 1) * HEAD_DIM] = result[:, h * size : (h + 1) * size].astype(
                jnp.bfloat16
            )
        l_ref[0] = m_s[...] + jnp.log(t_s[...])

    return pl.pallas_call(
        kernel,
        grid_spec=pltpu.PrefetchScalarGridSpec(
            num_scalar_prefetch=1,
            grid=(8,),
            in_specs=[
                pl.BlockSpec((1, 1, size), lambda f, info: (f, 0, 0)),
                pl.BlockSpec((depth, size), lambda f, info: (0, f)),
                pl.BlockSpec((4, 8, size, 2 * HEAD_DIM), lambda f, info: (0, 0, 0, 0)),
            ],
            out_specs=[
                pl.BlockSpec((depth, size), lambda f, info: (0, f)),
                pl.BlockSpec((1, 1, span), lambda f, info: (f, 0, 0)),
            ],
            scratch_shapes=[
                pltpu.VMEM((HEAD_DIM, span), jnp.bfloat16),
                pltpu.VMEM((1, span), jnp.float32),
                pltpu.VMEM((1, span), jnp.float32),
                pltpu.VMEM((HEAD_DIM, span), jnp.float32),
            ],
        ),
        out_shape=[
            jax.ShapeDtypeStruct((depth, slots), jnp.bfloat16),
            jax.ShapeDtypeStruct((8, 1, span), jnp.float32),
        ],
        compiler_params=pltpu.CompilerParams(vmem_limit_bytes=40 << 20),
        cost_estimate=lasting(75),
        name="attend",
    )(info, begins, queries, pair)


def attend_back(info, begins, queries, pair, outputs, grads, totals):
    depth, slots = queries.shape
    heads = depth // HEAD_DIM
    size = slots // 8
    span = heads * size

    def kernel(
        info_ref, begin_ref, q_ref, kv_ref, o_ref, g_ref, l_ref, dq_ref, dkv_ref, q_s, g_s, d_s, a_s, w_s
    ):
        f = pl.program_id(0)
        low, middle, own = info_ref[f, 0], info_ref[f, 1], info_ref[f, 2]

        @pl.when(f == 0)
        def _():
            w_s[...] = jnp.zeros_like(w_s)

        q_s[...] = head_lanes(q_ref[...], heads)
        g_s[...] = head_lanes(g_ref[...], heads)
        out_lanes = head_lanes(o_ref[...], heads).astype(jnp.float32)
        d_s[...] = jnp.sum(out_lanes * g_s[...].astype(jnp.float32), axis=0, keepdims=True)
        a_s[...] = jnp.zeros_like(a_s)

        def step(g, masked):
            block = kv_ref[lax.rem(g, 4), lax.div(g, 4)]
            keys, values = block[:, :HEAD_DIM], block[:, HEAD_DIM:]
            key_cols = keys.astype(jnp.float32).T.astype(jnp.bfloat16)
            if masked:
                seen = seen_keys(begin_ref[0], g * size, own * size, (size, size))
            grad_keys = jnp.zeros((HEAD_DIM, size), jnp.float32)
            grad_values = jnp.zeros((HEAD_DIM, size), jnp.float32)
            for h in range(heads):
                lanes = pl.ds(h * size, size)
                query, grad = q_s[:, lanes], g_s[:, lanes]
                raised = jnp.exp(dot_nn(keys, query) - l_ref[0, :, lanes])
                if masked:
                    raised = jnp.where(seen, raised, 0.0)
                grad_probs = dot_nn(values, grad)
                scores = (raised * (grad_probs - d_s[:, lanes])).astype(jnp.bfloat16)
                grad_values += outer_cols(grad, raised.astype(jnp.bfloat16))
                grad_keys += outer_cols(query, scores)
                a_s[:, lanes] += dot_nn(key_cols, scores)
            w_s[lax.rem(g, 4), lax.div(g, 4), :HEAD_DIM] += grad_keys
            w_s[lax.rem(g, 4), lax.div(g, 4), HEAD_DIM:] += grad_values

        def masked_step(g, carry):
            step(g, True)
            return carry

        def plain_step(g, carry):
            step(g, False)
            return carry

        step(own, True)
        lax.fori_loop(low, middle, masked_step, 0)
        lax.fori_loop(middle, own, plain_step, 0)
        result = a_s[...] * HEAD_DIM ** (-0.5)
        for h in range(heads):
            dq_ref[h * HEAD_DIM : (h + 1) * HEAD_DIM] = result[:, h * size : (h + 1) * size]

        @pl.when(f == 7)
        def _():
            dkv_ref[...] = w_s[...].astype(jnp.bfloat16)

    return pl.pallas_call(
        kernel,
        grid_spec=pltpu.PrefetchScalarGridSpec(
            num_scalar_prefetch=1,
            grid=(8,),
            in_specs=[
                pl.BlockSpec((1, 1, size), lambda f, info: (f, 0, 0)),
                pl.BlockSpec((depth, size), lambda f, info: (0, f)),
                pl.BlockSpec((4, 8, size, 2 * HEAD_DIM), lambda f, info: (0, 0, 0, 0)),
                pl.BlockSpec((depth, size), lambda f, info: (0, f)),
                pl.BlockSpec((depth, size), lambda f, info: (0, f)),
                pl.BlockSpec((1, 1, span), lambda f, info: (f, 0, 0)),
            ],
            out_specs=[
                pl.BlockSpec((depth, size), lambda f, info: (0, f)),
                pl.BlockSpec((4, 8, 2 * HEAD_DIM, size), lambda f, info: (0, 0, 0, 0)),
            ],
            scratch_shapes=[
                pltpu.VMEM((HEAD_DIM, span), jnp.bfloat16),
                pltpu.VMEM((HEAD_DIM, span), jnp.bfloat16),
                pltpu.VMEM((1, span), jnp.float32),
                pltpu.VMEM((HEAD_DIM, span), jnp.float32),
                pltpu.VMEM((4, 8, 2 * HEAD_DIM, size), jnp.float32),
            ],
        ),
        out_shape=[
            jax.ShapeDtypeStruct((depth, slots), jnp.float32),
            jax.ShapeDtypeStruct((4, 8, 2 * HEAD_DIM, size), jnp.bfloat16),
        ],
        compiler_params=pltpu.CompilerParams(vmem_limit_bytes=40 << 20),
        cost_estimate=lasting(80),
        name="attend_back",
    )(info, begins, queries, pair, outputs, grads, totals)


def turn(values, cosine, sine_table):
    heads = values.shape[0] // HEAD_DIM
    split = values.reshape(heads, 2, HEAD_DIM // 2, values.shape[1])
    first, second = split[:, 0], split[:, 1]
    turned = jnp.stack(
        [first * cosine - second * sine_table, second * cosine + first * sine_table], axis=1
    )
    return turned.reshape(values.shape)


def turn_back(values, cosine, sine_table):
    return turn(values, cosine, -sine_table)


def segment_begins(slots, lengths):
    seq_index = jnp.arange(lengths.shape[0], dtype=jnp.int32)
    ends = jnp.sum(jnp.where(seq_index[:, None] >= seq_index[None, :], lengths[None, :], 0), axis=1)
    passed = slots[:, None] >= ends[None, :]
    begins = jnp.sum(jnp.where(passed, lengths[None, :], 0), axis=1)
    return begins, slots < ends[-1]


def local_plane(
    tokens,
    attn_gain,
    query_weight,
    key_weight,
    value_weight,
    output_weight,
    mlp_gain,
    gate_weight,
    up_weight,
    down_weight,
    out_grad,
    lengths,
):
    size, width = tokens.shape
    f = lax.axis_index("fsdp")
    t = lax.axis_index("tp")
    block = query_weight.shape[0]
    head_rows = query_weight.shape[1] // 2
    units = gate_weight.shape[1] // 8
    bf16, f32 = jnp.bfloat16, jnp.float32

    inner_own = jnp.concatenate([query_weight.T, key_weight.T, value_weight.T], axis=0)
    hidden_parts = [w.reshape(8, units, block) for w in (down_weight, gate_weight.T, up_weight.T)]
    gains_own = jnp.stack([attn_gain, mlp_gain]).astype(f32)
    down_part, gate_part, up_part, inner_all, gains_all = first_exchange(
        hidden_parts, inner_own, gains_own, 1
    )
    down_rows = lax.all_gather(down_part, "tp", axis=0, tiled=True)
    gate_rows = lax.all_gather(gate_part, "tp", axis=0, tiled=True)
    up_rows = lax.all_gather(up_part, "tp", axis=0, tiled=True)
    gains = jnp.moveaxis(gains_all, 0, 1).reshape(2, width)
    gain_first, gain_second = gains[0:1], gains[1:2]

    my_slots = (f * 4 + t) * size + jnp.arange(size, dtype=jnp.int32)
    _, my_valid = segment_begins(my_slots, lengths)
    valid_rows = my_valid[:, None]
    chunk_index = jnp.arange(8, dtype=jnp.int32) * 4 + t
    plane_slots = (chunk_index[:, None] * size + jnp.arange(size, dtype=jnp.int32)[None, :]).reshape(-1)
    begins, plane_valid = segment_begins(plane_slots, lengths)
    positions = jnp.where(plane_valid, plane_slots - begins, 0)
    begins = begins.reshape(8, 1, size)
    info = jnp.stack(
        [
            begins[:, 0, 0] // size,
            jnp.minimum((begins[:, 0, size - 1] + size - 1) // size, chunk_index),
            chunk_index,
        ],
        axis=1,
    ).astype(jnp.int32)
    ladder = jnp.arange(HEAD_DIM // 2).astype(f32)
    frequency = 10000.0 ** (-2.0 * ladder / HEAD_DIM)
    angles = positions.astype(f32)[None, :] * frequency[:, None]
    cosine, sine_table = jnp.cos(angles), jnp.sin(angles)

    rows_first, queries, pair, inner_rows_w, output_rows = first_rows(
        tokens, gains_all, inner_all, output_weight, cosine, sine_table, 2
    )
    attended, totals = attend(info, begins, queries, pair)
    grad_rows_own = jnp.where(valid_rows, out_grad, jnp.zeros_like(out_grad))
    middle, row_second, grad_rows = forward_output(
        attended, output_rows, tokens, gain_second, grad_rows_own, 4
    )
    rows_second, hidden, grad_gate_low, grad_up_low = forward_hidden(
        row_second, grad_rows, gate_rows, up_rows, down_rows, 5
    )
    (
        grad_middle,
        gain_second_part,
        grad_output_w,
        grad_attended,
        hidden_grads,
    ) = backward_middle(
        grad_gate_low,
        grad_up_low,
        hidden,
        gate_rows,
        up_rows,
        rows_second,
        grad_rows,
        output_rows,
        attended,
        middle,
        grad_rows_own,
        gain_second,
        6,
    )
    hidden_grads = lax.psum_scatter(
        hidden_grads.reshape(12 * units, width), "tp", scatter_dimension=0, tiled=True
    )
    grad_queries, grad_pair_parts = attend_back(
        info, begins, queries, pair, attended, grad_attended, totals
    )
    grad_pair, layer_out, output_parts = backward_pairs(
        grad_pair_parts, hidden, down_rows, middle, valid_rows.astype(f32), grad_output_w, 7
    )
    grad_pair = jnp.moveaxis(grad_pair, 0, 1).reshape(2 * HEAD_DIM, 8 * size)
    grad_query_low = turn_back(grad_queries, cosine, sine_table).astype(bf16)
    grad_key_low = turn_back(grad_pair[:HEAD_DIM], cosine, sine_table)
    first_core = lax.rem(f, 2) == 0
    grad_single = jnp.where(first_core, grad_key_low, grad_pair[HEAD_DIM:]).astype(bf16)
    grad_inner = jnp.concatenate([grad_query_low, grad_single], axis=0)
    single_rows = jnp.where(
        first_core,
        inner_rows_w[head_rows : head_rows + HEAD_DIM],
        inner_rows_w[head_rows + HEAD_DIM :],
    )
    single_weights = jnp.concatenate([inner_rows_w[:head_rows], single_rows], axis=0)
    tokens_grad, gain_first_part, inner_parts = backward_first(
        grad_inner, single_weights, rows_first, tokens, grad_middle, gain_first, 8
    )

    def along_z(parts):
        rows = parts.shape[1]
        flat = parts.reshape(8 * rows, block)
        return lax.psum_scatter(flat, "tp", scatter_dimension=0, tiled=True).reshape(2, rows, block)

    output_parts, hidden_grads = lax.optimization_barrier((output_parts, hidden_grads))
    output_own = along_z(output_parts)
    inner_parts, output_own = lax.optimization_barrier((inner_parts, output_own))
    inner_grads = along_z(inner_parts)
    gain_parts = jnp.concatenate([gain_first_part, gain_second_part], axis=0)
    gain_parts = jnp.moveaxis(gain_parts.reshape(2, 8, block), 1, 0)
    hidden_own, gain_sums = last_exchange(hidden_grads.reshape(3, units, width), gain_parts, 9)
    own_down, own_gate, own_up = (hidden_own[:, n].reshape(8 * units, block) for n in range(3))
    return (
        layer_out,
        tokens_grad,
        gain_sums[0],
        inner_grads[:, :head_rows].reshape(2 * head_rows, block).T.astype(f32),
        inner_grads[0, head_rows:].T.astype(f32),
        inner_grads[1, head_rows:].T.astype(f32),
        output_own.reshape(2 * head_rows, block).astype(f32),
        gain_sums[1],
        own_gate.T.astype(f32),
        own_up.T.astype(f32),
        own_down.astype(f32),
    )


def solution(mesh):
    plane = dict(mesh.shape) == {"fsdp": 8, "tp": 4}
    body = local_plane if plane else local
    in_specs = (
        P(("fsdp", "tp"), None),
        P("fsdp"),
        P("fsdp", "tp"),
        P("fsdp", "tp"),
        P("fsdp", "tp"),
        P("tp", "fsdp"),
        P("fsdp"),
        P("fsdp", "tp"),
        P("fsdp", "tp"),
        P("tp", "fsdp"),
        P(("fsdp", "tp"), None),
        P(),
    )
    out_specs = (
        P(("fsdp", "tp"), None),
        P(("fsdp", "tp"), None),
        P("fsdp"),
        P("fsdp", "tp"),
        P("fsdp", "tp"),
        P("fsdp", "tp"),
        P("tp", "fsdp"),
        P("fsdp"),
        P("fsdp", "tp"),
        P("fsdp", "tp"),
        P("tp", "fsdp"),
    )
    return jax.shard_map(body, mesh=mesh, in_specs=in_specs, out_specs=out_specs, check_vma=False)
```

```python
import jax
import jax.numpy as jnp
from jax import lax
from jax.experimental import pallas as pl
from jax.experimental.pallas import tpu as pltpu
from jax.sharding import PartitionSpec as P

HEAD_DIM = 64
MAX_SPAN = 4096


epsilon = 1e-05


def passed_along(block, axis, distance):
    devices = range(lax.axis_size(axis))
    route = [(i - distance, i) for i in devices if i - distance in devices]
    return lax.ppermute(block, axis, route)


def stream_layout(slots, lengths):
    seq_count = lengths.shape[0]
    seq_index = jnp.arange(seq_count, dtype=jnp.int32)
    ends = jnp.sum(jnp.where(seq_index[:, None] >= seq_index[None, :], lengths[None, :], 0), axis=1)
    starts = ends - lengths
    segment = jnp.sum((slots[:, None] >= ends[None, :]).astype(jnp.int32), axis=1)
    start_of = jnp.sum(
        jnp.where(segment[:, None] == seq_index[None, :], starts[None, :], 0), axis=1
    )
    position = jnp.where((segment < seq_count) & (slots >= 0), slots - start_of, 0)
    segment = jnp.where(slots < 0, -1, segment)
    return (segment, position)


def rotary_tables(positions, head_width):
    ladder = jnp.arange(head_width // 2).astype(jnp.float32)
    frequency = 10000.0 ** (-2.0 * ladder / head_width)
    angle_half = positions.astype(jnp.float32)[:, None] * frequency[None, :]
    angles = jnp.concatenate([angle_half, angle_half], axis=1)
    return (jnp.cos(angles)[:, None, :], jnp.sin(angles)[:, None, :])


def rotate(values, cosine, sine_table):
    middle = values.shape[-1] // 2
    turned = jnp.concatenate([-values[..., middle:], values[..., :middle]], axis=-1)
    return values * cosine + turned * sine_table


def rotate_back(values, cosine, sine_table):
    middle = values.shape[-1] // 2
    scaled = values * sine_table
    turned = jnp.concatenate([scaled[..., middle:], -scaled[..., :middle]], axis=-1)
    return values * cosine + turned


def inner_rows(left, right):
    return lax.dot_general(
        left, right, (((0,), (0,)), ((), ())), preferred_element_type=jnp.float32
    )


def outer_cols(left, right):
    return lax.dot_general(
        left, right, (((1,), (1,)), ((), ())), preferred_element_type=jnp.float32
    )


def norm_back(grad_normed, gain_wide, normed, inverse):
    scaled_grad = grad_normed * gain_wide
    return inverse * (scaled_grad - normed * jnp.mean(scaled_grad * normed, axis=1, keepdims=True))


def local(
    tokens,
    attn_gain,
    query_weight,
    key_weight,
    value_weight,
    output_weight,
    mlp_gain,
    gate_weight,
    up_weight,
    down_weight,
    out_grad,
    lengths,
):
    row_count = tokens.shape[0]
    tp_count = lax.axis_size("tp")
    block_rows = row_count * tp_count
    slot_total = block_rows * lax.axis_size("fsdp")
    longest = min(MAX_SPAN, slot_total // 2)
    reach_count = (longest - 2) // block_rows + 1
    window = (reach_count + 1) * block_rows
    front_rows = reach_count * block_rows
    block_index = lax.axis_index("fsdp")
    tp_index = lax.axis_index("tp")
    head_width = HEAD_DIM
    query_width = query_weight.shape[1]
    key_width = key_weight.shape[1]
    heads_here = query_width // head_width
    score_scale = head_width ** (-0.5)
    seq_count = lengths.shape[0]
    row_base = (block_index * tp_count + tp_index) * row_count
    my_slots = row_base + jnp.arange(row_count, dtype=jnp.int32)
    my_segments, my_positions = stream_layout(my_slots, lengths)
    valid_rows = (my_segments < seq_count)[:, None]
    gathered = (
        lax.all_gather(query_weight, "fsdp", axis=0, tiled=True),
        lax.all_gather(key_weight, "fsdp", axis=0, tiled=True),
        lax.all_gather(value_weight, "fsdp", axis=0, tiled=True),
        lax.all_gather(output_weight, "fsdp", axis=1, tiled=True),
        lax.all_gather(gate_weight, "fsdp", axis=0, tiled=True),
        lax.all_gather(up_weight, "fsdp", axis=0, tiled=True),
        lax.all_gather(down_weight, "fsdp", axis=1, tiled=True),
        lax.all_gather(attn_gain, "fsdp", axis=0, tiled=True),
        lax.all_gather(mlp_gain, "fsdp", axis=0, tiled=True),
    )
    (
        full_query,
        full_key,
        full_value,
        full_output,
        full_gate,
        full_up,
        full_down,
        gain_first,
        gain_second,
    ) = gathered
    w_inner = jnp.concatenate([full_query, full_key, full_value], axis=1)
    gain_first_wide = gain_first.astype(jnp.float32)
    gain_second_wide = gain_second.astype(jnp.float32)
    tokens_wide = tokens.astype(jnp.float32)
    inverse_first = lax.rsqrt(jnp.mean(tokens_wide * tokens_wide, axis=1, keepdims=True) + epsilon)
    normed_first = tokens_wide * inverse_first
    scaled_first = (normed_first * gain_first_wide).astype(jnp.bfloat16)
    rows_first = lax.all_gather(scaled_first, "tp", axis=0, tiled=True)
    projected = jnp.dot(rows_first, w_inner, preferred_element_type=jnp.float32)
    block_base = block_index * block_rows
    key_slots = block_base - front_rows + jnp.arange(window, dtype=jnp.int32)
    key_segments, key_positions = stream_layout(key_slots, lengths)
    query_segments = key_segments[front_rows:]
    block_positions = key_positions[front_rows:]
    cosine, sine_table = rotary_tables(block_positions, head_width)
    queries = rotate(
        projected[:, :query_width].reshape(block_rows, heads_here, head_width), cosine, sine_table
    ).astype(jnp.bfloat16)
    keys_local = rotate(
        projected[:, query_width : query_width + key_width].reshape(block_rows, 1, head_width),
        cosine,
        sine_table,
    )
    keys_local = keys_local.reshape(block_rows, head_width).astype(jnp.bfloat16)
    values_local = projected[:, query_width + key_width :].astype(jnp.bfloat16)
    pair_local = jnp.concatenate([keys_local, values_local], axis=1)
    pieces = []
    for offset in range(reach_count, 0, -1):
        pieces.append(passed_along(pair_local, "fsdp", offset))
    pair_window = jnp.concatenate(pieces + [pair_local], axis=0)
    key_window = pair_window[:, :head_width]
    value_window = pair_window[:, head_width:]
    key_seen = (key_segments[None, :] == query_segments[:, None]) & (
        key_positions[None, :] <= block_positions[:, None]
    )

    def head_scores(query_head):
        scores = outer_cols(query_head, key_window) * score_scale
        return jnp.where(key_seen, scores, -1e30)

    def head_forward(query_head):
        scores = head_scores(query_head)
        largest = jnp.max(scores, axis=1, keepdims=True)
        raised = jnp.exp(scores - largest)
        row_total = jnp.sum(raised, axis=1, keepdims=True)
        attn_probs = (raised / row_total).astype(jnp.bfloat16)
        head_out = jnp.dot(attn_probs, value_window, preferred_element_type=jnp.float32)
        return (head_out, (largest + jnp.log(row_total))[:, 0])

    query_heads = jnp.moveaxis(queries, 1, 0)
    head_outs, log_totals = lax.map(head_forward, query_heads)
    attended = jnp.moveaxis(head_outs, 0, 1).reshape(block_rows, query_width).astype(jnp.bfloat16)
    attn_share = lax.psum_scatter(
        jnp.dot(attended, full_output, preferred_element_type=jnp.float32).astype(jnp.bfloat16),
        "tp",
        scatter_dimension=0,
        tiled=True,
    ).astype(jnp.float32)
    middle = tokens_wide + attn_share
    inverse_second = lax.rsqrt(jnp.mean(middle * middle, axis=1, keepdims=True) + epsilon)
    normed_second = middle * inverse_second
    scaled_second = (normed_second * gain_second_wide).astype(jnp.bfloat16)
    rows_second = lax.all_gather(scaled_second, "tp", axis=0, tiled=True)
    gate_proj = jnp.dot(rows_second, full_gate, preferred_element_type=jnp.float32)
    up_proj = jnp.dot(rows_second, full_up, preferred_element_type=jnp.float32)
    gate_sigmoid = jax.nn.sigmoid(gate_proj)
    gate_active = gate_proj * gate_sigmoid
    hidden = (gate_active * up_proj).astype(jnp.bfloat16)
    mlp_share = lax.psum_scatter(
        jnp.dot(hidden, full_down, preferred_element_type=jnp.float32).astype(jnp.bfloat16),
        "tp",
        scatter_dimension=0,
        tiled=True,
    ).astype(jnp.float32)
    layer_out = jnp.where(valid_rows, middle + mlp_share, 0.0).astype(jnp.bfloat16)
    grad_rows = jnp.where(valid_rows, out_grad.astype(jnp.float32), 0.0)
    grad_low = grad_rows.astype(jnp.bfloat16)
    regathered = (
        lax.all_gather(query_weight, "fsdp", axis=0, tiled=True),
        lax.all_gather(key_weight, "fsdp", axis=0, tiled=True),
        lax.all_gather(value_weight, "fsdp", axis=0, tiled=True),
        lax.all_gather(output_weight, "fsdp", axis=1, tiled=True),
        lax.all_gather(gate_weight, "fsdp", axis=0, tiled=True),
        lax.all_gather(up_weight, "fsdp", axis=0, tiled=True),
        lax.all_gather(down_weight, "fsdp", axis=1, tiled=True),
        lax.all_gather(attn_gain, "fsdp", axis=0, tiled=True),
        lax.all_gather(mlp_gain, "fsdp", axis=0, tiled=True),
    )
    (
        full_query,
        full_key,
        full_value,
        full_output,
        full_gate,
        full_up,
        full_down,
        gain_first,
        gain_second,
    ) = regathered
    w_inner = jnp.concatenate([full_query, full_key, full_value], axis=1)
    grad_down_rows = lax.all_gather(grad_low, "tp", axis=0, tiled=True)
    grad_down_w = inner_rows(hidden, grad_down_rows)
    grad_hidden = outer_cols(grad_down_rows, full_down)
    grad_up_low = (grad_hidden * gate_active).astype(jnp.bfloat16)
    grad_gate_low = (
        grad_hidden * up_proj * gate_sigmoid * (1.0 + gate_proj * (1.0 - gate_sigmoid))
    ).astype(jnp.bfloat16)
    grad_gate_w = inner_rows(rows_second, grad_gate_low)
    grad_up_w = inner_rows(rows_second, grad_up_low)
    grad_second = lax.psum_scatter(
        (outer_cols(grad_gate_low, full_gate) + outer_cols(grad_up_low, full_up)).astype(
            jnp.bfloat16
        ),
        "tp",
        scatter_dimension=0,
        tiled=True,
    ).astype(jnp.float32)
    gain_second_part = jnp.sum(grad_second * normed_second, axis=0)
    grad_middle = grad_rows + norm_back(
        grad_second, gain_second_wide, normed_second, inverse_second
    )
    middle_low = grad_middle.astype(jnp.bfloat16)
    grad_attn_rows = lax.all_gather(middle_low, "tp", axis=0, tiled=True)
    grad_output_w = inner_rows(attended, grad_attn_rows)
    grad_attended = outer_cols(grad_attn_rows, full_output).astype(jnp.bfloat16)
    grad_heads = jnp.moveaxis(grad_attended.reshape(block_rows, heads_here, head_width), 1, 0)

    def head_backward(packed):
        query_head, grad_head, log_total = packed
        attn_probs = jnp.exp(head_scores(query_head) - log_total[:, None])
        probs_low = attn_probs.astype(jnp.bfloat16)
        grad_value_head = inner_rows(probs_low, grad_head)
        grad_probs = outer_cols(grad_head, value_window)
        grad_scores = (
            attn_probs * (grad_probs - jnp.sum(attn_probs * grad_probs, axis=1, keepdims=True))
        ).astype(jnp.bfloat16)
        grad_query_head = (
            jnp.dot(grad_scores, key_window, preferred_element_type=jnp.float32) * score_scale
        )
        grad_key_head = inner_rows(grad_scores, query_head) * score_scale
        return (grad_query_head, grad_key_head, grad_value_head)

    grad_query_heads, grad_key_heads, grad_value_heads = lax.map(
        head_backward, (query_heads, grad_heads, log_totals)
    )
    grad_pair = jnp.concatenate(
        [jnp.sum(grad_key_heads, axis=0), jnp.sum(grad_value_heads, axis=0)], axis=1
    )
    own_grad = grad_pair[front_rows:]
    for offset in range(1, reach_count + 1):
        piece_start = (reach_count - offset) * block_rows
        own_grad = own_grad + passed_along(
            grad_pair[piece_start : piece_start + block_rows].astype(jnp.bfloat16), "fsdp", -offset
        ).astype(jnp.float32)
    grad_key_lin = rotate_back(
        own_grad[:, :head_width].reshape(block_rows, 1, head_width), cosine, sine_table
    )
    grad_key_low = grad_key_lin.reshape(block_rows, head_width).astype(jnp.bfloat16)
    grad_value_low = own_grad[:, head_width:].astype(jnp.bfloat16)
    grad_query_lin = rotate_back(jnp.moveaxis(grad_query_heads, 0, 1), cosine, sine_table)
    grad_query_low = grad_query_lin.reshape(block_rows, query_width).astype(jnp.bfloat16)
    grad_inner = jnp.concatenate([grad_query_low, grad_key_low, grad_value_low], axis=1)
    grad_inner_w = inner_rows(rows_first, grad_inner)
    grad_first = lax.psum_scatter(
        outer_cols(grad_inner, w_inner).astype(jnp.bfloat16), "tp", scatter_dimension=0, tiled=True
    ).astype(jnp.float32)
    gain_first_part = jnp.sum(grad_first * normed_first, axis=0)
    tokens_grad = grad_middle + norm_back(grad_first, gain_first_wide, normed_first, inverse_first)
    reduced = (
        lax.psum_scatter(
            grad_inner_w[:, :query_width].astype(jnp.bfloat16),
            "fsdp",
            scatter_dimension=0,
            tiled=True,
        ).astype(jnp.float32),
        lax.psum_scatter(
            grad_inner_w[:, query_width : query_width + key_width].astype(jnp.bfloat16),
            "fsdp",
            scatter_dimension=0,
            tiled=True,
        ).astype(jnp.float32),
        lax.psum_scatter(
            grad_inner_w[:, query_width + key_width :].astype(jnp.bfloat16),
            "fsdp",
            scatter_dimension=0,
            tiled=True,
        ).astype(jnp.float32),
        lax.psum_scatter(
            grad_output_w.astype(jnp.bfloat16), "fsdp", scatter_dimension=1, tiled=True
        ).astype(jnp.float32),
        lax.psum_scatter(
            grad_gate_w.astype(jnp.bfloat16), "fsdp", scatter_dimension=0, tiled=True
        ).astype(jnp.float32),
        lax.psum_scatter(
            grad_up_w.astype(jnp.bfloat16), "fsdp", scatter_dimension=0, tiled=True
        ).astype(jnp.float32),
        lax.psum_scatter(
            grad_down_w.astype(jnp.bfloat16), "fsdp", scatter_dimension=1, tiled=True
        ).astype(jnp.float32),
        lax.psum_scatter(
            gain_first_part.astype(jnp.bfloat16), "fsdp", scatter_dimension=0, tiled=True
        ).astype(jnp.float32),
        lax.psum_scatter(
            gain_second_part.astype(jnp.bfloat16), "fsdp", scatter_dimension=0, tiled=True
        ).astype(jnp.float32),
    )
    gain_sums = lax.psum((reduced[7], reduced[8]), "tp")
    return (
        layer_out,
        tokens_grad,
        gain_sums[0],
        reduced[0],
        reduced[1],
        reduced[2],
        reduced[3],
        gain_sums[1],
        reduced[4],
        reduced[5],
        reduced[6],
    )


MESH = pl.DeviceIdType.MESH
CORE, ALONG_X, ALONG_Y = 1, 2, 4
PARTS = 4
VMEM_MOST = 60 << 20


def greet(partners):
    barrier = pltpu.get_barrier_semaphore()
    for partner in partners:
        pl.semaphore_signal(barrier, inc=1, device_id=partner, device_id_type=MESH)
    pl.semaphore_wait(barrier, len(partners))


def remote(source, target, sent, arrived, partner):
    return pltpu.make_async_remote_copy(
        src_ref=source,
        dst_ref=target,
        send_sem=sent,
        recv_sem=arrived,
        device_id=partner,
        device_id_type=MESH,
    )


def comm_params(number, vmem=None):
    return pltpu.CompilerParams(
        collective_id=number, has_side_effects=True, vmem_limit_bytes=vmem
    )


def lasting(microseconds):
    return pl.CostEstimate(
        flops=int(microseconds * 1.1e9), bytes_accessed=1_000_000, transcendentals=0
    )


ANYWHERE = pl.BlockSpec(memory_space=pl.ANY)
IN_VMEM = pl.BlockSpec(memory_space=pltpu.VMEM)


def columns(index, width):
    return pl.ds(pl.multiple_of(index * width, width), width)


class PlaneGather:
    def __init__(self, store, sent, arrived):
        self.f, self.t = lax.axis_index("fsdp"), lax.axis_index("tp")
        self.store, self.sent, self.arrived = store, sent, arrived
        self.piece = store.shape[1] // PARTS
        self.near = [(self.f ^ k, self.t) for k in (CORE, ALONG_X, ALONG_Y)]
        self.copies, self.on = [], {}

    def send(self, owner, j, way, slot):
        place = self.store.at[owner, pl.ds(j * self.piece, self.piece)]
        c = remote(
            place, place, self.sent.at[slot, j], self.arrived.at[slot, j], self.near[way]
        )
        c.start()
        self.copies.append(c)
        self.on[slot, j] = c

    def begin(self):
        for k in range(PARTS):
            self.send(self.f, k, 1, 1)
            self.send(self.f, (k + PARTS // 2) % PARTS, 2, 2)
        for k in range(PARTS):
            self.send(self.f, k, 0, 0)

    def arrive(self, slot, j):
        self.on[slot, j].wait_recv()

    def advance(self, k):
        jx, jy = k, (k + PARTS // 2) % PARTS
        self.arrive(1, jx)
        if jx < PARTS // 2:
            self.send(self.f ^ ALONG_X, jx, 2, 6)
        self.send(self.f ^ ALONG_X, jx, 0, 3)
        self.arrive(2, jy)
        if jy >= PARTS // 2:
            self.send(self.f ^ ALONG_Y, jy, 1, 6)
        self.send(self.f ^ ALONG_Y, jy, 0, 4)

    def far(self):
        for k in range(PARTS // 2):
            for j in (k, k + PARTS // 2):
                self.arrive(6, j)
                self.send(self.f ^ ALONG_X ^ ALONG_Y, j, 0, 5)

    def wait_core(self, *slots):
        for slot in slots:
            for j in range(PARTS):
                self.arrive(slot, j)

    def finish(self):
        for c in self.copies:
            c.wait_send()


GATHER_SEMAPHORES = [pltpu.SemaphoreType.DMA((7, PARTS)), pltpu.SemaphoreType.DMA((7, PARTS))]


class PlaneSum:
    masks = (ALONG_X ^ ALONG_Y, ALONG_X, ALONG_Y, 0)

    def __init__(self, stage, other, held, from_x, from_y, last, sent, arrived):
        self.f, self.t = lax.axis_index("fsdp"), lax.axis_index("tp")
        self.stage, self.other, self.held = stage, other, held
        self.from_x, self.from_y, self.last = from_x, from_y, last
        self.sent, self.arrived = sent, arrived
        self.near = [(self.f ^ k, self.t) for k in (CORE, ALONG_X, ALONG_Y)]
        self.copies, self.on = [], {}
        half = held.shape[1] // 2
        self.top, self.low = pl.ds(0, half), pl.ds(half, half)

    def send(self, source, target, slot, way):
        c = remote(source, target, self.sent.at[slot], self.arrived.at[slot], self.near[way])
        c.start()
        self.copies.append(c)
        self.on[slot] = c

    def begin(self, write_part, after=None):
        for i, mask in enumerate(self.masks):
            if i >= 2:
                self.on[i - 2].wait_send()
                self.copies = [c for c in self.copies if c is not self.on[i - 2]]
            write_part(self.f ^ CORE ^ mask, self.stage.at[i % 2])
            self.send(self.stage.at[i % 2], self.other.at[i], i, 0)
            write_part(self.f ^ mask, self.held.at[i])
            if after is not None:
                after(i)
            self.on[i].wait_recv()
            self.held[i] = (
                self.held[i].astype(jnp.float32) + self.other[i].astype(jnp.float32)
            ).astype(jnp.bfloat16)
            if i == 0:
                self.send(self.held.at[0, self.top], self.from_x.at[0], 4, 1)
                self.send(self.held.at[0, self.low], self.from_y.at[0], 5, 2)
            if i == 1:
                self.send(self.held.at[1, self.top], self.from_x.at[1], 6, 1)
            if i == 2:
                self.send(self.held.at[2, self.low], self.from_y.at[1], 7, 2)

    def turn(self):
        self.on[4].wait_recv()
        self.held[2, self.top] = (
            self.held[2, self.top].astype(jnp.float32) + self.from_x[0].astype(jnp.float32)
        ).astype(jnp.bfloat16)
        self.send(self.held.at[2, self.top], self.last.at[0], 8, 2)
        self.on[5].wait_recv()
        self.held[1, self.low] = (
            self.held[1, self.low].astype(jnp.float32) + self.from_y[0].astype(jnp.float32)
        ).astype(jnp.bfloat16)
        self.send(self.held.at[1, self.low], self.last.at[1], 9, 1)

    def end(self, total):
        for rows, first, second, take in (
            (self.top, 6, 8, lambda: self.from_x[1]),
            (self.low, 7, 9, lambda: self.from_y[1]),
        ):
            self.on[first].wait_recv()
            part = self.held[3, rows].astype(jnp.float32) + take().astype(jnp.float32)
            self.on[second].wait_recv()
            total[rows] = part + self.last[second - 8].astype(jnp.float32)

    def finish(self):
        for c in self.copies:
            c.wait_send()


def sum_scratch(height, width):
    chunks = [pltpu.VMEM((n, height, width), jnp.bfloat16) for n in (2, 4, 4)]
    return chunks + [pltpu.VMEM((2, height // 2, width), jnp.bfloat16)] * 3 + [pltpu.SemaphoreType.DMA((10,)), pltpu.SemaphoreType.DMA((10,))]


NARROW = 512


def chunk_part(pairs, size):
    def write_part(owner, ref):
        lanes = columns(owner, size)
        lefts = [left[:, lanes] for left, _ in pairs]

        def step(n, carry):
            wide = columns(n, NARROW)
            total = inner_rows(lefts[0], pairs[0][1][:, wide])
            for left, (_, right) in zip(lefts[1:], pairs[1:]):
                total += inner_rows(left, right[:, wide])
            ref[:, wide] = total.astype(jnp.bfloat16)
            return carry

        lax.fori_loop(0, ref.shape[1] // NARROW, step, 0)

    return write_part


def plane_greet():
    f, t = lax.axis_index("fsdp"), lax.axis_index("tp")
    greet([(f ^ k, t) for k in (CORE, ALONG_X, ALONG_Y)])


def forward_output(attended, output_rows, tokens, gain, number):
    size, width = tokens.shape
    f32, bf16 = jnp.float32, jnp.bfloat16

    def kernel(
        o_ref, w_ref, x_ref, gain_ref,
        middle_ref, row_ref,
        stage, other, held, from_x, from_y, last, sum_sent, sum_arrived,
    ):
        plane_greet()
        total = PlaneSum(stage, other, held, from_x, from_y, last, sum_sent, sum_arrived)
        total.begin(chunk_part([(o_ref, w_ref)], size))
        total.turn()
        total.end(middle_ref)
        middle = x_ref[...].astype(f32) + middle_ref[...]
        middle_ref[...] = middle
        inverse = lax.rsqrt(jnp.mean(middle * middle, axis=1, keepdims=True) + epsilon)
        row_ref[...] = (middle * inverse * gain_ref[...]).astype(bf16)
        total.finish()

    return pl.pallas_call(
        kernel,
        out_shape=[
            jax.ShapeDtypeStruct((size, width), f32),
            jax.ShapeDtypeStruct((size, width), bf16),
        ],
        in_specs=[IN_VMEM] * 4,
        out_specs=[IN_VMEM] * 2,
        scratch_shapes=sum_scratch(size, width),
        compiler_params=comm_params(number, 40 << 20),
        cost_estimate=lasting(45),
        name="forward_output",
    )(attended, output_rows, tokens, gain)


def forward_hidden(row, dys, gate_rows, up_rows, down_rows, number):
    size, width = row.shape
    units = gate_rows.shape[0]
    f32, bf16 = jnp.float32, jnp.bfloat16

    def kernel(
        row_ref, dys_hbm, gate_hbm, up_hbm, down_hbm,
        rows_ref, hidden_ref, dgate_ref, dup_ref, down_grad_ref,
        rows, rows_sent, rows_arrived, dys, gate_w, up_w, down_w, load_sem, dh, out, out_sem, keep_sem, down_grad,
    ):
        f = lax.axis_index("fsdp")
        loads = [
            pltpu.make_async_copy(source, target, load_sem.at[i])
            for i, (source, target) in enumerate(
                ((down_hbm, down_w), (dys_hbm, dys), (gate_hbm, gate_w), (up_hbm, up_w))
            )
        ]
        for load in loads:
            load.start()
        rows[f] = row_ref[...]
        plane_greet()
        gather_rows = PlaneGather(rows, rows_sent, rows_arrived)
        gather_rows.begin()
        loads[0].wait()
        loads[1].wait()

        def grad_chunk(i, carry):
            dh[i] = outer_cols(down_w[...], dys[i])
            return carry

        for k in range(PARTS):
            lax.fori_loop(2 * k, 2 * k + 2, grad_chunk, 0)
            gather_rows.advance(k)
        loads[2].wait()
        loads[3].wait()

        def out_copies(slot, owner):
            return [
                pltpu.make_async_copy(
                    out.at[slot, n], target.at[:, columns(owner, size)], out_sem.at[slot, n]
                )
                for n, target in enumerate((hidden_ref, dgate_ref, dup_ref))
            ]

        def chunk(i, carry):
            owner = f ^ i
            slot = lax.rem(i, 2)

            @pl.when(i >= 2)
            def _():
                for c in out_copies(slot, owner):
                    c.wait()

            gate = outer_cols(gate_w[...], rows[owner])
            up = outer_cols(up_w[...], rows[owner])
            sigmoid = jax.nn.sigmoid(gate)
            active = gate * sigmoid
            grad = dh[owner]
            hidden = (active * up).astype(bf16)
            out[slot, 0] = hidden
            down_grad[...] += dot_nn(hidden, dys[owner])
            out[slot, 1] = (grad * up * sigmoid * (1.0 + gate * (1.0 - sigmoid))).astype(bf16)
            out[slot, 2] = (grad * active).astype(bf16)
            for c in out_copies(slot, owner):
                c.start()
            return carry

        down_grad[...] = jnp.zeros_like(down_grad)
        gather_rows.wait_core(0)
        lax.fori_loop(0, 2, chunk, 0)
        gather_rows.wait_core(3, 4)
        lax.fori_loop(2, 4, chunk, 0)
        gather_rows.far()
        lax.fori_loop(4, 6, chunk, 0)
        gather_rows.wait_core(5)
        keep = pltpu.make_async_copy(rows, rows_ref, keep_sem)
        keep.start()
        lax.fori_loop(6, 8, chunk, 0)
        down_grad_ref[...] = down_grad[...].astype(bf16)
        for i in (6, 7):
            for c in out_copies(i % 2, f ^ i):
                c.wait()
        keep.wait()
        gather_rows.finish()

    store = pltpu.VMEM((8, size, width), bf16)
    weights = pltpu.VMEM((units, width), bf16)
    return pl.pallas_call(
        kernel,
        out_shape=[jax.ShapeDtypeStruct((8, size, width), bf16)]
        + [jax.ShapeDtypeStruct((units, 8 * size), bf16)] * 3
        + [jax.ShapeDtypeStruct((units, width), bf16)],
        in_specs=[IN_VMEM] + [ANYWHERE] * 4,
        out_specs=[ANYWHERE] * 4 + [IN_VMEM],
        scratch_shapes=[store]
        + GATHER_SEMAPHORES
        + [store]
        + [weights] * 3
        + [
            pltpu.SemaphoreType.DMA((4,)),
            pltpu.VMEM((8, units, size), f32),
            pltpu.VMEM((2, 3, units, size), bf16),
            pltpu.SemaphoreType.DMA((2, 3)),
            pltpu.SemaphoreType.DMA,
            pltpu.VMEM((units, width), f32),
        ],
        compiler_params=comm_params(number, 56 << 20),
        cost_estimate=lasting(50),
        name="forward_hidden",
    )(row, dys, gate_rows, up_rows, down_rows)


def backward_middle(
    dgate, dup, gate_rows, up_rows, rows, output_rows, attended, middle, grads, gain, number
):
    size, width = middle.shape
    units = gate_rows.shape[0]
    depth = output_rows.shape[0]
    blocks = width // size
    f32, bf16 = jnp.float32, jnp.bfloat16
    early = 5

    def kernel(
        dgate_hbm, dup_hbm, gate_hbm, up_hbm, rows_hbm,
        w_ref, o_ref, middle_ref, dy_ref, gain_ref,
        grad_ref, gain_grad_ref, grad_o_ref, do_ref, units_ref,
        stage, other, held, from_x, from_y, last, sum_sent, sum_arrived,
        store, store_sent, store_arrived,
        dgate_v, dup_v, gate_w, up_w, load_sem,
        tall, tall_sem, out, out_sem, o_sum,
    ):
        f = lax.axis_index("fsdp")
        loads = [
            pltpu.make_async_copy(source, target, load_sem.at[i])
            for i, (source, target) in enumerate(
                (
                    (dgate_hbm, dgate_v),
                    (gate_hbm, gate_w),
                    (dup_hbm, dup_v),
                    (up_hbm, up_w),
                )
            )
        ]
        for load in loads:
            load.start()

        def tall_load(n, slot):
            return pltpu.make_async_copy(
                rows_hbm.at[:, :, columns(n, size)], tall.at[slot], tall_sem.at[slot]
            )

        tall_load(0, 0).start()
        plane_greet()
        total = PlaneSum(stage, other, held, from_x, from_y, last, sum_sent, sum_arrived)
        gather = PlaneGather(store, store_sent, store_arrived)
        for load in loads:
            load.wait()
        total.begin(chunk_part([(dgate_v, gate_w), (dup_v, up_w)], size))
        total.turn()

        def out_copies(n, slot):
            return [
                pltpu.make_async_copy(
                    out.at[slot, i], units_ref.at[:, i, :, columns(n, size)], out_sem.at[slot, i]
                )
                for i in range(2)
            ]

        def block(n, carry):
            slot = lax.rem(n, 2)

            @pl.when(n + 1 < blocks)
            def _():
                tall_load(n + 1, 1 - slot).start()

            tall_load(n, slot).wait()

            @pl.when(n >= 2)
            def _():
                for c in out_copies(n, slot):
                    c.wait()

            row_cols = tall[slot].reshape(8 * size, size)
            for i, left in enumerate((dgate_v, dup_v)):
                out[slot, i] = dot_nn(left[...], row_cols).astype(bf16).reshape(4, units // 4, size)
            for c in out_copies(n, slot):
                c.start()
            return carry

        lax.fori_loop(0, early, block, 0)
        total.end(grad_ref)
        middle = middle_ref[...]
        inverse = lax.rsqrt(jnp.mean(middle * middle, axis=1, keepdims=True) + epsilon)
        normed = middle * inverse
        grad = grad_ref[...]
        gain_grad_ref[...] = jnp.sum(grad * normed, axis=0, keepdims=True)
        grad = dy_ref[...].astype(f32) + norm_back(grad, gain_ref[...], normed, inverse)
        grad_ref[...] = grad
        store[f] = grad.astype(bf16)
        gather.begin()
        gather.advance(0)
        lax.fori_loop(early, early + 1, block, 0)
        gather.advance(1)
        lax.fori_loop(early + 1, early + 2, block, 0)
        gather.advance(2)
        lax.fori_loop(early + 2, blocks, block, 0)
        gather.advance(3)

        def chunk(i, carry):
            owner = f ^ i
            lanes = columns(owner, size)
            do_ref[:, lanes] = outer_cols(w_ref[...], store[owner]).astype(bf16)
            o_sum[...] += dot_nn(o_ref[:, lanes], store[owner])
            return carry

        o_sum[...] = jnp.zeros_like(o_sum)
        gather.wait_core(0)
        lax.fori_loop(0, 2, chunk, 0)
        gather.wait_core(3, 4)
        lax.fori_loop(2, 6, chunk, 0)
        gather.far()
        gather.wait_core(5)
        lax.fori_loop(6, 8, chunk, 0)
        grad_o_ref[...] = o_sum[...].astype(bf16)
        for n in (blocks - 2, blocks - 1):
            for c in out_copies(n, n % 2):
                c.wait()
        total.finish()
        gather.finish()

    weights = pltpu.VMEM((units, width), bf16)
    return pl.pallas_call(
        kernel,
        out_shape=[
            jax.ShapeDtypeStruct((size, width), f32),
            jax.ShapeDtypeStruct((1, width), f32),
            jax.ShapeDtypeStruct((depth, width), bf16),
            jax.ShapeDtypeStruct((depth, 8 * size), bf16),
        ]
        + [jax.ShapeDtypeStruct((4, 2, units // 4, width), bf16)],
        in_specs=[ANYWHERE] * 5 + [IN_VMEM] * 5,
        out_specs=[IN_VMEM] * 4 + [ANYWHERE],
        scratch_shapes=sum_scratch(size, width)
        + [pltpu.VMEM((8, size, width), bf16)]
        + GATHER_SEMAPHORES
        + [weights] * 4
        + [
            pltpu.SemaphoreType.DMA((4,)),
            pltpu.VMEM((2, 8, size, size), bf16),
            pltpu.SemaphoreType.DMA((2,)),
            pltpu.VMEM((2, 2, 4, units // 4, size), bf16),
            pltpu.SemaphoreType.DMA((2, 2)),
            pltpu.VMEM((depth, width), f32),
        ],
        compiler_params=comm_params(number, VMEM_MOST),
        cost_estimate=lasting(92),
        name="backward_middle",
    )(dgate, dup, gate_rows, up_rows, rows, output_rows, attended, middle, grads, gain)


class LineGather:
    def __init__(self, own, store, sent, arrived):
        self.f, self.t = lax.axis_index("fsdp"), lax.axis_index("tp")
        self.own, self.store, self.sent, self.arrived = own, store, sent, arrived

    def copy(self, way, hop):
        step = 1 if way == 0 else -1
        place = self.store.at[self.t - step * (hop - 1)]
        source = self.own if hop == 1 else place
        return remote(
            source, place, self.sent.at[way, hop], self.arrived.at[way, hop], (self.f, self.t + step)
        )

    def goes(self, way, hop):
        if way == 0:
            return (self.t < 3) & (self.t >= hop - 1)
        return (self.t > 0) & (self.t <= 4 - hop)

    def came(self, way, hop):
        return self.t >= hop if way == 0 else self.t <= 3 - hop

    def send(self, hop):
        for way in (0, 1):
            pl.when(self.goes(way, hop))(lambda way=way: self.copy(way, hop).start())

    def begin(self):
        self.send(1)

    def take(self, hop):
        for way in (0, 1):

            @pl.when(self.came(way, hop))
            def _(way=way):
                spot = self.store.at[self.t - hop if way == 0 else self.t + hop]
                remote(
                    spot, spot, self.sent.at[way, hop], self.arrived.at[way, hop], (self.f, self.t)
                ).wait_recv()

        if hop < 3:
            self.send(hop + 1)

    def finish(self):
        for hop in (1, 2, 3):
            for way in (0, 1):
                pl.when(self.goes(way, hop))(lambda way=way, hop=hop: self.copy(way, hop).wait_send())


LINE_SEMAPHORES = [pltpu.SemaphoreType.DMA((2, 4)), pltpu.SemaphoreType.DMA((2, 4))]


def line_greet(f, t):
    barrier = pltpu.get_barrier_semaphore()
    for k in range(1, 8):
        pl.semaphore_signal(barrier, inc=1, device_id=(f ^ k, t), device_id_type=MESH)
    for there, step in ((t < 3, 1), (t > 0, -1)):

        @pl.when(there)
        def _(step=step):
            pl.semaphore_signal(barrier, inc=1, device_id=(f, t + step), device_id_type=MESH)

    ends = (t == 0).astype(jnp.int32) + (t == 3).astype(jnp.int32)
    pl.semaphore_wait(barrier, 9 - ends)


def everyone(f, t):
    return [(f ^ k, t) for k in range(1, 8)] + [(f, lax.rem(t + k, 4)) for k in (1, 2, 3)]


def first_exchange(parts, inner, gains, number):
    _, units, block = parts[0].shape
    count = len(parts)
    far_first = (6, 7, 2, 4, 3, 5, 1)

    def kernel(*refs):
        sources, (inner_ref, gains_ref) = refs[:count], refs[count : count + 2]
        targets, (inner_all, gains_all) = refs[count + 2 : 2 * count + 2], refs[2 * count + 2 : 2 * count + 4]
        sent, arrived, z_sent, z_arrived, kept_sem = refs[2 * count + 4 :]
        f, t = lax.axis_index("fsdp"), lax.axis_index("tp")
        place = columns(f, block)
        kept = [
            pltpu.make_async_copy(s.at[f], o.at[:, place], kept_sem.at[i])
            for i, (s, o) in enumerate(zip(sources, targets))
        ] + [pltpu.make_async_copy(inner_ref, inner_all.at[t], kept_sem.at[count])]
        for c in kept:
            c.start()
        gains_all[f] = gains_ref[...]
        line_greet(f, t)
        line = LineGather(inner_ref, inner_all, z_sent, z_arrived)
        line.begin()
        copies = []
        for k in far_first:
            copies.append(
                remote(gains_ref, gains_all.at[f], sent.at[k, count], arrived.at[k, count], (f ^ k, t))
            )
        for i, (s, o) in enumerate(zip(sources, targets)):
            for k in far_first:
                copies.append(
                    remote(s.at[f ^ k], o.at[:, place], sent.at[k, i], arrived.at[k, i], (f ^ k, t))
                )
        for c in copies:
            c.start()
        for hop in (1, 2, 3):
            line.take(hop)
        for c in kept + copies:
            c.wait()
        line.finish()

    return pl.pallas_call(
        kernel,
        out_shape=[jax.ShapeDtypeStruct((units, 8 * block), jnp.bfloat16)] * count
        + [
            jax.ShapeDtypeStruct((4, *inner.shape), inner.dtype),
            jax.ShapeDtypeStruct((8, *gains.shape), gains.dtype),
        ],
        in_specs=[ANYWHERE] * (count + 1) + [IN_VMEM],
        out_specs=[ANYWHERE] * (count + 1) + [IN_VMEM],
        scratch_shapes=[
            pltpu.SemaphoreType.DMA((8, count + 1)),
            pltpu.SemaphoreType.DMA((8, count + 1)),
            *LINE_SEMAPHORES,
            pltpu.SemaphoreType.DMA((count + 1,)),
        ],
        compiler_params=comm_params(number),
        cost_estimate=lasting(32),
        name="first_exchange",
    )(*parts, inner, gains)


def turn_heads(values, cosine, sine_table):
    half = HEAD_DIM // 2
    turned = []
    for h in range(values.shape[0] // HEAD_DIM):
        first = values[h * HEAD_DIM : h * HEAD_DIM + half]
        second = values[h * HEAD_DIM + half : (h + 1) * HEAD_DIM]
        turned.append(first * cosine - second * sine_table)
        turned.append(second * cosine + first * sine_table)
    return jnp.concatenate(turned, axis=0)


def first_rows(tokens, gains, inner_all, output_own, cosine, sine_table, grads, number):
    size, width = tokens.shape
    block = width // 8
    quarter_rows = output_own.shape[0]
    depth = quarter_rows // 2
    pair_rows = 2 * HEAD_DIM
    f32, bf16 = jnp.float32, jnp.bfloat16

    def kernel(
        x_ref, gains_ref, inner_ref, own_ref, cos_ref, sin_ref, dy_ref,
        rows_ref, q_ref, pair_ref, w_ref, wo_ref, wo_all, dys_ref,
        rows, rows_sent, rows_arrived, dys, dys_sent, dys_arrived, pair_v,
        w_sent, w_arrived, o_sent, o_arrived, z_sent, z_arrived,
        p_sent, p_arrived, on_sent, on_arrived, kept_sem,
    ):
        f, t = lax.axis_index("fsdp"), lax.axis_index("tp")
        place = columns(f, block)
        far_first = (6, 7, 2, 4, 3, 5, 1)

        def inner_slices(j):
            quarter, side = lax.div(j, 2), lax.rem(j, 2)
            return [
                (
                    inner_ref.at[quarter, pl.ds(pl.multiple_of(side * depth, depth), depth)],
                    w_ref.at[pl.ds(0, depth), place],
                ),
                (
                    inner_ref.at[quarter, pl.ds(2 * depth, pair_rows)],
                    w_ref.at[pl.ds(depth, pair_rows), place],
                ),
            ]

        def output_slice(j):
            quarter, side = lax.div(j, 2), lax.rem(j, 2)
            return (
                wo_all.at[quarter, pl.ds(pl.multiple_of(side * depth, depth), depth)],
                wo_ref.at[:, place],
            )

        kept = [
            pltpu.make_async_copy(s, o, kept_sem.at[i]) for i, (s, o) in enumerate(inner_slices(f))
        ]
        kept.append(pltpu.make_async_copy(own_ref, wo_all.at[t], kept_sem.at[2]))
        for c in kept:
            c.start()
        greet(everyone(f, t))
        line_output = LineGather(own_ref, wo_all, z_sent, z_arrived)
        line_output.begin()
        copies, weights = [], []
        for k in far_first:
            for i, (s, o) in enumerate(inner_slices(f ^ k)):
                c = remote(s, o, w_sent.at[k, i], w_arrived.at[k, i], (f ^ k, t))
                c.start()
                weights.append(c)
        gain = jnp.concatenate([gains_ref[j, 0:1] for j in range(8)], axis=1)
        wide = x_ref[...].astype(f32)
        inverse = lax.rsqrt(jnp.mean(wide * wide, axis=1, keepdims=True) + epsilon)
        rows[f] = (wide * inverse * gain).astype(bf16)
        gather = PlaneGather(rows, rows_sent, rows_arrived)
        gather.begin()
        dys[f] = dy_ref[...]
        for k in range(PARTS):
            gather.advance(k)
        gather_dys = PlaneGather(dys, dys_sent, dys_arrived)
        gather_dys.begin()
        for c in kept[:2]:
            c.wait()
        for c in weights:
            c.wait_recv()
        line_output.take(1)

        def chunk(i, carry):
            owner = f ^ i
            lanes = columns(owner, size)
            projected = outer_cols(w_ref[...], rows[owner])
            cosine, sine = cos_ref[:, lanes], sin_ref[:, lanes]
            queries = turn_heads(projected[:depth], cosine, sine).astype(bf16)
            q_ref[:, lanes] = (queries.astype(f32) * HEAD_DIM ** (-0.5)).astype(bf16)
            keys = turn_heads(projected[depth : depth + HEAD_DIM], cosine, sine)
            pair = jnp.concatenate([keys, projected[depth + HEAD_DIM :]], axis=0)
            pair_v[owner] = pair.T.astype(bf16)
            return carry

        spread = []

        def spread_pair(i):
            for k in (2, 1, 3):
                c = remote(
                    pair_v.at[f ^ i],
                    pair_ref.at[t, f ^ i],
                    p_sent.at[i // 2, k],
                    p_arrived.at[i // 2, k],
                    (f, lax.rem(t + k, 4)),
                )
                c.start()
                spread.append((i, k, c))

        gather.wait_core(0)
        lax.fori_loop(0, 2, chunk, 0)
        spread_pair(0)
        gather.wait_core(3, 4)
        lax.fori_loop(2, 6, chunk, 0)
        spread_pair(2)
        spread_pair(4)
        line_output.take(2)
        gather.far()
        gather.wait_core(5)
        lax.fori_loop(6, 8, chunk, 0)
        spread_pair(6)
        own_pair = pltpu.make_async_copy(pair_v, pair_ref.at[t], kept_sem.at[3])
        own_pair.start()
        keep_rows = pltpu.make_async_copy(rows, rows_ref, kept_sem.at[4])
        keep_rows.start()
        kept[2].wait()
        line_output.take(3)
        for k in far_first:
            s, o = output_slice(f ^ k)
            c = remote(s, o, o_sent.at[k], o_arrived.at[k], (f ^ k, t))
            c.start()
            copies.append(c)
        s, o = output_slice(f)
        keep_output = pltpu.make_async_copy(s, o, kept_sem.at[5])
        keep_output.start()
        for k in range(PARTS):
            gather_dys.advance(k)
        passed = []
        for i, k, c in spread:
            c.wait_recv()
            spot = pair_ref.at[lax.rem(t + 4 - k, 4), f ^ i]
            d = remote(spot, spot, on_sent.at[i // 2, k], on_arrived.at[i // 2, k], (f ^ CORE, t))
            d.start()
            passed.append(d)
        gather_dys.wait_core(0, 3, 4)
        gather_dys.far()
        gather_dys.wait_core(5)
        keep_dys = pltpu.make_async_copy(dys, dys_ref, kept_sem.at[6])
        keep_dys.start()
        for c in passed + copies:
            c.wait()
        for c in weights + [c for _, _, c in spread]:
            c.wait_send()
        line_output.finish()
        gather.finish()
        gather_dys.finish()
        own_pair.wait()
        keep_rows.wait()
        keep_output.wait()
        keep_dys.wait()

    dma = pltpu.SemaphoreType.DMA
    return pl.pallas_call(
        kernel,
        out_shape=[
            jax.ShapeDtypeStruct((8, size, width), bf16),
            jax.ShapeDtypeStruct((depth, 8 * size), bf16),
            jax.ShapeDtypeStruct((4, 8, size, pair_rows), bf16),
            jax.ShapeDtypeStruct((depth + pair_rows, width), bf16),
            jax.ShapeDtypeStruct((depth, width), bf16),
            jax.ShapeDtypeStruct((4, quarter_rows, block), bf16),
            jax.ShapeDtypeStruct((8, size, width), bf16),
        ],
        in_specs=[IN_VMEM, IN_VMEM, ANYWHERE, ANYWHERE, IN_VMEM, IN_VMEM, IN_VMEM],
        out_specs=[ANYWHERE, IN_VMEM, ANYWHERE, IN_VMEM, ANYWHERE, ANYWHERE, ANYWHERE],
        scratch_shapes=[pltpu.VMEM((8, size, width), bf16)]
        + GATHER_SEMAPHORES
        + [pltpu.VMEM((8, size, width), bf16)]
        + GATHER_SEMAPHORES
        + [
            pltpu.VMEM((8, size, pair_rows), bf16),
            dma((8, 2)),
            dma((8, 2)),
            dma((8,)),
            dma((8,)),
            *LINE_SEMAPHORES,
            dma((4, 4)),
            dma((4, 4)),
            dma((4, 4)),
            dma((4, 4)),
            dma((7,)),
        ],
        compiler_params=comm_params(number, 40 << 20),
        cost_estimate=lasting(100),
        name="first_rows",
    )(tokens, gains, inner_all, output_own, cosine, sine_table, grads)


def backward_pairs(pair_parts, hidden, down_rows, middle, valid, grad_output, number):
    size, width = middle.shape
    units = hidden.shape[0]
    depth = grad_output.shape[0]
    _, chunks, height, _ = pair_parts.shape
    half = chunks // 2
    f32, bf16 = jnp.float32, jnp.bfloat16

    def kernel(
        p_ref, hidden_hbm, down_hbm, middle_ref, valid_ref, g_ref,
        pair_ref, out_ref, spread_ref,
        stage, other, held, from_x, from_y, last, sum_sent, sum_arrived,
        hidden_v, down_w, load_sem, ra, s, rz, sent, arrived, g_sent, g_arrived, share,
    ):
        f, t = lax.axis_index("fsdp"), lax.axis_index("tp")
        loads = [
            pltpu.make_async_copy(hidden_hbm, hidden_v, load_sem.at[0]),
            pltpu.make_async_copy(down_hbm, down_w, load_sem.at[1]),
            pltpu.make_async_copy(g_ref.at[:, columns(f, size)], spread_ref.at[f], load_sem.at[2]),
        ]
        for c in loads:
            c.start()
        side = lax.rem(f, 2)
        mine, theirs = pl.ds(side * half, half), pl.ds((1 - side) * half, half)
        core = (f ^ CORE, t)
        greet(everyone(f, t))
        first = []
        for k in (2, 1, 3, 0):
            plane = lax.rem(t + k, 4)
            c = remote(p_ref.at[plane, theirs], ra.at[k], sent.at[k], arrived.at[k], core)
            c.start()
            first.append((k, c))
        out = []
        for k, c in first:
            c.wait_recv()
            plane = lax.rem(t + k, 4)
            both = p_ref[plane, mine].astype(f32) + ra[k].astype(f32)
            if k:
                s[k] = both.astype(bf16)
                d = remote(s.at[k], rz.at[k], sent.at[3 + k], arrived.at[3 + k], (f, plane))
                d.start()
                out.append((k, d))
            else:
                pair_ref[mine] = both
        for c in loads[:2]:
            c.wait()
        total = PlaneSum(stage, other, held, from_x, from_y, last, sum_sent, sum_arrived)
        total.begin(chunk_part([(hidden_v, down_w)], size))
        spread = []
        for k in (6, 7, 2, 4, 3, 5, 1):
            c = remote(
                g_ref.at[:, columns(f ^ k, size)],
                spread_ref.at[f],
                g_sent.at[k],
                g_arrived.at[k],
                (f ^ k, t),
            )
            c.start()
            spread.append(c)
        total.turn()
        for k, d in out:
            d.wait_recv()
            pair_ref[mine] += rz[k].astype(f32)
        back = remote(pair_ref.at[mine], pair_ref.at[mine], sent.at[7], arrived.at[7], core)
        back.start()
        total.end(share)
        out_ref[...] = jnp.where(valid_ref[...] > 0, middle_ref[...] + share[...], 0.0).astype(bf16)
        back.wait()
        for c in spread:
            c.wait()
        loads[2].wait()
        for k, c in first + out:
            c.wait_send()
        total.finish()

    dma = pltpu.SemaphoreType.DMA
    return pl.pallas_call(
        kernel,
        out_shape=[
            jax.ShapeDtypeStruct((chunks, height, size), f32),
            jax.ShapeDtypeStruct((size, width), bf16),
            jax.ShapeDtypeStruct((8, depth, size), bf16),
        ],
        in_specs=[IN_VMEM, ANYWHERE, ANYWHERE, IN_VMEM, IN_VMEM, ANYWHERE],
        out_specs=[IN_VMEM, IN_VMEM, ANYWHERE],
        scratch_shapes=sum_scratch(size, width)
        + [pltpu.VMEM((units, 8 * size), bf16), pltpu.VMEM((units, width), bf16), dma((3,))]
        + [pltpu.VMEM((4, half, height, size), bf16)] * 3
        + [dma((8,)), dma((8,)), dma((8,)), dma((8,)), pltpu.VMEM((size, width), f32)],
        compiler_params=comm_params(number, VMEM_MOST),
        cost_estimate=lasting(50),
        name="backward_pairs",
    )(pair_parts, hidden, down_rows, middle, valid, grad_output)


def backward_first(grad_inner, weights, rows, tokens, grad_middle, gain, number):
    size, width = tokens.shape
    depth = grad_inner.shape[0]
    block = width // 8
    f32, bf16 = jnp.float32, jnp.bfloat16

    def kernel(
        g_ref, w_ref, rows_hbm, x_ref, middle_ref, gain_ref,
        tokens_grad_ref, gain_grad_ref, spread_ref,
        stage, other, held, from_x, from_y, last, sum_sent, sum_arrived,
        rows_v, load_sem, w_grad, sent, arrived,
    ):
        f, t = lax.axis_index("fsdp"), lax.axis_index("tp")
        load = pltpu.make_async_copy(rows_hbm, rows_v, load_sem.at[0])
        load.start()
        greet([(f ^ k, t) for k in range(1, 8)])
        total = PlaneSum(stage, other, held, from_x, from_y, last, sum_sent, sum_arrived)
        total.begin(chunk_part([(g_ref, w_ref)], size))
        load.wait()
        spread = []

        def weight_grad(k):
            j = f ^ k
            right = rows_v[:, :, columns(j, block)].reshape(8 * size, block)
            w_grad[k] = dot_nn(g_ref[...], right).astype(bf16)
            if k:
                c = remote(w_grad.at[k], spread_ref.at[f], sent.at[k], arrived.at[k], (j, t))
                c.start()
                spread.append(c)

        for k in (6, 7, 2, 4):
            weight_grad(k)
        total.turn()
        for k in (3, 5, 1, 0):
            weight_grad(k)
        keep = pltpu.make_async_copy(w_grad.at[0], spread_ref.at[f], load_sem.at[1])
        keep.start()
        wide = x_ref[...].astype(f32)
        inverse = lax.rsqrt(jnp.mean(wide * wide, axis=1, keepdims=True) + epsilon)
        normed = wide * inverse
        total.end(tokens_grad_ref)
        grad = tokens_grad_ref[...]
        gain_grad_ref[...] = jnp.sum(grad * normed, axis=0, keepdims=True)
        tokens_grad_ref[...] = middle_ref[...] + norm_back(grad, gain_ref[...], normed, inverse)
        for c in spread:
            c.wait()
        keep.wait()
        total.finish()

    dma = pltpu.SemaphoreType.DMA
    return pl.pallas_call(
        kernel,
        out_shape=[
            jax.ShapeDtypeStruct((size, width), f32),
            jax.ShapeDtypeStruct((1, width), f32),
            jax.ShapeDtypeStruct((8, depth, block), bf16),
        ],
        in_specs=[IN_VMEM, IN_VMEM, ANYWHERE, IN_VMEM, IN_VMEM, IN_VMEM],
        out_specs=[IN_VMEM, IN_VMEM, ANYWHERE],
        scratch_shapes=sum_scratch(size, width)
        + [
            pltpu.VMEM((8, size, width), bf16),
            dma((2,)),
            pltpu.VMEM((8, depth, block), bf16),
            dma((8,)),
            dma((8,)),
        ],
        compiler_params=comm_params(number, VMEM_MOST),
        cost_estimate=lasting(60),
        name="backward_first",
    )(grad_inner, weights, rows, tokens, grad_middle, gain)


def last_exchange(down_grads, hidden_grads, gain_parts, number):
    _, units, width = hidden_grads.shape
    arrays = (down_grads, hidden_grads)
    block = width // 8
    f32, bf16 = jnp.float32, jnp.bfloat16
    far_first = (6, 7, 2, 4, 3, 5, 1)

    def kernel(
        source_0, source_1, gains_ref, target_0, target_1, sums_ref, taken, planes, sent, arrived, z_sent, z_arrived, kept_sem
    ):
        f, t = lax.axis_index("fsdp"), lax.axis_index("tp")
        ways = ((source_0, target_0), (source_1, target_1))
        kept = [
            pltpu.make_async_copy(s.at[:, :, columns(f, block)], o.at[f], kept_sem.at[i])
            for i, (s, o) in enumerate(ways)
        ]
        for c in kept:
            c.start()
        greet(everyone(f, t))
        gains = []
        for k in far_first:
            c = remote(
                gains_ref.at[f ^ k], taken.at[k], sent.at[k, 0], arrived.at[k, 0], (f ^ k, t)
            )
            c.start()
            gains.append(c)
        copies = []
        for i, (s, o) in enumerate(ways):
            for k in far_first:
                c = remote(
                    s.at[:, :, columns(f ^ k, block)],
                    o.at[f],
                    sent.at[k, 1 + i],
                    arrived.at[k, 1 + i],
                    (f ^ k, t),
                )
                c.start()
                copies.append(c)
        total = gains_ref[f]
        for k, c in zip(far_first, gains):
            c.wait_recv()
            total += taken[k]
        planes[0] = total
        along_z = []
        for k in (1, 2, 3):
            c = remote(planes.at[0], planes.at[k], z_sent.at[k], z_arrived.at[k], (f, lax.rem(t + k, 4)))
            c.start()
            along_z.append(c)
        for c in along_z:
            c.wait_recv()
        sums = planes[lax.rem(t, 4)]
        for plane in (1, 2, 3):
            sums += planes[lax.rem(t + 4 - plane, 4)]
        sums_ref[...] = sums
        for c in kept + copies:
            c.wait()
        for c in gains + along_z:
            c.wait_send()

    dma = pltpu.SemaphoreType.DMA
    return pl.pallas_call(
        kernel,
        out_shape=[
            *(jax.ShapeDtypeStruct((8, len(x), units, block), bf16) for x in arrays),
            jax.ShapeDtypeStruct(gain_parts.shape[1:], f32),
        ],
        in_specs=[ANYWHERE, ANYWHERE, IN_VMEM],
        out_specs=[ANYWHERE, ANYWHERE, IN_VMEM],
        scratch_shapes=[
            pltpu.VMEM(gain_parts.shape, f32),
            pltpu.VMEM((4, *gain_parts.shape[1:]), f32),
            dma((8, 3)),
            dma((8, 3)),
            dma((4,)),
            dma((4,)),
            dma((2,)),
        ],
        compiler_params=comm_params(number),
        cost_estimate=lasting(28),
        name="last_exchange",
    )(down_grads, hidden_grads, gain_parts)


def dot_nn(left, right):
    return jnp.dot(left, right, preferred_element_type=jnp.float32)


def seen_keys(begin_row, first_key, first_query, shape):
    key_slot = first_key + lax.broadcasted_iota(jnp.int32, shape, 0)
    query_slot = first_query + lax.broadcasted_iota(jnp.int32, (1, shape[1]), 1)
    return (key_slot <= query_slot) & (key_slot >= begin_row)


def head_lanes(block, heads):
    return jnp.concatenate([block[h * HEAD_DIM : (h + 1) * HEAD_DIM] for h in range(heads)], axis=1)


WIDE = 2

def key_block(kv_ref, g, count):
    blocks = [kv_ref[lax.rem(g + n, 4), lax.div(g + n, 4)] for n in range(count)]
    return blocks[0] if count == 1 else jnp.concatenate(blocks, axis=0)


def attend(info, begins, queries, pair):
    depth, slots = queries.shape
    heads = depth // HEAD_DIM
    size = slots // 8
    span = heads * size

    def kernel(info_ref, begin_ref, q_ref, kv_ref, o_ref, l_ref, q_s, m_s, t_s, a_s):
        f = pl.program_id(0)
        low, middle, own = info_ref[f, 0], info_ref[f, 1], info_ref[f, 2]
        middle = middle + lax.rem(own - middle, WIDE)
        q_s[...] = head_lanes(q_ref[...], heads)
        m_s[...] = jnp.full_like(m_s, -1e30)
        t_s[...] = jnp.zeros_like(t_s)
        a_s[...] = jnp.zeros_like(a_s)

        def step(g, count, masked):
            block = key_block(kv_ref, g, count)
            keys, values = block[:, :HEAD_DIM], block[:, HEAD_DIM:]
            value_cols = values.astype(jnp.float32).T.astype(jnp.bfloat16)
            if masked:
                seen = seen_keys(begin_ref[0], g * size, own * size, (size, size))
                seen = jnp.concatenate([seen] * heads, axis=1)
            scores = dot_nn(keys, q_s[...])
            if masked:
                scores = jnp.where(seen, scores, -1e30)
            largest = m_s[...]
            higher = jnp.maximum(largest, jnp.max(scores, axis=0, keepdims=True))
            raised = jnp.exp(scores - higher)
            fade = jnp.exp(largest - higher)
            m_s[...] = higher
            t_s[...] = t_s[...] * fade + jnp.sum(raised, axis=0, keepdims=True)
            a_s[...] = a_s[...] * fade + dot_nn(
                value_cols, raised.astype(jnp.bfloat16)
            )

        def masked_step(g, carry):
            step(g, 1, True)
            return carry

        def plain_step(n, carry):
            step(middle + n * WIDE, WIDE, False)
            return carry

        step(own, 1, True)
        lax.fori_loop(low, middle, masked_step, 0)
        lax.fori_loop(0, lax.div(own - middle, WIDE), plain_step, 0)
        result = a_s[...] / t_s[...]
        for h in range(heads):
            o_ref[h * HEAD_DIM : (h + 1) * HEAD_DIM] = result[:, h * size : (h + 1) * size].astype(
                jnp.bfloat16
            )
        l_ref[0] = m_s[...] + jnp.log(t_s[...])
    return pl.pallas_call(
        kernel,
        grid_spec=pltpu.PrefetchScalarGridSpec(
            num_scalar_prefetch=1,
            grid=(8,),
            in_specs=[
                pl.BlockSpec((1, 1, size), lambda f, info: (f, 0, 0)),
                pl.BlockSpec((depth, size), lambda f, info: (0, f)),
                pl.BlockSpec((4, 8, size, 2 * HEAD_DIM), lambda f, info: (0, 0, 0, 0)),
            ],
            out_specs=[
                pl.BlockSpec((depth, size), lambda f, info: (0, f)),
                pl.BlockSpec((1, 1, span), lambda f, info: (f, 0, 0)),
            ],
            scratch_shapes=[
                pltpu.VMEM((HEAD_DIM, span), jnp.bfloat16),
                pltpu.VMEM((1, span), jnp.float32),
                pltpu.VMEM((1, span), jnp.float32),
                pltpu.VMEM((HEAD_DIM, span), jnp.float32),
            ],
        ),
        out_shape=[
            jax.ShapeDtypeStruct((depth, slots), jnp.bfloat16),
            jax.ShapeDtypeStruct((8, 1, span), jnp.float32),
        ],
        compiler_params=pltpu.CompilerParams(vmem_limit_bytes=40 << 20),
        cost_estimate=lasting(50),
        name="attend",
    )(info, begins, queries, pair)


def attend_back(info, begins, queries, pair, outputs, grads, totals):
    depth, slots = queries.shape
    heads = depth // HEAD_DIM
    size = slots // 8
    span = heads * size

    def kernel(
        info_ref, begin_ref, q_ref, kv_ref, o_ref, g_ref, l_ref, dq_ref, dkv_ref, q_s, g_s, d_s, a_s, w_s
    ):
        f = pl.program_id(0)
        low, middle, own = info_ref[f, 0], info_ref[f, 1], info_ref[f, 2]
        middle = middle + lax.rem(own - middle, WIDE)

        @pl.when(f == 0)
        def _():
            w_s[...] = jnp.zeros_like(w_s)

        q_s[...] = head_lanes(q_ref[...], heads)
        g_s[...] = head_lanes(g_ref[...], heads)
        out_lanes = head_lanes(o_ref[...], heads).astype(jnp.float32)
        d_s[...] = jnp.sum(out_lanes * g_s[...].astype(jnp.float32), axis=0, keepdims=True)
        a_s[...] = jnp.zeros_like(a_s)

        def step(g, count, masked):
            block = key_block(kv_ref, g, count)
            keys, values = block[:, :HEAD_DIM], block[:, HEAD_DIM:]
            key_cols = keys.astype(jnp.float32).T.astype(jnp.bfloat16)
            if masked:
                seen = seen_keys(begin_ref[0], g * size, own * size, (size, size))
                seen = jnp.concatenate([seen] * heads, axis=1)
            grad_keys = jnp.zeros((HEAD_DIM, count * size), jnp.float32)
            grad_values = jnp.zeros((HEAD_DIM, count * size), jnp.float32)
            query, grad = q_s[...], g_s[...]
            raised = jnp.exp(dot_nn(keys, query) - l_ref[0])
            if masked:
                raised = jnp.where(seen, raised, 0.0)
            grad_probs = dot_nn(values, grad)
            scores = (raised * (grad_probs - d_s[...])).astype(jnp.bfloat16)
            grad_values += outer_cols(grad, raised.astype(jnp.bfloat16))
            grad_keys += outer_cols(query, scores)
            a_s[...] += dot_nn(key_cols, scores)
            for n in range(count):
                keep = slice(n * size, (n + 1) * size)
                w_s[lax.rem(g + n, 4), lax.div(g + n, 4), :HEAD_DIM] += grad_keys[:, keep]
                w_s[lax.rem(g + n, 4), lax.div(g + n, 4), HEAD_DIM:] += grad_values[:, keep]

        def masked_step(g, carry):
            step(g, 1, True)
            return carry

        def plain_step(n, carry):
            step(middle + n * WIDE, WIDE, False)
            return carry

        step(own, 1, True)
        lax.fori_loop(low, middle, masked_step, 0)
        lax.fori_loop(0, lax.div(own - middle, WIDE), plain_step, 0)
        result = a_s[...] * HEAD_DIM ** (-0.5)
        for h in range(heads):
            dq_ref[h * HEAD_DIM : (h + 1) * HEAD_DIM] = result[:, h * size : (h + 1) * size]

        @pl.when(f == 7)
        def _():
            dkv_ref[...] = w_s[...].astype(jnp.bfloat16)

    return pl.pallas_call(
        kernel,
        grid_spec=pltpu.PrefetchScalarGridSpec(
            num_scalar_prefetch=1,
            grid=(8,),
            in_specs=[
                pl.BlockSpec((1, 1, size), lambda f, info: (f, 0, 0)),
                pl.BlockSpec((depth, size), lambda f, info: (0, f)),
                pl.BlockSpec((4, 8, size, 2 * HEAD_DIM), lambda f, info: (0, 0, 0, 0)),
                pl.BlockSpec((depth, size), lambda f, info: (0, f)),
                pl.BlockSpec((depth, size), lambda f, info: (0, f)),
                pl.BlockSpec((1, 1, span), lambda f, info: (f, 0, 0)),
            ],
            out_specs=[
                pl.BlockSpec((depth, size), lambda f, info: (0, f)),
                pl.BlockSpec((4, 8, 2 * HEAD_DIM, size), lambda f, info: (0, 0, 0, 0)),
            ],
            scratch_shapes=[
                pltpu.VMEM((HEAD_DIM, span), jnp.bfloat16),
                pltpu.VMEM((HEAD_DIM, span), jnp.bfloat16),
                pltpu.VMEM((1, span), jnp.float32),
                pltpu.VMEM((HEAD_DIM, span), jnp.float32),
                pltpu.VMEM((4, 8, 2 * HEAD_DIM, size), jnp.float32),
            ],
        ),
        out_shape=[
            jax.ShapeDtypeStruct((depth, slots), jnp.float32),
            jax.ShapeDtypeStruct((4, 8, 2 * HEAD_DIM, size), jnp.bfloat16),
        ],
        compiler_params=pltpu.CompilerParams(vmem_limit_bytes=40 << 20),
        cost_estimate=lasting(65),
        name="attend_back",
    )(info, begins, queries, pair, outputs, grads, totals)


def turn(values, cosine, sine_table):
    heads = values.shape[0] // HEAD_DIM
    split = values.reshape(heads, 2, HEAD_DIM // 2, values.shape[1])
    first, second = split[:, 0], split[:, 1]
    turned = jnp.stack(
        [first * cosine - second * sine_table, second * cosine + first * sine_table], axis=1
    )
    return turned.reshape(values.shape)


def turn_back(values, cosine, sine_table):
    return turn(values, cosine, -sine_table)


def segment_begins(slots, lengths):
    seq_index = jnp.arange(lengths.shape[0], dtype=jnp.int32)
    ends = jnp.sum(jnp.where(seq_index[:, None] >= seq_index[None, :], lengths[None, :], 0), axis=1)
    passed = slots[:, None] >= ends[None, :]
    begins = jnp.sum(jnp.where(passed, lengths[None, :], 0), axis=1)
    return begins, slots < ends[-1]


def local_plane(
    tokens,
    attn_gain,
    query_weight,
    key_weight,
    value_weight,
    output_weight,
    mlp_gain,
    gate_weight,
    up_weight,
    down_weight,
    out_grad,
    lengths,
):
    size, width = tokens.shape
    f = lax.axis_index("fsdp")
    t = lax.axis_index("tp")
    block = query_weight.shape[0]
    head_rows = query_weight.shape[1] // 2
    units = gate_weight.shape[1] // 8
    bf16, f32 = jnp.bfloat16, jnp.float32

    inner_own = jnp.concatenate([query_weight.T, key_weight.T, value_weight.T], axis=0)
    hidden_parts = [w.reshape(8, units, block) for w in (down_weight, gate_weight.T, up_weight.T)]
    gains_own = jnp.stack([attn_gain, mlp_gain]).astype(f32)
    down_part, gate_part, up_part, inner_all, gains_all = first_exchange(
        hidden_parts, inner_own, gains_own, 1
    )
    down_rows = lax.all_gather(down_part, "tp", axis=0, tiled=True)
    gate_rows = lax.all_gather(gate_part, "tp", axis=0, tiled=True)
    up_rows = lax.all_gather(up_part, "tp", axis=0, tiled=True)
    gains = jnp.moveaxis(gains_all, 0, 1).reshape(2, width)
    gain_first, gain_second = gains[0:1], gains[1:2]

    my_slots = (f * 4 + t) * size + jnp.arange(size, dtype=jnp.int32)
    _, my_valid = segment_begins(my_slots, lengths)
    valid_rows = my_valid[:, None]
    chunk_index = jnp.arange(8, dtype=jnp.int32) * 4 + t
    plane_slots = (chunk_index[:, None] * size + jnp.arange(size, dtype=jnp.int32)[None, :]).reshape(-1)
    begins, plane_valid = segment_begins(plane_slots, lengths)
    positions = jnp.where(plane_valid, plane_slots - begins, 0)
    begins = begins.reshape(8, 1, size)
    info = jnp.stack(
        [
            begins[:, 0, 0] // size,
            jnp.minimum((begins[:, 0, size - 1] + size - 1) // size, chunk_index),
            chunk_index,
        ],
        axis=1,
    ).astype(jnp.int32)
    ladder = jnp.arange(HEAD_DIM // 2).astype(f32)
    frequency = 10000.0 ** (-2.0 * ladder / HEAD_DIM)
    angles = positions.astype(f32)[None, :] * frequency[:, None]
    cosine, sine_table = jnp.cos(angles), jnp.sin(angles)

    grad_rows_own = jnp.where(valid_rows, out_grad, jnp.zeros_like(out_grad))
    rows_first, queries, pair, inner_rows_w, output_rows, _, grad_rows = first_rows(
        tokens, gains_all, inner_all, output_weight, cosine, sine_table, grad_rows_own, 2
    )
    attended, totals = attend(info, begins, queries, pair)
    middle, row_second = forward_output(attended, output_rows, tokens, gain_second, 4)
    rows_second, hidden, grad_gate_low, grad_up_low, down_grads = forward_hidden(
        row_second, grad_rows, gate_rows, up_rows, down_rows, 5
    )
    (
        grad_middle,
        gain_second_part,
        grad_output_w,
        grad_attended,
        hidden_grads,
    ) = backward_middle(
        grad_gate_low,
        grad_up_low,
        gate_rows,
        up_rows,
        rows_second,
        output_rows,
        attended,
        middle,
        grad_rows_own,
        gain_second,
        6,
    )
    down_grads = lax.psum_scatter(down_grads, "tp", scatter_dimension=0, tiled=True)
    hidden_grads, down_grads = lax.optimization_barrier((hidden_grads, down_grads))
    hidden_grads = lax.psum_scatter(
        hidden_grads.reshape(8 * units, width), "tp", scatter_dimension=0, tiled=True
    )
    grad_queries, grad_pair_parts = attend_back(
        info, begins, queries, pair, attended, grad_attended, totals
    )
    grad_pair, layer_out, output_parts = backward_pairs(
        grad_pair_parts, hidden, down_rows, middle, valid_rows.astype(f32), grad_output_w, 7
    )
    grad_pair = jnp.moveaxis(grad_pair, 0, 1).reshape(2 * HEAD_DIM, 8 * size)
    grad_query_low = turn_back(grad_queries, cosine, sine_table).astype(bf16)
    grad_key_low = turn_back(grad_pair[:HEAD_DIM], cosine, sine_table)
    first_core = lax.rem(f, 2) == 0
    grad_single = jnp.where(first_core, grad_key_low, grad_pair[HEAD_DIM:]).astype(bf16)
    grad_inner = jnp.concatenate([grad_query_low, grad_single], axis=0)
    single_rows = jnp.where(
        first_core,
        inner_rows_w[head_rows : head_rows + HEAD_DIM],
        inner_rows_w[head_rows + HEAD_DIM :],
    )
    single_weights = jnp.concatenate([inner_rows_w[:head_rows], single_rows], axis=0)
    tokens_grad, gain_first_part, inner_parts = backward_first(
        grad_inner, single_weights, rows_first, tokens, grad_middle, gain_first, 8
    )

    def along_z(parts):
        rows = parts.shape[1]
        flat = parts.reshape(8 * rows, block)
        return lax.psum_scatter(flat, "tp", scatter_dimension=0, tiled=True).reshape(2, rows, block)

    output_parts, hidden_grads = lax.optimization_barrier((output_parts, hidden_grads))
    output_own = along_z(output_parts)
    inner_parts, output_own = lax.optimization_barrier((inner_parts, output_own))
    inner_grads = along_z(inner_parts)
    gain_parts = jnp.concatenate([gain_first_part, gain_second_part], axis=0)
    gain_parts = jnp.moveaxis(gain_parts.reshape(2, 8, block), 1, 0)
    own_down, hidden_own, gain_sums = last_exchange(
        down_grads.reshape(1, units, width), hidden_grads.reshape(2, units, width), gain_parts, 9
    )
    own_gate, own_up = (hidden_own[:, n].reshape(8 * units, block) for n in range(2))
    return (
        layer_out,
        tokens_grad,
        gain_sums[0],
        inner_grads[:, :head_rows].reshape(2 * head_rows, block).T.astype(f32),
        inner_grads[0, head_rows:].T.astype(f32),
        inner_grads[1, head_rows:].T.astype(f32),
        output_own.reshape(2 * head_rows, block).astype(f32),
        gain_sums[1],
        own_gate.T.astype(f32),
        own_up.T.astype(f32),
        own_down.reshape(8 * units, block).astype(f32),
    )


def solution(mesh):
    plane = dict(mesh.shape) == {"fsdp": 8, "tp": 4}
    body = local_plane if plane else local
    in_specs = (
        P(("fsdp", "tp"), None),
        P("fsdp"),
        P("fsdp", "tp"),
        P("fsdp", "tp"),
        P("fsdp", "tp"),
        P("tp", "fsdp"),
        P("fsdp"),
        P("fsdp", "tp"),
        P("fsdp", "tp"),
        P("tp", "fsdp"),
        P(("fsdp", "tp"), None),
        P(),
    )
    out_specs = (
        P(("fsdp", "tp"), None),
        P(("fsdp", "tp"), None),
        P("fsdp"),
        P("fsdp", "tp"),
        P("fsdp", "tp"),
        P("fsdp", "tp"),
        P("tp", "fsdp"),
        P("fsdp"),
        P("fsdp", "tp"),
        P("fsdp", "tp"),
        P("tp", "fsdp"),
    )
    return jax.shard_map(body, mesh=mesh, in_specs=in_specs, out_specs=out_specs, check_vma=False)
```

```python
import jax
import jax.numpy as jnp
from jax import lax
from jax.experimental import pallas as pl
from jax.experimental.pallas import tpu as pltpu
from jax.sharding import PartitionSpec as P

HEAD_DIM = 64
MAX_SPAN = 4096


epsilon = 1e-05


def passed_along(block, axis, distance):
    devices = range(lax.axis_size(axis))
    route = [(i - distance, i) for i in devices if i - distance in devices]
    return lax.ppermute(block, axis, route)


def stream_layout(slots, lengths):
    seq_count = lengths.shape[0]
    seq_index = jnp.arange(seq_count, dtype=jnp.int32)
    ends = jnp.sum(jnp.where(seq_index[:, None] >= seq_index[None, :], lengths[None, :], 0), axis=1)
    starts = ends - lengths
    segment = jnp.sum((slots[:, None] >= ends[None, :]).astype(jnp.int32), axis=1)
    start_of = jnp.sum(
        jnp.where(segment[:, None] == seq_index[None, :], starts[None, :], 0), axis=1
    )
    position = jnp.where((segment < seq_count) & (slots >= 0), slots - start_of, 0)
    segment = jnp.where(slots < 0, -1, segment)
    return (segment, position)


def rotary_tables(positions, head_width):
    ladder = jnp.arange(head_width // 2).astype(jnp.float32)
    frequency = 10000.0 ** (-2.0 * ladder / head_width)
    angle_half = positions.astype(jnp.float32)[:, None] * frequency[None, :]
    angles = jnp.concatenate([angle_half, angle_half], axis=1)
    return (jnp.cos(angles)[:, None, :], jnp.sin(angles)[:, None, :])


def rotate(values, cosine, sine_table):
    middle = values.shape[-1] // 2
    turned = jnp.concatenate([-values[..., middle:], values[..., :middle]], axis=-1)
    return values * cosine + turned * sine_table


def rotate_back(values, cosine, sine_table):
    middle = values.shape[-1] // 2
    scaled = values * sine_table
    turned = jnp.concatenate([scaled[..., middle:], -scaled[..., :middle]], axis=-1)
    return values * cosine + turned


def inner_rows(left, right):
    return lax.dot_general(
        left, right, (((0,), (0,)), ((), ())), preferred_element_type=jnp.float32
    )


def outer_cols(left, right):
    return lax.dot_general(
        left, right, (((1,), (1,)), ((), ())), preferred_element_type=jnp.float32
    )


def norm_back(grad_normed, gain_wide, normed, inverse):
    scaled_grad = grad_normed * gain_wide
    return inverse * (scaled_grad - normed * jnp.mean(scaled_grad * normed, axis=1, keepdims=True))


def local(
    tokens,
    attn_gain,
    query_weight,
    key_weight,
    value_weight,
    output_weight,
    mlp_gain,
    gate_weight,
    up_weight,
    down_weight,
    out_grad,
    lengths,
):
    row_count = tokens.shape[0]
    tp_count = lax.axis_size("tp")
    block_rows = row_count * tp_count
    slot_total = block_rows * lax.axis_size("fsdp")
    longest = min(MAX_SPAN, slot_total // 2)
    reach_count = (longest - 2) // block_rows + 1
    window = (reach_count + 1) * block_rows
    front_rows = reach_count * block_rows
    block_index = lax.axis_index("fsdp")
    tp_index = lax.axis_index("tp")
    head_width = HEAD_DIM
    query_width = query_weight.shape[1]
    key_width = key_weight.shape[1]
    heads_here = query_width // head_width
    score_scale = head_width ** (-0.5)
    seq_count = lengths.shape[0]
    row_base = (block_index * tp_count + tp_index) * row_count
    my_slots = row_base + jnp.arange(row_count, dtype=jnp.int32)
    my_segments, my_positions = stream_layout(my_slots, lengths)
    valid_rows = (my_segments < seq_count)[:, None]
    gathered = (
        lax.all_gather(query_weight, "fsdp", axis=0, tiled=True),
        lax.all_gather(key_weight, "fsdp", axis=0, tiled=True),
        lax.all_gather(value_weight, "fsdp", axis=0, tiled=True),
        lax.all_gather(output_weight, "fsdp", axis=1, tiled=True),
        lax.all_gather(gate_weight, "fsdp", axis=0, tiled=True),
        lax.all_gather(up_weight, "fsdp", axis=0, tiled=True),
        lax.all_gather(down_weight, "fsdp", axis=1, tiled=True),
        lax.all_gather(attn_gain, "fsdp", axis=0, tiled=True),
        lax.all_gather(mlp_gain, "fsdp", axis=0, tiled=True),
    )
    (
        full_query,
        full_key,
        full_value,
        full_output,
        full_gate,
        full_up,
        full_down,
        gain_first,
        gain_second,
    ) = gathered
    w_inner = jnp.concatenate([full_query, full_key, full_value], axis=1)
    gain_first_wide = gain_first.astype(jnp.float32)
    gain_second_wide = gain_second.astype(jnp.float32)
    tokens_wide = tokens.astype(jnp.float32)
    inverse_first = lax.rsqrt(jnp.mean(tokens_wide * tokens_wide, axis=1, keepdims=True) + epsilon)
    normed_first = tokens_wide * inverse_first
    scaled_first = (normed_first * gain_first_wide).astype(jnp.bfloat16)
    rows_first = lax.all_gather(scaled_first, "tp", axis=0, tiled=True)
    projected = jnp.dot(rows_first, w_inner, preferred_element_type=jnp.float32)
    block_base = block_index * block_rows
    key_slots = block_base - front_rows + jnp.arange(window, dtype=jnp.int32)
    key_segments, key_positions = stream_layout(key_slots, lengths)
    query_segments = key_segments[front_rows:]
    block_positions = key_positions[front_rows:]
    cosine, sine_table = rotary_tables(block_positions, head_width)
    queries = rotate(
        projected[:, :query_width].reshape(block_rows, heads_here, head_width), cosine, sine_table
    ).astype(jnp.bfloat16)
    keys_local = rotate(
        projected[:, query_width : query_width + key_width].reshape(block_rows, 1, head_width),
        cosine,
        sine_table,
    )
    keys_local = keys_local.reshape(block_rows, head_width).astype(jnp.bfloat16)
    values_local = projected[:, query_width + key_width :].astype(jnp.bfloat16)
    pair_local = jnp.concatenate([keys_local, values_local], axis=1)
    pieces = []
    for offset in range(reach_count, 0, -1):
        pieces.append(passed_along(pair_local, "fsdp", offset))
    pair_window = jnp.concatenate(pieces + [pair_local], axis=0)
    key_window = pair_window[:, :head_width]
    value_window = pair_window[:, head_width:]
    key_seen = (key_segments[None, :] == query_segments[:, None]) & (
        key_positions[None, :] <= block_positions[:, None]
    )

    def head_scores(query_head):
        scores = outer_cols(query_head, key_window) * score_scale
        return jnp.where(key_seen, scores, -1e30)

    def head_forward(query_head):
        scores = head_scores(query_head)
        largest = jnp.max(scores, axis=1, keepdims=True)
        raised = jnp.exp(scores - largest)
        row_total = jnp.sum(raised, axis=1, keepdims=True)
        attn_probs = (raised / row_total).astype(jnp.bfloat16)
        head_out = jnp.dot(attn_probs, value_window, preferred_element_type=jnp.float32)
        return (head_out, (largest + jnp.log(row_total))[:, 0])

    query_heads = jnp.moveaxis(queries, 1, 0)
    head_outs, log_totals = lax.map(head_forward, query_heads)
    attended = jnp.moveaxis(head_outs, 0, 1).reshape(block_rows, query_width).astype(jnp.bfloat16)
    attn_share = lax.psum_scatter(
        jnp.dot(attended, full_output, preferred_element_type=jnp.float32).astype(jnp.bfloat16),
        "tp",
        scatter_dimension=0,
        tiled=True,
    ).astype(jnp.float32)
    middle = tokens_wide + attn_share
    inverse_second = lax.rsqrt(jnp.mean(middle * middle, axis=1, keepdims=True) + epsilon)
    normed_second = middle * inverse_second
    scaled_second = (normed_second * gain_second_wide).astype(jnp.bfloat16)
    rows_second = lax.all_gather(scaled_second, "tp", axis=0, tiled=True)
    gate_proj = jnp.dot(rows_second, full_gate, preferred_element_type=jnp.float32)
    up_proj = jnp.dot(rows_second, full_up, preferred_element_type=jnp.float32)
    gate_sigmoid = jax.nn.sigmoid(gate_proj)
    gate_active = gate_proj * gate_sigmoid
    hidden = (gate_active * up_proj).astype(jnp.bfloat16)
    mlp_share = lax.psum_scatter(
        jnp.dot(hidden, full_down, preferred_element_type=jnp.float32).astype(jnp.bfloat16),
        "tp",
        scatter_dimension=0,
        tiled=True,
    ).astype(jnp.float32)
    layer_out = jnp.where(valid_rows, middle + mlp_share, 0.0).astype(jnp.bfloat16)
    grad_rows = jnp.where(valid_rows, out_grad.astype(jnp.float32), 0.0)
    grad_low = grad_rows.astype(jnp.bfloat16)
    regathered = (
        lax.all_gather(query_weight, "fsdp", axis=0, tiled=True),
        lax.all_gather(key_weight, "fsdp", axis=0, tiled=True),
        lax.all_gather(value_weight, "fsdp", axis=0, tiled=True),
        lax.all_gather(output_weight, "fsdp", axis=1, tiled=True),
        lax.all_gather(gate_weight, "fsdp", axis=0, tiled=True),
        lax.all_gather(up_weight, "fsdp", axis=0, tiled=True),
        lax.all_gather(down_weight, "fsdp", axis=1, tiled=True),
        lax.all_gather(attn_gain, "fsdp", axis=0, tiled=True),
        lax.all_gather(mlp_gain, "fsdp", axis=0, tiled=True),
    )
    (
        full_query,
        full_key,
        full_value,
        full_output,
        full_gate,
        full_up,
        full_down,
        gain_first,
        gain_second,
    ) = regathered
    w_inner = jnp.concatenate([full_query, full_key, full_value], axis=1)
    grad_down_rows = lax.all_gather(grad_low, "tp", axis=0, tiled=True)
    grad_down_w = inner_rows(hidden, grad_down_rows)
    grad_hidden = outer_cols(grad_down_rows, full_down)
    grad_up_low = (grad_hidden * gate_active).astype(jnp.bfloat16)
    grad_gate_low = (
        grad_hidden * up_proj * gate_sigmoid * (1.0 + gate_proj * (1.0 - gate_sigmoid))
    ).astype(jnp.bfloat16)
    grad_gate_w = inner_rows(rows_second, grad_gate_low)
    grad_up_w = inner_rows(rows_second, grad_up_low)
    grad_second = lax.psum_scatter(
        (outer_cols(grad_gate_low, full_gate) + outer_cols(grad_up_low, full_up)).astype(
            jnp.bfloat16
        ),
        "tp",
        scatter_dimension=0,
        tiled=True,
    ).astype(jnp.float32)
    gain_second_part = jnp.sum(grad_second * normed_second, axis=0)
    grad_middle = grad_rows + norm_back(
        grad_second, gain_second_wide, normed_second, inverse_second
    )
    middle_low = grad_middle.astype(jnp.bfloat16)
    grad_attn_rows = lax.all_gather(middle_low, "tp", axis=0, tiled=True)
    grad_output_w = inner_rows(attended, grad_attn_rows)
    grad_attended = outer_cols(grad_attn_rows, full_output).astype(jnp.bfloat16)
    grad_heads = jnp.moveaxis(grad_attended.reshape(block_rows, heads_here, head_width), 1, 0)

    def head_backward(packed):
        query_head, grad_head, log_total = packed
        attn_probs = jnp.exp(head_scores(query_head) - log_total[:, None])
        probs_low = attn_probs.astype(jnp.bfloat16)
        grad_value_head = inner_rows(probs_low, grad_head)
        grad_probs = outer_cols(grad_head, value_window)
        grad_scores = (
            attn_probs * (grad_probs - jnp.sum(attn_probs * grad_probs, axis=1, keepdims=True))
        ).astype(jnp.bfloat16)
        grad_query_head = (
            jnp.dot(grad_scores, key_window, preferred_element_type=jnp.float32) * score_scale
        )
        grad_key_head = inner_rows(grad_scores, query_head) * score_scale
        return (grad_query_head, grad_key_head, grad_value_head)

    grad_query_heads, grad_key_heads, grad_value_heads = lax.map(
        head_backward, (query_heads, grad_heads, log_totals)
    )
    grad_pair = jnp.concatenate(
        [jnp.sum(grad_key_heads, axis=0), jnp.sum(grad_value_heads, axis=0)], axis=1
    )
    own_grad = grad_pair[front_rows:]
    for offset in range(1, reach_count + 1):
        piece_start = (reach_count - offset) * block_rows
        own_grad = own_grad + passed_along(
            grad_pair[piece_start : piece_start + block_rows].astype(jnp.bfloat16), "fsdp", -offset
        ).astype(jnp.float32)
    grad_key_lin = rotate_back(
        own_grad[:, :head_width].reshape(block_rows, 1, head_width), cosine, sine_table
    )
    grad_key_low = grad_key_lin.reshape(block_rows, head_width).astype(jnp.bfloat16)
    grad_value_low = own_grad[:, head_width:].astype(jnp.bfloat16)
    grad_query_lin = rotate_back(jnp.moveaxis(grad_query_heads, 0, 1), cosine, sine_table)
    grad_query_low = grad_query_lin.reshape(block_rows, query_width).astype(jnp.bfloat16)
    grad_inner = jnp.concatenate([grad_query_low, grad_key_low, grad_value_low], axis=1)
    grad_inner_w = inner_rows(rows_first, grad_inner)
    grad_first = lax.psum_scatter(
        outer_cols(grad_inner, w_inner).astype(jnp.bfloat16), "tp", scatter_dimension=0, tiled=True
    ).astype(jnp.float32)
    gain_first_part = jnp.sum(grad_first * normed_first, axis=0)
    tokens_grad = grad_middle + norm_back(grad_first, gain_first_wide, normed_first, inverse_first)
    reduced = (
        lax.psum_scatter(
            grad_inner_w[:, :query_width].astype(jnp.bfloat16),
            "fsdp",
            scatter_dimension=0,
            tiled=True,
        ).astype(jnp.float32),
        lax.psum_scatter(
            grad_inner_w[:, query_width : query_width + key_width].astype(jnp.bfloat16),
            "fsdp",
            scatter_dimension=0,
            tiled=True,
        ).astype(jnp.float32),
        lax.psum_scatter(
            grad_inner_w[:, query_width + key_width :].astype(jnp.bfloat16),
            "fsdp",
            scatter_dimension=0,
            tiled=True,
        ).astype(jnp.float32),
        lax.psum_scatter(
            grad_output_w.astype(jnp.bfloat16), "fsdp", scatter_dimension=1, tiled=True
        ).astype(jnp.float32),
        lax.psum_scatter(
            grad_gate_w.astype(jnp.bfloat16), "fsdp", scatter_dimension=0, tiled=True
        ).astype(jnp.float32),
        lax.psum_scatter(
            grad_up_w.astype(jnp.bfloat16), "fsdp", scatter_dimension=0, tiled=True
        ).astype(jnp.float32),
        lax.psum_scatter(
            grad_down_w.astype(jnp.bfloat16), "fsdp", scatter_dimension=1, tiled=True
        ).astype(jnp.float32),
        lax.psum_scatter(
            gain_first_part.astype(jnp.bfloat16), "fsdp", scatter_dimension=0, tiled=True
        ).astype(jnp.float32),
        lax.psum_scatter(
            gain_second_part.astype(jnp.bfloat16), "fsdp", scatter_dimension=0, tiled=True
        ).astype(jnp.float32),
    )
    gain_sums = lax.psum((reduced[7], reduced[8]), "tp")
    return (
        layer_out,
        tokens_grad,
        gain_sums[0],
        reduced[0],
        reduced[1],
        reduced[2],
        reduced[3],
        gain_sums[1],
        reduced[4],
        reduced[5],
        reduced[6],
    )


MESH = pl.DeviceIdType.MESH
CORE, ALONG_X, ALONG_Y = 1, 2, 4
PARTS = 4
VMEM_MOST = 60 << 20


def greet(partners):
    barrier = pltpu.get_barrier_semaphore()
    for partner in partners:
        pl.semaphore_signal(barrier, inc=1, device_id=partner, device_id_type=MESH)
    pl.semaphore_wait(barrier, len(partners))


def remote(source, target, sent, arrived, partner):
    return pltpu.make_async_remote_copy(
        src_ref=source,
        dst_ref=target,
        send_sem=sent,
        recv_sem=arrived,
        device_id=partner,
        device_id_type=MESH,
    )


def comm_params(number, vmem=None):
    return pltpu.CompilerParams(
        collective_id=number, has_side_effects=True, vmem_limit_bytes=vmem
    )


def lasting(microseconds):
    return pl.CostEstimate(
        flops=int(microseconds * 1.1e9), bytes_accessed=1_000_000, transcendentals=0
    )


ANYWHERE = pl.BlockSpec(memory_space=pl.ANY)
IN_VMEM = pl.BlockSpec(memory_space=pltpu.VMEM)


def columns(index, width):
    return pl.ds(pl.multiple_of(index * width, width), width)


class PlaneGather:
    def __init__(self, store, sent, arrived):
        self.f, self.t = lax.axis_index("fsdp"), lax.axis_index("tp")
        self.store, self.sent, self.arrived = store, sent, arrived
        self.piece = store.shape[1] // PARTS
        self.near = [(self.f ^ k, self.t) for k in (CORE, ALONG_X, ALONG_Y)]
        self.copies, self.on = [], {}

    def send(self, owner, j, way, slot):
        place = self.store.at[owner, pl.ds(j * self.piece, self.piece)]
        c = remote(
            place, place, self.sent.at[slot, j], self.arrived.at[slot, j], self.near[way]
        )
        c.start()
        self.copies.append(c)
        self.on[slot, j] = c

    def begin(self):
        for k in range(PARTS):
            self.send(self.f, k, 1, 1)
            self.send(self.f, (k + PARTS // 2) % PARTS, 2, 2)
        for k in range(PARTS):
            self.send(self.f, k, 0, 0)

    def arrive(self, slot, j):
        self.on[slot, j].wait_recv()

    def advance(self, k):
        jx, jy = k, (k + PARTS // 2) % PARTS
        self.arrive(1, jx)
        if jx < PARTS // 2:
            self.send(self.f ^ ALONG_X, jx, 2, 6)
        self.send(self.f ^ ALONG_X, jx, 0, 3)
        self.arrive(2, jy)
        if jy >= PARTS // 2:
            self.send(self.f ^ ALONG_Y, jy, 1, 6)
        self.send(self.f ^ ALONG_Y, jy, 0, 4)

    def far(self):
        for k in range(PARTS // 2):
            for j in (k, k + PARTS // 2):
                self.arrive(6, j)
                self.send(self.f ^ ALONG_X ^ ALONG_Y, j, 0, 5)

    def wait_core(self, *slots):
        for slot in slots:
            for j in range(PARTS):
                self.arrive(slot, j)

    def finish(self):
        for c in self.copies:
            c.wait_send()


GATHER_SEMAPHORES = [pltpu.SemaphoreType.DMA((7, PARTS)), pltpu.SemaphoreType.DMA((7, PARTS))]


class PlaneSum:
    masks = (ALONG_X ^ ALONG_Y, ALONG_X, ALONG_Y, 0)

    def __init__(self, stage, other, held, from_x, from_y, last, sent, arrived):
        self.f, self.t = lax.axis_index("fsdp"), lax.axis_index("tp")
        self.stage, self.other, self.held = stage, other, held
        self.from_x, self.from_y, self.last = from_x, from_y, last
        self.sent, self.arrived = sent, arrived
        self.near = [(self.f ^ k, self.t) for k in (CORE, ALONG_X, ALONG_Y)]
        self.copies, self.on = [], {}
        half = held.shape[1] // 2
        self.top, self.low = pl.ds(0, half), pl.ds(half, half)

    def send(self, source, target, slot, way):
        c = remote(source, target, self.sent.at[slot], self.arrived.at[slot], self.near[way])
        c.start()
        self.copies.append(c)
        self.on[slot] = c

    def begin(self, write_part, after=None):
        for i, mask in enumerate(self.masks):
            if i >= 2:
                self.on[i - 2].wait_send()
                self.copies = [c for c in self.copies if c is not self.on[i - 2]]
            write_part(self.f ^ CORE ^ mask, self.stage.at[i % 2])
            self.send(self.stage.at[i % 2], self.other.at[i], i, 0)
            write_part(self.f ^ mask, self.held.at[i])
            if after is not None:
                after(i)
            self.on[i].wait_recv()
            self.held[i] = (
                self.held[i].astype(jnp.float32) + self.other[i].astype(jnp.float32)
            ).astype(jnp.bfloat16)
            if i == 0:
                self.send(self.held.at[0, self.top], self.from_x.at[0], 4, 1)
                self.send(self.held.at[0, self.low], self.from_y.at[0], 5, 2)
            if i == 1:
                self.send(self.held.at[1, self.top], self.from_x.at[1], 6, 1)
            if i == 2:
                self.send(self.held.at[2, self.low], self.from_y.at[1], 7, 2)

    def turn(self):
        self.on[4].wait_recv()
        self.held[2, self.top] = (
            self.held[2, self.top].astype(jnp.float32) + self.from_x[0].astype(jnp.float32)
        ).astype(jnp.bfloat16)
        self.send(self.held.at[2, self.top], self.last.at[0], 8, 2)
        self.on[5].wait_recv()
        self.held[1, self.low] = (
            self.held[1, self.low].astype(jnp.float32) + self.from_y[0].astype(jnp.float32)
        ).astype(jnp.bfloat16)
        self.send(self.held.at[1, self.low], self.last.at[1], 9, 1)

    def end(self, total):
        for rows, first, second, take in (
            (self.top, 6, 8, lambda: self.from_x[1]),
            (self.low, 7, 9, lambda: self.from_y[1]),
        ):
            self.on[first].wait_recv()
            part = self.held[3, rows].astype(jnp.float32) + take().astype(jnp.float32)
            self.on[second].wait_recv()
            total[rows] = part + self.last[second - 8].astype(jnp.float32)

    def finish(self):
        for c in self.copies:
            c.wait_send()


def sum_scratch(height, width):
    chunks = [pltpu.VMEM((n, height, width), jnp.bfloat16) for n in (2, 4, 4)]
    return chunks + [pltpu.VMEM((2, height // 2, width), jnp.bfloat16)] * 3 + [pltpu.SemaphoreType.DMA((10,)), pltpu.SemaphoreType.DMA((10,))]


NARROW = 512


def chunk_part(pairs, size):
    def write_part(owner, ref):
        lanes = columns(owner, size)
        lefts = [left[:, lanes] for left, _ in pairs]

        def step(n, carry):
            wide = columns(n, NARROW)
            total = inner_rows(lefts[0], pairs[0][1][:, wide])
            for left, (_, right) in zip(lefts[1:], pairs[1:]):
                total += inner_rows(left, right[:, wide])
            ref[:, wide] = total.astype(jnp.bfloat16)
            return carry

        lax.fori_loop(0, ref.shape[1] // NARROW, step, 0)

    return write_part


def plane_greet():
    f, t = lax.axis_index("fsdp"), lax.axis_index("tp")
    greet([(f ^ k, t) for k in (CORE, ALONG_X, ALONG_Y)])


def forward_output(attended, output_rows, tokens, gain, dys, down_all, number):
    size, width = tokens.shape
    units = down_all.shape[2]
    f32, bf16 = jnp.float32, jnp.bfloat16

    def kernel(
        o_ref, x_ref, gain_ref, w_hbm, dys_hbm, down_hbm,
        middle_ref, row_ref, dh_ref,
        stage, other, held, from_x, from_y, last, sum_sent, sum_arrived,
        dys, down_w, dys_sem, load_sem, dh, dh_sem, w, w_sem,
    ):
        load = pltpu.make_async_copy(dys_hbm, dys, dys_sem)
        loads = unit_loads(lambda j: down_hbm.at[:, j], down_w, load_sem)
        output_loads = column_loads(w_hbm, w, w_sem)
        for c in output_loads + loads + [load]:
            c.start()
        plane_greet()
        for c in output_loads:
            c.wait()
        total = PlaneSum(stage, other, held, from_x, from_y, last, sum_sent, sum_arrived)
        total.begin(chunk_part([(o_ref, w)], size))
        for c in loads + [load]:
            c.wait()

        def out_copy(i):
            return pltpu.make_async_copy(dh.at[i], dh_ref.at[i], dh_sem.at[i])

        def grad_chunk(i, carry):
            dh[i] = outer_cols(as_rows(down_w), dys[i])
            out_copy(i).start()
            return carry

        lax.fori_loop(0, 6, grad_chunk, 0)
        total.turn()
        lax.fori_loop(6, 8, grad_chunk, 0)
        total.end(middle_ref)
        middle = x_ref[...].astype(f32) + middle_ref[...]
        middle_ref[...] = middle
        inverse = lax.rsqrt(jnp.mean(middle * middle, axis=1, keepdims=True) + epsilon)
        row_ref[...] = (middle * inverse * gain_ref[...]).astype(bf16)
        for i in range(8):
            out_copy(i).wait()
        total.finish()

    dma = pltpu.SemaphoreType.DMA
    chunks = (8, 4 * units, size)
    return pl.pallas_call(
        kernel,
        out_shape=[
            jax.ShapeDtypeStruct((size, width), f32),
            jax.ShapeDtypeStruct((size, width), bf16),
            jax.ShapeDtypeStruct(chunks, f32),
        ],
        in_specs=[IN_VMEM] * 3 + [ANYWHERE] * 3,
        out_specs=[IN_VMEM] * 2 + [ANYWHERE],
        scratch_shapes=sum_scratch(size, width)
        + [
            pltpu.VMEM((8, size, width), bf16),
            pltpu.VMEM((4, units, width), bf16),
            dma,
            dma((8,)),
            pltpu.VMEM(chunks, f32),
            dma((8,)),
            pltpu.VMEM((attended.shape[0], width), bf16),
            dma((8,)),
        ],
        compiler_params=comm_params(number, VMEM_MOST),
        cost_estimate=lasting(45),
        name="forward_output",
    )(attended, tokens, gain, output_rows, dys, down_all)


def forward_hidden(row, dys, dh_all, gate_up, number):
    size, width = row.shape
    quarter = gate_up.shape[3]
    units = 4 * quarter
    f32, bf16 = jnp.float32, jnp.bfloat16

    def kernel(
        row_ref, dys_hbm, dh_hbm, gate_up_hbm,
        rows_ref, hidden_ref, dgate_ref, dup_ref, down_grad_ref,
        rows, rows_sent, rows_arrived, dys, gate_w, up_w, load_sem, unit_sem, dh, out, out_sem, keep_sem, down_grad,
    ):
        f = lax.axis_index("fsdp")
        loads = [
            pltpu.make_async_copy(source, target, load_sem.at[i])
            for i, (source, target) in enumerate(((dys_hbm, dys), (dh_hbm, dh)))
        ]
        for i, w in enumerate((gate_w, up_w)):
            loads += unit_loads(lambda j, i=i: gate_up_hbm.at[:, j, i], w, unit_sem.at[i])
        for load in loads:
            load.start()
        rows[f] = row_ref[...]
        plane_greet()
        gather_rows = PlaneGather(rows, rows_sent, rows_arrived)
        gather_rows.begin()
        for load in loads:
            load.wait()

        half = size // 2
        halves = (slice(0, half), slice(half, size))

        def owners(i, crossed):
            return f ^ i, f ^ (i ^ ALONG_X ^ ALONG_Y if crossed else i)

        def out_copies(slot, pair):
            return [
                pltpu.make_async_copy(
                    out.at[slot, n, :, lanes],
                    target.at[
                        :, pl.ds(pl.multiple_of(owner * size + side * half, half), half)
                    ],
                    out_sem.at[slot, n, side],
                )
                for n, target in enumerate((hidden_ref, dgate_ref, dup_ref))
                for side, (owner, lanes) in enumerate(zip(pair, halves))
            ]

        def unit(crossed):
            def body(i, carry):
                pair = owners(i, crossed)
                slot = lax.rem(i, 2)

                @pl.when(i >= 2)
                def _():
                    for c in out_copies(slot, pair):
                        c.wait()

                right = jnp.concatenate([rows[o, r] for o, r in zip(pair, halves)], axis=0)
                gate = outer_cols(as_rows(gate_w), right)
                up = outer_cols(as_rows(up_w), right)
                sigmoid = jax.nn.sigmoid(gate)
                active = gate * sigmoid
                grad = jnp.concatenate([dh[o, :, r] for o, r in zip(pair, halves)], axis=1)
                hidden = (active * up).astype(bf16)
                out[slot, 0] = hidden
                out[slot, 1] = (grad * up * sigmoid * (1.0 + gate * (1.0 - sigmoid))).astype(bf16)
                out[slot, 2] = (grad * active).astype(bf16)
                for c in out_copies(slot, pair):
                    c.start()
                cotangent = jnp.concatenate([dys[o, r] for o, r in zip(pair, halves)], axis=0)
                down_grad[...] += dot_nn(hidden, cotangent)
                return carry

            return body

        def take(*pieces):
            for slot, j in pieces:
                gather_rows.arrive(slot, j)

        down_grad[...] = jnp.zeros_like(down_grad)
        gather_rows.advance(0)
        lax.fori_loop(0, 1, unit(False), 0)
        gather_rows.advance(1)
        gather_rows.wait_core(0)
        lax.fori_loop(1, 2, unit(False), 0)
        lax.fori_loop(2, 3, unit(True), 0)
        gather_rows.advance(2)
        take((3, 0), (3, 1), (4, 2), (4, 3))
        lax.fori_loop(3, 4, unit(True), 0)
        gather_rows.advance(3)
        lax.fori_loop(4, 5, unit(True), 0)
        take((3, 2), (3, 3), (4, 0), (4, 1))
        lax.fori_loop(5, 6, unit(True), 0)
        gather_rows.far()
        lax.fori_loop(6, 7, unit(False), 0)
        gather_rows.wait_core(5)
        keep = pltpu.make_async_copy(rows, rows_ref, keep_sem)
        keep.start()
        lax.fori_loop(7, 8, unit(False), 0)
        for j in range(8):
            part = down_grad[:, j * size : (j + 1) * size].astype(bf16)
            down_grad_ref[:, j] = part.reshape(4, quarter, size)
        for i in (6, 7):
            for c in out_copies(i % 2, owners(i, False)):
                c.wait()
        keep.wait()
        gather_rows.finish()

    store = pltpu.VMEM((8, size, width), bf16)
    weights = pltpu.VMEM((4, quarter, width), bf16)
    return pl.pallas_call(
        kernel,
        out_shape=[jax.ShapeDtypeStruct((8, size, width), bf16)]
        + [jax.ShapeDtypeStruct((units, 8 * size), bf16)] * 3
        + [jax.ShapeDtypeStruct((4, 8, quarter, size), bf16)],
        in_specs=[IN_VMEM] + [ANYWHERE] * 3,
        out_specs=[ANYWHERE] * 4 + [IN_VMEM],
        scratch_shapes=[store]
        + GATHER_SEMAPHORES
        + [store]
        + [weights] * 2
        + [
            pltpu.SemaphoreType.DMA((2,)),
            pltpu.SemaphoreType.DMA((2, 8)),
            pltpu.VMEM((8, units, size), f32),
            pltpu.VMEM((2, 3, units, size), bf16),
            pltpu.SemaphoreType.DMA((2, 3, 2)),
            pltpu.SemaphoreType.DMA,
            pltpu.VMEM((units, width), f32),
        ],
        compiler_params=comm_params(number, VMEM_MOST),
        cost_estimate=lasting(50),
        name="forward_hidden",
    )(row, dys, dh_all, gate_up)


def backward_middle(
    dgate, dup, gate_up, rows, dys, output_rows, attended, middle, gain, number
):
    size, width = middle.shape
    quarter = gate_up.shape[3]
    units = 4 * quarter
    depth = output_rows.shape[1]
    blocks = width // size
    f32, bf16 = jnp.float32, jnp.bfloat16
    early = 5

    def kernel(
        dgate_hbm, dup_hbm, gate_up_hbm, rows_hbm,
        dys_hbm, w_hbm, o_ref, middle_ref, gain_ref,
        grad_ref, gain_grad_ref, grad_o_ref, do_ref, gate_g_ref, up_g_ref,
        stage, other, held, from_x, from_y, last, sum_sent, sum_arrived,
        store, store_sent, store_arrived,
        dgate_v, dup_v, gate_w, up_w, load_sem, unit_sem,
        tall, tall_sem, out, out_sem, o_sum, dy, dy_sem, w_ref, w_sem,
    ):
        f = lax.axis_index("fsdp")
        loads = [
            pltpu.make_async_copy(source, target, load_sem.at[i])
            for i, (source, target) in enumerate(((dgate_hbm, dgate_v), (dup_hbm, dup_v)))
        ]
        for i, w in enumerate((gate_w, up_w)):
            loads += unit_loads(lambda j, i=i: gate_up_hbm.at[:, j, i], w, unit_sem.at[i])
        for load in loads:
            load.start()

        load_dy = pltpu.make_async_copy(dys_hbm.at[f], dy, dy_sem)
        load_dy.start()
        output_loads = column_loads(w_hbm, w_ref, w_sem)
        for c in output_loads:
            c.start()

        def tall_load(n, slot):
            return pltpu.make_async_copy(
                rows_hbm.at[:, :, columns(n, size)], tall.at[slot], tall_sem.at[slot]
            )

        tall_load(0, 0).start()
        plane_greet()
        total = PlaneSum(stage, other, held, from_x, from_y, last, sum_sent, sum_arrived)
        gather = PlaneGather(store, store_sent, store_arrived)
        for load in loads:
            load.wait()
        total.begin(chunk_part([(dgate_v, Rows(gate_w)), (dup_v, Rows(up_w))], size))
        total.turn()

        def out_copies(n, slot):
            return [
                pltpu.make_async_copy(
                    out.at[slot, i], target.at[:, n], out_sem.at[slot, i]
                )
                for i, target in enumerate((gate_g_ref, up_g_ref))
            ]

        def block(n, carry):
            slot = lax.rem(n, 2)

            @pl.when(n + 1 < blocks)
            def _():
                tall_load(n + 1, 1 - slot).start()

            tall_load(n, slot).wait()

            @pl.when(n >= 2)
            def _():
                for c in out_copies(n, slot):
                    c.wait()

            row_cols = tall[slot].reshape(8 * size, size)
            for i, left in enumerate((dgate_v, dup_v)):
                out[slot, i] = dot_nn(left[...], row_cols).astype(bf16).reshape(4, quarter, size)
            for c in out_copies(n, slot):
                c.start()
            return carry

        lax.fori_loop(0, early, block, 0)
        total.end(grad_ref)
        middle = middle_ref[...]
        inverse = lax.rsqrt(jnp.mean(middle * middle, axis=1, keepdims=True) + epsilon)
        normed = middle * inverse
        grad = grad_ref[...]
        gain_grad_ref[...] = jnp.sum(grad * normed, axis=0, keepdims=True)
        load_dy.wait()
        for c in output_loads:
            c.wait()
        grad = dy[...].astype(f32) + norm_back(grad, gain_ref[...], normed, inverse)
        grad_ref[...] = grad
        store[f] = grad.astype(bf16)
        gather.begin()
        gather.advance(0)
        lax.fori_loop(early, early + 1, block, 0)
        gather.advance(1)
        lax.fori_loop(early + 1, early + 2, block, 0)
        gather.advance(2)
        lax.fori_loop(early + 2, blocks, block, 0)
        gather.advance(3)

        def chunk(i, carry):
            owner = f ^ i
            lanes = columns(owner, size)
            do_ref[:, lanes] = outer_cols(w_ref[...], store[owner]).astype(bf16)
            o_sum[...] += dot_nn(o_ref[:, lanes], store[owner])
            return carry

        o_sum[...] = jnp.zeros_like(o_sum)
        gather.wait_core(0)
        lax.fori_loop(0, 2, chunk, 0)
        gather.wait_core(3, 4)
        lax.fori_loop(2, 6, chunk, 0)
        gather.far()
        gather.wait_core(5)
        lax.fori_loop(6, 8, chunk, 0)
        for j in range(8):
            grad_o_ref[j] = o_sum[:, j * size : (j + 1) * size].astype(bf16)
        for n in (blocks - 2, blocks - 1):
            for c in out_copies(n, n % 2):
                c.wait()
        total.finish()
        gather.finish()

    tall_units = pltpu.VMEM((units, width), bf16)
    weights = pltpu.VMEM((4, quarter, width), bf16)
    return pl.pallas_call(
        kernel,
        out_shape=[
            jax.ShapeDtypeStruct((size, width), f32),
            jax.ShapeDtypeStruct((1, width), f32),
            jax.ShapeDtypeStruct((8, depth, size), bf16),
            jax.ShapeDtypeStruct((depth, 8 * size), bf16),
        ]
        + [jax.ShapeDtypeStruct((4, blocks, quarter, size), bf16)] * 2,
        in_specs=[ANYWHERE] * 6 + [IN_VMEM] * 3,
        out_specs=[IN_VMEM] * 4 + [ANYWHERE] * 2,
        scratch_shapes=sum_scratch(size, width)
        + [pltpu.VMEM((8, size, width), bf16)]
        + GATHER_SEMAPHORES
        + [tall_units] * 2
        + [weights] * 2
        + [
            pltpu.SemaphoreType.DMA((2,)),
            pltpu.SemaphoreType.DMA((2, 8)),
            pltpu.VMEM((2, 8, size, size), bf16),
            pltpu.SemaphoreType.DMA((2,)),
            pltpu.VMEM((2, 2, 4, quarter, size), bf16),
            pltpu.SemaphoreType.DMA((2, 2)),
            pltpu.VMEM((depth, width), f32),
            pltpu.VMEM((size, width), bf16),
            pltpu.SemaphoreType.DMA,
            pltpu.VMEM((depth, width), bf16),
            pltpu.SemaphoreType.DMA((8,)),
        ],
        compiler_params=comm_params(number, VMEM_MOST),
        cost_estimate=lasting(92),
        name="backward_middle",
    )(dgate, dup, gate_up, rows, dys, output_rows, attended, middle, gain)


class LineGather:
    def __init__(self, own, store, sent, arrived):
        self.f, self.t = lax.axis_index("fsdp"), lax.axis_index("tp")
        self.own, self.store, self.sent, self.arrived = own, store, sent, arrived

    def copy(self, way, hop):
        step = 1 if way == 0 else -1
        place = self.store.at[self.t - step * (hop - 1)]
        source = self.own if hop == 1 else place
        return remote(
            source, place, self.sent.at[way, hop], self.arrived.at[way, hop], (self.f, self.t + step)
        )

    def goes(self, way, hop):
        if way == 0:
            return (self.t < 3) & (self.t >= hop - 1)
        return (self.t > 0) & (self.t <= 4 - hop)

    def came(self, way, hop):
        return self.t >= hop if way == 0 else self.t <= 3 - hop

    def send(self, hop):
        for way in (0, 1):
            pl.when(self.goes(way, hop))(lambda way=way: self.copy(way, hop).start())

    def begin(self):
        self.send(1)

    def take(self, hop):
        for way in (0, 1):

            @pl.when(self.came(way, hop))
            def _(way=way):
                spot = self.store.at[self.t - hop if way == 0 else self.t + hop]
                remote(
                    spot, spot, self.sent.at[way, hop], self.arrived.at[way, hop], (self.f, self.t)
                ).wait_recv()

        if hop < 3:
            self.send(hop + 1)

    def finish(self):
        for hop in (1, 2, 3):
            for way in (0, 1):
                pl.when(self.goes(way, hop))(lambda way=way, hop=hop: self.copy(way, hop).wait_send())


LINE_SEMAPHORES = [pltpu.SemaphoreType.DMA((2, 4)), pltpu.SemaphoreType.DMA((2, 4))]


def everyone(f, t):
    return [(f ^ k, t) for k in range(1, 8)] + [(f, lax.rem(t + k, 4)) for k in (1, 2, 3)]


def unit_loads(source, target, sems):
    block = target.shape[2] // 8
    return [
        pltpu.make_async_copy(source(j), target.at[:, :, pl.ds(j * block, block)], sems.at[j])
        for j in range(8)
    ]


class Rows:
    def __init__(self, ref):
        self.ref = ref

    def __getitem__(self, index):
        block = self.ref[:, :, index[1]]
        return block.reshape(4 * block.shape[1], block.shape[2])


def column_loads(source, target, sems):
    block = source.shape[2]
    return [
        pltpu.make_async_copy(source.at[j], target.at[:, pl.ds(j * block, block)], sems.at[j])
        for j in range(8)
    ]


def as_rows(ref):
    return ref[...].reshape(4 * ref.shape[1], ref.shape[2])


def turn_heads(values, cosine, sine_table):
    half = HEAD_DIM // 2
    turned = []
    for h in range(values.shape[0] // HEAD_DIM):
        first = values[h * HEAD_DIM : h * HEAD_DIM + half]
        second = values[h * HEAD_DIM + half : (h + 1) * HEAD_DIM]
        turned.append(first * cosine - second * sine_table)
        turned.append(second * cosine + first * sine_table)
    return jnp.concatenate(turned, axis=0)


def first_forms(gate, up, query, key_rows, value_rows):
    bf16, f32 = jnp.bfloat16, jnp.float32
    block, hidden = gate.shape
    across = query.shape[1]
    units = hidden // 8

    def turned(ref):
        return ref[...].astype(f32).T.astype(bf16)

    def kernel(gate_ref, up_ref, q_ref, k_ref, v_ref, units_ref, inner_ref):
        inner_ref[:across] = turned(q_ref)
        inner_ref[across : across + HEAD_DIM] = k_ref[...]
        inner_ref[across + HEAD_DIM :] = v_ref[...]
        units_ref[:, 0] = turned(gate_ref).reshape(8, units, block)
        units_ref[:, 1] = turned(up_ref).reshape(8, units, block)

    return pl.pallas_call(
        kernel,
        out_shape=[
            jax.ShapeDtypeStruct((8, 2, units, block), bf16),
            jax.ShapeDtypeStruct((across + 2 * HEAD_DIM, block), bf16),
        ],
        in_specs=[IN_VMEM] * 5,
        out_specs=[IN_VMEM] * 2,
        compiler_params=pltpu.CompilerParams(vmem_limit_bytes=VMEM_MOST),
        cost_estimate=lasting(5),
        name="first_forms",
    )(gate, up, query, key_rows, value_rows)


def first_rows(tokens, gains_own, inner_all, output_own, cosine, sine_table, grads, valid, number):
    size, width = tokens.shape
    block = width // 8
    quarter_rows = output_own.shape[0]
    depth = quarter_rows // 2
    pair_rows = 2 * HEAD_DIM
    f32, bf16 = jnp.float32, jnp.bfloat16

    def kernel(
        x_ref, gains_own_ref, inner_ref, own_ref, cos_ref, sin_ref, dy_ref, valid_ref,
        rows_ref, q_ref, pair_ref, w_ref, wo_all, dys_ref, gains_ref,
        rows, rows_sent, rows_arrived, dys, dys_sent, dys_arrived, pair_v,
        w_sent, w_arrived, z_sent, z_arrived,
        p_sent, p_arrived, on_sent, on_arrived, g_sent, g_arrived, kept_sem,
    ):
        f, t = lax.axis_index("fsdp"), lax.axis_index("tp")
        gains_ref[f] = gains_own_ref[...]
        place = columns(f, block)
        far_first = (6, 7, 2, 4, 3, 5, 1)

        def inner_slices(j):
            quarter, side = lax.div(j, 2), lax.rem(j, 2)
            return [
                (
                    inner_ref.at[quarter, pl.ds(pl.multiple_of(side * depth, depth), depth)],
                    w_ref.at[pl.ds(0, depth), place],
                ),
                (
                    inner_ref.at[quarter, pl.ds(2 * depth, pair_rows)],
                    w_ref.at[pl.ds(depth, pair_rows), place],
                ),
            ]

        kept = [
            pltpu.make_async_copy(s, o, kept_sem.at[i]) for i, (s, o) in enumerate(inner_slices(f))
        ]
        kept.append(pltpu.make_async_copy(own_ref, wo_all.at[t], kept_sem.at[2]))
        for c in kept:
            c.start()
        greet(everyone(f, t))
        line_output = LineGather(own_ref, wo_all, z_sent, z_arrived)
        line_output.begin()
        weights, gains = [], []
        for k in far_first:
            c = remote(
                gains_own_ref, gains_ref.at[f], g_sent.at[k], g_arrived.at[k], (f ^ k, t)
            )
            c.start()
            gains.append(c)
        for k in far_first:
            for i, (s, o) in enumerate(inner_slices(f ^ k)):
                c = remote(s, o, w_sent.at[k, i], w_arrived.at[k, i], (f ^ k, t))
                c.start()
                weights.append(c)
        wide = x_ref[...].astype(f32)
        inverse = lax.rsqrt(jnp.mean(wide * wide, axis=1, keepdims=True) + epsilon)
        for c in gains:
            c.wait()
        gain = jnp.concatenate([gains_ref[j, 0:1] for j in range(8)], axis=1)
        rows[f] = (wide * inverse * gain).astype(bf16)
        gather = PlaneGather(rows, rows_sent, rows_arrived)
        gather.begin()
        dys[f] = jnp.where(valid_ref[...] > 0, dy_ref[...].astype(f32), 0.0).astype(bf16)
        for k in range(PARTS):
            gather.advance(k)
        gather_dys = PlaneGather(dys, dys_sent, dys_arrived)
        gather_dys.begin()
        for c in kept[:2]:
            c.wait()
        for c in weights:
            c.wait_recv()

        def chunk(i, carry):
            owner = f ^ i
            lanes = columns(owner, size)
            projected = outer_cols(w_ref[...], rows[owner])
            cosine, sine = cos_ref[:, lanes], sin_ref[:, lanes]
            queries = turn_heads(projected[:depth], cosine, sine).astype(bf16)
            q_ref[:, lanes] = (queries.astype(f32) * HEAD_DIM ** (-0.5)).astype(bf16)
            keys = turn_heads(projected[depth : depth + HEAD_DIM], cosine, sine)
            pair = jnp.concatenate([keys, projected[depth + HEAD_DIM :]], axis=0)
            pair_v[owner] = pair.T.astype(bf16)
            return carry

        spread = []

        def spread_pair(i):
            for k in (2, 1, 3):
                c = remote(
                    pair_v.at[f ^ i],
                    pair_ref.at[t, f ^ i],
                    p_sent.at[i // 2, k],
                    p_arrived.at[i // 2, k],
                    (f, lax.rem(t + k, 4)),
                )
                c.start()
                spread.append((i, k, c))

        gather.wait_core(0)
        lax.fori_loop(0, 2, chunk, 0)
        spread_pair(0)
        gather.wait_core(3, 4)
        lax.fori_loop(2, 6, chunk, 0)
        spread_pair(2)
        spread_pair(4)
        gather.far()
        gather.wait_core(5)
        lax.fori_loop(6, 8, chunk, 0)
        spread_pair(6)
        own_pair = pltpu.make_async_copy(pair_v, pair_ref.at[t], kept_sem.at[3])
        own_pair.start()
        keep_rows = pltpu.make_async_copy(rows, rows_ref, kept_sem.at[4])
        keep_rows.start()
        line_output.take(1)
        for k in range(PARTS):
            gather_dys.advance(k)
        line_output.take(2)
        passed = []
        for i, k, c in spread:
            c.wait_recv()
            spot = pair_ref.at[lax.rem(t + 4 - k, 4), f ^ i]
            d = remote(spot, spot, on_sent.at[i // 2, k], on_arrived.at[i // 2, k], (f ^ CORE, t))
            d.start()
            passed.append(d)
        gather_dys.wait_core(0, 3, 4)
        gather_dys.far()
        gather_dys.wait_core(5)
        keep_dys = pltpu.make_async_copy(dys, dys_ref, kept_sem.at[6])
        keep_dys.start()
        line_output.take(3)
        for c in passed:
            c.wait()
        for c in weights + [c for _, _, c in spread]:
            c.wait_send()
        line_output.finish()
        gather.finish()
        gather_dys.finish()
        own_pair.wait()
        keep_rows.wait()
        kept[2].wait()
        keep_dys.wait()

    dma = pltpu.SemaphoreType.DMA
    return pl.pallas_call(
        kernel,
        out_shape=[
            jax.ShapeDtypeStruct((8, size, width), bf16),
            jax.ShapeDtypeStruct((depth, 8 * size), bf16),
            jax.ShapeDtypeStruct((4, 8, size, pair_rows), bf16),
            jax.ShapeDtypeStruct((depth + pair_rows, width), bf16),
            jax.ShapeDtypeStruct((4, quarter_rows, block), bf16),
            jax.ShapeDtypeStruct((8, size, width), bf16),
            jax.ShapeDtypeStruct((8, *gains_own.shape), f32),
        ],
        in_specs=[IN_VMEM, IN_VMEM, ANYWHERE, ANYWHERE] + [IN_VMEM] * 4,
        out_specs=[ANYWHERE, IN_VMEM, ANYWHERE, IN_VMEM, ANYWHERE, ANYWHERE, IN_VMEM],
        scratch_shapes=[pltpu.VMEM((8, size, width), bf16)]
        + GATHER_SEMAPHORES
        + [pltpu.VMEM((8, size, width), bf16)]
        + GATHER_SEMAPHORES
        + [
            pltpu.VMEM((8, size, pair_rows), bf16),
            dma((8, 2)),
            dma((8, 2)),
            *LINE_SEMAPHORES,
            dma((4, 4)),
            dma((4, 4)),
            dma((4, 4)),
            dma((4, 4)),
            dma((8,)),
            dma((8,)),
            dma((7,)),
        ],
        compiler_params=comm_params(number, VMEM_MOST),
        cost_estimate=lasting(100),
        name="first_rows",
    )(tokens, gains_own, inner_all, output_own, cosine, sine_table, grads, valid)


def grads_across(left_ref, rows_v, out_v, target_ref, sent, arrived, kept_sem):
    f, t = lax.axis_index("fsdp"), lax.axis_index("tp")
    _, size, width = rows_v.shape
    block = width // 8
    copies = []

    def step(k):
        right = rows_v[:, :, columns(f ^ k, block)].reshape(8 * size, block)
        out_v[k] = dot_nn(left_ref[...], right).astype(jnp.bfloat16)
        if k:
            c = remote(out_v.at[k], target_ref.at[f], sent.at[k], arrived.at[k], (f ^ k, t))
        else:
            c = pltpu.make_async_copy(out_v.at[0], target_ref.at[f], kept_sem)
        c.start()
        copies.append(c)

    return step, copies


def exchange_begin(ways, sent, arrived, kept_sem):
    f, t = lax.axis_index("fsdp"), lax.axis_index("tp")
    copies = []
    for i, (source, target) in enumerate(ways):
        for k in (6, 7, 2, 4, 3, 5, 1):
            copies.append(
                remote(
                    source.at[f ^ k], target.at[f], sent.at[k, i], arrived.at[k, i], (f ^ k, t)
                )
            )
        copies.append(pltpu.make_async_copy(source.at[f], target.at[f], kept_sem.at[i]))
    for c in copies:
        c.start()
    return copies


def backward_pairs(pair_parts, hidden, down_all, middle, valid, grad_query, rows, cosine, sine_table, number):
    size, width = middle.shape
    units = hidden.shape[0]
    depth = grad_query.shape[0]
    _, chunks, height, _ = pair_parts.shape
    half = chunks // 2
    f32, bf16 = jnp.float32, jnp.bfloat16

    def kernel(
        p_ref, hidden_hbm, down_hbm, middle_ref, valid_ref, g_ref, rows_hbm, cos_ref, sin_ref,
        single_ref, out_ref, spread_ref,
        stage, other, held, from_x, from_y, last, sum_sent, sum_arrived,
        hidden_v, down_w, load_sem, unit_sem, ra, s, rz, sent, arrived, share, pair,
        rows_v, w_grad, w_sent, w_arrived,
    ):
        f, t = lax.axis_index("fsdp"), lax.axis_index("tp")
        loads = [pltpu.make_async_copy(hidden_hbm, hidden_v, load_sem.at[0])]
        loads += unit_loads(lambda j: down_hbm.at[:, j], down_w, unit_sem)
        load_rows = pltpu.make_async_copy(rows_hbm, rows_v, load_sem.at[1])
        for c in loads + [load_rows]:
            c.start()
        side = lax.rem(f, 2)
        mine, theirs = pl.ds(side * half, half), pl.ds((1 - side) * half, half)
        core = (f ^ CORE, t)
        greet(everyone(f, t))
        first = []
        for k in (2, 1, 3, 0):
            plane = lax.rem(t + k, 4)
            c = remote(p_ref.at[plane, theirs], ra.at[k], sent.at[k], arrived.at[k], core)
            c.start()
            first.append((k, c))
        out = []
        for k, c in first:
            c.wait_recv()
            plane = lax.rem(t + k, 4)
            both = p_ref[plane, mine].astype(f32) + ra[k].astype(f32)
            if k:
                s[k] = both.astype(bf16)
                d = remote(s.at[k], rz.at[k], sent.at[3 + k], arrived.at[3 + k], (f, plane))
                d.start()
                out.append((k, d))
            else:
                pair[mine] = both
        for c in loads:
            c.wait()
        total = PlaneSum(stage, other, held, from_x, from_y, last, sum_sent, sum_arrived)
        total.begin(chunk_part([(hidden_v, Rows(down_w))], size))
        load_rows.wait()
        query_grads, copies = grads_across(
            g_ref, rows_v, w_grad, spread_ref, w_sent, w_arrived, load_sem.at[2]
        )
        for k in (6, 7, 2, 4, 3, 5, 1, 0):
            query_grads(k)
        total.turn()
        for k, d in out:
            d.wait_recv()
            pair[mine] += rz[k].astype(f32)
        back = remote(pair.at[mine], pair.at[mine], sent.at[7], arrived.at[7], core)
        back.start()
        back.wait()
        for j in range(chunks):
            lanes = slice(j * size, (j + 1) * size)
            keys = turn_heads(pair[j, :HEAD_DIM], cos_ref[:, lanes], -sin_ref[:, lanes])
            single_ref[:, lanes] = jnp.where(side == 0, keys, pair[j, HEAD_DIM:]).astype(bf16)
        total.end(share)
        out_ref[...] = jnp.where(valid_ref[...] > 0, middle_ref[...] + share[...], 0.0).astype(bf16)
        for c in copies:
            c.wait()
        for k, c in first + out:
            c.wait_send()
        total.finish()

    dma = pltpu.SemaphoreType.DMA
    return pl.pallas_call(
        kernel,
        out_shape=[
            jax.ShapeDtypeStruct((HEAD_DIM, chunks * size), bf16),
            jax.ShapeDtypeStruct((size, width), bf16),
            jax.ShapeDtypeStruct((8, depth, width // 8), bf16),
        ],
        in_specs=[IN_VMEM, ANYWHERE, ANYWHERE, IN_VMEM, IN_VMEM, IN_VMEM, ANYWHERE, IN_VMEM, IN_VMEM],
        out_specs=[IN_VMEM, IN_VMEM, ANYWHERE],
        scratch_shapes=sum_scratch(size, width)
        + [pltpu.VMEM((units, 8 * size), bf16), pltpu.VMEM((4, units // 4, width), bf16)]
        + [dma((3,)), dma((8,))]
        + [pltpu.VMEM((4, half, height, size), bf16)] * 3
        + [dma((8,)), dma((8,)), pltpu.VMEM((size, width), f32)]
        + [
            pltpu.VMEM((chunks, height, size), f32),
            pltpu.VMEM((8, size, width), bf16),
            pltpu.VMEM((8, depth, width // 8), bf16),
            dma((8,)),
            dma((8,)),
        ],
        compiler_params=comm_params(number, VMEM_MOST),
        cost_estimate=lasting(55),
        name="backward_pairs",
    )(pair_parts, hidden, down_all, middle, valid, grad_query, rows, cosine, sine_table)


def backward_first(
    grad_query, single, weights, rows, tokens, grad_middle, gain, down_grads, gate_grads, number
):
    size, width = tokens.shape
    depth = grad_query.shape[0]
    block = width // 8
    f32, bf16 = jnp.float32, jnp.bfloat16

    def kernel(
        g_ref, single_ref, w_ref, rows_hbm, x_ref, middle_ref, gain_ref, down_ref, gate_ref,
        tokens_grad_ref, gain_grad_ref, spread_ref, own_down_ref, own_gate_ref,
        stage, other, held, from_x, from_y, last, sum_sent, sum_arrived,
        rows_v, load_sem, w_grad, sent, arrived, single_w, e_sent, e_arrived, e_kept,
    ):
        f, t = lax.axis_index("fsdp"), lax.axis_index("tp")
        load = pltpu.make_async_copy(rows_hbm, rows_v, load_sem.at[0])
        load.start()
        side = lax.rem(f, 2)
        single_w[...] = w_ref[
            pl.ds(pl.multiple_of(depth + side * HEAD_DIM, HEAD_DIM), HEAD_DIM), :
        ]
        greet([(f ^ k, t) for k in range(1, 8)])
        total = PlaneSum(stage, other, held, from_x, from_y, last, sum_sent, sum_arrived)
        total.begin(chunk_part([(g_ref, w_ref.at[pl.ds(0, depth)]), (single_ref, single_w)], size))
        load.wait()
        single_grads, copies = grads_across(
            single_ref, rows_v, w_grad, spread_ref, sent, arrived, load_sem.at[1]
        )
        for k in (6, 7, 2, 4, 3, 5, 1, 0):
            single_grads(k)
        total.turn()
        exchange = exchange_begin(
            ((down_ref, own_down_ref), (gate_ref, own_gate_ref)), e_sent, e_arrived, e_kept
        )
        wide = x_ref[...].astype(f32)
        inverse = lax.rsqrt(jnp.mean(wide * wide, axis=1, keepdims=True) + epsilon)
        normed = wide * inverse
        total.end(tokens_grad_ref)
        grad = tokens_grad_ref[...]
        gain_grad_ref[...] = jnp.sum(grad * normed, axis=0, keepdims=True)
        tokens_grad_ref[...] = middle_ref[...] + norm_back(grad, gain_ref[...], normed, inverse)
        for c in copies + exchange:
            c.wait()
        total.finish()

    dma = pltpu.SemaphoreType.DMA
    return pl.pallas_call(
        kernel,
        out_shape=[
            jax.ShapeDtypeStruct((size, width), f32),
            jax.ShapeDtypeStruct((1, width), f32),
            jax.ShapeDtypeStruct((8, HEAD_DIM, block), bf16),
            jax.ShapeDtypeStruct(down_grads.shape, bf16),
            jax.ShapeDtypeStruct(gate_grads.shape, bf16),
        ],
        in_specs=[IN_VMEM] * 3 + [ANYWHERE] + [IN_VMEM] * 3 + [ANYWHERE] * 2,
        out_specs=[IN_VMEM, IN_VMEM, ANYWHERE, ANYWHERE, ANYWHERE],
        scratch_shapes=sum_scratch(size, width)
        + [
            pltpu.VMEM((8, size, width), bf16),
            dma((2,)),
            pltpu.VMEM((8, HEAD_DIM, block), bf16),
            dma((8,)),
            dma((8,)),
            pltpu.VMEM((HEAD_DIM, width), bf16),
            dma((8, 2)),
            dma((8, 2)),
            dma((2,)),
        ],
        compiler_params=comm_params(number, VMEM_MOST),
        cost_estimate=lasting(62),
        name="backward_first",
    )(grad_query, single, weights, rows, tokens, grad_middle, gain, down_grads, gate_grads)


def last_sums(gain_first, gain_second, pair_parts, up_grads, number):
    width = gain_first.shape[1]
    block = width // 8
    f32 = jnp.float32

    def kernel(
        first_ref, second_ref, p_ref, up_ref, sums_ref, pair_ref, own_up_ref,
        gains, taken, planes, pairs, sent, arrived, z_sent, z_arrived, p_sent, p_arrived, e_sent, e_arrived, e_kept,
    ):
        f, t = lax.axis_index("fsdp"), lax.axis_index("tp")
        for j in range(8):
            lanes = slice(j * block, (j + 1) * block)
            gains[j] = jnp.concatenate([first_ref[:, lanes], second_ref[:, lanes]], axis=0)
        greet(everyone(f, t))
        copies = []
        for k in (2, 1, 3):
            plane = lax.rem(t + k, 4)
            c = remote(
                p_ref.at[pl.ds(2 * plane, 2)], pairs.at[k], p_sent.at[k], p_arrived.at[k], (f, plane)
            )
            c.start()
            copies.append(c)
        spread = []
        for k in (6, 7, 2, 4, 3, 5, 1):
            c = remote(gains.at[f ^ k], taken.at[k], sent.at[k], arrived.at[k], (f ^ k, t))
            c.start()
            spread.append((k, c))
        exchange = exchange_begin(((up_ref, own_up_ref),), e_sent, e_arrived, e_kept)
        total = gains[f]
        for k, c in spread:
            c.wait_recv()
            total += taken[k]
        planes[0] = total
        along_z = []
        for k in (1, 2, 3):
            c = remote(planes.at[0], planes.at[k], z_sent.at[k], z_arrived.at[k], (f, lax.rem(t + k, 4)))
            c.start()
            along_z.append(c)
        pair = p_ref[pl.ds(2 * t, 2)].astype(f32)
        for k, c in zip((2, 1, 3), copies):
            c.wait_recv()
            pair += pairs[k].astype(f32)
        pair_ref[...] = pair
        for c in along_z:
            c.wait_recv()
        sums = planes[t]
        for plane in (1, 2, 3):
            sums += planes[lax.rem(t + 4 - plane, 4)]
        sums_ref[...] = sums
        for c in [c for _, c in spread] + along_z + copies:
            c.wait_send()
        for c in exchange:
            c.wait()

    dma = pltpu.SemaphoreType.DMA
    return pl.pallas_call(
        kernel,
        out_shape=[
            jax.ShapeDtypeStruct((2, block), f32),
            jax.ShapeDtypeStruct((2, *pair_parts.shape[1:]), f32),
            jax.ShapeDtypeStruct(up_grads.shape, up_grads.dtype),
        ],
        in_specs=[IN_VMEM] * 3 + [ANYWHERE],
        out_specs=[IN_VMEM] * 2 + [ANYWHERE],
        scratch_shapes=[
            pltpu.VMEM((8, 2, block), f32),
            pltpu.VMEM((8, 2, block), f32),
            pltpu.VMEM((4, 2, block), f32),
            pltpu.VMEM((4, 2, *pair_parts.shape[1:]), pair_parts.dtype),
            dma((8,)),
            dma((8,)),
            dma((4,)),
            dma((4,)),
            dma((4,)),
            dma((4,)),
            dma((8, 1)),
            dma((8, 1)),
            dma((1,)),
        ],
        compiler_params=comm_params(number, VMEM_MOST),
        cost_estimate=lasting(16),
        name="last_sums",
    )(gain_first, gain_second, pair_parts, up_grads)


def last_forms(layer_out, tokens_grad, grad_query, grad_output, grad_down, grad_gate, grad_up):
    f32 = jnp.float32
    across = grad_query.shape[0]
    block = grad_query.shape[1]
    units = grad_down.shape[1]
    tall = 8 * units

    def kernel(
        out_in, tokens_in, query_in, output_in, down_in, gate_in, up_in,
        out_o, tokens_o, query_o, output_o, gate_o, up_o, down_o,
        out_v, tokens_v, query_v, output_v, down_v, gate_v, up_v,
        query_w, output_w, gate_w, up_w, down_w, in_sem, out_sem,
    ):
        loads = [
            pltpu.make_async_copy(source, target, in_sem.at[i])
            for i, (source, target) in enumerate(
                (
                    (gate_in, gate_v),
                    (up_in, up_v),
                    (down_in, down_v),
                    (out_in, out_v),
                    (tokens_in, tokens_v),
                    (query_in, query_v),
                    (output_in, output_v),
                )
            )
        ]
        for c in loads:
            c.start()
        stores = []

        def store(source, target):
            c = pltpu.make_async_copy(source, target, out_sem.at[len(stores)])
            c.start()
            stores.append(c)

        for n, (tight, wide, target) in enumerate(((gate_v, gate_w, gate_o), (up_v, up_w, up_o))):
            loads[n].wait()
            wide[...] = tight[...].reshape(tall, block).astype(f32).T
            store(wide, target)
        loads[2].wait()
        down_w[...] = down_v[...].reshape(tall, block).astype(f32)
        store(down_w, down_o)
        loads[3].wait()
        store(out_v, out_o)
        loads[4].wait()
        store(tokens_v, tokens_o)
        loads[5].wait()
        query_w[...] = query_v[...].astype(f32).T
        store(query_w, query_o)
        loads[6].wait()
        output_w[...] = output_v[...].astype(f32)
        store(output_w, output_o)
        for c in stores:
            c.wait()

    operands = (layer_out, tokens_grad, grad_query, grad_output, grad_down, grad_gate, grad_up)
    results = [
        jax.ShapeDtypeStruct(layer_out.shape, layer_out.dtype),
        jax.ShapeDtypeStruct(tokens_grad.shape, f32),
        jax.ShapeDtypeStruct((block, across), f32),
        jax.ShapeDtypeStruct((across, block), f32),
        jax.ShapeDtypeStruct((block, tall), f32),
        jax.ShapeDtypeStruct((block, tall), f32),
        jax.ShapeDtypeStruct((tall, block), f32),
    ]
    return pl.pallas_call(
        kernel,
        out_shape=results,
        in_specs=[ANYWHERE] * 7,
        out_specs=[ANYWHERE] * 7,
        scratch_shapes=[pltpu.VMEM(x.shape, x.dtype) for x in operands]
        + [pltpu.VMEM(x.shape, x.dtype) for x in results[2:]]
        + [pltpu.SemaphoreType.DMA((7,)), pltpu.SemaphoreType.DMA((7,))],
        compiler_params=pltpu.CompilerParams(vmem_limit_bytes=VMEM_MOST),
        cost_estimate=lasting(8),
        name="last_forms",
    )(*operands)


def dot_nn(left, right):
    return jnp.dot(left, right, preferred_element_type=jnp.float32)


def seen_keys(begin_row, first_key, first_query, shape):
    key_slot = first_key + lax.broadcasted_iota(jnp.int32, shape, 0)
    query_slot = first_query + lax.broadcasted_iota(jnp.int32, (1, shape[1]), 1)
    return (key_slot <= query_slot) & (key_slot >= begin_row)


def head_lanes(block, heads):
    return jnp.concatenate([block[h * HEAD_DIM : (h + 1) * HEAD_DIM] for h in range(heads)], axis=1)


WIDE = 2

def key_block(kv_ref, g, count):
    blocks = [kv_ref[lax.rem(g + n, 4), lax.div(g + n, 4)] for n in range(count)]
    return blocks[0] if count == 1 else jnp.concatenate(blocks, axis=0)


def attend(info, begins, queries, pair):
    depth, slots = queries.shape
    heads = depth // HEAD_DIM
    size = slots // 8
    span = heads * size

    def kernel(info_ref, begin_ref, q_ref, kv_ref, o_ref, l_ref, q_s, m_s, t_s, a_s):
        f = pl.program_id(0)
        low, middle, own = info_ref[f, 0], info_ref[f, 1], info_ref[f, 2]
        middle = middle + lax.rem(own - middle, WIDE)
        q_s[...] = head_lanes(q_ref[...], heads)
        m_s[...] = jnp.full_like(m_s, -1e30)
        t_s[...] = jnp.zeros_like(t_s)
        a_s[...] = jnp.zeros_like(a_s)

        def step(g, count, masked):
            block = key_block(kv_ref, g, count)
            keys, values = block[:, :HEAD_DIM], block[:, HEAD_DIM:]
            value_cols = values.astype(jnp.float32).T.astype(jnp.bfloat16)
            if masked:
                seen = seen_keys(begin_ref[0], g * size, own * size, (size, size))
                seen = jnp.concatenate([seen] * heads, axis=1)
            scores = dot_nn(keys, q_s[...])
            if masked:
                scores = jnp.where(seen, scores, -1e30)
            largest = m_s[...]
            higher = jnp.maximum(largest, jnp.max(scores, axis=0, keepdims=True))
            raised = jnp.exp(scores - higher)
            fade = jnp.exp(largest - higher)
            m_s[...] = higher
            t_s[...] = t_s[...] * fade + jnp.sum(raised, axis=0, keepdims=True)
            a_s[...] = a_s[...] * fade + dot_nn(
                value_cols, raised.astype(jnp.bfloat16)
            )

        def masked_step(g, carry):
            step(g, 1, True)
            return carry

        def plain_step(n, carry):
            step(middle + n * WIDE, WIDE, False)
            return carry

        step(own, 1, True)
        lax.fori_loop(low, middle, masked_step, 0)
        lax.fori_loop(0, lax.div(own - middle, WIDE), plain_step, 0)
        result = a_s[...] / t_s[...]
        for h in range(heads):
            o_ref[h * HEAD_DIM : (h + 1) * HEAD_DIM] = result[:, h * size : (h + 1) * size].astype(
                jnp.bfloat16
            )
        l_ref[0] = m_s[...] + jnp.log(t_s[...])
    return pl.pallas_call(
        kernel,
        grid_spec=pltpu.PrefetchScalarGridSpec(
            num_scalar_prefetch=1,
            grid=(8,),
            in_specs=[
                pl.BlockSpec((1, 1, size), lambda f, info: (f, 0, 0)),
                pl.BlockSpec((depth, size), lambda f, info: (0, f)),
                pl.BlockSpec((4, 8, size, 2 * HEAD_DIM), lambda f, info: (0, 0, 0, 0)),
            ],
            out_specs=[
                pl.BlockSpec((depth, size), lambda f, info: (0, f)),
                pl.BlockSpec((1, 1, span), lambda f, info: (f, 0, 0)),
            ],
            scratch_shapes=[
                pltpu.VMEM((HEAD_DIM, span), jnp.bfloat16),
                pltpu.VMEM((1, span), jnp.float32),
                pltpu.VMEM((1, span), jnp.float32),
                pltpu.VMEM((HEAD_DIM, span), jnp.float32),
            ],
        ),
        out_shape=[
            jax.ShapeDtypeStruct((depth, slots), jnp.bfloat16),
            jax.ShapeDtypeStruct((8, 1, span), jnp.float32),
        ],
        compiler_params=pltpu.CompilerParams(vmem_limit_bytes=VMEM_MOST),
        cost_estimate=lasting(50),
        name="attend",
    )(info, begins, queries, pair)


def attend_back(info, begins, queries, pair, outputs, grads, totals, cosine, sine_table):
    depth, slots = queries.shape
    heads = depth // HEAD_DIM
    size = slots // 8
    span = heads * size

    def kernel(
        info_ref, begin_ref, q_ref, kv_ref, o_ref, g_ref, l_ref, cos_ref, sin_ref, dq_ref, dkv_ref, q_s, g_s, d_s, a_s, w_s
    ):
        f = pl.program_id(0)
        low, middle, own = info_ref[f, 0], info_ref[f, 1], info_ref[f, 2]
        middle = middle + lax.rem(own - middle, WIDE)

        @pl.when(f == 0)
        def _():
            w_s[...] = jnp.zeros_like(w_s)

        q_s[...] = head_lanes(q_ref[...], heads)
        g_s[...] = head_lanes(g_ref[...], heads)
        out_lanes = head_lanes(o_ref[...], heads).astype(jnp.float32)
        d_s[...] = jnp.sum(out_lanes * g_s[...].astype(jnp.float32), axis=0, keepdims=True)
        a_s[...] = jnp.zeros_like(a_s)

        def step(g, count, masked):
            block = key_block(kv_ref, g, count)
            keys, values = block[:, :HEAD_DIM], block[:, HEAD_DIM:]
            key_cols = keys.astype(jnp.float32).T.astype(jnp.bfloat16)
            if masked:
                seen = seen_keys(begin_ref[0], g * size, own * size, (size, size))
                seen = jnp.concatenate([seen] * heads, axis=1)
            grad_keys = jnp.zeros((HEAD_DIM, count * size), jnp.float32)
            grad_values = jnp.zeros((HEAD_DIM, count * size), jnp.float32)
            query, grad = q_s[...], g_s[...]
            raised = jnp.exp(dot_nn(keys, query) - l_ref[0])
            if masked:
                raised = jnp.where(seen, raised, 0.0)
            grad_probs = dot_nn(values, grad)
            scores = (raised * (grad_probs - d_s[...])).astype(jnp.bfloat16)
            grad_values += outer_cols(grad, raised.astype(jnp.bfloat16))
            grad_keys += outer_cols(query, scores)
            a_s[...] += dot_nn(key_cols, scores)
            for n in range(count):
                keep = slice(n * size, (n + 1) * size)
                w_s[lax.rem(g + n, 4), lax.div(g + n, 4), :HEAD_DIM] += grad_keys[:, keep]
                w_s[lax.rem(g + n, 4), lax.div(g + n, 4), HEAD_DIM:] += grad_values[:, keep]

        def masked_step(g, carry):
            step(g, 1, True)
            return carry

        def plain_step(n, carry):
            step(middle + n * WIDE, WIDE, False)
            return carry

        step(own, 1, True)
        lax.fori_loop(low, middle, masked_step, 0)
        lax.fori_loop(0, lax.div(own - middle, WIDE), plain_step, 0)
        result = a_s[...] * HEAD_DIM ** (-0.5)
        result = jnp.concatenate([result[:, h * size : (h + 1) * size] for h in range(heads)], axis=0)
        dq_ref[...] = turn_heads(result, cos_ref[...], -sin_ref[...]).astype(jnp.bfloat16)

        @pl.when(f == 7)
        def _():
            dkv_ref[...] = w_s[...].astype(jnp.bfloat16)

    return pl.pallas_call(
        kernel,
        grid_spec=pltpu.PrefetchScalarGridSpec(
            num_scalar_prefetch=1,
            grid=(8,),
            in_specs=[
                pl.BlockSpec((1, 1, size), lambda f, info: (f, 0, 0)),
                pl.BlockSpec((depth, size), lambda f, info: (0, f)),
                pl.BlockSpec((4, 8, size, 2 * HEAD_DIM), lambda f, info: (0, 0, 0, 0)),
                pl.BlockSpec((depth, size), lambda f, info: (0, f)),
                pl.BlockSpec((depth, size), lambda f, info: (0, f)),
                pl.BlockSpec((1, 1, span), lambda f, info: (f, 0, 0)),
                pl.BlockSpec((HEAD_DIM // 2, size), lambda f, info: (0, f)),
                pl.BlockSpec((HEAD_DIM // 2, size), lambda f, info: (0, f)),
            ],
            out_specs=[
                pl.BlockSpec((depth, size), lambda f, info: (0, f)),
                pl.BlockSpec((4, 8, 2 * HEAD_DIM, size), lambda f, info: (0, 0, 0, 0)),
            ],
            scratch_shapes=[
                pltpu.VMEM((HEAD_DIM, span), jnp.bfloat16),
                pltpu.VMEM((HEAD_DIM, span), jnp.bfloat16),
                pltpu.VMEM((1, span), jnp.float32),
                pltpu.VMEM((HEAD_DIM, span), jnp.float32),
                pltpu.VMEM((4, 8, 2 * HEAD_DIM, size), jnp.float32),
            ],
        ),
        out_shape=[
            jax.ShapeDtypeStruct((depth, slots), jnp.bfloat16),
            jax.ShapeDtypeStruct((4, 8, 2 * HEAD_DIM, size), jnp.bfloat16),
        ],
        compiler_params=pltpu.CompilerParams(vmem_limit_bytes=VMEM_MOST),
        cost_estimate=lasting(65),
        name="attend_back",
    )(info, begins, queries, pair, outputs, grads, totals, cosine, sine_table)


def segment_begins(slots, lengths):
    seq_index = jnp.arange(lengths.shape[0], dtype=jnp.int32)
    ends = jnp.sum(jnp.where(seq_index[:, None] >= seq_index[None, :], lengths[None, :], 0), axis=1)
    passed = slots[:, None] >= ends[None, :]
    begins = jnp.sum(jnp.where(passed, lengths[None, :], 0), axis=1)
    return begins, slots < ends[-1]


def local_plane(
    tokens,
    attn_gain,
    query_weight,
    key_weight,
    value_weight,
    output_weight,
    mlp_gain,
    gate_weight,
    up_weight,
    down_weight,
    out_grad,
    lengths,
):
    size, width = tokens.shape
    f = lax.axis_index("fsdp")
    t = lax.axis_index("tp")
    block = query_weight.shape[0]
    head_rows = query_weight.shape[1] // 2
    units = gate_weight.shape[1] // 8
    bf16, f32 = jnp.bfloat16, jnp.float32

    def across_plane(parts):
        return lax.all_to_all(parts, "fsdp", 0, 0, tiled=False)

    def planes_together(part):
        flat = part.reshape(-1, block)
        return lax.all_gather(flat, "tp", axis=0, tiled=True).reshape(4, *part.shape)

    gate_up, inner_own = first_forms(
        gate_weight, up_weight, query_weight, key_weight.T, value_weight.T
    )
    inner_all = planes_together(inner_own)
    down_all = across_plane(down_weight.reshape(8, units, block))
    gate_up = across_plane(gate_up)
    tokens, down_all = lax.optimization_barrier((tokens, down_all))
    down_all = planes_together(down_all)
    gains_own = jnp.stack([attn_gain, mlp_gain]).astype(f32)

    my_slots = (f * 4 + t) * size + jnp.arange(size, dtype=jnp.int32)
    _, my_valid = segment_begins(my_slots, lengths)
    valid_rows = my_valid[:, None]
    chunk_index = jnp.arange(8, dtype=jnp.int32) * 4 + t
    plane_slots = (chunk_index[:, None] * size + jnp.arange(size, dtype=jnp.int32)[None, :]).reshape(-1)
    begins, plane_valid = segment_begins(plane_slots, lengths)
    positions = jnp.where(plane_valid, plane_slots - begins, 0)
    begins = begins.reshape(8, 1, size)
    info = jnp.stack(
        [
            begins[:, 0, 0] // size,
            jnp.minimum((begins[:, 0, size - 1] + size - 1) // size, chunk_index),
            chunk_index,
        ],
        axis=1,
    ).astype(jnp.int32)
    ladder = jnp.arange(HEAD_DIM // 2).astype(f32)
    frequency = 10000.0 ** (-2.0 * ladder / HEAD_DIM)
    angles = positions.astype(f32)[None, :] * frequency[:, None]
    cosine, sine_table = jnp.cos(angles), jnp.sin(angles)

    valid_rows = valid_rows.astype(f32)
    rows_first, queries, pair, inner_rows_w, output_all, grad_rows, gains_all = first_rows(
        tokens, gains_own, inner_all, output_weight, cosine, sine_table, out_grad, valid_rows, 2
    )
    output_rows = across_plane(output_all.reshape(8, head_rows, block))
    gate_up, pair = lax.optimization_barrier((gate_up, pair))
    gate_up = planes_together(gate_up)
    gains = jnp.moveaxis(gains_all, 0, 1).reshape(2, width)
    gain_first, gain_second = gains[0:1], gains[1:2]
    attended, totals = attend(info, begins, queries, pair)
    middle, row_second, grad_hidden = forward_output(
        attended, output_rows, tokens, gain_second, grad_rows, down_all, 4
    )
    rows_second, hidden, grad_gate_low, grad_up_low, down_grads = forward_hidden(
        row_second, grad_rows, grad_hidden, gate_up, 5
    )
    (
        grad_middle,
        gain_second_part,
        grad_output_w,
        grad_attended,
        gate_grads,
        up_grads,
    ) = backward_middle(
        grad_gate_low,
        grad_up_low,
        gate_up,
        rows_second,
        grad_rows,
        output_rows,
        attended,
        middle,
        gain_second,
        6,
    )
    def own_plane(parts, *shape):
        flat = parts.reshape(-1, block)
        return lax.psum_scatter(flat, "tp", scatter_dimension=0, tiled=True).reshape(*shape)

    down_grads = own_plane(down_grads, 8, units, block)
    gate_grads, down_grads = lax.optimization_barrier((gate_grads, down_grads))
    gate_grads = own_plane(gate_grads, 8, units, block)
    output_parts = across_plane(grad_output_w)
    output_parts, gate_grads = lax.optimization_barrier((output_parts, gate_grads))
    output_own = own_plane(output_parts, 2 * head_rows, block)
    grad_query, grad_pair_parts = attend_back(
        info, begins, queries, pair, attended, grad_attended, totals, cosine, sine_table
    )
    single, layer_out, query_parts = backward_pairs(
        grad_pair_parts,
        hidden,
        down_all,
        middle,
        valid_rows,
        grad_query,
        rows_first,
        cosine,
        sine_table,
        7,
    )
    up_grads, query_parts, output_own = lax.optimization_barrier((up_grads, query_parts, output_own))
    up_grads = own_plane(up_grads, 8, units, block)
    tokens_grad, gain_first_part, single_parts, own_down, own_gate = backward_first(
        grad_query,
        single,
        inner_rows_w,
        rows_first,
        tokens,
        grad_middle,
        gain_first,
        down_grads,
        gate_grads,
        8,
    )
    query_parts, up_grads = lax.optimization_barrier((query_parts, up_grads))
    query_own = own_plane(query_parts, 2 * head_rows, block)
    gain_sums, pair_own, own_up = last_sums(
        gain_first_part, gain_second_part, single_parts, up_grads, 9
    )
    layer_out, tokens_grad, query, output, gate, up, down = last_forms(
        layer_out, tokens_grad, query_own, output_own, own_down, own_gate, own_up
    )
    return (
        layer_out,
        tokens_grad,
        gain_sums[0],
        query,
        pair_own[0].T,
        pair_own[1].T,
        output,
        gain_sums[1],
        gate,
        up,
        down,
    )


def solution(mesh):
    plane = dict(mesh.shape) == {"fsdp": 8, "tp": 4}
    body = local_plane if plane else local
    in_specs = (
        P(("fsdp", "tp"), None),
        P("fsdp"),
        P("fsdp", "tp"),
        P("fsdp", "tp"),
        P("fsdp", "tp"),
        P("tp", "fsdp"),
        P("fsdp"),
        P("fsdp", "tp"),
        P("fsdp", "tp"),
        P("tp", "fsdp"),
        P(("fsdp", "tp"), None),
        P(),
    )
    out_specs = (
        P(("fsdp", "tp"), None),
        P(("fsdp", "tp"), None),
        P("fsdp"),
        P("fsdp", "tp"),
        P("fsdp", "tp"),
        P("fsdp", "tp"),
        P("tp", "fsdp"),
        P("fsdp"),
        P("fsdp", "tp"),
        P("fsdp", "tp"),
        P("tp", "fsdp"),
    )
    return jax.shard_map(body, mesh=mesh, in_specs=in_specs, out_specs=out_specs, check_vma=False)
```

```python
import jax
import jax.numpy as jnp
from jax import lax
from jax.experimental import pallas as pl
from jax.experimental.pallas import tpu as pltpu
from jax.sharding import PartitionSpec as P

HEAD_DIM = 64
MAX_SPAN = 4096


epsilon = 1e-05


def passed_along(block, axis, distance):
    devices = range(lax.axis_size(axis))
    route = [(i - distance, i) for i in devices if i - distance in devices]
    return lax.ppermute(block, axis, route)


def stream_layout(slots, lengths):
    seq_count = lengths.shape[0]
    seq_index = jnp.arange(seq_count, dtype=jnp.int32)
    ends = jnp.sum(jnp.where(seq_index[:, None] >= seq_index[None, :], lengths[None, :], 0), axis=1)
    starts = ends - lengths
    segment = jnp.sum((slots[:, None] >= ends[None, :]).astype(jnp.int32), axis=1)
    start_of = jnp.sum(
        jnp.where(segment[:, None] == seq_index[None, :], starts[None, :], 0), axis=1
    )
    position = jnp.where((segment < seq_count) & (slots >= 0), slots - start_of, 0)
    segment = jnp.where(slots < 0, -1, segment)
    return (segment, position)


def rotary_tables(positions, head_width):
    ladder = jnp.arange(head_width // 2).astype(jnp.float32)
    frequency = 10000.0 ** (-2.0 * ladder / head_width)
    angle_half = positions.astype(jnp.float32)[:, None] * frequency[None, :]
    angles = jnp.concatenate([angle_half, angle_half], axis=1)
    return (jnp.cos(angles)[:, None, :], jnp.sin(angles)[:, None, :])


def rotate(values, cosine, sine_table):
    middle = values.shape[-1] // 2
    turned = jnp.concatenate([-values[..., middle:], values[..., :middle]], axis=-1)
    return values * cosine + turned * sine_table


def rotate_back(values, cosine, sine_table):
    middle = values.shape[-1] // 2
    scaled = values * sine_table
    turned = jnp.concatenate([scaled[..., middle:], -scaled[..., :middle]], axis=-1)
    return values * cosine + turned


def inner_rows(left, right):
    return lax.dot_general(
        left, right, (((0,), (0,)), ((), ())), preferred_element_type=jnp.float32
    )


def outer_cols(left, right):
    return lax.dot_general(
        left, right, (((1,), (1,)), ((), ())), preferred_element_type=jnp.float32
    )


def norm_back(grad_normed, gain_wide, normed, inverse):
    scaled_grad = grad_normed * gain_wide
    return inverse * (scaled_grad - normed * jnp.mean(scaled_grad * normed, axis=1, keepdims=True))


def local(
    tokens,
    attn_gain,
    query_weight,
    key_weight,
    value_weight,
    output_weight,
    mlp_gain,
    gate_weight,
    up_weight,
    down_weight,
    out_grad,
    lengths,
):
    row_count = tokens.shape[0]
    tp_count = lax.axis_size("tp")
    block_rows = row_count * tp_count
    slot_total = block_rows * lax.axis_size("fsdp")
    longest = min(MAX_SPAN, slot_total // 2)
    reach_count = (longest - 2) // block_rows + 1
    window = (reach_count + 1) * block_rows
    front_rows = reach_count * block_rows
    block_index = lax.axis_index("fsdp")
    tp_index = lax.axis_index("tp")
    head_width = HEAD_DIM
    query_width = query_weight.shape[1]
    key_width = key_weight.shape[1]
    heads_here = query_width // head_width
    score_scale = head_width ** (-0.5)
    seq_count = lengths.shape[0]
    row_base = (block_index * tp_count + tp_index) * row_count
    my_slots = row_base + jnp.arange(row_count, dtype=jnp.int32)
    my_segments, my_positions = stream_layout(my_slots, lengths)
    valid_rows = (my_segments < seq_count)[:, None]
    gathered = (
        lax.all_gather(query_weight, "fsdp", axis=0, tiled=True),
        lax.all_gather(key_weight, "fsdp", axis=0, tiled=True),
        lax.all_gather(value_weight, "fsdp", axis=0, tiled=True),
        lax.all_gather(output_weight, "fsdp", axis=1, tiled=True),
        lax.all_gather(gate_weight, "fsdp", axis=0, tiled=True),
        lax.all_gather(up_weight, "fsdp", axis=0, tiled=True),
        lax.all_gather(down_weight, "fsdp", axis=1, tiled=True),
        lax.all_gather(attn_gain, "fsdp", axis=0, tiled=True),
        lax.all_gather(mlp_gain, "fsdp", axis=0, tiled=True),
    )
    (
        full_query,
        full_key,
        full_value,
        full_output,
        full_gate,
        full_up,
        full_down,
        gain_first,
        gain_second,
    ) = gathered
    w_inner = jnp.concatenate([full_query, full_key, full_value], axis=1)
    gain_first_wide = gain_first.astype(jnp.float32)
    gain_second_wide = gain_second.astype(jnp.float32)
    tokens_wide = tokens.astype(jnp.float32)
    inverse_first = lax.rsqrt(jnp.mean(tokens_wide * tokens_wide, axis=1, keepdims=True) + epsilon)
    normed_first = tokens_wide * inverse_first
    scaled_first = (normed_first * gain_first_wide).astype(jnp.bfloat16)
    rows_first = lax.all_gather(scaled_first, "tp", axis=0, tiled=True)
    projected = jnp.dot(rows_first, w_inner, preferred_element_type=jnp.float32)
    block_base = block_index * block_rows
    key_slots = block_base - front_rows + jnp.arange(window, dtype=jnp.int32)
    key_segments, key_positions = stream_layout(key_slots, lengths)
    query_segments = key_segments[front_rows:]
    block_positions = key_positions[front_rows:]
    cosine, sine_table = rotary_tables(block_positions, head_width)
    queries = rotate(
        projected[:, :query_width].reshape(block_rows, heads_here, head_width), cosine, sine_table
    ).astype(jnp.bfloat16)
    keys_local = rotate(
        projected[:, query_width : query_width + key_width].reshape(block_rows, 1, head_width),
        cosine,
        sine_table,
    )
    keys_local = keys_local.reshape(block_rows, head_width).astype(jnp.bfloat16)
    values_local = projected[:, query_width + key_width :].astype(jnp.bfloat16)
    pair_local = jnp.concatenate([keys_local, values_local], axis=1)
    pieces = []
    for offset in range(reach_count, 0, -1):
        pieces.append(passed_along(pair_local, "fsdp", offset))
    pair_window = jnp.concatenate(pieces + [pair_local], axis=0)
    key_window = pair_window[:, :head_width]
    value_window = pair_window[:, head_width:]
    key_seen = (key_segments[None, :] == query_segments[:, None]) & (
        key_positions[None, :] <= block_positions[:, None]
    )

    def head_scores(query_head):
        scores = outer_cols(query_head, key_window) * score_scale
        return jnp.where(key_seen, scores, -1e30)

    def head_forward(query_head):
        scores = head_scores(query_head)
        largest = jnp.max(scores, axis=1, keepdims=True)
        raised = jnp.exp(scores - largest)
        row_total = jnp.sum(raised, axis=1, keepdims=True)
        attn_probs = (raised / row_total).astype(jnp.bfloat16)
        head_out = jnp.dot(attn_probs, value_window, preferred_element_type=jnp.float32)
        return (head_out, (largest + jnp.log(row_total))[:, 0])

    query_heads = jnp.moveaxis(queries, 1, 0)
    head_outs, log_totals = lax.map(head_forward, query_heads)
    attended = jnp.moveaxis(head_outs, 0, 1).reshape(block_rows, query_width).astype(jnp.bfloat16)
    attn_share = lax.psum_scatter(
        jnp.dot(attended, full_output, preferred_element_type=jnp.float32).astype(jnp.bfloat16),
        "tp",
        scatter_dimension=0,
        tiled=True,
    ).astype(jnp.float32)
    middle = tokens_wide + attn_share
    inverse_second = lax.rsqrt(jnp.mean(middle * middle, axis=1, keepdims=True) + epsilon)
    normed_second = middle * inverse_second
    scaled_second = (normed_second * gain_second_wide).astype(jnp.bfloat16)
    rows_second = lax.all_gather(scaled_second, "tp", axis=0, tiled=True)
    gate_proj = jnp.dot(rows_second, full_gate, preferred_element_type=jnp.float32)
    up_proj = jnp.dot(rows_second, full_up, preferred_element_type=jnp.float32)
    gate_sigmoid = jax.nn.sigmoid(gate_proj)
    gate_active = gate_proj * gate_sigmoid
    hidden = (gate_active * up_proj).astype(jnp.bfloat16)
    mlp_share = lax.psum_scatter(
        jnp.dot(hidden, full_down, preferred_element_type=jnp.float32).astype(jnp.bfloat16),
        "tp",
        scatter_dimension=0,
        tiled=True,
    ).astype(jnp.float32)
    layer_out = jnp.where(valid_rows, middle + mlp_share, 0.0).astype(jnp.bfloat16)
    grad_rows = jnp.where(valid_rows, out_grad.astype(jnp.float32), 0.0)
    grad_low = grad_rows.astype(jnp.bfloat16)
    regathered = (
        lax.all_gather(query_weight, "fsdp", axis=0, tiled=True),
        lax.all_gather(key_weight, "fsdp", axis=0, tiled=True),
        lax.all_gather(value_weight, "fsdp", axis=0, tiled=True),
        lax.all_gather(output_weight, "fsdp", axis=1, tiled=True),
        lax.all_gather(gate_weight, "fsdp", axis=0, tiled=True),
        lax.all_gather(up_weight, "fsdp", axis=0, tiled=True),
        lax.all_gather(down_weight, "fsdp", axis=1, tiled=True),
        lax.all_gather(attn_gain, "fsdp", axis=0, tiled=True),
        lax.all_gather(mlp_gain, "fsdp", axis=0, tiled=True),
    )
    (
        full_query,
        full_key,
        full_value,
        full_output,
        full_gate,
        full_up,
        full_down,
        gain_first,
        gain_second,
    ) = regathered
    w_inner = jnp.concatenate([full_query, full_key, full_value], axis=1)
    grad_down_rows = lax.all_gather(grad_low, "tp", axis=0, tiled=True)
    grad_down_w = inner_rows(hidden, grad_down_rows)
    grad_hidden = outer_cols(grad_down_rows, full_down)
    grad_up_low = (grad_hidden * gate_active).astype(jnp.bfloat16)
    grad_gate_low = (
        grad_hidden * up_proj * gate_sigmoid * (1.0 + gate_proj * (1.0 - gate_sigmoid))
    ).astype(jnp.bfloat16)
    grad_gate_w = inner_rows(rows_second, grad_gate_low)
    grad_up_w = inner_rows(rows_second, grad_up_low)
    grad_second = lax.psum_scatter(
        (outer_cols(grad_gate_low, full_gate) + outer_cols(grad_up_low, full_up)).astype(
            jnp.bfloat16
        ),
        "tp",
        scatter_dimension=0,
        tiled=True,
    ).astype(jnp.float32)
    gain_second_part = jnp.sum(grad_second * normed_second, axis=0)
    grad_middle = grad_rows + norm_back(
        grad_second, gain_second_wide, normed_second, inverse_second
    )
    middle_low = grad_middle.astype(jnp.bfloat16)
    grad_attn_rows = lax.all_gather(middle_low, "tp", axis=0, tiled=True)
    grad_output_w = inner_rows(attended, grad_attn_rows)
    grad_attended = outer_cols(grad_attn_rows, full_output).astype(jnp.bfloat16)
    grad_heads = jnp.moveaxis(grad_attended.reshape(block_rows, heads_here, head_width), 1, 0)

    def head_backward(packed):
        query_head, grad_head, log_total = packed
        attn_probs = jnp.exp(head_scores(query_head) - log_total[:, None])
        probs_low = attn_probs.astype(jnp.bfloat16)
        grad_value_head = inner_rows(probs_low, grad_head)
        grad_probs = outer_cols(grad_head, value_window)
        grad_scores = (
            attn_probs * (grad_probs - jnp.sum(attn_probs * grad_probs, axis=1, keepdims=True))
        ).astype(jnp.bfloat16)
        grad_query_head = (
            jnp.dot(grad_scores, key_window, preferred_element_type=jnp.float32) * score_scale
        )
        grad_key_head = inner_rows(grad_scores, query_head) * score_scale
        return (grad_query_head, grad_key_head, grad_value_head)

    grad_query_heads, grad_key_heads, grad_value_heads = lax.map(
        head_backward, (query_heads, grad_heads, log_totals)
    )
    grad_pair = jnp.concatenate(
        [jnp.sum(grad_key_heads, axis=0), jnp.sum(grad_value_heads, axis=0)], axis=1
    )
    own_grad = grad_pair[front_rows:]
    for offset in range(1, reach_count + 1):
        piece_start = (reach_count - offset) * block_rows
        own_grad = own_grad + passed_along(
            grad_pair[piece_start : piece_start + block_rows].astype(jnp.bfloat16), "fsdp", -offset
        ).astype(jnp.float32)
    grad_key_lin = rotate_back(
        own_grad[:, :head_width].reshape(block_rows, 1, head_width), cosine, sine_table
    )
    grad_key_low = grad_key_lin.reshape(block_rows, head_width).astype(jnp.bfloat16)
    grad_value_low = own_grad[:, head_width:].astype(jnp.bfloat16)
    grad_query_lin = rotate_back(jnp.moveaxis(grad_query_heads, 0, 1), cosine, sine_table)
    grad_query_low = grad_query_lin.reshape(block_rows, query_width).astype(jnp.bfloat16)
    grad_inner = jnp.concatenate([grad_query_low, grad_key_low, grad_value_low], axis=1)
    grad_inner_w = inner_rows(rows_first, grad_inner)
    grad_first = lax.psum_scatter(
        outer_cols(grad_inner, w_inner).astype(jnp.bfloat16), "tp", scatter_dimension=0, tiled=True
    ).astype(jnp.float32)
    gain_first_part = jnp.sum(grad_first * normed_first, axis=0)
    tokens_grad = grad_middle + norm_back(grad_first, gain_first_wide, normed_first, inverse_first)
    reduced = (
        lax.psum_scatter(
            grad_inner_w[:, :query_width].astype(jnp.bfloat16),
            "fsdp",
            scatter_dimension=0,
            tiled=True,
        ).astype(jnp.float32),
        lax.psum_scatter(
            grad_inner_w[:, query_width : query_width + key_width].astype(jnp.bfloat16),
            "fsdp",
            scatter_dimension=0,
            tiled=True,
        ).astype(jnp.float32),
        lax.psum_scatter(
            grad_inner_w[:, query_width + key_width :].astype(jnp.bfloat16),
            "fsdp",
            scatter_dimension=0,
            tiled=True,
        ).astype(jnp.float32),
        lax.psum_scatter(
            grad_output_w.astype(jnp.bfloat16), "fsdp", scatter_dimension=1, tiled=True
        ).astype(jnp.float32),
        lax.psum_scatter(
            grad_gate_w.astype(jnp.bfloat16), "fsdp", scatter_dimension=0, tiled=True
        ).astype(jnp.float32),
        lax.psum_scatter(
            grad_up_w.astype(jnp.bfloat16), "fsdp", scatter_dimension=0, tiled=True
        ).astype(jnp.float32),
        lax.psum_scatter(
            grad_down_w.astype(jnp.bfloat16), "fsdp", scatter_dimension=1, tiled=True
        ).astype(jnp.float32),
        lax.psum_scatter(
            gain_first_part.astype(jnp.bfloat16), "fsdp", scatter_dimension=0, tiled=True
        ).astype(jnp.float32),
        lax.psum_scatter(
            gain_second_part.astype(jnp.bfloat16), "fsdp", scatter_dimension=0, tiled=True
        ).astype(jnp.float32),
    )
    gain_sums = lax.psum((reduced[7], reduced[8]), "tp")
    return (
        layer_out,
        tokens_grad,
        gain_sums[0],
        reduced[0],
        reduced[1],
        reduced[2],
        reduced[3],
        gain_sums[1],
        reduced[4],
        reduced[5],
        reduced[6],
    )


MESH = pl.DeviceIdType.MESH
CORE, ALONG_X, ALONG_Y = 1, 2, 4
PARTS = 4
VMEM_MOST = 60 << 20


def greet(partners):
    barrier = pltpu.get_barrier_semaphore()
    for partner in partners:
        pl.semaphore_signal(barrier, inc=1, device_id=partner, device_id_type=MESH)
    pl.semaphore_wait(barrier, len(partners))


def remote(source, target, sent, arrived, partner):
    return pltpu.make_async_remote_copy(
        src_ref=source,
        dst_ref=target,
        send_sem=sent,
        recv_sem=arrived,
        device_id=partner,
        device_id_type=MESH,
    )


def comm_params(number, vmem=None):
    return pltpu.CompilerParams(
        collective_id=number, has_side_effects=True, vmem_limit_bytes=vmem
    )


def lasting(microseconds):
    return pl.CostEstimate(
        flops=int(microseconds * 1.1e9), bytes_accessed=1_000_000, transcendentals=0
    )


ANYWHERE = pl.BlockSpec(memory_space=pl.ANY)
IN_VMEM = pl.BlockSpec(memory_space=pltpu.VMEM)


def columns(index, width):
    return pl.ds(pl.multiple_of(index * width, width), width)


class PlaneGather:
    def __init__(self, store, sent, arrived):
        self.f, self.t = lax.axis_index("fsdp"), lax.axis_index("tp")
        self.store, self.sent, self.arrived = store, sent, arrived
        self.piece = store.shape[1] // PARTS
        self.near = [(self.f ^ k, self.t) for k in (CORE, ALONG_X, ALONG_Y)]
        self.copies, self.on = [], {}

    def send(self, owner, j, way, slot):
        place = self.store.at[owner, pl.ds(j * self.piece, self.piece)]
        c = remote(
            place, place, self.sent.at[slot, j], self.arrived.at[slot, j], self.near[way]
        )
        c.start()
        self.copies.append(c)
        self.on[slot, j] = c

    def begin(self):
        for k in range(PARTS):
            self.send(self.f, k, 1, 1)
            self.send(self.f, (k + PARTS // 2) % PARTS, 2, 2)
        for k in range(PARTS):
            self.send(self.f, k, 0, 0)

    def arrive(self, slot, j):
        self.on[slot, j].wait_recv()

    def advance(self, k):
        jx, jy = k, (k + PARTS // 2) % PARTS
        self.arrive(1, jx)
        if jx < PARTS // 2:
            self.send(self.f ^ ALONG_X, jx, 2, 6)
        self.send(self.f ^ ALONG_X, jx, 0, 3)
        self.arrive(2, jy)
        if jy >= PARTS // 2:
            self.send(self.f ^ ALONG_Y, jy, 1, 6)
        self.send(self.f ^ ALONG_Y, jy, 0, 4)

    def far(self):
        for k in range(PARTS // 2):
            for j in (k, k + PARTS // 2):
                self.arrive(6, j)
                self.send(self.f ^ ALONG_X ^ ALONG_Y, j, 0, 5)

    def wait_core(self, *slots):
        for slot in slots:
            for j in range(PARTS):
                self.arrive(slot, j)

    def finish(self):
        for c in self.copies:
            c.wait_send()


GATHER_SEMAPHORES = [pltpu.SemaphoreType.DMA((7, PARTS)), pltpu.SemaphoreType.DMA((7, PARTS))]


class PlaneSum:
    masks = (ALONG_X ^ ALONG_Y, ALONG_X, ALONG_Y, 0)

    def __init__(self, stage, other, held, from_x, from_y, last, sent, arrived):
        self.f, self.t = lax.axis_index("fsdp"), lax.axis_index("tp")
        self.stage, self.other, self.held = stage, other, held
        self.from_x, self.from_y, self.last = from_x, from_y, last
        self.sent, self.arrived = sent, arrived
        self.near = [(self.f ^ k, self.t) for k in (CORE, ALONG_X, ALONG_Y)]
        self.copies, self.on = [], {}
        half = held.shape[1] // 2
        self.top, self.low = pl.ds(0, half), pl.ds(half, half)

    def send(self, source, target, slot, way):
        c = remote(source, target, self.sent.at[slot], self.arrived.at[slot], self.near[way])
        c.start()
        self.copies.append(c)
        self.on[slot] = c

    def begin(self, write_part, after=None):
        for i, mask in enumerate(self.masks):
            if i >= 2:
                self.on[i - 2].wait_send()
                self.copies = [c for c in self.copies if c is not self.on[i - 2]]
            write_part(self.f ^ CORE ^ mask, self.stage.at[i % 2])
            self.send(self.stage.at[i % 2], self.other.at[i], i, 0)
            write_part(self.f ^ mask, self.held.at[i])
            if after is not None:
                after(i)
            self.on[i].wait_recv()
            self.held[i] = (
                self.held[i].astype(jnp.float32) + self.other[i].astype(jnp.float32)
            ).astype(jnp.bfloat16)
            if i == 0:
                self.send(self.held.at[0, self.top], self.from_x.at[0], 4, 1)
                self.send(self.held.at[0, self.low], self.from_y.at[0], 5, 2)
            if i == 1:
                self.send(self.held.at[1, self.top], self.from_x.at[1], 6, 1)
            if i == 2:
                self.send(self.held.at[2, self.low], self.from_y.at[1], 7, 2)

    def turn(self):
        self.on[4].wait_recv()
        self.held[2, self.top] = (
            self.held[2, self.top].astype(jnp.float32) + self.from_x[0].astype(jnp.float32)
        ).astype(jnp.bfloat16)
        self.send(self.held.at[2, self.top], self.last.at[0], 8, 2)
        self.on[5].wait_recv()
        self.held[1, self.low] = (
            self.held[1, self.low].astype(jnp.float32) + self.from_y[0].astype(jnp.float32)
        ).astype(jnp.bfloat16)
        self.send(self.held.at[1, self.low], self.last.at[1], 9, 1)

    def end(self, total):
        for rows, first, second, take in (
            (self.top, 6, 8, lambda: self.from_x[1]),
            (self.low, 7, 9, lambda: self.from_y[1]),
        ):
            self.on[first].wait_recv()
            part = self.held[3, rows].astype(jnp.float32) + take().astype(jnp.float32)
            self.on[second].wait_recv()
            total[rows] = part + self.last[second - 8].astype(jnp.float32)

    def finish(self):
        for c in self.copies:
            c.wait_send()


def sum_scratch(height, width):
    chunks = [pltpu.VMEM((n, height, width), jnp.bfloat16) for n in (2, 4, 4)]
    return chunks + [pltpu.VMEM((2, height // 2, width), jnp.bfloat16)] * 3 + [pltpu.SemaphoreType.DMA((10,)), pltpu.SemaphoreType.DMA((10,))]


NARROW = 512


def chunk_part(pairs, size):
    def write_part(owner, ref):
        lanes = columns(owner, size)
        lefts = [left[:, lanes] for left, _ in pairs]

        def step(n, carry):
            wide = columns(n, NARROW)
            total = inner_rows(lefts[0], pairs[0][1][:, wide])
            for left, (_, right) in zip(lefts[1:], pairs[1:]):
                total += inner_rows(left, right[:, wide])
            ref[:, wide] = total.astype(jnp.bfloat16)
            return carry

        lax.fori_loop(0, ref.shape[1] // NARROW, step, 0)

    return write_part


def plane_greet():
    f, t = lax.axis_index("fsdp"), lax.axis_index("tp")
    greet([(f ^ k, t) for k in (CORE, ALONG_X, ALONG_Y)])


def forward_output(attended, output_rows, tokens, gain, dys, down_all, number):
    size, width = tokens.shape
    units = down_all.shape[2]
    f32, bf16 = jnp.float32, jnp.bfloat16

    def kernel(
        o_ref, x_ref, gain_ref, w_hbm, dys_hbm, down_hbm,
        middle_ref, row_ref, dh_ref,
        stage, other, held, from_x, from_y, last, sum_sent, sum_arrived,
        dys, down_w, dys_sem, load_sem, dh, dh_sem, w, w_sem,
    ):
        load = pltpu.make_async_copy(dys_hbm, dys, dys_sem)
        loads = unit_loads(lambda j: down_hbm.at[:, j], down_w, load_sem)
        output_loads = column_loads(w_hbm, w, w_sem)
        for c in output_loads + loads + [load]:
            c.start()
        plane_greet()
        for c in output_loads:
            c.wait()
        total = PlaneSum(stage, other, held, from_x, from_y, last, sum_sent, sum_arrived)
        total.begin(chunk_part([(o_ref, w)], size))
        for c in loads + [load]:
            c.wait()

        def out_copy(i):
            return pltpu.make_async_copy(dh.at[i], dh_ref.at[i], dh_sem.at[i])

        def grad_chunk(i, carry):
            dh[i] = outer_cols(as_rows(down_w), dys[i])
            out_copy(i).start()
            return carry

        lax.fori_loop(0, 6, grad_chunk, 0)
        total.turn()
        lax.fori_loop(6, 8, grad_chunk, 0)
        total.end(middle_ref)
        middle = x_ref[...].astype(f32) + middle_ref[...]
        middle_ref[...] = middle
        inverse = lax.rsqrt(jnp.mean(middle * middle, axis=1, keepdims=True) + epsilon)
        row_ref[...] = (middle * inverse * gain_ref[...]).astype(bf16)
        for i in range(8):
            out_copy(i).wait()
        total.finish()

    dma = pltpu.SemaphoreType.DMA
    chunks = (8, 4 * units, size)
    return pl.pallas_call(
        kernel,
        out_shape=[
            jax.ShapeDtypeStruct((size, width), f32),
            jax.ShapeDtypeStruct((size, width), bf16),
            jax.ShapeDtypeStruct(chunks, f32),
        ],
        in_specs=[IN_VMEM] * 3 + [ANYWHERE] * 3,
        out_specs=[IN_VMEM] * 2 + [ANYWHERE],
        scratch_shapes=sum_scratch(size, width)
        + [
            pltpu.VMEM((8, size, width), bf16),
            pltpu.VMEM((4, units, width), bf16),
            dma,
            dma((8,)),
            pltpu.VMEM(chunks, f32),
            dma((8,)),
            pltpu.VMEM((attended.shape[0], width), bf16),
            dma((8,)),
        ],
        compiler_params=comm_params(number, VMEM_MOST),
        cost_estimate=lasting(45),
        name="forward_output",
    )(attended, tokens, gain, output_rows, dys, down_all)


def forward_hidden(row, dys, dh_all, gate_up, number):
    size, width = row.shape
    quarter = gate_up.shape[3]
    units = 4 * quarter
    f32, bf16 = jnp.float32, jnp.bfloat16

    def kernel(
        row_ref, dys_hbm, dh_hbm, gate_up_hbm,
        rows_ref, hidden_ref, dgate_ref, dup_ref, down_grad_ref,
        rows, rows_sent, rows_arrived, dys, gate_w, up_w, load_sem, unit_sem, dh, out, out_sem, keep_sem, down_grad,
    ):
        f = lax.axis_index("fsdp")
        loads = [
            pltpu.make_async_copy(source, target, load_sem.at[i])
            for i, (source, target) in enumerate(((dys_hbm, dys), (dh_hbm, dh)))
        ]
        for i, w in enumerate((gate_w, up_w)):
            loads += unit_loads(lambda j, i=i: gate_up_hbm.at[:, j, i], w, unit_sem.at[i])
        for load in loads:
            load.start()
        rows[f] = row_ref[...]
        plane_greet()
        gather_rows = PlaneGather(rows, rows_sent, rows_arrived)
        gather_rows.begin()
        for load in loads:
            load.wait()

        half = size // 2
        halves = (slice(0, half), slice(half, size))

        def owners(i, crossed):
            return f ^ i, f ^ (i ^ ALONG_X ^ ALONG_Y if crossed else i)

        def out_copies(slot, pair):
            return [
                pltpu.make_async_copy(
                    out.at[slot, n, :, lanes],
                    target.at[
                        :, pl.ds(pl.multiple_of(owner * size + side * half, half), half)
                    ],
                    out_sem.at[slot, n, side],
                )
                for n, target in enumerate((hidden_ref, dgate_ref, dup_ref))
                for side, (owner, lanes) in enumerate(zip(pair, halves))
            ]

        def unit(crossed):
            def body(i, carry):
                pair = owners(i, crossed)
                slot = lax.rem(i, 2)

                @pl.when(i >= 2)
                def _():
                    for c in out_copies(slot, pair):
                        c.wait()

                right = jnp.concatenate([rows[o, r] for o, r in zip(pair, halves)], axis=0)
                gate = outer_cols(as_rows(gate_w), right)
                up = outer_cols(as_rows(up_w), right)
                sigmoid = jax.nn.sigmoid(gate)
                active = gate * sigmoid
                grad = jnp.concatenate([dh[o, :, r] for o, r in zip(pair, halves)], axis=1)
                hidden = (active * up).astype(bf16)
                out[slot, 0] = hidden
                out[slot, 1] = (grad * up * sigmoid * (1.0 + gate * (1.0 - sigmoid))).astype(bf16)
                out[slot, 2] = (grad * active).astype(bf16)
                for c in out_copies(slot, pair):
                    c.start()
                cotangent = jnp.concatenate([dys[o, r] for o, r in zip(pair, halves)], axis=0)
                down_grad[...] += dot_nn(hidden, cotangent)
                return carry

            return body

        def take(*pieces):
            for slot, j in pieces:
                gather_rows.arrive(slot, j)

        down_grad[...] = jnp.zeros_like(down_grad)
        gather_rows.advance(0)
        lax.fori_loop(0, 1, unit(False), 0)
        gather_rows.advance(1)
        gather_rows.wait_core(0)
        lax.fori_loop(1, 2, unit(False), 0)
        lax.fori_loop(2, 3, unit(True), 0)
        gather_rows.advance(2)
        take((3, 0), (3, 1), (4, 2), (4, 3))
        lax.fori_loop(3, 4, unit(True), 0)
        gather_rows.advance(3)
        lax.fori_loop(4, 5, unit(True), 0)
        take((3, 2), (3, 3), (4, 0), (4, 1))
        lax.fori_loop(5, 6, unit(True), 0)
        gather_rows.far()
        lax.fori_loop(6, 7, unit(False), 0)
        gather_rows.wait_core(5)
        keep = pltpu.make_async_copy(rows, rows_ref, keep_sem)
        keep.start()
        lax.fori_loop(7, 8, unit(False), 0)
        for j in range(8):
            part = down_grad[:, j * size : (j + 1) * size].astype(bf16)
            down_grad_ref[:, j] = part.reshape(4, quarter, size)
        for i in (6, 7):
            for c in out_copies(i % 2, owners(i, False)):
                c.wait()
        keep.wait()
        gather_rows.finish()

    store = pltpu.VMEM((8, size, width), bf16)
    weights = pltpu.VMEM((4, quarter, width), bf16)
    return pl.pallas_call(
        kernel,
        out_shape=[jax.ShapeDtypeStruct((8, size, width), bf16)]
        + [jax.ShapeDtypeStruct((units, 8 * size), bf16)] * 3
        + [jax.ShapeDtypeStruct((4, 8, quarter, size), bf16)],
        in_specs=[IN_VMEM] + [ANYWHERE] * 3,
        out_specs=[ANYWHERE] * 4 + [IN_VMEM],
        scratch_shapes=[store]
        + GATHER_SEMAPHORES
        + [store]
        + [weights] * 2
        + [
            pltpu.SemaphoreType.DMA((2,)),
            pltpu.SemaphoreType.DMA((2, 8)),
            pltpu.VMEM((8, units, size), f32),
            pltpu.VMEM((2, 3, units, size), bf16),
            pltpu.SemaphoreType.DMA((2, 3, 2)),
            pltpu.SemaphoreType.DMA,
            pltpu.VMEM((units, width), f32),
        ],
        compiler_params=comm_params(number, VMEM_MOST),
        cost_estimate=lasting(50),
        name="forward_hidden",
    )(row, dys, dh_all, gate_up)


def backward_middle(
    dgate, dup, gate_up, rows, dys, output_rows, attended, middle, gain, number
):
    size, width = middle.shape
    quarter = gate_up.shape[3]
    units = 4 * quarter
    depth = output_rows.shape[1]
    blocks = width // size
    f32, bf16 = jnp.float32, jnp.bfloat16
    early = 5

    def kernel(
        dgate_hbm, dup_hbm, gate_up_hbm, rows_hbm,
        dys_hbm, w_hbm, o_ref, middle_ref, gain_ref,
        grad_ref, gain_grad_ref, grad_o_ref, do_ref, gate_g_ref, up_g_ref,
        stage, other, held, from_x, from_y, last, sum_sent, sum_arrived,
        store, store_sent, store_arrived,
        dgate_v, dup_v, gate_w, up_w, load_sem, unit_sem,
        tall, tall_sem, out, out_sem, o_sum, dy, dy_sem, w_ref, w_sem,
    ):
        f = lax.axis_index("fsdp")
        loads = [
            pltpu.make_async_copy(source, target, load_sem.at[i])
            for i, (source, target) in enumerate(((dgate_hbm, dgate_v), (dup_hbm, dup_v)))
        ]
        for i, w in enumerate((gate_w, up_w)):
            loads += unit_loads(lambda j, i=i: gate_up_hbm.at[:, j, i], w, unit_sem.at[i])
        for load in loads:
            load.start()

        load_dy = pltpu.make_async_copy(dys_hbm.at[f], dy, dy_sem)
        load_dy.start()
        output_loads = column_loads(w_hbm, w_ref, w_sem)
        for c in output_loads:
            c.start()

        def tall_load(n, slot):
            return pltpu.make_async_copy(
                rows_hbm.at[:, :, columns(n, size)], tall.at[slot], tall_sem.at[slot]
            )

        tall_load(0, 0).start()
        plane_greet()
        total = PlaneSum(stage, other, held, from_x, from_y, last, sum_sent, sum_arrived)
        gather = PlaneGather(store, store_sent, store_arrived)
        for load in loads:
            load.wait()
        total.begin(chunk_part([(dgate_v, Rows(gate_w)), (dup_v, Rows(up_w))], size))
        total.turn()

        def out_copies(n, slot):
            return [
                pltpu.make_async_copy(
                    out.at[slot, i], target.at[:, n], out_sem.at[slot, i]
                )
                for i, target in enumerate((gate_g_ref, up_g_ref))
            ]

        def block(n, carry):
            slot = lax.rem(n, 2)

            @pl.when(n + 1 < blocks)
            def _():
                tall_load(n + 1, 1 - slot).start()

            tall_load(n, slot).wait()

            @pl.when(n >= 2)
            def _():
                for c in out_copies(n, slot):
                    c.wait()

            row_cols = tall[slot].reshape(8 * size, size)
            for i, left in enumerate((dgate_v, dup_v)):
                out[slot, i] = dot_nn(left[...], row_cols).astype(bf16).reshape(4, quarter, size)
            for c in out_copies(n, slot):
                c.start()
            return carry

        lax.fori_loop(0, early, block, 0)
        total.end(grad_ref)
        middle = middle_ref[...]
        inverse = lax.rsqrt(jnp.mean(middle * middle, axis=1, keepdims=True) + epsilon)
        normed = middle * inverse
        grad = grad_ref[...]
        gain_grad_ref[...] = jnp.sum(grad * normed, axis=0, keepdims=True)
        load_dy.wait()
        for c in output_loads:
            c.wait()
        grad = dy[...].astype(f32) + norm_back(grad, gain_ref[...], normed, inverse)
        grad_ref[...] = grad
        store[f] = grad.astype(bf16)
        gather.begin()
        gather.advance(0)
        lax.fori_loop(early, early + 1, block, 0)
        gather.advance(1)
        lax.fori_loop(early + 1, early + 2, block, 0)
        gather.advance(2)
        lax.fori_loop(early + 2, blocks, block, 0)
        gather.advance(3)

        def chunk(i, carry):
            owner = f ^ i
            lanes = columns(owner, size)
            do_ref[:, lanes] = outer_cols(w_ref[...], store[owner]).astype(bf16)
            o_sum[...] += dot_nn(o_ref[:, lanes], store[owner])
            return carry

        o_sum[...] = jnp.zeros_like(o_sum)
        gather.wait_core(0)
        lax.fori_loop(0, 2, chunk, 0)
        gather.wait_core(3, 4)
        lax.fori_loop(2, 6, chunk, 0)
        gather.far()
        gather.wait_core(5)
        lax.fori_loop(6, 8, chunk, 0)
        for j in range(8):
            grad_o_ref[j] = o_sum[:, j * size : (j + 1) * size].astype(bf16)
        for n in (blocks - 2, blocks - 1):
            for c in out_copies(n, n % 2):
                c.wait()
        total.finish()
        gather.finish()

    tall_units = pltpu.VMEM((units, width), bf16)
    weights = pltpu.VMEM((4, quarter, width), bf16)
    return pl.pallas_call(
        kernel,
        out_shape=[
            jax.ShapeDtypeStruct((size, width), f32),
            jax.ShapeDtypeStruct((1, width), f32),
            jax.ShapeDtypeStruct((8, depth, size), bf16),
            jax.ShapeDtypeStruct((depth, 8 * size), bf16),
        ]
        + [jax.ShapeDtypeStruct((4, blocks, quarter, size), bf16)] * 2,
        in_specs=[ANYWHERE] * 6 + [IN_VMEM] * 3,
        out_specs=[IN_VMEM] * 4 + [ANYWHERE] * 2,
        scratch_shapes=sum_scratch(size, width)
        + [pltpu.VMEM((8, size, width), bf16)]
        + GATHER_SEMAPHORES
        + [tall_units] * 2
        + [weights] * 2
        + [
            pltpu.SemaphoreType.DMA((2,)),
            pltpu.SemaphoreType.DMA((2, 8)),
            pltpu.VMEM((2, 8, size, size), bf16),
            pltpu.SemaphoreType.DMA((2,)),
            pltpu.VMEM((2, 2, 4, quarter, size), bf16),
            pltpu.SemaphoreType.DMA((2, 2)),
            pltpu.VMEM((depth, width), f32),
            pltpu.VMEM((size, width), bf16),
            pltpu.SemaphoreType.DMA,
            pltpu.VMEM((depth, width), bf16),
            pltpu.SemaphoreType.DMA((8,)),
        ],
        compiler_params=comm_params(number, VMEM_MOST),
        cost_estimate=lasting(92),
        name="backward_middle",
    )(dgate, dup, gate_up, rows, dys, output_rows, attended, middle, gain)


class LineGather:
    def __init__(self, own, store, sent, arrived):
        self.f, self.t = lax.axis_index("fsdp"), lax.axis_index("tp")
        self.own, self.store, self.sent, self.arrived = own, store, sent, arrived

    def copy(self, way, hop):
        step = 1 if way == 0 else -1
        place = self.store.at[self.t - step * (hop - 1)]
        source = self.own if hop == 1 else place
        return remote(
            source, place, self.sent.at[way, hop], self.arrived.at[way, hop], (self.f, self.t + step)
        )

    def goes(self, way, hop):
        if way == 0:
            return (self.t < 3) & (self.t >= hop - 1)
        return (self.t > 0) & (self.t <= 4 - hop)

    def came(self, way, hop):
        return self.t >= hop if way == 0 else self.t <= 3 - hop

    def send(self, hop):
        for way in (0, 1):
            pl.when(self.goes(way, hop))(lambda way=way: self.copy(way, hop).start())

    def begin(self):
        self.send(1)

    def take(self, hop):
        for way in (0, 1):

            @pl.when(self.came(way, hop))
            def _(way=way):
                spot = self.store.at[self.t - hop if way == 0 else self.t + hop]
                remote(
                    spot, spot, self.sent.at[way, hop], self.arrived.at[way, hop], (self.f, self.t)
                ).wait_recv()

        if hop < 3:
            self.send(hop + 1)

    def finish(self):
        for hop in (1, 2, 3):
            for way in (0, 1):
                pl.when(self.goes(way, hop))(lambda way=way, hop=hop: self.copy(way, hop).wait_send())


LINE_SEMAPHORES = [pltpu.SemaphoreType.DMA((2, 4)), pltpu.SemaphoreType.DMA((2, 4))]


def everyone(f, t):
    return [(f ^ k, t) for k in range(1, 8)] + [(f, lax.rem(t + k, 4)) for k in (1, 2, 3)]


def unit_loads(source, target, sems):
    block = target.shape[2] // 8
    return [
        pltpu.make_async_copy(source(j), target.at[:, :, pl.ds(j * block, block)], sems.at[j])
        for j in range(8)
    ]


class Rows:
    def __init__(self, ref):
        self.ref = ref

    def __getitem__(self, index):
        block = self.ref[:, :, index[1]]
        return block.reshape(4 * block.shape[1], block.shape[2])


def column_loads(source, target, sems):
    block = source.shape[2]
    return [
        pltpu.make_async_copy(source.at[j], target.at[:, pl.ds(j * block, block)], sems.at[j])
        for j in range(8)
    ]


def as_rows(ref):
    return ref[...].reshape(4 * ref.shape[1], ref.shape[2])


def turn_heads(values, cosine, sine_table):
    half = HEAD_DIM // 2
    turned = []
    for h in range(values.shape[0] // HEAD_DIM):
        first = values[h * HEAD_DIM : h * HEAD_DIM + half]
        second = values[h * HEAD_DIM + half : (h + 1) * HEAD_DIM]
        turned.append(first * cosine - second * sine_table)
        turned.append(second * cosine + first * sine_table)
    return jnp.concatenate(turned, axis=0)


def first_forms(gate, up, query, key_rows, value_rows):
    bf16, f32 = jnp.bfloat16, jnp.float32
    block, hidden = gate.shape
    across = query.shape[1]
    units = hidden // 8

    def turned(ref):
        return ref[...].astype(f32).T.astype(bf16)

    def kernel(gate_ref, up_ref, q_ref, k_ref, v_ref, units_ref, inner_ref):
        inner_ref[:across] = turned(q_ref)
        inner_ref[across : across + HEAD_DIM] = k_ref[...]
        inner_ref[across + HEAD_DIM :] = v_ref[...]
        units_ref[:, 0] = turned(gate_ref).reshape(8, units, block)
        units_ref[:, 1] = turned(up_ref).reshape(8, units, block)

    return pl.pallas_call(
        kernel,
        out_shape=[
            jax.ShapeDtypeStruct((8, 2, units, block), bf16),
            jax.ShapeDtypeStruct((across + 2 * HEAD_DIM, block), bf16),
        ],
        in_specs=[IN_VMEM] * 5,
        out_specs=[IN_VMEM] * 2,
        compiler_params=pltpu.CompilerParams(vmem_limit_bytes=VMEM_MOST),
        cost_estimate=lasting(5),
        name="first_forms",
    )(gate, up, query, key_rows, value_rows)


def first_rows(tokens, gains_own, inner_all, output_own, cosine, sine_table, grads, valid, number):
    size, width = tokens.shape
    block = width // 8
    quarter_rows = output_own.shape[0]
    depth = quarter_rows // 2
    pair_rows = 2 * HEAD_DIM
    f32, bf16 = jnp.float32, jnp.bfloat16

    def kernel(
        x_ref, gains_own_ref, inner_ref, own_ref, cos_ref, sin_ref, dy_ref, valid_ref,
        rows_ref, q_ref, pair_ref, w_ref, wo_all, dys_ref, gains_ref,
        rows, rows_sent, rows_arrived, dys, dys_sent, dys_arrived, pair_v,
        w_sent, w_arrived, z_sent, z_arrived,
        p_sent, p_arrived, on_sent, on_arrived, g_sent, g_arrived, kept_sem,
    ):
        f, t = lax.axis_index("fsdp"), lax.axis_index("tp")
        gains_ref[f] = gains_own_ref[...]
        place = columns(f, block)
        far_first = (6, 7, 2, 4, 3, 5, 1)

        def inner_slices(j):
            quarter, side = lax.div(j, 2), lax.rem(j, 2)
            return [
                (
                    inner_ref.at[quarter, pl.ds(pl.multiple_of(side * depth, depth), depth)],
                    w_ref.at[pl.ds(0, depth), place],
                ),
                (
                    inner_ref.at[quarter, pl.ds(2 * depth, pair_rows)],
                    w_ref.at[pl.ds(depth, pair_rows), place],
                ),
            ]

        kept = [
            pltpu.make_async_copy(s, o, kept_sem.at[i]) for i, (s, o) in enumerate(inner_slices(f))
        ]
        kept.append(pltpu.make_async_copy(own_ref, wo_all.at[t], kept_sem.at[2]))
        for c in kept:
            c.start()
        greet(everyone(f, t))
        line_output = LineGather(own_ref, wo_all, z_sent, z_arrived)
        line_output.begin()
        weights, gains = [], []
        for k in far_first:
            c = remote(
                gains_own_ref, gains_ref.at[f], g_sent.at[k], g_arrived.at[k], (f ^ k, t)
            )
            c.start()
            gains.append(c)
        for k in far_first:
            for i, (s, o) in enumerate(inner_slices(f ^ k)):
                c = remote(s, o, w_sent.at[k, i], w_arrived.at[k, i], (f ^ k, t))
                c.start()
                weights.append(c)
        wide = x_ref[...].astype(f32)
        inverse = lax.rsqrt(jnp.mean(wide * wide, axis=1, keepdims=True) + epsilon)
        for c in gains:
            c.wait()
        gain = jnp.concatenate([gains_ref[j, 0:1] for j in range(8)], axis=1)
        rows[f] = (wide * inverse * gain).astype(bf16)
        gather = PlaneGather(rows, rows_sent, rows_arrived)
        gather.begin()
        dys[f] = jnp.where(valid_ref[...] > 0, dy_ref[...].astype(f32), 0.0).astype(bf16)
        for k in range(PARTS):
            gather.advance(k)
            if k in (2, 3):
                line_output.take(k - 1)
        gather_dys = PlaneGather(dys, dys_sent, dys_arrived)
        gather_dys.begin()
        for c in kept[:2]:
            c.wait()
        for c in weights:
            c.wait_recv()

        def chunk(i, carry):
            owner = f ^ i
            lanes = columns(owner, size)
            projected = outer_cols(w_ref[...], rows[owner])
            cosine, sine = cos_ref[:, lanes], sin_ref[:, lanes]
            queries = turn_heads(projected[:depth], cosine, sine).astype(bf16)
            q_ref[:, lanes] = (queries.astype(f32) * HEAD_DIM ** (-0.5)).astype(bf16)
            keys = turn_heads(projected[depth : depth + HEAD_DIM], cosine, sine)
            pair = jnp.concatenate([keys, projected[depth + HEAD_DIM :]], axis=0)
            pair_v[owner] = pair.T.astype(bf16)
            return carry

        spread = []

        def spread_pair(i):
            for k in (2, 1, 3):
                c = remote(
                    pair_v.at[f ^ i],
                    pair_ref.at[t, f ^ i],
                    p_sent.at[i // 2, k],
                    p_arrived.at[i // 2, k],
                    (f, lax.rem(t + k, 4)),
                )
                c.start()
                spread.append((i, k, c))

        gather.wait_core(0)
        lax.fori_loop(0, 2, chunk, 0)
        spread_pair(0)
        gather.wait_core(3, 4)
        lax.fori_loop(2, 6, chunk, 0)
        spread_pair(2)
        spread_pair(4)
        gather.far()
        gather.wait_core(5)
        lax.fori_loop(6, 8, chunk, 0)
        spread_pair(6)
        own_pair = pltpu.make_async_copy(pair_v, pair_ref.at[t], kept_sem.at[3])
        own_pair.start()
        keep_rows = pltpu.make_async_copy(rows, rows_ref, kept_sem.at[4])
        keep_rows.start()
        for k in range(PARTS):
            gather_dys.advance(k)
        passed = []
        for i, k, c in spread:
            c.wait_recv()
            spot = pair_ref.at[lax.rem(t + 4 - k, 4), f ^ i]
            d = remote(spot, spot, on_sent.at[i // 2, k], on_arrived.at[i // 2, k], (f ^ CORE, t))
            d.start()
            passed.append(d)
        gather_dys.wait_core(0, 3, 4)
        gather_dys.far()
        gather_dys.wait_core(5)
        keep_dys = pltpu.make_async_copy(dys, dys_ref, kept_sem.at[6])
        keep_dys.start()
        line_output.take(3)
        for c in passed:
            c.wait()
        for c in weights + [c for _, _, c in spread]:
            c.wait_send()
        line_output.finish()
        gather.finish()
        gather_dys.finish()
        own_pair.wait()
        keep_rows.wait()
        kept[2].wait()
        keep_dys.wait()

    dma = pltpu.SemaphoreType.DMA
    return pl.pallas_call(
        kernel,
        out_shape=[
            jax.ShapeDtypeStruct((8, size, width), bf16),
            jax.ShapeDtypeStruct((depth, 8 * size), bf16),
            jax.ShapeDtypeStruct((4, 8, size, pair_rows), bf16),
            jax.ShapeDtypeStruct((depth + pair_rows, width), bf16),
            jax.ShapeDtypeStruct((4, quarter_rows, block), bf16),
            jax.ShapeDtypeStruct((8, size, width), bf16),
            jax.ShapeDtypeStruct((8, *gains_own.shape), f32),
        ],
        in_specs=[IN_VMEM, IN_VMEM, ANYWHERE, ANYWHERE] + [IN_VMEM] * 4,
        out_specs=[ANYWHERE, IN_VMEM, ANYWHERE, IN_VMEM, ANYWHERE, ANYWHERE, IN_VMEM],
        scratch_shapes=[pltpu.VMEM((8, size, width), bf16)]
        + GATHER_SEMAPHORES
        + [pltpu.VMEM((8, size, width), bf16)]
        + GATHER_SEMAPHORES
        + [
            pltpu.VMEM((8, size, pair_rows), bf16),
            dma((8, 2)),
            dma((8, 2)),
            *LINE_SEMAPHORES,
            dma((4, 4)),
            dma((4, 4)),
            dma((4, 4)),
            dma((4, 4)),
            dma((8,)),
            dma((8,)),
            dma((7,)),
        ],
        compiler_params=comm_params(number, VMEM_MOST),
        cost_estimate=lasting(100),
        name="first_rows",
    )(tokens, gains_own, inner_all, output_own, cosine, sine_table, grads, valid)


def grads_across(left_ref, rows_v, out_v, target_ref, sent, arrived, kept_sem):
    f, t = lax.axis_index("fsdp"), lax.axis_index("tp")
    _, size, width = rows_v.shape
    block = width // 8
    copies = []

    def step(k):
        right = rows_v[:, :, columns(f ^ k, block)].reshape(8 * size, block)
        out_v[k] = dot_nn(left_ref[...], right).astype(jnp.bfloat16)
        if k:
            c = remote(out_v.at[k], target_ref.at[f], sent.at[k], arrived.at[k], (f ^ k, t))
        else:
            c = pltpu.make_async_copy(out_v.at[0], target_ref.at[f], kept_sem)
        c.start()
        copies.append(c)

    return step, copies


def exchange_begin(ways, sent, arrived, kept_sem):
    f, t = lax.axis_index("fsdp"), lax.axis_index("tp")
    copies = []
    for i, (source, target) in enumerate(ways):
        for k in (6, 7, 2, 4, 3, 5, 1):
            copies.append(
                remote(
                    source.at[f ^ k], target.at[f], sent.at[k, i], arrived.at[k, i], (f ^ k, t)
                )
            )
        copies.append(pltpu.make_async_copy(source.at[f], target.at[f], kept_sem.at[i]))
    for c in copies:
        c.start()
    return copies


def backward_pairs(pair_parts, hidden, down_all, middle, valid, grad_query, rows, cosine, sine_table, number):
    size, width = middle.shape
    units = hidden.shape[0]
    depth = grad_query.shape[0]
    _, chunks, height, _ = pair_parts.shape
    half = chunks // 2
    f32, bf16 = jnp.float32, jnp.bfloat16

    def kernel(
        p_ref, hidden_hbm, down_hbm, middle_ref, valid_ref, g_ref, rows_hbm, cos_ref, sin_ref,
        single_ref, out_ref, spread_ref,
        stage, other, held, from_x, from_y, last, sum_sent, sum_arrived,
        hidden_v, down_w, load_sem, unit_sem, ra, s, rz, sent, arrived, share, pair,
        rows_v, w_grad, w_sent, w_arrived,
    ):
        f, t = lax.axis_index("fsdp"), lax.axis_index("tp")
        loads = [pltpu.make_async_copy(hidden_hbm, hidden_v, load_sem.at[0])]
        loads += unit_loads(lambda j: down_hbm.at[:, j], down_w, unit_sem)
        load_rows = pltpu.make_async_copy(rows_hbm, rows_v, load_sem.at[1])
        for c in loads + [load_rows]:
            c.start()
        side = lax.rem(f, 2)
        mine, theirs = pl.ds(side * half, half), pl.ds((1 - side) * half, half)
        core = (f ^ CORE, t)
        greet(everyone(f, t))
        first = []
        for k in (2, 1, 3, 0):
            plane = lax.rem(t + k, 4)
            c = remote(p_ref.at[plane, theirs], ra.at[k], sent.at[k], arrived.at[k], core)
            c.start()
            first.append((k, c))
        out = []
        for k, c in first:
            c.wait_recv()
            plane = lax.rem(t + k, 4)
            both = p_ref[plane, mine].astype(f32) + ra[k].astype(f32)
            if k:
                s[k] = both.astype(bf16)
                d = remote(s.at[k], rz.at[k], sent.at[3 + k], arrived.at[3 + k], (f, plane))
                d.start()
                out.append((k, d))
            else:
                pair[mine] = both
        for c in loads:
            c.wait()
        total = PlaneSum(stage, other, held, from_x, from_y, last, sum_sent, sum_arrived)
        total.begin(chunk_part([(hidden_v, Rows(down_w))], size))
        load_rows.wait()
        query_grads, copies = grads_across(
            g_ref, rows_v, w_grad, spread_ref, w_sent, w_arrived, load_sem.at[2]
        )
        for k in (6, 7, 2, 4, 3, 5, 1, 0):
            query_grads(k)
        total.turn()
        for k, d in out:
            d.wait_recv()
            pair[mine] += rz[k].astype(f32)
        back = remote(pair.at[mine], pair.at[mine], sent.at[7], arrived.at[7], core)
        back.start()
        back.wait()
        for j in range(chunks):
            lanes = slice(j * size, (j + 1) * size)
            keys = turn_heads(pair[j, :HEAD_DIM], cos_ref[:, lanes], -sin_ref[:, lanes])
            single_ref[:, lanes] = jnp.where(side == 0, keys, pair[j, HEAD_DIM:]).astype(bf16)
        total.end(share)
        out_ref[...] = jnp.where(valid_ref[...] > 0, middle_ref[...] + share[...], 0.0).astype(bf16)
        for c in copies:
            c.wait()
        for k, c in first + out:
            c.wait_send()
        total.finish()

    dma = pltpu.SemaphoreType.DMA
    return pl.pallas_call(
        kernel,
        out_shape=[
            jax.ShapeDtypeStruct((HEAD_DIM, chunks * size), bf16),
            jax.ShapeDtypeStruct((size, width), bf16),
            jax.ShapeDtypeStruct((8, depth, width // 8), bf16),
        ],
        in_specs=[IN_VMEM, ANYWHERE, ANYWHERE, IN_VMEM, IN_VMEM, IN_VMEM, ANYWHERE, IN_VMEM, IN_VMEM],
        out_specs=[IN_VMEM, IN_VMEM, ANYWHERE],
        scratch_shapes=sum_scratch(size, width)
        + [pltpu.VMEM((units, 8 * size), bf16), pltpu.VMEM((4, units // 4, width), bf16)]
        + [dma((3,)), dma((8,))]
        + [pltpu.VMEM((4, half, height, size), bf16)] * 3
        + [dma((8,)), dma((8,)), pltpu.VMEM((size, width), f32)]
        + [
            pltpu.VMEM((chunks, height, size), f32),
            pltpu.VMEM((8, size, width), bf16),
            pltpu.VMEM((8, depth, width // 8), bf16),
            dma((8,)),
            dma((8,)),
        ],
        compiler_params=comm_params(number, VMEM_MOST),
        cost_estimate=lasting(55),
        name="backward_pairs",
    )(pair_parts, hidden, down_all, middle, valid, grad_query, rows, cosine, sine_table)


def backward_first(
    grad_query, single, weights, rows, tokens, grad_middle, gain, down_grads, gate_grads, number
):
    size, width = tokens.shape
    depth = grad_query.shape[0]
    block = width // 8
    f32, bf16 = jnp.float32, jnp.bfloat16

    def kernel(
        g_ref, single_ref, w_ref, rows_hbm, x_ref, middle_ref, gain_ref, down_ref, gate_ref,
        tokens_grad_ref, gain_grad_ref, spread_ref, own_down_ref, own_gate_ref,
        stage, other, held, from_x, from_y, last, sum_sent, sum_arrived,
        rows_v, load_sem, w_grad, sent, arrived, single_w, e_sent, e_arrived, e_kept,
    ):
        f, t = lax.axis_index("fsdp"), lax.axis_index("tp")
        load = pltpu.make_async_copy(rows_hbm, rows_v, load_sem.at[0])
        load.start()
        side = lax.rem(f, 2)
        single_w[...] = w_ref[
            pl.ds(pl.multiple_of(depth + side * HEAD_DIM, HEAD_DIM), HEAD_DIM), :
        ]
        greet([(f ^ k, t) for k in range(1, 8)])
        total = PlaneSum(stage, other, held, from_x, from_y, last, sum_sent, sum_arrived)
        total.begin(chunk_part([(g_ref, w_ref.at[pl.ds(0, depth)]), (single_ref, single_w)], size))
        load.wait()
        single_grads, copies = grads_across(
            single_ref, rows_v, w_grad, spread_ref, sent, arrived, load_sem.at[1]
        )
        for k in (6, 7, 2, 4, 3, 5, 1, 0):
            single_grads(k)
        total.turn()
        exchange = exchange_begin(
            ((down_ref, own_down_ref), (gate_ref, own_gate_ref)), e_sent, e_arrived, e_kept
        )
        wide = x_ref[...].astype(f32)
        inverse = lax.rsqrt(jnp.mean(wide * wide, axis=1, keepdims=True) + epsilon)
        normed = wide * inverse
        total.end(tokens_grad_ref)
        grad = tokens_grad_ref[...]
        gain_grad_ref[...] = jnp.sum(grad * normed, axis=0, keepdims=True)
        tokens_grad_ref[...] = middle_ref[...] + norm_back(grad, gain_ref[...], normed, inverse)
        for c in copies + exchange:
            c.wait()
        total.finish()

    dma = pltpu.SemaphoreType.DMA
    return pl.pallas_call(
        kernel,
        out_shape=[
            jax.ShapeDtypeStruct((size, width), f32),
            jax.ShapeDtypeStruct((1, width), f32),
            jax.ShapeDtypeStruct((8, HEAD_DIM, block), bf16),
            jax.ShapeDtypeStruct(down_grads.shape, bf16),
            jax.ShapeDtypeStruct(gate_grads.shape, bf16),
        ],
        in_specs=[IN_VMEM] * 3 + [ANYWHERE] + [IN_VMEM] * 3 + [ANYWHERE] * 2,
        out_specs=[IN_VMEM, IN_VMEM, ANYWHERE, ANYWHERE, ANYWHERE],
        scratch_shapes=sum_scratch(size, width)
        + [
            pltpu.VMEM((8, size, width), bf16),
            dma((2,)),
            pltpu.VMEM((8, HEAD_DIM, block), bf16),
            dma((8,)),
            dma((8,)),
            pltpu.VMEM((HEAD_DIM, width), bf16),
            dma((8, 2)),
            dma((8, 2)),
            dma((2,)),
        ],
        compiler_params=comm_params(number, VMEM_MOST),
        cost_estimate=lasting(62),
        name="backward_first",
    )(grad_query, single, weights, rows, tokens, grad_middle, gain, down_grads, gate_grads)


def last_sums(gain_first, gain_second, pair_parts, up_grads, number):
    width = gain_first.shape[1]
    block = width // 8
    f32 = jnp.float32

    def kernel(
        first_ref, second_ref, p_ref, up_ref, sums_ref, pair_ref, own_up_ref,
        gains, taken, planes, pairs, sent, arrived, z_sent, z_arrived, p_sent, p_arrived, e_sent, e_arrived, e_kept,
    ):
        f, t = lax.axis_index("fsdp"), lax.axis_index("tp")
        for j in range(8):
            lanes = slice(j * block, (j + 1) * block)
            gains[j] = jnp.concatenate([first_ref[:, lanes], second_ref[:, lanes]], axis=0)
        greet(everyone(f, t))
        copies = []
        for k in (2, 1, 3):
            plane = lax.rem(t + k, 4)
            c = remote(
                p_ref.at[pl.ds(2 * plane, 2)], pairs.at[k], p_sent.at[k], p_arrived.at[k], (f, plane)
            )
            c.start()
            copies.append(c)
        spread = []
        for k in (6, 7, 2, 4, 3, 5, 1):
            c = remote(gains.at[f ^ k], taken.at[k], sent.at[k], arrived.at[k], (f ^ k, t))
            c.start()
            spread.append((k, c))
        exchange = exchange_begin(((up_ref, own_up_ref),), e_sent, e_arrived, e_kept)
        total = gains[f]
        for k, c in spread:
            c.wait_recv()
            total += taken[k]
        planes[0] = total
        along_z = []
        for k in (1, 2, 3):
            c = remote(planes.at[0], planes.at[k], z_sent.at[k], z_arrived.at[k], (f, lax.rem(t + k, 4)))
            c.start()
            along_z.append(c)
        pair = p_ref[pl.ds(2 * t, 2)].astype(f32)
        for k, c in zip((2, 1, 3), copies):
            c.wait_recv()
            pair += pairs[k].astype(f32)
        pair_ref[...] = pair
        for c in along_z:
            c.wait_recv()
        sums = planes[t]
        for plane in (1, 2, 3):
            sums += planes[lax.rem(t + 4 - plane, 4)]
        sums_ref[...] = sums
        for c in [c for _, c in spread] + along_z + copies:
            c.wait_send()
        for c in exchange:
            c.wait()

    dma = pltpu.SemaphoreType.DMA
    return pl.pallas_call(
        kernel,
        out_shape=[
            jax.ShapeDtypeStruct((2, block), f32),
            jax.ShapeDtypeStruct((2, *pair_parts.shape[1:]), f32),
            jax.ShapeDtypeStruct(up_grads.shape, up_grads.dtype),
        ],
        in_specs=[IN_VMEM] * 3 + [ANYWHERE],
        out_specs=[IN_VMEM] * 2 + [ANYWHERE],
        scratch_shapes=[
            pltpu.VMEM((8, 2, block), f32),
            pltpu.VMEM((8, 2, block), f32),
            pltpu.VMEM((4, 2, block), f32),
            pltpu.VMEM((4, 2, *pair_parts.shape[1:]), pair_parts.dtype),
            dma((8,)),
            dma((8,)),
            dma((4,)),
            dma((4,)),
            dma((4,)),
            dma((4,)),
            dma((8, 1)),
            dma((8, 1)),
            dma((1,)),
        ],
        compiler_params=comm_params(number, VMEM_MOST),
        cost_estimate=lasting(16),
        name="last_sums",
    )(gain_first, gain_second, pair_parts, up_grads)


def last_forms(layer_out, tokens_grad, grad_query, grad_output, grad_down, grad_gate, grad_up):
    f32 = jnp.float32
    across = grad_query.shape[0]
    block = grad_query.shape[1]
    units = grad_down.shape[1]
    tall = 8 * units

    def kernel(
        out_in, tokens_in, query_in, output_in, down_in, gate_in, up_in,
        out_o, tokens_o, query_o, output_o, gate_o, up_o, down_o,
        out_v, tokens_v, query_v, output_v, down_v, gate_v, up_v,
        query_w, output_w, gate_w, up_w, down_w, in_sem, out_sem,
    ):
        loads = [
            pltpu.make_async_copy(source, target, in_sem.at[i])
            for i, (source, target) in enumerate(
                (
                    (gate_in, gate_v),
                    (up_in, up_v),
                    (down_in, down_v),
                    (out_in, out_v),
                    (tokens_in, tokens_v),
                    (query_in, query_v),
                    (output_in, output_v),
                )
            )
        ]
        for c in loads:
            c.start()
        stores = []

        def store(source, target):
            c = pltpu.make_async_copy(source, target, out_sem.at[len(stores)])
            c.start()
            stores.append(c)

        for n, (tight, wide, target) in enumerate(((gate_v, gate_w, gate_o), (up_v, up_w, up_o))):
            loads[n].wait()
            wide[...] = tight[...].reshape(tall, block).astype(f32).T
            store(wide, target)
        loads[2].wait()
        down_w[...] = down_v[...].reshape(tall, block).astype(f32)
        store(down_w, down_o)
        loads[3].wait()
        store(out_v, out_o)
        loads[4].wait()
        store(tokens_v, tokens_o)
        loads[5].wait()
        query_w[...] = query_v[...].astype(f32).T
        store(query_w, query_o)
        loads[6].wait()
        output_w[...] = output_v[...].astype(f32)
        store(output_w, output_o)
        for c in stores:
            c.wait()

    operands = (layer_out, tokens_grad, grad_query, grad_output, grad_down, grad_gate, grad_up)
    results = [
        jax.ShapeDtypeStruct(layer_out.shape, layer_out.dtype),
        jax.ShapeDtypeStruct(tokens_grad.shape, f32),
        jax.ShapeDtypeStruct((block, across), f32),
        jax.ShapeDtypeStruct((across, block), f32),
        jax.ShapeDtypeStruct((block, tall), f32),
        jax.ShapeDtypeStruct((block, tall), f32),
        jax.ShapeDtypeStruct((tall, block), f32),
    ]
    return pl.pallas_call(
        kernel,
        out_shape=results,
        in_specs=[ANYWHERE] * 7,
        out_specs=[ANYWHERE] * 7,
        scratch_shapes=[pltpu.VMEM(x.shape, x.dtype) for x in operands]
        + [pltpu.VMEM(x.shape, x.dtype) for x in results[2:]]
        + [pltpu.SemaphoreType.DMA((7,)), pltpu.SemaphoreType.DMA((7,))],
        compiler_params=pltpu.CompilerParams(vmem_limit_bytes=VMEM_MOST),
        cost_estimate=lasting(8),
        name="last_forms",
    )(*operands)


def dot_nn(left, right):
    return jnp.dot(left, right, preferred_element_type=jnp.float32)


def seen_keys(begin_row, first_key, first_query, shape):
    key_slot = first_key + lax.broadcasted_iota(jnp.int32, shape, 0)
    query_slot = first_query + lax.broadcasted_iota(jnp.int32, (1, shape[1]), 1)
    return (key_slot <= query_slot) & (key_slot >= begin_row)


def head_lanes(block, heads):
    return jnp.concatenate([block[h * HEAD_DIM : (h + 1) * HEAD_DIM] for h in range(heads)], axis=1)


WIDE = 2

def key_block(kv_ref, g, count):
    blocks = [kv_ref[lax.rem(g + n, 4), lax.div(g + n, 4)] for n in range(count)]
    return blocks[0] if count == 1 else jnp.concatenate(blocks, axis=0)


def attend(info, begins, queries, pair):
    depth, slots = queries.shape
    heads = depth // HEAD_DIM
    size = slots // 8
    span = heads * size

    def kernel(info_ref, begin_ref, q_ref, kv_ref, o_ref, l_ref, q_s, m_s, t_s, a_s, even_s, odd_s):
        f = pl.program_id(0)
        low, middle, own = info_ref[f, 0], info_ref[f, 1], info_ref[f, 2]
        q_s[...] = head_lanes(q_ref[...], heads)
        m_s[...] = jnp.full_like(m_s, -1e30)
        t_s[...] = jnp.zeros_like(t_s)
        a_s[...] = jnp.zeros_like(a_s)

        def scores_of(g, count):
            return dot_nn(key_block(kv_ref, g, count)[:, :HEAD_DIM], q_s[...])

        def add(scores, g, count):
            values = key_block(kv_ref, g, count)[:, HEAD_DIM:]
            value_cols = values.astype(jnp.float32).T.astype(jnp.bfloat16)
            largest = m_s[...]
            higher = jnp.maximum(largest, jnp.max(scores, axis=0, keepdims=True))
            raised = jnp.exp(scores - higher)
            fade = jnp.exp(largest - higher)
            m_s[...] = higher
            t_s[...] = t_s[...] * fade + jnp.sum(raised, axis=0, keepdims=True)
            a_s[...] = a_s[...] * fade + dot_nn(value_cols, raised.astype(jnp.bfloat16))

        def step(g, count, masked):
            scores = scores_of(g, count)
            if masked:
                seen = seen_keys(begin_ref[0], g * size, own * size, (count * size, size))
                seen = jnp.concatenate([seen] * heads, axis=1)
                scores = jnp.where(seen, scores, -1e30)
            add(scores, g, count)

        count = own + 1 - low
        odd = lax.rem(count, WIDE) == 1

        @pl.when(odd)
        def _():
            step(own, 1, True)

        @pl.when(jnp.logical_not(odd))
        def _():
            step(own - 1, WIDE, True)

        units = lax.div(count - 1, WIDE)
        bounded = jnp.minimum(lax.div(middle - low + WIDE - 1, WIDE), units)

        def masked_step(n, carry):
            step(low + n * WIDE, WIDE, True)
            return carry

        lax.fori_loop(0, bounded, masked_step, 0)
        def unit(n):
            return low + jnp.minimum(n, units - 1) * WIDE

        def two(j, carry):
            n = bounded + 2 * j
            odd_s[...] = scores_of(unit(n + 1), WIDE)
            add(even_s[...], unit(n), WIDE)
            even_s[...] = scores_of(unit(n + 2), WIDE)
            add(odd_s[...], unit(n + 1), WIDE)
            return carry

        rest = units - bounded

        @pl.when(rest > 0)
        def _():
            even_s[...] = scores_of(unit(bounded), WIDE)
            lax.fori_loop(0, lax.div(rest, 2), two, 0)

            @pl.when(lax.rem(rest, 2) == 1)
            def _():
                add(even_s[...], unit(units - 1), WIDE)

        result = a_s[...] / t_s[...]
        for h in range(heads):
            o_ref[h * HEAD_DIM : (h + 1) * HEAD_DIM] = result[:, h * size : (h + 1) * size].astype(
                jnp.bfloat16
            )
        l_ref[0] = m_s[...] + jnp.log(t_s[...])
    return pl.pallas_call(
        kernel,
        grid_spec=pltpu.PrefetchScalarGridSpec(
            num_scalar_prefetch=1,
            grid=(8,),
            in_specs=[
                pl.BlockSpec((1, 1, size), lambda f, info: (f, 0, 0)),
                pl.BlockSpec((depth, size), lambda f, info: (0, f)),
                pl.BlockSpec((4, 8, size, 2 * HEAD_DIM), lambda f, info: (0, 0, 0, 0)),
            ],
            out_specs=[
                pl.BlockSpec((depth, size), lambda f, info: (0, f)),
                pl.BlockSpec((1, 1, span), lambda f, info: (f, 0, 0)),
            ],
            scratch_shapes=[
                pltpu.VMEM((HEAD_DIM, span), jnp.bfloat16),
                pltpu.VMEM((1, span), jnp.float32),
                pltpu.VMEM((1, span), jnp.float32),
                pltpu.VMEM((HEAD_DIM, span), jnp.float32),
                pltpu.VMEM((WIDE * size, span), jnp.float32),
                pltpu.VMEM((WIDE * size, span), jnp.float32),
            ],
        ),
        out_shape=[
            jax.ShapeDtypeStruct((depth, slots), jnp.bfloat16),
            jax.ShapeDtypeStruct((8, 1, span), jnp.float32),
        ],
        compiler_params=pltpu.CompilerParams(vmem_limit_bytes=VMEM_MOST),
        cost_estimate=lasting(50),
        name="attend",
    )(info, begins, queries, pair)


def attend_back(info, begins, queries, pair, outputs, grads, totals, cosine, sine_table):
    depth, slots = queries.shape
    heads = depth // HEAD_DIM
    size = slots // 8
    span = heads * size

    def kernel(
        info_ref, begin_ref, q_ref, kv_ref, o_ref, g_ref, l_ref, cos_ref, sin_ref, dq_ref, dkv_ref, q_s, g_s, d_s, a_s, w_s
    ):
        f = pl.program_id(0)
        low, middle, own = info_ref[f, 0], info_ref[f, 1], info_ref[f, 2]
        middle = middle + lax.rem(own - middle, WIDE)

        @pl.when(f == 0)
        def _():
            w_s[...] = jnp.zeros_like(w_s)

        q_s[...] = head_lanes(q_ref[...], heads)
        g_s[...] = head_lanes(g_ref[...], heads)
        out_lanes = head_lanes(o_ref[...], heads).astype(jnp.float32)
        d_s[...] = jnp.sum(out_lanes * g_s[...].astype(jnp.float32), axis=0, keepdims=True)
        a_s[...] = jnp.zeros_like(a_s)

        def step(g, count, masked):
            block = key_block(kv_ref, g, count)
            keys, values = block[:, :HEAD_DIM], block[:, HEAD_DIM:]
            key_cols = keys.astype(jnp.float32).T.astype(jnp.bfloat16)
            if masked:
                seen = seen_keys(begin_ref[0], g * size, own * size, (size, size))
                seen = jnp.concatenate([seen] * heads, axis=1)
            grad_keys = jnp.zeros((HEAD_DIM, count * size), jnp.float32)
            grad_values = jnp.zeros((HEAD_DIM, count * size), jnp.float32)
            query, grad = q_s[...], g_s[...]
            raised = jnp.exp(dot_nn(keys, query) - l_ref[0])
            if masked:
                raised = jnp.where(seen, raised, 0.0)
            grad_probs = dot_nn(values, grad)
            scores = (raised * (grad_probs - d_s[...])).astype(jnp.bfloat16)
            grad_values += outer_cols(grad, raised.astype(jnp.bfloat16))
            grad_keys += outer_cols(query, scores)
            a_s[...] += dot_nn(key_cols, scores)
            for n in range(count):
                keep = slice(n * size, (n + 1) * size)
                w_s[lax.rem(g + n, 4), lax.div(g + n, 4), :HEAD_DIM] += grad_keys[:, keep]
                w_s[lax.rem(g + n, 4), lax.div(g + n, 4), HEAD_DIM:] += grad_values[:, keep]

        def masked_step(g, carry):
            step(g, 1, True)
            return carry

        def plain_step(n, carry):
            step(middle + n * WIDE, WIDE, False)
            return carry

        step(own, 1, True)
        lax.fori_loop(low, middle, masked_step, 0)
        lax.fori_loop(0, lax.div(own - middle, WIDE), plain_step, 0)
        result = a_s[...] * HEAD_DIM ** (-0.5)
        result = jnp.concatenate([result[:, h * size : (h + 1) * size] for h in range(heads)], axis=0)
        dq_ref[...] = turn_heads(result, cos_ref[...], -sin_ref[...]).astype(jnp.bfloat16)

        @pl.when(f == 7)
        def _():
            dkv_ref[...] = w_s[...].astype(jnp.bfloat16)

    return pl.pallas_call(
        kernel,
        grid_spec=pltpu.PrefetchScalarGridSpec(
            num_scalar_prefetch=1,
            grid=(8,),
            in_specs=[
                pl.BlockSpec((1, 1, size), lambda f, info: (f, 0, 0)),
                pl.BlockSpec((depth, size), lambda f, info: (0, f)),
                pl.BlockSpec((4, 8, size, 2 * HEAD_DIM), lambda f, info: (0, 0, 0, 0)),
                pl.BlockSpec((depth, size), lambda f, info: (0, f)),
                pl.BlockSpec((depth, size), lambda f, info: (0, f)),
                pl.BlockSpec((1, 1, span), lambda f, info: (f, 0, 0)),
                pl.BlockSpec((HEAD_DIM // 2, size), lambda f, info: (0, f)),
                pl.BlockSpec((HEAD_DIM // 2, size), lambda f, info: (0, f)),
            ],
            out_specs=[
                pl.BlockSpec((depth, size), lambda f, info: (0, f)),
                pl.BlockSpec((4, 8, 2 * HEAD_DIM, size), lambda f, info: (0, 0, 0, 0)),
            ],
            scratch_shapes=[
                pltpu.VMEM((HEAD_DIM, span), jnp.bfloat16),
                pltpu.VMEM((HEAD_DIM, span), jnp.bfloat16),
                pltpu.VMEM((1, span), jnp.float32),
                pltpu.VMEM((HEAD_DIM, span), jnp.float32),
                pltpu.VMEM((4, 8, 2 * HEAD_DIM, size), jnp.float32),
            ],
        ),
        out_shape=[
            jax.ShapeDtypeStruct((depth, slots), jnp.bfloat16),
            jax.ShapeDtypeStruct((4, 8, 2 * HEAD_DIM, size), jnp.bfloat16),
        ],
        compiler_params=pltpu.CompilerParams(vmem_limit_bytes=VMEM_MOST),
        cost_estimate=lasting(65),
        name="attend_back",
    )(info, begins, queries, pair, outputs, grads, totals, cosine, sine_table)


def segment_begins(slots, lengths):
    seq_index = jnp.arange(lengths.shape[0], dtype=jnp.int32)
    ends = jnp.sum(jnp.where(seq_index[:, None] >= seq_index[None, :], lengths[None, :], 0), axis=1)
    passed = slots[:, None] >= ends[None, :]
    begins = jnp.sum(jnp.where(passed, lengths[None, :], 0), axis=1)
    return begins, slots < ends[-1]


def local_plane(
    tokens,
    attn_gain,
    query_weight,
    key_weight,
    value_weight,
    output_weight,
    mlp_gain,
    gate_weight,
    up_weight,
    down_weight,
    out_grad,
    lengths,
):
    size, width = tokens.shape
    f = lax.axis_index("fsdp")
    t = lax.axis_index("tp")
    block = query_weight.shape[0]
    head_rows = query_weight.shape[1] // 2
    units = gate_weight.shape[1] // 8
    bf16, f32 = jnp.bfloat16, jnp.float32

    def across_plane(parts):
        return lax.all_to_all(parts, "fsdp", 0, 0, tiled=False)

    def planes_together(part):
        flat = part.reshape(-1, block)
        return lax.all_gather(flat, "tp", axis=0, tiled=True).reshape(4, *part.shape)

    gate_up, inner_own = first_forms(
        gate_weight, up_weight, query_weight, key_weight.T, value_weight.T
    )
    inner_all = planes_together(inner_own)
    down_all = across_plane(down_weight.reshape(8, units, block))
    gate_up = across_plane(gate_up)
    tokens, down_all = lax.optimization_barrier((tokens, down_all))
    down_all = planes_together(down_all)
    gains_own = jnp.stack([attn_gain, mlp_gain]).astype(f32)

    my_slots = (f * 4 + t) * size + jnp.arange(size, dtype=jnp.int32)
    _, my_valid = segment_begins(my_slots, lengths)
    valid_rows = my_valid[:, None]
    chunk_index = jnp.arange(8, dtype=jnp.int32) * 4 + t
    plane_slots = (chunk_index[:, None] * size + jnp.arange(size, dtype=jnp.int32)[None, :]).reshape(-1)
    begins, plane_valid = segment_begins(plane_slots, lengths)
    positions = jnp.where(plane_valid, plane_slots - begins, 0)
    begins = begins.reshape(8, 1, size)
    info = jnp.stack(
        [
            begins[:, 0, 0] // size,
            jnp.minimum((begins[:, 0, size - 1] + size - 1) // size, chunk_index),
            chunk_index,
        ],
        axis=1,
    ).astype(jnp.int32)
    ladder = jnp.arange(HEAD_DIM // 2).astype(f32)
    frequency = 10000.0 ** (-2.0 * ladder / HEAD_DIM)
    angles = positions.astype(f32)[None, :] * frequency[:, None]
    cosine, sine_table = jnp.cos(angles), jnp.sin(angles)

    valid_rows = valid_rows.astype(f32)
    cosine, gate_up = lax.optimization_barrier((cosine, gate_up))
    gate_up = planes_together(gate_up)
    rows_first, queries, pair, inner_rows_w, output_all, grad_rows, gains_all = first_rows(
        tokens, gains_own, inner_all, output_weight, cosine, sine_table, out_grad, valid_rows, 2
    )
    output_rows = across_plane(output_all.reshape(8, head_rows, block))
    gains = jnp.moveaxis(gains_all, 0, 1).reshape(2, width)
    gain_first, gain_second = gains[0:1], gains[1:2]
    attended, totals = attend(info, begins, queries, pair)
    middle, row_second, grad_hidden = forward_output(
        attended, output_rows, tokens, gain_second, grad_rows, down_all, 4
    )
    rows_second, hidden, grad_gate_low, grad_up_low, down_grads = forward_hidden(
        row_second, grad_rows, grad_hidden, gate_up, 5
    )
    (
        grad_middle,
        gain_second_part,
        grad_output_w,
        grad_attended,
        gate_grads,
        up_grads,
    ) = backward_middle(
        grad_gate_low,
        grad_up_low,
        gate_up,
        rows_second,
        grad_rows,
        output_rows,
        attended,
        middle,
        gain_second,
        6,
    )
    def own_plane(parts, *shape):
        flat = parts.reshape(-1, block)
        return lax.psum_scatter(flat, "tp", scatter_dimension=0, tiled=True).reshape(*shape)

    down_grads = own_plane(down_grads, 8, units, block)
    gate_grads, down_grads = lax.optimization_barrier((gate_grads, down_grads))
    gate_grads = own_plane(gate_grads, 8, units, block)
    output_parts = across_plane(grad_output_w)
    output_parts, gate_grads = lax.optimization_barrier((output_parts, gate_grads))
    output_own = own_plane(output_parts, 2 * head_rows, block)
    grad_query, grad_pair_parts = attend_back(
        info, begins, queries, pair, attended, grad_attended, totals, cosine, sine_table
    )
    single, layer_out, query_parts = backward_pairs(
        grad_pair_parts,
        hidden,
        down_all,
        middle,
        valid_rows,
        grad_query,
        rows_first,
        cosine,
        sine_table,
        7,
    )
    up_grads, query_parts, output_own = lax.optimization_barrier((up_grads, query_parts, output_own))
    up_grads = own_plane(up_grads, 8, units, block)
    tokens_grad, gain_first_part, single_parts, own_down, own_gate = backward_first(
        grad_query,
        single,
        inner_rows_w,
        rows_first,
        tokens,
        grad_middle,
        gain_first,
        down_grads,
        gate_grads,
        8,
    )
    query_parts, up_grads = lax.optimization_barrier((query_parts, up_grads))
    query_own = own_plane(query_parts, 2 * head_rows, block)
    gain_sums, pair_own, own_up = last_sums(
        gain_first_part, gain_second_part, single_parts, up_grads, 9
    )
    layer_out, tokens_grad, query, output, gate, up, down = last_forms(
        layer_out, tokens_grad, query_own, output_own, own_down, own_gate, own_up
    )
    return (
        layer_out,
        tokens_grad,
        gain_sums[0],
        query,
        pair_own[0].T,
        pair_own[1].T,
        output,
        gain_sums[1],
        gate,
        up,
        down,
    )


def solution(mesh):
    plane = dict(mesh.shape) == {"fsdp": 8, "tp": 4}
    body = local_plane if plane else local
    in_specs = (
        P(("fsdp", "tp"), None),
        P("fsdp"),
        P("fsdp", "tp"),
        P("fsdp", "tp"),
        P("fsdp", "tp"),
        P("tp", "fsdp"),
        P("fsdp"),
        P("fsdp", "tp"),
        P("fsdp", "tp"),
        P("tp", "fsdp"),
        P(("fsdp", "tp"), None),
        P(),
    )
    out_specs = (
        P(("fsdp", "tp"), None),
        P(("fsdp", "tp"), None),
        P("fsdp"),
        P("fsdp", "tp"),
        P("fsdp", "tp"),
        P("fsdp", "tp"),
        P("tp", "fsdp"),
        P("fsdp"),
        P("fsdp", "tp"),
        P("fsdp", "tp"),
        P("tp", "fsdp"),
    )
    return jax.shard_map(body, mesh=mesh, in_specs=in_specs, out_specs=out_specs, check_vma=False)
```

```python
import jax
import jax.numpy as jnp
from jax import lax
from jax.experimental import pallas as pl
from jax.experimental.pallas import tpu as pltpu
from jax.sharding import PartitionSpec as P

HEAD_DIM = 64
MAX_SPAN = 4096


epsilon = 1e-05


def passed_along(block, axis, distance):
    devices = range(lax.axis_size(axis))
    route = [(i - distance, i) for i in devices if i - distance in devices]
    return lax.ppermute(block, axis, route)


def stream_layout(slots, lengths):
    seq_count = lengths.shape[0]
    seq_index = jnp.arange(seq_count, dtype=jnp.int32)
    ends = jnp.sum(jnp.where(seq_index[:, None] >= seq_index[None, :], lengths[None, :], 0), axis=1)
    starts = ends - lengths
    segment = jnp.sum((slots[:, None] >= ends[None, :]).astype(jnp.int32), axis=1)
    start_of = jnp.sum(
        jnp.where(segment[:, None] == seq_index[None, :], starts[None, :], 0), axis=1
    )
    position = jnp.where((segment < seq_count) & (slots >= 0), slots - start_of, 0)
    segment = jnp.where(slots < 0, -1, segment)
    return (segment, position)


def rotary_tables(positions, head_width):
    ladder = jnp.arange(head_width // 2).astype(jnp.float32)
    frequency = 10000.0 ** (-2.0 * ladder / head_width)
    angle_half = positions.astype(jnp.float32)[:, None] * frequency[None, :]
    angles = jnp.concatenate([angle_half, angle_half], axis=1)
    return (jnp.cos(angles)[:, None, :], jnp.sin(angles)[:, None, :])


def rotate(values, cosine, sine_table):
    middle = values.shape[-1] // 2
    turned = jnp.concatenate([-values[..., middle:], values[..., :middle]], axis=-1)
    return values * cosine + turned * sine_table


def rotate_back(values, cosine, sine_table):
    middle = values.shape[-1] // 2
    scaled = values * sine_table
    turned = jnp.concatenate([scaled[..., middle:], -scaled[..., :middle]], axis=-1)
    return values * cosine + turned


def inner_rows(left, right):
    return lax.dot_general(
        left, right, (((0,), (0,)), ((), ())), preferred_element_type=jnp.float32
    )


def outer_cols(left, right):
    return lax.dot_general(
        left, right, (((1,), (1,)), ((), ())), preferred_element_type=jnp.float32
    )


def norm_back(grad_normed, gain_wide, normed, inverse):
    scaled_grad = grad_normed * gain_wide
    return inverse * (scaled_grad - normed * jnp.mean(scaled_grad * normed, axis=1, keepdims=True))


def local(
    tokens,
    attn_gain,
    query_weight,
    key_weight,
    value_weight,
    output_weight,
    mlp_gain,
    gate_weight,
    up_weight,
    down_weight,
    out_grad,
    lengths,
):
    row_count = tokens.shape[0]
    tp_count = lax.axis_size("tp")
    block_rows = row_count * tp_count
    slot_total = block_rows * lax.axis_size("fsdp")
    longest = min(MAX_SPAN, slot_total // 2)
    reach_count = (longest - 2) // block_rows + 1
    window = (reach_count + 1) * block_rows
    front_rows = reach_count * block_rows
    block_index = lax.axis_index("fsdp")
    tp_index = lax.axis_index("tp")
    head_width = HEAD_DIM
    query_width = query_weight.shape[1]
    key_width = key_weight.shape[1]
    heads_here = query_width // head_width
    score_scale = head_width ** (-0.5)
    seq_count = lengths.shape[0]
    row_base = (block_index * tp_count + tp_index) * row_count
    my_slots = row_base + jnp.arange(row_count, dtype=jnp.int32)
    my_segments, my_positions = stream_layout(my_slots, lengths)
    valid_rows = (my_segments < seq_count)[:, None]
    gathered = (
        lax.all_gather(query_weight, "fsdp", axis=0, tiled=True),
        lax.all_gather(key_weight, "fsdp", axis=0, tiled=True),
        lax.all_gather(value_weight, "fsdp", axis=0, tiled=True),
        lax.all_gather(output_weight, "fsdp", axis=1, tiled=True),
        lax.all_gather(gate_weight, "fsdp", axis=0, tiled=True),
        lax.all_gather(up_weight, "fsdp", axis=0, tiled=True),
        lax.all_gather(down_weight, "fsdp", axis=1, tiled=True),
        lax.all_gather(attn_gain, "fsdp", axis=0, tiled=True),
        lax.all_gather(mlp_gain, "fsdp", axis=0, tiled=True),
    )
    (
        full_query,
        full_key,
        full_value,
        full_output,
        full_gate,
        full_up,
        full_down,
        gain_first,
        gain_second,
    ) = gathered
    w_inner = jnp.concatenate([full_query, full_key, full_value], axis=1)
    gain_first_wide = gain_first.astype(jnp.float32)
    gain_second_wide = gain_second.astype(jnp.float32)
    tokens_wide = tokens.astype(jnp.float32)
    inverse_first = lax.rsqrt(jnp.mean(tokens_wide * tokens_wide, axis=1, keepdims=True) + epsilon)
    normed_first = tokens_wide * inverse_first
    scaled_first = (normed_first * gain_first_wide).astype(jnp.bfloat16)
    rows_first = lax.all_gather(scaled_first, "tp", axis=0, tiled=True)
    projected = jnp.dot(rows_first, w_inner, preferred_element_type=jnp.float32)
    block_base = block_index * block_rows
    key_slots = block_base - front_rows + jnp.arange(window, dtype=jnp.int32)
    key_segments, key_positions = stream_layout(key_slots, lengths)
    query_segments = key_segments[front_rows:]
    block_positions = key_positions[front_rows:]
    cosine, sine_table = rotary_tables(block_positions, head_width)
    queries = rotate(
        projected[:, :query_width].reshape(block_rows, heads_here, head_width), cosine, sine_table
    ).astype(jnp.bfloat16)
    keys_local = rotate(
        projected[:, query_width : query_width + key_width].reshape(block_rows, 1, head_width),
        cosine,
        sine_table,
    )
    keys_local = keys_local.reshape(block_rows, head_width).astype(jnp.bfloat16)
    values_local = projected[:, query_width + key_width :].astype(jnp.bfloat16)
    pair_local = jnp.concatenate([keys_local, values_local], axis=1)
    pieces = []
    for offset in range(reach_count, 0, -1):
        pieces.append(passed_along(pair_local, "fsdp", offset))
    pair_window = jnp.concatenate(pieces + [pair_local], axis=0)
    key_window = pair_window[:, :head_width]
    value_window = pair_window[:, head_width:]
    key_seen = (key_segments[None, :] == query_segments[:, None]) & (
        key_positions[None, :] <= block_positions[:, None]
    )

    def head_scores(query_head):
        scores = outer_cols(query_head, key_window) * score_scale
        return jnp.where(key_seen, scores, -1e30)

    def head_forward(query_head):
        scores = head_scores(query_head)
        largest = jnp.max(scores, axis=1, keepdims=True)
        raised = jnp.exp(scores - largest)
        row_total = jnp.sum(raised, axis=1, keepdims=True)
        attn_probs = (raised / row_total).astype(jnp.bfloat16)
        head_out = jnp.dot(attn_probs, value_window, preferred_element_type=jnp.float32)
        return (head_out, (largest + jnp.log(row_total))[:, 0])

    query_heads = jnp.moveaxis(queries, 1, 0)
    head_outs, log_totals = lax.map(head_forward, query_heads)
    attended = jnp.moveaxis(head_outs, 0, 1).reshape(block_rows, query_width).astype(jnp.bfloat16)
    attn_share = lax.psum_scatter(
        jnp.dot(attended, full_output, preferred_element_type=jnp.float32).astype(jnp.bfloat16),
        "tp",
        scatter_dimension=0,
        tiled=True,
    ).astype(jnp.float32)
    middle = tokens_wide + attn_share
    inverse_second = lax.rsqrt(jnp.mean(middle * middle, axis=1, keepdims=True) + epsilon)
    normed_second = middle * inverse_second
    scaled_second = (normed_second * gain_second_wide).astype(jnp.bfloat16)
    rows_second = lax.all_gather(scaled_second, "tp", axis=0, tiled=True)
    gate_proj = jnp.dot(rows_second, full_gate, preferred_element_type=jnp.float32)
    up_proj = jnp.dot(rows_second, full_up, preferred_element_type=jnp.float32)
    gate_sigmoid = jax.nn.sigmoid(gate_proj)
    gate_active = gate_proj * gate_sigmoid
    hidden = (gate_active * up_proj).astype(jnp.bfloat16)
    mlp_share = lax.psum_scatter(
        jnp.dot(hidden, full_down, preferred_element_type=jnp.float32).astype(jnp.bfloat16),
        "tp",
        scatter_dimension=0,
        tiled=True,
    ).astype(jnp.float32)
    layer_out = jnp.where(valid_rows, middle + mlp_share, 0.0).astype(jnp.bfloat16)
    grad_rows = jnp.where(valid_rows, out_grad.astype(jnp.float32), 0.0)
    grad_low = grad_rows.astype(jnp.bfloat16)
    regathered = (
        lax.all_gather(query_weight, "fsdp", axis=0, tiled=True),
        lax.all_gather(key_weight, "fsdp", axis=0, tiled=True),
        lax.all_gather(value_weight, "fsdp", axis=0, tiled=True),
        lax.all_gather(output_weight, "fsdp", axis=1, tiled=True),
        lax.all_gather(gate_weight, "fsdp", axis=0, tiled=True),
        lax.all_gather(up_weight, "fsdp", axis=0, tiled=True),
        lax.all_gather(down_weight, "fsdp", axis=1, tiled=True),
        lax.all_gather(attn_gain, "fsdp", axis=0, tiled=True),
        lax.all_gather(mlp_gain, "fsdp", axis=0, tiled=True),
    )
    (
        full_query,
        full_key,
        full_value,
        full_output,
        full_gate,
        full_up,
        full_down,
        gain_first,
        gain_second,
    ) = regathered
    w_inner = jnp.concatenate([full_query, full_key, full_value], axis=1)
    grad_down_rows = lax.all_gather(grad_low, "tp", axis=0, tiled=True)
    grad_down_w = inner_rows(hidden, grad_down_rows)
    grad_hidden = outer_cols(grad_down_rows, full_down)
    grad_up_low = (grad_hidden * gate_active).astype(jnp.bfloat16)
    grad_gate_low = (
        grad_hidden * up_proj * gate_sigmoid * (1.0 + gate_proj * (1.0 - gate_sigmoid))
    ).astype(jnp.bfloat16)
    grad_gate_w = inner_rows(rows_second, grad_gate_low)
    grad_up_w = inner_rows(rows_second, grad_up_low)
    grad_second = lax.psum_scatter(
        (outer_cols(grad_gate_low, full_gate) + outer_cols(grad_up_low, full_up)).astype(
            jnp.bfloat16
        ),
        "tp",
        scatter_dimension=0,
        tiled=True,
    ).astype(jnp.float32)
    gain_second_part = jnp.sum(grad_second * normed_second, axis=0)
    grad_middle = grad_rows + norm_back(
        grad_second, gain_second_wide, normed_second, inverse_second
    )
    middle_low = grad_middle.astype(jnp.bfloat16)
    grad_attn_rows = lax.all_gather(middle_low, "tp", axis=0, tiled=True)
    grad_output_w = inner_rows(attended, grad_attn_rows)
    grad_attended = outer_cols(grad_attn_rows, full_output).astype(jnp.bfloat16)
    grad_heads = jnp.moveaxis(grad_attended.reshape(block_rows, heads_here, head_width), 1, 0)

    def head_backward(packed):
        query_head, grad_head, log_total = packed
        attn_probs = jnp.exp(head_scores(query_head) - log_total[:, None])
        probs_low = attn_probs.astype(jnp.bfloat16)
        grad_value_head = inner_rows(probs_low, grad_head)
        grad_probs = outer_cols(grad_head, value_window)
        grad_scores = (
            attn_probs * (grad_probs - jnp.sum(attn_probs * grad_probs, axis=1, keepdims=True))
        ).astype(jnp.bfloat16)
        grad_query_head = (
            jnp.dot(grad_scores, key_window, preferred_element_type=jnp.float32) * score_scale
        )
        grad_key_head = inner_rows(grad_scores, query_head) * score_scale
        return (grad_query_head, grad_key_head, grad_value_head)

    grad_query_heads, grad_key_heads, grad_value_heads = lax.map(
        head_backward, (query_heads, grad_heads, log_totals)
    )
    grad_pair = jnp.concatenate(
        [jnp.sum(grad_key_heads, axis=0), jnp.sum(grad_value_heads, axis=0)], axis=1
    )
    own_grad = grad_pair[front_rows:]
    for offset in range(1, reach_count + 1):
        piece_start = (reach_count - offset) * block_rows
        own_grad = own_grad + passed_along(
            grad_pair[piece_start : piece_start + block_rows].astype(jnp.bfloat16), "fsdp", -offset
        ).astype(jnp.float32)
    grad_key_lin = rotate_back(
        own_grad[:, :head_width].reshape(block_rows, 1, head_width), cosine, sine_table
    )
    grad_key_low = grad_key_lin.reshape(block_rows, head_width).astype(jnp.bfloat16)
    grad_value_low = own_grad[:, head_width:].astype(jnp.bfloat16)
    grad_query_lin = rotate_back(jnp.moveaxis(grad_query_heads, 0, 1), cosine, sine_table)
    grad_query_low = grad_query_lin.reshape(block_rows, query_width).astype(jnp.bfloat16)
    grad_inner = jnp.concatenate([grad_query_low, grad_key_low, grad_value_low], axis=1)
    grad_inner_w = inner_rows(rows_first, grad_inner)
    grad_first = lax.psum_scatter(
        outer_cols(grad_inner, w_inner).astype(jnp.bfloat16), "tp", scatter_dimension=0, tiled=True
    ).astype(jnp.float32)
    gain_first_part = jnp.sum(grad_first * normed_first, axis=0)
    tokens_grad = grad_middle + norm_back(grad_first, gain_first_wide, normed_first, inverse_first)
    reduced = (
        lax.psum_scatter(
            grad_inner_w[:, :query_width].astype(jnp.bfloat16),
            "fsdp",
            scatter_dimension=0,
            tiled=True,
        ).astype(jnp.float32),
        lax.psum_scatter(
            grad_inner_w[:, query_width : query_width + key_width].astype(jnp.bfloat16),
            "fsdp",
            scatter_dimension=0,
            tiled=True,
        ).astype(jnp.float32),
        lax.psum_scatter(
            grad_inner_w[:, query_width + key_width :].astype(jnp.bfloat16),
            "fsdp",
            scatter_dimension=0,
            tiled=True,
        ).astype(jnp.float32),
        lax.psum_scatter(
            grad_output_w.astype(jnp.bfloat16), "fsdp", scatter_dimension=1, tiled=True
        ).astype(jnp.float32),
        lax.psum_scatter(
            grad_gate_w.astype(jnp.bfloat16), "fsdp", scatter_dimension=0, tiled=True
        ).astype(jnp.float32),
        lax.psum_scatter(
            grad_up_w.astype(jnp.bfloat16), "fsdp", scatter_dimension=0, tiled=True
        ).astype(jnp.float32),
        lax.psum_scatter(
            grad_down_w.astype(jnp.bfloat16), "fsdp", scatter_dimension=1, tiled=True
        ).astype(jnp.float32),
        lax.psum_scatter(
            gain_first_part.astype(jnp.bfloat16), "fsdp", scatter_dimension=0, tiled=True
        ).astype(jnp.float32),
        lax.psum_scatter(
            gain_second_part.astype(jnp.bfloat16), "fsdp", scatter_dimension=0, tiled=True
        ).astype(jnp.float32),
    )
    gain_sums = lax.psum((reduced[7], reduced[8]), "tp")
    return (
        layer_out,
        tokens_grad,
        gain_sums[0],
        reduced[0],
        reduced[1],
        reduced[2],
        reduced[3],
        gain_sums[1],
        reduced[4],
        reduced[5],
        reduced[6],
    )


MESH = pl.DeviceIdType.MESH
CORE, ALONG_X, ALONG_Y = 1, 2, 4
PARTS = 4
VMEM_MOST = 60 << 20


def greet(partners):
    barrier = pltpu.get_barrier_semaphore()
    for partner in partners:
        pl.semaphore_signal(barrier, inc=1, device_id=partner, device_id_type=MESH)
    pl.semaphore_wait(barrier, len(partners))


def remote(source, target, sent, arrived, partner):
    return pltpu.make_async_remote_copy(
        src_ref=source,
        dst_ref=target,
        send_sem=sent,
        recv_sem=arrived,
        device_id=partner,
        device_id_type=MESH,
    )


def comm_params(number, vmem=None):
    return pltpu.CompilerParams(
        collective_id=number, has_side_effects=True, vmem_limit_bytes=vmem
    )


def lasting(microseconds):
    return pl.CostEstimate(
        flops=int(microseconds * 1.1e9), bytes_accessed=1_000_000, transcendentals=0
    )


ANYWHERE = pl.BlockSpec(memory_space=pl.ANY)
IN_VMEM = pl.BlockSpec(memory_space=pltpu.VMEM)


def columns(index, width):
    return pl.ds(pl.multiple_of(index * width, width), width)


class PlaneGather:
    def __init__(self, store, sent, arrived):
        self.f, self.t = lax.axis_index("fsdp"), lax.axis_index("tp")
        self.store, self.sent, self.arrived = store, sent, arrived
        self.piece = store.shape[1] // PARTS
        self.near = [(self.f ^ k, self.t) for k in (CORE, ALONG_X, ALONG_Y)]
        self.copies, self.on = [], {}

    def send(self, owner, j, way, slot):
        place = self.store.at[owner, pl.ds(j * self.piece, self.piece)]
        c = remote(
            place, place, self.sent.at[slot, j], self.arrived.at[slot, j], self.near[way]
        )
        c.start()
        self.copies.append(c)
        self.on[slot, j] = c

    def begin(self):
        for k in range(PARTS):
            self.send(self.f, k, 1, 1)
            self.send(self.f, (k + PARTS // 2) % PARTS, 2, 2)
        for k in range(PARTS):
            self.send(self.f, k, 0, 0)

    def arrive(self, slot, j):
        self.on[slot, j].wait_recv()

    def advance(self, k):
        jx, jy = k, (k + PARTS // 2) % PARTS
        self.arrive(1, jx)
        if jx < PARTS // 2:
            self.send(self.f ^ ALONG_X, jx, 2, 6)
        self.send(self.f ^ ALONG_X, jx, 0, 3)
        self.arrive(2, jy)
        if jy >= PARTS // 2:
            self.send(self.f ^ ALONG_Y, jy, 1, 6)
        self.send(self.f ^ ALONG_Y, jy, 0, 4)

    def far(self):
        for k in range(PARTS // 2):
            for j in (k, k + PARTS // 2):
                self.arrive(6, j)
                self.send(self.f ^ ALONG_X ^ ALONG_Y, j, 0, 5)

    def wait_core(self, *slots):
        for slot in slots:
            for j in range(PARTS):
                self.arrive(slot, j)

    def finish(self):
        for c in self.copies:
            c.wait_send()


GATHER_SEMAPHORES = [pltpu.SemaphoreType.DMA((7, PARTS)), pltpu.SemaphoreType.DMA((7, PARTS))]


class PlaneSum:
    masks = (ALONG_X ^ ALONG_Y, ALONG_X, ALONG_Y, 0)

    def __init__(self, stage, other, held, from_x, from_y, last, sent, arrived):
        self.f, self.t = lax.axis_index("fsdp"), lax.axis_index("tp")
        self.stage, self.other, self.held = stage, other, held
        self.from_x, self.from_y, self.last = from_x, from_y, last
        self.sent, self.arrived = sent, arrived
        self.near = [(self.f ^ k, self.t) for k in (CORE, ALONG_X, ALONG_Y)]
        self.copies, self.on = [], {}
        half = held.shape[1] // 2
        self.top, self.low = pl.ds(0, half), pl.ds(half, half)

    def send(self, source, target, slot, way):
        c = remote(source, target, self.sent.at[slot], self.arrived.at[slot], self.near[way])
        c.start()
        self.copies.append(c)
        self.on[slot] = c

    def begin(self, write_part, after=None):
        for i, mask in enumerate(self.masks):
            if i >= 2:
                self.on[i - 2].wait_send()
                self.copies = [c for c in self.copies if c is not self.on[i - 2]]
            write_part(self.f ^ CORE ^ mask, self.stage.at[i % 2])
            self.send(self.stage.at[i % 2], self.other.at[i], i, 0)
            write_part(self.f ^ mask, self.held.at[i])
            if after is not None:
                after(i)
            self.on[i].wait_recv()
            self.held[i] = (
                self.held[i].astype(jnp.float32) + self.other[i].astype(jnp.float32)
            ).astype(jnp.bfloat16)
            if i == 0:
                self.send(self.held.at[0, self.top], self.from_x.at[0], 4, 1)
                self.send(self.held.at[0, self.low], self.from_y.at[0], 5, 2)
            if i == 1:
                self.send(self.held.at[1, self.top], self.from_x.at[1], 6, 1)
            if i == 2:
                self.send(self.held.at[2, self.low], self.from_y.at[1], 7, 2)

    def turn(self):
        self.on[4].wait_recv()
        self.held[2, self.top] = (
            self.held[2, self.top].astype(jnp.float32) + self.from_x[0].astype(jnp.float32)
        ).astype(jnp.bfloat16)
        self.send(self.held.at[2, self.top], self.last.at[0], 8, 2)
        self.on[5].wait_recv()
        self.held[1, self.low] = (
            self.held[1, self.low].astype(jnp.float32) + self.from_y[0].astype(jnp.float32)
        ).astype(jnp.bfloat16)
        self.send(self.held.at[1, self.low], self.last.at[1], 9, 1)

    def end(self, total):
        for rows, first, second, take in (
            (self.top, 6, 8, lambda: self.from_x[1]),
            (self.low, 7, 9, lambda: self.from_y[1]),
        ):
            self.on[first].wait_recv()
            part = self.held[3, rows].astype(jnp.float32) + take().astype(jnp.float32)
            self.on[second].wait_recv()
            total[rows] = part + self.last[second - 8].astype(jnp.float32)

    def finish(self):
        for c in self.copies:
            c.wait_send()


def sum_scratch(height, width):
    chunks = [pltpu.VMEM((n, height, width), jnp.bfloat16) for n in (2, 4, 4)]
    return chunks + [pltpu.VMEM((2, height // 2, width), jnp.bfloat16)] * 3 + [pltpu.SemaphoreType.DMA((10,)), pltpu.SemaphoreType.DMA((10,))]


NARROW = 1024


def chunk_part(pairs, size):
    def write_part(owner, ref):
        lanes = columns(owner, size)
        lefts = [left[:, lanes] for left, _ in pairs]

        def step(n, carry):
            wide = columns(n, NARROW)
            total = inner_rows(lefts[0], pairs[0][1][:, wide])
            for left, (_, right) in zip(lefts[1:], pairs[1:]):
                total += inner_rows(left, right[:, wide])
            ref[:, wide] = total.astype(jnp.bfloat16)
            return carry

        lax.fori_loop(0, ref.shape[1] // NARROW, step, 0)

    return write_part


def plane_greet():
    f, t = lax.axis_index("fsdp"), lax.axis_index("tp")
    greet([(f ^ k, t) for k in (CORE, ALONG_X, ALONG_Y)])


def forward_output(attended, output_rows, tokens, gain, dys, down_all, number):
    size, width = tokens.shape
    units = down_all.shape[2]
    f32, bf16 = jnp.float32, jnp.bfloat16

    def kernel(
        o_ref, x_ref, gain_ref, w_hbm, dys_hbm, down_hbm,
        middle_ref, row_ref, dh_ref,
        stage, other, held, from_x, from_y, last, sum_sent, sum_arrived,
        dys, down_w, dys_sem, load_sem, dh, dh_sem, w, w_sem,
    ):
        load = pltpu.make_async_copy(dys_hbm, dys, dys_sem)
        loads = unit_loads(lambda j: down_hbm.at[:, j], down_w, load_sem)
        output_loads = column_loads(w_hbm, w, w_sem)
        for c in output_loads + loads + [load]:
            c.start()
        plane_greet()
        for c in output_loads:
            c.wait()
        total = PlaneSum(stage, other, held, from_x, from_y, last, sum_sent, sum_arrived)
        total.begin(chunk_part([(o_ref, w)], size))
        for c in loads + [load]:
            c.wait()

        def out_copy(i):
            return pltpu.make_async_copy(dh.at[i], dh_ref.at[i], dh_sem.at[i])

        def grad_chunk(i, carry):
            dh[i] = outer_cols(as_rows(down_w), dys[i])
            out_copy(i).start()
            return carry

        lax.fori_loop(0, 6, grad_chunk, 0)
        total.turn()
        lax.fori_loop(6, 8, grad_chunk, 0)
        total.end(middle_ref)
        middle = x_ref[...].astype(f32) + middle_ref[...]
        middle_ref[...] = middle
        inverse = lax.rsqrt(jnp.mean(middle * middle, axis=1, keepdims=True) + epsilon)
        row_ref[...] = (middle * inverse * gain_ref[...]).astype(bf16)
        for i in range(8):
            out_copy(i).wait()
        total.finish()

    dma = pltpu.SemaphoreType.DMA
    chunks = (8, 4 * units, size)
    return pl.pallas_call(
        kernel,
        out_shape=[
            jax.ShapeDtypeStruct((size, width), f32),
            jax.ShapeDtypeStruct((size, width), bf16),
            jax.ShapeDtypeStruct(chunks, f32),
        ],
        in_specs=[IN_VMEM] * 3 + [ANYWHERE] * 3,
        out_specs=[IN_VMEM] * 2 + [ANYWHERE],
        scratch_shapes=sum_scratch(size, width)
        + [
            pltpu.VMEM((8, size, width), bf16),
            pltpu.VMEM((4, units, width), bf16),
            dma,
            dma((8,)),
            pltpu.VMEM(chunks, f32),
            dma((8,)),
            pltpu.VMEM((attended.shape[0], width), bf16),
            dma((8,)),
        ],
        compiler_params=comm_params(number, VMEM_MOST),
        cost_estimate=lasting(45),
        name="forward_output",
    )(attended, tokens, gain, output_rows, dys, down_all)


def forward_hidden(row, dys, dh_all, gate_up, number):
    size, width = row.shape
    quarter = gate_up.shape[3]
    units = 4 * quarter
    f32, bf16 = jnp.float32, jnp.bfloat16

    def kernel(
        row_ref, dys_hbm, dh_hbm, gate_up_hbm,
        rows_ref, hidden_ref, dgate_ref, dup_ref, down_grad_ref,
        rows, rows_sent, rows_arrived, dys, gate_w, up_w, load_sem, unit_sem, dh, out, out_sem, keep_sem, down_grad,
    ):
        f = lax.axis_index("fsdp")
        loads = [
            pltpu.make_async_copy(source, target, load_sem.at[i])
            for i, (source, target) in enumerate(((dys_hbm, dys), (dh_hbm, dh)))
        ]
        for i, w in enumerate((gate_w, up_w)):
            loads += unit_loads(lambda j, i=i: gate_up_hbm.at[:, j, i], w, unit_sem.at[i])
        for load in loads:
            load.start()
        rows[f] = row_ref[...]
        plane_greet()
        gather_rows = PlaneGather(rows, rows_sent, rows_arrived)
        gather_rows.begin()
        for load in loads:
            load.wait()

        half = size // 2
        halves = (slice(0, half), slice(half, size))

        def owners(i, crossed):
            return f ^ i, f ^ (i ^ ALONG_X ^ ALONG_Y if crossed else i)

        def out_copies(slot, pair):
            return [
                pltpu.make_async_copy(
                    out.at[slot, n, :, lanes],
                    target.at[
                        :, pl.ds(pl.multiple_of(owner * size + side * half, half), half)
                    ],
                    out_sem.at[slot, n, side],
                )
                for n, target in enumerate((hidden_ref, dgate_ref, dup_ref))
                for side, (owner, lanes) in enumerate(zip(pair, halves))
            ]

        def unit(crossed):
            def body(i, carry):
                pair = owners(i, crossed)
                slot = lax.rem(i, 2)

                @pl.when(i >= 2)
                def _():
                    for c in out_copies(slot, pair):
                        c.wait()

                right = jnp.concatenate([rows[o, r] for o, r in zip(pair, halves)], axis=0)
                gate = outer_cols(as_rows(gate_w), right)
                up = outer_cols(as_rows(up_w), right)
                sigmoid = jax.nn.sigmoid(gate)
                active = gate * sigmoid
                grad = jnp.concatenate([dh[o, :, r] for o, r in zip(pair, halves)], axis=1)
                hidden = (active * up).astype(bf16)
                out[slot, 0] = hidden
                out[slot, 1] = (grad * up * sigmoid * (1.0 + gate * (1.0 - sigmoid))).astype(bf16)
                out[slot, 2] = (grad * active).astype(bf16)
                for c in out_copies(slot, pair):
                    c.start()
                cotangent = jnp.concatenate([dys[o, r] for o, r in zip(pair, halves)], axis=0)
                down_grad[...] += dot_nn(hidden, cotangent)
                return carry

            return body

        def take(*pieces):
            for slot, j in pieces:
                gather_rows.arrive(slot, j)

        down_grad[...] = jnp.zeros_like(down_grad)
        gather_rows.advance(0)
        lax.fori_loop(0, 1, unit(False), 0)
        gather_rows.advance(1)
        gather_rows.wait_core(0)
        lax.fori_loop(1, 2, unit(False), 0)
        lax.fori_loop(2, 3, unit(True), 0)
        gather_rows.advance(2)
        take((3, 0), (3, 1), (4, 2), (4, 3))
        lax.fori_loop(3, 4, unit(True), 0)
        gather_rows.advance(3)
        lax.fori_loop(4, 5, unit(True), 0)
        take((3, 2), (3, 3), (4, 0), (4, 1))
        lax.fori_loop(5, 6, unit(True), 0)
        gather_rows.far()
        lax.fori_loop(6, 7, unit(False), 0)
        gather_rows.wait_core(5)
        keep = pltpu.make_async_copy(rows, rows_ref, keep_sem)
        keep.start()
        lax.fori_loop(7, 8, unit(False), 0)
        for j in range(8):
            part = down_grad[:, j * size : (j + 1) * size].astype(bf16)
            down_grad_ref[:, j] = part.reshape(4, quarter, size)
        for i in (6, 7):
            for c in out_copies(i % 2, owners(i, False)):
                c.wait()
        keep.wait()
        gather_rows.finish()

    store = pltpu.VMEM((8, size, width), bf16)
    weights = pltpu.VMEM((4, quarter, width), bf16)
    return pl.pallas_call(
        kernel,
        out_shape=[jax.ShapeDtypeStruct((8, size, width), bf16)]
        + [jax.ShapeDtypeStruct((units, 8 * size), bf16)] * 3
        + [jax.ShapeDtypeStruct((4, 8, quarter, size), bf16)],
        in_specs=[IN_VMEM] + [ANYWHERE] * 3,
        out_specs=[ANYWHERE] * 4 + [IN_VMEM],
        scratch_shapes=[store]
        + GATHER_SEMAPHORES
        + [store]
        + [weights] * 2
        + [
            pltpu.SemaphoreType.DMA((2,)),
            pltpu.SemaphoreType.DMA((2, 8)),
            pltpu.VMEM((8, units, size), f32),
            pltpu.VMEM((2, 3, units, size), bf16),
            pltpu.SemaphoreType.DMA((2, 3, 2)),
            pltpu.SemaphoreType.DMA,
            pltpu.VMEM((units, width), f32),
        ],
        compiler_params=comm_params(number, VMEM_MOST),
        cost_estimate=lasting(50),
        name="forward_hidden",
    )(row, dys, dh_all, gate_up)


def backward_middle(
    dgate, dup, gate_up, rows, dys, output_rows, attended, middle, gain, number
):
    size, width = middle.shape
    quarter = gate_up.shape[3]
    units = 4 * quarter
    depth = output_rows.shape[1]
    blocks = width // size
    f32, bf16 = jnp.float32, jnp.bfloat16
    early = 5

    def kernel(
        dgate_hbm, dup_hbm, gate_up_hbm, rows_hbm,
        dys_hbm, w_hbm, o_ref, middle_ref, gain_ref,
        grad_ref, gain_grad_ref, grad_o_ref, do_ref, gate_g_ref, up_g_ref,
        stage, other, held, from_x, from_y, last, sum_sent, sum_arrived,
        store, store_sent, store_arrived,
        dgate_v, dup_v, gate_w, up_w, load_sem, unit_sem,
        tall, tall_sem, out, out_sem, o_sum, dy, dy_sem, w_ref, w_sem,
    ):
        f = lax.axis_index("fsdp")
        loads = [
            pltpu.make_async_copy(source, target, load_sem.at[i])
            for i, (source, target) in enumerate(((dgate_hbm, dgate_v), (dup_hbm, dup_v)))
        ]
        for i, w in enumerate((gate_w, up_w)):
            loads += unit_loads(lambda j, i=i: gate_up_hbm.at[:, j, i], w, unit_sem.at[i])
        for load in loads:
            load.start()

        load_dy = pltpu.make_async_copy(dys_hbm.at[f], dy, dy_sem)
        load_dy.start()
        output_loads = column_loads(w_hbm, w_ref, w_sem)
        for c in output_loads:
            c.start()

        def tall_load(n, slot):
            return pltpu.make_async_copy(
                rows_hbm.at[:, :, columns(n, size)], tall.at[slot], tall_sem.at[slot]
            )

        tall_load(0, 0).start()
        plane_greet()
        total = PlaneSum(stage, other, held, from_x, from_y, last, sum_sent, sum_arrived)
        gather = PlaneGather(store, store_sent, store_arrived)
        for load in loads:
            load.wait()
        total.begin(chunk_part([(dgate_v, Rows(gate_w)), (dup_v, Rows(up_w))], size))
        total.turn()

        def out_copies(n, slot):
            return [
                pltpu.make_async_copy(
                    out.at[slot, i], target.at[:, n], out_sem.at[slot, i]
                )
                for i, target in enumerate((gate_g_ref, up_g_ref))
            ]

        def block(n, carry):
            slot = lax.rem(n, 2)

            @pl.when(n + 1 < blocks)
            def _():
                tall_load(n + 1, 1 - slot).start()

            tall_load(n, slot).wait()

            @pl.when(n >= 2)
            def _():
                for c in out_copies(n, slot):
                    c.wait()

            row_cols = tall[slot].reshape(8 * size, size)
            for i, left in enumerate((dgate_v, dup_v)):
                out[slot, i] = dot_nn(left[...], row_cols).astype(bf16).reshape(4, quarter, size)
            for c in out_copies(n, slot):
                c.start()
            return carry

        lax.fori_loop(0, early, block, 0)
        total.end(grad_ref)
        middle = middle_ref[...]
        inverse = lax.rsqrt(jnp.mean(middle * middle, axis=1, keepdims=True) + epsilon)
        normed = middle * inverse
        grad = grad_ref[...]
        gain_grad_ref[...] = jnp.sum(grad * normed, axis=0, keepdims=True)
        load_dy.wait()
        for c in output_loads:
            c.wait()
        grad = dy[...].astype(f32) + norm_back(grad, gain_ref[...], normed, inverse)
        grad_ref[...] = grad
        store[f] = grad.astype(bf16)
        gather.begin()
        gather.advance(0)
        lax.fori_loop(early, early + 1, block, 0)
        gather.advance(1)
        lax.fori_loop(early + 1, early + 2, block, 0)
        gather.advance(2)
        lax.fori_loop(early + 2, blocks, block, 0)
        gather.advance(3)

        def chunk(i, carry):
            owner = f ^ i
            lanes = columns(owner, size)
            do_ref[:, lanes] = outer_cols(w_ref[...], store[owner]).astype(bf16)
            o_sum[...] += dot_nn(o_ref[:, lanes], store[owner])
            return carry

        o_sum[...] = jnp.zeros_like(o_sum)
        gather.wait_core(0)
        lax.fori_loop(0, 2, chunk, 0)
        gather.wait_core(3, 4)
        lax.fori_loop(2, 6, chunk, 0)
        gather.far()
        gather.wait_core(5)
        lax.fori_loop(6, 8, chunk, 0)
        for j in range(8):
            grad_o_ref[j] = o_sum[:, j * size : (j + 1) * size].astype(bf16)
        for n in (blocks - 2, blocks - 1):
            for c in out_copies(n, n % 2):
                c.wait()
        total.finish()
        gather.finish()

    tall_units = pltpu.VMEM((units, width), bf16)
    weights = pltpu.VMEM((4, quarter, width), bf16)
    return pl.pallas_call(
        kernel,
        out_shape=[
            jax.ShapeDtypeStruct((size, width), f32),
            jax.ShapeDtypeStruct((1, width), f32),
            jax.ShapeDtypeStruct((8, depth, size), bf16),
            jax.ShapeDtypeStruct((depth, 8 * size), bf16),
        ]
        + [jax.ShapeDtypeStruct((4, blocks, quarter, size), bf16)] * 2,
        in_specs=[ANYWHERE] * 6 + [IN_VMEM] * 3,
        out_specs=[IN_VMEM] * 4 + [ANYWHERE] * 2,
        scratch_shapes=sum_scratch(size, width)
        + [pltpu.VMEM((8, size, width), bf16)]
        + GATHER_SEMAPHORES
        + [tall_units] * 2
        + [weights] * 2
        + [
            pltpu.SemaphoreType.DMA((2,)),
            pltpu.SemaphoreType.DMA((2, 8)),
            pltpu.VMEM((2, 8, size, size), bf16),
            pltpu.SemaphoreType.DMA((2,)),
            pltpu.VMEM((2, 2, 4, quarter, size), bf16),
            pltpu.SemaphoreType.DMA((2, 2)),
            pltpu.VMEM((depth, width), f32),
            pltpu.VMEM((size, width), bf16),
            pltpu.SemaphoreType.DMA,
            pltpu.VMEM((depth, width), bf16),
            pltpu.SemaphoreType.DMA((8,)),
        ],
        compiler_params=comm_params(number, VMEM_MOST),
        cost_estimate=lasting(92),
        name="backward_middle",
    )(dgate, dup, gate_up, rows, dys, output_rows, attended, middle, gain)


class LineGather:
    def __init__(self, own, store, sent, arrived):
        self.f, self.t = lax.axis_index("fsdp"), lax.axis_index("tp")
        self.own, self.store, self.sent, self.arrived = own, store, sent, arrived

    def copy(self, way, hop):
        step = 1 if way == 0 else -1
        place = self.store.at[self.t - step * (hop - 1)]
        source = self.own if hop == 1 else place
        return remote(
            source, place, self.sent.at[way, hop], self.arrived.at[way, hop], (self.f, self.t + step)
        )

    def goes(self, way, hop):
        if way == 0:
            return (self.t < 3) & (self.t >= hop - 1)
        return (self.t > 0) & (self.t <= 4 - hop)

    def came(self, way, hop):
        return self.t >= hop if way == 0 else self.t <= 3 - hop

    def send(self, hop):
        for way in (0, 1):
            pl.when(self.goes(way, hop))(lambda way=way: self.copy(way, hop).start())

    def begin(self):
        self.send(1)

    def take(self, hop):
        for way in (0, 1):

            @pl.when(self.came(way, hop))
            def _(way=way):
                spot = self.store.at[self.t - hop if way == 0 else self.t + hop]
                remote(
                    spot, spot, self.sent.at[way, hop], self.arrived.at[way, hop], (self.f, self.t)
                ).wait_recv()

        if hop < 3:
            self.send(hop + 1)

    def finish(self):
        for hop in (1, 2, 3):
            for way in (0, 1):
                pl.when(self.goes(way, hop))(lambda way=way, hop=hop: self.copy(way, hop).wait_send())


LINE_SEMAPHORES = [pltpu.SemaphoreType.DMA((2, 4)), pltpu.SemaphoreType.DMA((2, 4))]


def everyone(f, t):
    return [(f ^ k, t) for k in range(1, 8)] + [(f, lax.rem(t + k, 4)) for k in (1, 2, 3)]


def unit_loads(source, target, sems):
    block = target.shape[2] // 8
    return [
        pltpu.make_async_copy(source(j), target.at[:, :, pl.ds(j * block, block)], sems.at[j])
        for j in range(8)
    ]


class Rows:
    def __init__(self, ref):
        self.ref = ref

    def __getitem__(self, index):
        block = self.ref[:, :, index[1]]
        return block.reshape(4 * block.shape[1], block.shape[2])


def column_loads(source, target, sems):
    block = source.shape[2]
    return [
        pltpu.make_async_copy(source.at[j], target.at[:, pl.ds(j * block, block)], sems.at[j])
        for j in range(8)
    ]


def as_rows(ref):
    return ref[...].reshape(4 * ref.shape[1], ref.shape[2])


def turn_heads(values, cosine, sine_table):
    half = HEAD_DIM // 2
    turned = []
    for h in range(values.shape[0] // HEAD_DIM):
        first = values[h * HEAD_DIM : h * HEAD_DIM + half]
        second = values[h * HEAD_DIM + half : (h + 1) * HEAD_DIM]
        turned.append(first * cosine - second * sine_table)
        turned.append(second * cosine + first * sine_table)
    return jnp.concatenate(turned, axis=0)


def first_forms(gate, up, query, key_rows, value_rows):
    bf16, f32 = jnp.bfloat16, jnp.float32
    block, hidden = gate.shape
    across = query.shape[1]
    units = hidden // 8

    def turned(ref):
        return ref[...].astype(f32).T.astype(bf16)

    def kernel(gate_ref, up_ref, q_ref, k_ref, v_ref, units_ref, inner_ref):
        inner_ref[:across] = turned(q_ref)
        inner_ref[across : across + HEAD_DIM] = k_ref[...]
        inner_ref[across + HEAD_DIM :] = v_ref[...]
        units_ref[:, 0] = turned(gate_ref).reshape(8, units, block)
        units_ref[:, 1] = turned(up_ref).reshape(8, units, block)

    return pl.pallas_call(
        kernel,
        out_shape=[
            jax.ShapeDtypeStruct((8, 2, units, block), bf16),
            jax.ShapeDtypeStruct((across + 2 * HEAD_DIM, block), bf16),
        ],
        in_specs=[IN_VMEM] * 5,
        out_specs=[IN_VMEM] * 2,
        compiler_params=pltpu.CompilerParams(vmem_limit_bytes=VMEM_MOST),
        cost_estimate=lasting(5),
        name="first_forms",
    )(gate, up, query, key_rows, value_rows)


def first_rows(tokens, gains_own, inner_all, output_own, cosine, sine_table, grads, valid, number):
    size, width = tokens.shape
    block = width // 8
    quarter_rows = output_own.shape[0]
    depth = quarter_rows // 2
    pair_rows = 2 * HEAD_DIM
    f32, bf16 = jnp.float32, jnp.bfloat16

    def kernel(
        x_ref, gains_own_ref, inner_ref, own_ref, cos_ref, sin_ref, dy_ref, valid_ref,
        rows_ref, q_ref, pair_ref, w_ref, wo_all, dys_ref, gains_ref,
        rows, rows_sent, rows_arrived, dys, dys_sent, dys_arrived, pair_v,
        w_sent, w_arrived, z_sent, z_arrived,
        p_sent, p_arrived, on_sent, on_arrived, g_sent, g_arrived, kept_sem,
    ):
        f, t = lax.axis_index("fsdp"), lax.axis_index("tp")
        gains_ref[f] = gains_own_ref[...]
        place = columns(f, block)
        far_first = (6, 7, 2, 4, 3, 5, 1)

        def inner_slices(j):
            quarter, side = lax.div(j, 2), lax.rem(j, 2)
            return [
                (
                    inner_ref.at[quarter, pl.ds(pl.multiple_of(side * depth, depth), depth)],
                    w_ref.at[pl.ds(0, depth), place],
                ),
                (
                    inner_ref.at[quarter, pl.ds(2 * depth, pair_rows)],
                    w_ref.at[pl.ds(depth, pair_rows), place],
                ),
            ]

        kept = [
            pltpu.make_async_copy(s, o, kept_sem.at[i]) for i, (s, o) in enumerate(inner_slices(f))
        ]
        kept.append(pltpu.make_async_copy(own_ref, wo_all.at[t], kept_sem.at[2]))
        for c in kept:
            c.start()
        greet(everyone(f, t))
        line_output = LineGather(own_ref, wo_all, z_sent, z_arrived)
        line_output.begin()
        weights, gains = [], []
        for k in far_first:
            c = remote(
                gains_own_ref, gains_ref.at[f], g_sent.at[k], g_arrived.at[k], (f ^ k, t)
            )
            c.start()
            gains.append(c)
        for k in far_first:
            for i, (s, o) in enumerate(inner_slices(f ^ k)):
                c = remote(s, o, w_sent.at[k, i], w_arrived.at[k, i], (f ^ k, t))
                c.start()
                weights.append(c)
        wide = x_ref[...].astype(f32)
        inverse = lax.rsqrt(jnp.mean(wide * wide, axis=1, keepdims=True) + epsilon)
        for c in gains:
            c.wait()
        gain = jnp.concatenate([gains_ref[j, 0:1] for j in range(8)], axis=1)
        rows[f] = (wide * inverse * gain).astype(bf16)
        gather = PlaneGather(rows, rows_sent, rows_arrived)
        gather.begin()
        dys[f] = jnp.where(valid_ref[...] > 0, dy_ref[...].astype(f32), 0.0).astype(bf16)
        for k in range(PARTS):
            gather.advance(k)
            if k in (2, 3):
                line_output.take(k - 1)
        gather_dys = PlaneGather(dys, dys_sent, dys_arrived)
        gather_dys.begin()
        for c in kept[:2]:
            c.wait()
        for c in weights:
            c.wait_recv()

        def chunk(i, carry):
            owner = f ^ i
            lanes = columns(owner, size)
            projected = outer_cols(w_ref[...], rows[owner])
            cosine, sine = cos_ref[:, lanes], sin_ref[:, lanes]
            queries = turn_heads(projected[:depth], cosine, sine).astype(bf16)
            q_ref[:, lanes] = (queries.astype(f32) * HEAD_DIM ** (-0.5)).astype(bf16)
            keys = turn_heads(projected[depth : depth + HEAD_DIM], cosine, sine)
            pair = jnp.concatenate([keys, projected[depth + HEAD_DIM :]], axis=0)
            pair_v[owner] = pair.T.astype(bf16)
            return carry

        spread = []

        def spread_pair(i):
            for k in (2, 1, 3):
                c = remote(
                    pair_v.at[f ^ i],
                    pair_ref.at[t, f ^ i],
                    p_sent.at[i // 2, k],
                    p_arrived.at[i // 2, k],
                    (f, lax.rem(t + k, 4)),
                )
                c.start()
                spread.append((i, k, c))

        gather.wait_core(0)
        lax.fori_loop(0, 2, chunk, 0)
        spread_pair(0)
        gather.wait_core(3, 4)
        lax.fori_loop(2, 6, chunk, 0)
        spread_pair(2)
        spread_pair(4)
        gather.far()
        gather.wait_core(5)
        lax.fori_loop(6, 8, chunk, 0)
        spread_pair(6)
        own_pair = pltpu.make_async_copy(pair_v, pair_ref.at[t], kept_sem.at[3])
        own_pair.start()
        keep_rows = pltpu.make_async_copy(rows, rows_ref, kept_sem.at[4])
        keep_rows.start()
        for k in range(PARTS):
            gather_dys.advance(k)
        passed = []
        for i, k, c in spread:
            c.wait_recv()
            spot = pair_ref.at[lax.rem(t + 4 - k, 4), f ^ i]
            d = remote(spot, spot, on_sent.at[i // 2, k], on_arrived.at[i // 2, k], (f ^ CORE, t))
            d.start()
            passed.append(d)
        gather_dys.wait_core(0, 3, 4)
        gather_dys.far()
        gather_dys.wait_core(5)
        keep_dys = pltpu.make_async_copy(dys, dys_ref, kept_sem.at[6])
        keep_dys.start()
        line_output.take(3)
        for c in passed:
            c.wait()
        for c in weights + [c for _, _, c in spread]:
            c.wait_send()
        line_output.finish()
        gather.finish()
        gather_dys.finish()
        own_pair.wait()
        keep_rows.wait()
        kept[2].wait()
        keep_dys.wait()

    dma = pltpu.SemaphoreType.DMA
    return pl.pallas_call(
        kernel,
        out_shape=[
            jax.ShapeDtypeStruct((8, size, width), bf16),
            jax.ShapeDtypeStruct((depth, 8 * size), bf16),
            jax.ShapeDtypeStruct((4, 8, size, pair_rows), bf16),
            jax.ShapeDtypeStruct((depth + pair_rows, width), bf16),
            jax.ShapeDtypeStruct((4, quarter_rows, block), bf16),
            jax.ShapeDtypeStruct((8, size, width), bf16),
            jax.ShapeDtypeStruct((8, *gains_own.shape), f32),
        ],
        in_specs=[IN_VMEM, IN_VMEM, ANYWHERE, ANYWHERE] + [IN_VMEM] * 4,
        out_specs=[ANYWHERE, IN_VMEM, ANYWHERE, IN_VMEM, ANYWHERE, ANYWHERE, IN_VMEM],
        scratch_shapes=[pltpu.VMEM((8, size, width), bf16)]
        + GATHER_SEMAPHORES
        + [pltpu.VMEM((8, size, width), bf16)]
        + GATHER_SEMAPHORES
        + [
            pltpu.VMEM((8, size, pair_rows), bf16),
            dma((8, 2)),
            dma((8, 2)),
            *LINE_SEMAPHORES,
            dma((4, 4)),
            dma((4, 4)),
            dma((4, 4)),
            dma((4, 4)),
            dma((8,)),
            dma((8,)),
            dma((7,)),
        ],
        compiler_params=comm_params(number, VMEM_MOST),
        cost_estimate=lasting(100),
        name="first_rows",
    )(tokens, gains_own, inner_all, output_own, cosine, sine_table, grads, valid)


def grads_across(left_ref, rows_v, out_v, target_ref, sent, arrived, kept_sem):
    f, t = lax.axis_index("fsdp"), lax.axis_index("tp")
    _, size, width = rows_v.shape
    block = width // 8
    copies = []

    def step(k):
        right = rows_v[:, :, columns(f ^ k, block)].reshape(8 * size, block)
        out_v[k] = dot_nn(left_ref[...], right).astype(jnp.bfloat16)
        if k:
            c = remote(out_v.at[k], target_ref.at[f], sent.at[k], arrived.at[k], (f ^ k, t))
        else:
            c = pltpu.make_async_copy(out_v.at[0], target_ref.at[f], kept_sem)
        c.start()
        copies.append(c)

    return step, copies


def exchange_begin(ways, sent, arrived, kept_sem):
    f, t = lax.axis_index("fsdp"), lax.axis_index("tp")
    copies = []
    for i, (source, target) in enumerate(ways):
        for k in (6, 7, 2, 4, 3, 5, 1):
            copies.append(
                remote(
                    source.at[f ^ k], target.at[f], sent.at[k, i], arrived.at[k, i], (f ^ k, t)
                )
            )
        copies.append(pltpu.make_async_copy(source.at[f], target.at[f], kept_sem.at[i]))
    for c in copies:
        c.start()
    return copies


def backward_pairs(pair_parts, hidden, down_all, middle, valid, grad_query, rows, cosine, sine_table, number):
    size, width = middle.shape
    units = hidden.shape[0]
    depth = grad_query.shape[0]
    _, chunks, height, _ = pair_parts.shape
    half = chunks // 2
    f32, bf16 = jnp.float32, jnp.bfloat16

    def kernel(
        p_ref, hidden_hbm, down_hbm, middle_ref, valid_ref, g_ref, rows_hbm, cos_ref, sin_ref,
        single_ref, out_ref, spread_ref,
        stage, other, held, from_x, from_y, last, sum_sent, sum_arrived,
        hidden_v, down_w, load_sem, unit_sem, ra, s, rz, sent, arrived, share, pair,
        rows_v, w_grad, w_sent, w_arrived,
    ):
        f, t = lax.axis_index("fsdp"), lax.axis_index("tp")
        loads = [pltpu.make_async_copy(hidden_hbm, hidden_v, load_sem.at[0])]
        loads += unit_loads(lambda j: down_hbm.at[:, j], down_w, unit_sem)
        load_rows = pltpu.make_async_copy(rows_hbm, rows_v, load_sem.at[1])
        for c in loads + [load_rows]:
            c.start()
        side = lax.rem(f, 2)
        mine, theirs = pl.ds(side * half, half), pl.ds((1 - side) * half, half)
        core = (f ^ CORE, t)
        greet(everyone(f, t))
        first = []
        for k in (2, 1, 3, 0):
            plane = lax.rem(t + k, 4)
            c = remote(p_ref.at[plane, theirs], ra.at[k], sent.at[k], arrived.at[k], core)
            c.start()
            first.append((k, c))
        out = []
        for k, c in first:
            c.wait_recv()
            plane = lax.rem(t + k, 4)
            both = p_ref[plane, mine].astype(f32) + ra[k].astype(f32)
            if k:
                s[k] = both.astype(bf16)
                d = remote(s.at[k], rz.at[k], sent.at[3 + k], arrived.at[3 + k], (f, plane))
                d.start()
                out.append((k, d))
            else:
                pair[mine] = both
        for c in loads:
            c.wait()
        total = PlaneSum(stage, other, held, from_x, from_y, last, sum_sent, sum_arrived)
        total.begin(chunk_part([(hidden_v, Rows(down_w))], size))
        load_rows.wait()
        query_grads, copies = grads_across(
            g_ref, rows_v, w_grad, spread_ref, w_sent, w_arrived, load_sem.at[2]
        )
        for k in (6, 7, 2, 4, 3, 5, 1, 0):
            query_grads(k)
        total.turn()
        for k, d in out:
            d.wait_recv()
            pair[mine] += rz[k].astype(f32)
        back = remote(pair.at[mine], pair.at[mine], sent.at[7], arrived.at[7], core)
        back.start()
        back.wait()
        for j in range(chunks):
            lanes = slice(j * size, (j + 1) * size)
            keys = turn_heads(pair[j, :HEAD_DIM], cos_ref[:, lanes], -sin_ref[:, lanes])
            single_ref[:, lanes] = jnp.where(side == 0, keys, pair[j, HEAD_DIM:]).astype(bf16)
        total.end(share)
        out_ref[...] = jnp.where(valid_ref[...] > 0, middle_ref[...] + share[...], 0.0).astype(bf16)
        for c in copies:
            c.wait()
        for k, c in first + out:
            c.wait_send()
        total.finish()

    dma = pltpu.SemaphoreType.DMA
    return pl.pallas_call(
        kernel,
        out_shape=[
            jax.ShapeDtypeStruct((HEAD_DIM, chunks * size), bf16),
            jax.ShapeDtypeStruct((size, width), bf16),
            jax.ShapeDtypeStruct((8, depth, width // 8), bf16),
        ],
        in_specs=[IN_VMEM, ANYWHERE, ANYWHERE, IN_VMEM, IN_VMEM, IN_VMEM, ANYWHERE, IN_VMEM, IN_VMEM],
        out_specs=[IN_VMEM, IN_VMEM, ANYWHERE],
        scratch_shapes=sum_scratch(size, width)
        + [pltpu.VMEM((units, 8 * size), bf16), pltpu.VMEM((4, units // 4, width), bf16)]
        + [dma((3,)), dma((8,))]
        + [pltpu.VMEM((4, half, height, size), bf16)] * 3
        + [dma((8,)), dma((8,)), pltpu.VMEM((size, width), f32)]
        + [
            pltpu.VMEM((chunks, height, size), f32),
            pltpu.VMEM((8, size, width), bf16),
            pltpu.VMEM((8, depth, width // 8), bf16),
            dma((8,)),
            dma((8,)),
        ],
        compiler_params=comm_params(number, VMEM_MOST),
        cost_estimate=lasting(55),
        name="backward_pairs",
    )(pair_parts, hidden, down_all, middle, valid, grad_query, rows, cosine, sine_table)


def backward_first(
    grad_query, single, weights, rows, tokens, grad_middle, gain, down_grads, gate_grads, number
):
    size, width = tokens.shape
    depth = grad_query.shape[0]
    block = width // 8
    f32, bf16 = jnp.float32, jnp.bfloat16

    def kernel(
        g_ref, single_ref, w_ref, rows_hbm, x_ref, middle_ref, gain_ref, down_ref, gate_ref,
        tokens_grad_ref, gain_grad_ref, spread_ref, own_down_ref, own_gate_ref,
        stage, other, held, from_x, from_y, last, sum_sent, sum_arrived,
        rows_v, load_sem, w_grad, sent, arrived, single_w, e_sent, e_arrived, e_kept,
    ):
        f, t = lax.axis_index("fsdp"), lax.axis_index("tp")
        load = pltpu.make_async_copy(rows_hbm, rows_v, load_sem.at[0])
        load.start()
        side = lax.rem(f, 2)
        single_w[...] = w_ref[
            pl.ds(pl.multiple_of(depth + side * HEAD_DIM, HEAD_DIM), HEAD_DIM), :
        ]
        greet([(f ^ k, t) for k in range(1, 8)])
        total = PlaneSum(stage, other, held, from_x, from_y, last, sum_sent, sum_arrived)
        total.begin(chunk_part([(g_ref, w_ref.at[pl.ds(0, depth)]), (single_ref, single_w)], size))
        load.wait()
        single_grads, copies = grads_across(
            single_ref, rows_v, w_grad, spread_ref, sent, arrived, load_sem.at[1]
        )
        for k in (6, 7, 2, 4, 3, 5, 1, 0):
            single_grads(k)
        total.turn()
        exchange = exchange_begin(
            ((down_ref, own_down_ref), (gate_ref, own_gate_ref)), e_sent, e_arrived, e_kept
        )
        wide = x_ref[...].astype(f32)
        inverse = lax.rsqrt(jnp.mean(wide * wide, axis=1, keepdims=True) + epsilon)
        normed = wide * inverse
        total.end(tokens_grad_ref)
        grad = tokens_grad_ref[...]
        gain_grad_ref[...] = jnp.sum(grad * normed, axis=0, keepdims=True)
        tokens_grad_ref[...] = middle_ref[...] + norm_back(grad, gain_ref[...], normed, inverse)
        for c in copies + exchange:
            c.wait()
        total.finish()

    dma = pltpu.SemaphoreType.DMA
    return pl.pallas_call(
        kernel,
        out_shape=[
            jax.ShapeDtypeStruct((size, width), f32),
            jax.ShapeDtypeStruct((1, width), f32),
            jax.ShapeDtypeStruct((8, HEAD_DIM, block), bf16),
            jax.ShapeDtypeStruct(down_grads.shape, bf16),
            jax.ShapeDtypeStruct(gate_grads.shape, bf16),
        ],
        in_specs=[IN_VMEM] * 3 + [ANYWHERE] + [IN_VMEM] * 3 + [ANYWHERE] * 2,
        out_specs=[IN_VMEM, IN_VMEM, ANYWHERE, ANYWHERE, ANYWHERE],
        scratch_shapes=sum_scratch(size, width)
        + [
            pltpu.VMEM((8, size, width), bf16),
            dma((2,)),
            pltpu.VMEM((8, HEAD_DIM, block), bf16),
            dma((8,)),
            dma((8,)),
            pltpu.VMEM((HEAD_DIM, width), bf16),
            dma((8, 2)),
            dma((8, 2)),
            dma((2,)),
        ],
        compiler_params=comm_params(number, VMEM_MOST),
        cost_estimate=lasting(62),
        name="backward_first",
    )(grad_query, single, weights, rows, tokens, grad_middle, gain, down_grads, gate_grads)


def last_sums(gain_first, gain_second, pair_parts, up_grads, number):
    width = gain_first.shape[1]
    block = width // 8
    f32 = jnp.float32

    def kernel(
        first_ref, second_ref, p_ref, up_ref, sums_ref, pair_ref, own_up_ref,
        gains, taken, planes, pairs, sent, arrived, z_sent, z_arrived, p_sent, p_arrived, e_sent, e_arrived, e_kept,
    ):
        f, t = lax.axis_index("fsdp"), lax.axis_index("tp")
        for j in range(8):
            lanes = slice(j * block, (j + 1) * block)
            gains[j] = jnp.concatenate([first_ref[:, lanes], second_ref[:, lanes]], axis=0)
        greet(everyone(f, t))
        copies = []
        for k in (2, 1, 3):
            plane = lax.rem(t + k, 4)
            c = remote(
                p_ref.at[pl.ds(2 * plane, 2)], pairs.at[k], p_sent.at[k], p_arrived.at[k], (f, plane)
            )
            c.start()
            copies.append(c)
        spread = []
        for k in (6, 7, 2, 4, 3, 5, 1):
            c = remote(gains.at[f ^ k], taken.at[k], sent.at[k], arrived.at[k], (f ^ k, t))
            c.start()
            spread.append((k, c))
        exchange = exchange_begin(((up_ref, own_up_ref),), e_sent, e_arrived, e_kept)
        total = gains[f]
        for k, c in spread:
            c.wait_recv()
            total += taken[k]
        planes[0] = total
        along_z = []
        for k in (1, 2, 3):
            c = remote(planes.at[0], planes.at[k], z_sent.at[k], z_arrived.at[k], (f, lax.rem(t + k, 4)))
            c.start()
            along_z.append(c)
        pair = p_ref[pl.ds(2 * t, 2)].astype(f32)
        for k, c in zip((2, 1, 3), copies):
            c.wait_recv()
            pair += pairs[k].astype(f32)
        pair_ref[...] = pair
        for c in along_z:
            c.wait_recv()
        sums = planes[t]
        for plane in (1, 2, 3):
            sums += planes[lax.rem(t + 4 - plane, 4)]
        sums_ref[...] = sums
        for c in [c for _, c in spread] + along_z + copies:
            c.wait_send()
        for c in exchange:
            c.wait()

    dma = pltpu.SemaphoreType.DMA
    return pl.pallas_call(
        kernel,
        out_shape=[
            jax.ShapeDtypeStruct((2, block), f32),
            jax.ShapeDtypeStruct((2, *pair_parts.shape[1:]), f32),
            jax.ShapeDtypeStruct(up_grads.shape, up_grads.dtype),
        ],
        in_specs=[IN_VMEM] * 3 + [ANYWHERE],
        out_specs=[IN_VMEM] * 2 + [ANYWHERE],
        scratch_shapes=[
            pltpu.VMEM((8, 2, block), f32),
            pltpu.VMEM((8, 2, block), f32),
            pltpu.VMEM((4, 2, block), f32),
            pltpu.VMEM((4, 2, *pair_parts.shape[1:]), pair_parts.dtype),
            dma((8,)),
            dma((8,)),
            dma((4,)),
            dma((4,)),
            dma((4,)),
            dma((4,)),
            dma((8, 1)),
            dma((8, 1)),
            dma((1,)),
        ],
        compiler_params=comm_params(number, VMEM_MOST),
        cost_estimate=lasting(16),
        name="last_sums",
    )(gain_first, gain_second, pair_parts, up_grads)


def last_forms(layer_out, tokens_grad, grad_query, grad_output, grad_down, grad_gate, grad_up):
    f32 = jnp.float32
    across = grad_query.shape[0]
    block = grad_query.shape[1]
    units = grad_down.shape[1]
    tall = 8 * units

    def kernel(
        out_in, tokens_in, query_in, output_in, down_in, gate_in, up_in,
        out_o, tokens_o, query_o, output_o, gate_o, up_o, down_o,
        out_v, tokens_v, query_v, output_v, down_v, gate_v, up_v,
        query_w, output_w, gate_w, up_w, down_w, in_sem, out_sem,
    ):
        loads = [
            pltpu.make_async_copy(source, target, in_sem.at[i])
            for i, (source, target) in enumerate(
                (
                    (gate_in, gate_v),
                    (up_in, up_v),
                    (down_in, down_v),
                    (out_in, out_v),
                    (tokens_in, tokens_v),
                    (query_in, query_v),
                    (output_in, output_v),
                )
            )
        ]
        for c in loads:
            c.start()
        stores = []

        def store(source, target):
            c = pltpu.make_async_copy(source, target, out_sem.at[len(stores)])
            c.start()
            stores.append(c)

        for n, (tight, wide, target) in enumerate(((gate_v, gate_w, gate_o), (up_v, up_w, up_o))):
            loads[n].wait()
            wide[...] = tight[...].reshape(tall, block).astype(f32).T
            store(wide, target)
        loads[2].wait()
        down_w[...] = down_v[...].reshape(tall, block).astype(f32)
        store(down_w, down_o)
        loads[3].wait()
        store(out_v, out_o)
        loads[4].wait()
        store(tokens_v, tokens_o)
        loads[5].wait()
        query_w[...] = query_v[...].astype(f32).T
        store(query_w, query_o)
        loads[6].wait()
        output_w[...] = output_v[...].astype(f32)
        store(output_w, output_o)
        for c in stores:
            c.wait()

    operands = (layer_out, tokens_grad, grad_query, grad_output, grad_down, grad_gate, grad_up)
    results = [
        jax.ShapeDtypeStruct(layer_out.shape, layer_out.dtype),
        jax.ShapeDtypeStruct(tokens_grad.shape, f32),
        jax.ShapeDtypeStruct((block, across), f32),
        jax.ShapeDtypeStruct((across, block), f32),
        jax.ShapeDtypeStruct((block, tall), f32),
        jax.ShapeDtypeStruct((block, tall), f32),
        jax.ShapeDtypeStruct((tall, block), f32),
    ]
    return pl.pallas_call(
        kernel,
        out_shape=results,
        in_specs=[ANYWHERE] * 7,
        out_specs=[ANYWHERE] * 7,
        scratch_shapes=[pltpu.VMEM(x.shape, x.dtype) for x in operands]
        + [pltpu.VMEM(x.shape, x.dtype) for x in results[2:]]
        + [pltpu.SemaphoreType.DMA((7,)), pltpu.SemaphoreType.DMA((7,))],
        compiler_params=pltpu.CompilerParams(vmem_limit_bytes=VMEM_MOST),
        cost_estimate=lasting(8),
        name="last_forms",
    )(*operands)


def dot_nn(left, right):
    return jnp.dot(left, right, preferred_element_type=jnp.float32)


def seen_keys(begin_row, first_key, first_query, shape):
    key_slot = first_key + lax.broadcasted_iota(jnp.int32, shape, 0)
    query_slot = first_query + lax.broadcasted_iota(jnp.int32, (1, shape[1]), 1)
    return (key_slot <= query_slot) & (key_slot >= begin_row)


def head_lanes(block, heads):
    return jnp.concatenate([block[h * HEAD_DIM : (h + 1) * HEAD_DIM] for h in range(heads)], axis=1)


WIDE = 2

def key_block(kv_ref, g, count):
    blocks = [kv_ref[lax.rem(g + n, 4), lax.div(g + n, 4)] for n in range(count)]
    return blocks[0] if count == 1 else jnp.concatenate(blocks, axis=0)


def attend(info, begins, queries, pair):
    depth, slots = queries.shape
    heads = depth // HEAD_DIM
    size = slots // 8
    span = heads * size

    def kernel(info_ref, begin_ref, q_ref, kv_ref, o_ref, l_ref, q_s, m_s, t_s, a_s, even_s, odd_s):
        f = pl.program_id(0)
        low, middle, own = info_ref[f, 0], info_ref[f, 1], info_ref[f, 2]
        q_s[...] = head_lanes(q_ref[...], heads)
        m_s[...] = jnp.full_like(m_s, -1e30)
        t_s[...] = jnp.zeros_like(t_s)
        a_s[...] = jnp.zeros_like(a_s)

        def scores_of(g, count):
            return dot_nn(key_block(kv_ref, g, count)[:, :HEAD_DIM], q_s[...])

        def add(scores, g, count):
            values = key_block(kv_ref, g, count)[:, HEAD_DIM:]
            value_cols = values.astype(jnp.float32).T.astype(jnp.bfloat16)
            largest = m_s[...]
            higher = jnp.maximum(largest, jnp.max(scores, axis=0, keepdims=True))
            raised = jnp.exp(scores - higher)
            fade = jnp.exp(largest - higher)
            m_s[...] = higher
            t_s[...] = t_s[...] * fade + jnp.sum(raised, axis=0, keepdims=True)
            a_s[...] = a_s[...] * fade + dot_nn(value_cols, raised.astype(jnp.bfloat16))

        def step(g, count, masked):
            scores = scores_of(g, count)
            if masked:
                seen = seen_keys(begin_ref[0], g * size, own * size, (count * size, size))
                seen = jnp.concatenate([seen] * heads, axis=1)
                scores = jnp.where(seen, scores, -1e30)
            add(scores, g, count)

        count = own + 1 - low
        odd = lax.rem(count, WIDE) == 1

        @pl.when(odd)
        def _():
            step(own, 1, True)

        @pl.when(jnp.logical_not(odd))
        def _():
            step(own - 1, WIDE, True)

        units = lax.div(count - 1, WIDE)
        bounded = jnp.minimum(lax.div(middle - low + WIDE - 1, WIDE), units)

        def masked_step(n, carry):
            step(low + n * WIDE, WIDE, True)
            return carry

        lax.fori_loop(0, bounded, masked_step, 0)
        def unit(n):
            return low + jnp.minimum(n, units - 1) * WIDE

        def two(j, carry):
            n = bounded + 2 * j
            odd_s[...] = scores_of(unit(n + 1), WIDE)
            add(even_s[...], unit(n), WIDE)
            even_s[...] = scores_of(unit(n + 2), WIDE)
            add(odd_s[...], unit(n + 1), WIDE)
            return carry

        rest = units - bounded

        @pl.when(rest > 0)
        def _():
            even_s[...] = scores_of(unit(bounded), WIDE)
            lax.fori_loop(0, lax.div(rest, 2), two, 0)

            @pl.when(lax.rem(rest, 2) == 1)
            def _():
                add(even_s[...], unit(units - 1), WIDE)

        result = a_s[...] / t_s[...]
        for h in range(heads):
            o_ref[h * HEAD_DIM : (h + 1) * HEAD_DIM] = result[:, h * size : (h + 1) * size].astype(
                jnp.bfloat16
            )
        l_ref[0] = m_s[...] + jnp.log(t_s[...])
    return pl.pallas_call(
        kernel,
        grid_spec=pltpu.PrefetchScalarGridSpec(
            num_scalar_prefetch=1,
            grid=(8,),
            in_specs=[
                pl.BlockSpec((1, 1, size), lambda f, info: (f, 0, 0)),
                pl.BlockSpec((depth, size), lambda f, info: (0, f)),
                pl.BlockSpec((4, 8, size, 2 * HEAD_DIM), lambda f, info: (0, 0, 0, 0)),
            ],
            out_specs=[
                pl.BlockSpec((depth, size), lambda f, info: (0, f)),
                pl.BlockSpec((1, 1, span), lambda f, info: (f, 0, 0)),
            ],
            scratch_shapes=[
                pltpu.VMEM((HEAD_DIM, span), jnp.bfloat16),
                pltpu.VMEM((1, span), jnp.float32),
                pltpu.VMEM((1, span), jnp.float32),
                pltpu.VMEM((HEAD_DIM, span), jnp.float32),
                pltpu.VMEM((WIDE * size, span), jnp.float32),
                pltpu.VMEM((WIDE * size, span), jnp.float32),
            ],
        ),
        out_shape=[
            jax.ShapeDtypeStruct((depth, slots), jnp.bfloat16),
            jax.ShapeDtypeStruct((8, 1, span), jnp.float32),
        ],
        compiler_params=pltpu.CompilerParams(vmem_limit_bytes=VMEM_MOST),
        cost_estimate=lasting(50),
        name="attend",
    )(info, begins, queries, pair)


def attend_back(info, begins, queries, pair, outputs, grads, totals, cosine, sine_table):
    depth, slots = queries.shape
    heads = depth // HEAD_DIM
    size = slots // 8
    span = heads * size

    def kernel(
        info_ref, begin_ref, q_ref, kv_ref, o_ref, g_ref, l_ref, cos_ref, sin_ref, dq_ref, dkv_ref, q_s, g_s, d_s, a_s, w_s
    ):
        f = pl.program_id(0)
        low, middle, own = info_ref[f, 0], info_ref[f, 1], info_ref[f, 2]
        middle = middle + lax.rem(own - middle, WIDE)

        @pl.when(f == 0)
        def _():
            w_s[...] = jnp.zeros_like(w_s)

        q_s[...] = head_lanes(q_ref[...], heads)
        g_s[...] = head_lanes(g_ref[...], heads)
        out_lanes = head_lanes(o_ref[...], heads).astype(jnp.float32)
        d_s[...] = jnp.sum(out_lanes * g_s[...].astype(jnp.float32), axis=0, keepdims=True)
        a_s[...] = jnp.zeros_like(a_s)

        def step(g, count, masked):
            block = key_block(kv_ref, g, count)
            keys, values = block[:, :HEAD_DIM], block[:, HEAD_DIM:]
            key_cols = keys.astype(jnp.float32).T.astype(jnp.bfloat16)
            if masked:
                seen = seen_keys(begin_ref[0], g * size, own * size, (size, size))
                seen = jnp.concatenate([seen] * heads, axis=1)
            grad_keys = jnp.zeros((HEAD_DIM, count * size), jnp.float32)
            grad_values = jnp.zeros((HEAD_DIM, count * size), jnp.float32)
            query, grad = q_s[...], g_s[...]
            raised = jnp.exp(dot_nn(keys, query) - l_ref[0])
            if masked:
                raised = jnp.where(seen, raised, 0.0)
            grad_probs = dot_nn(values, grad)
            scores = (raised * (grad_probs - d_s[...])).astype(jnp.bfloat16)
            grad_values += outer_cols(grad, raised.astype(jnp.bfloat16))
            grad_keys += outer_cols(query, scores)
            a_s[...] += dot_nn(key_cols, scores)
            for n in range(count):
                keep = slice(n * size, (n + 1) * size)
                w_s[lax.rem(g + n, 4), lax.div(g + n, 4), :HEAD_DIM] += grad_keys[:, keep]
                w_s[lax.rem(g + n, 4), lax.div(g + n, 4), HEAD_DIM:] += grad_values[:, keep]

        def masked_step(g, carry):
            step(g, 1, True)
            return carry

        def plain_step(n, carry):
            step(middle + n * WIDE, WIDE, False)
            return carry

        step(own, 1, True)
        lax.fori_loop(low, middle, masked_step, 0)
        lax.fori_loop(0, lax.div(own - middle, WIDE), plain_step, 0)
        result = a_s[...] * HEAD_DIM ** (-0.5)
        result = jnp.concatenate([result[:, h * size : (h + 1) * size] for h in range(heads)], axis=0)
        dq_ref[...] = turn_heads(result, cos_ref[...], -sin_ref[...]).astype(jnp.bfloat16)

        @pl.when(f == 7)
        def _():
            dkv_ref[...] = w_s[...].astype(jnp.bfloat16)

    return pl.pallas_call(
        kernel,
        grid_spec=pltpu.PrefetchScalarGridSpec(
            num_scalar_prefetch=1,
            grid=(8,),
            in_specs=[
                pl.BlockSpec((1, 1, size), lambda f, info: (f, 0, 0)),
                pl.BlockSpec((depth, size), lambda f, info: (0, f)),
                pl.BlockSpec((4, 8, size, 2 * HEAD_DIM), lambda f, info: (0, 0, 0, 0)),
                pl.BlockSpec((depth, size), lambda f, info: (0, f)),
                pl.BlockSpec((depth, size), lambda f, info: (0, f)),
                pl.BlockSpec((1, 1, span), lambda f, info: (f, 0, 0)),
                pl.BlockSpec((HEAD_DIM // 2, size), lambda f, info: (0, f)),
                pl.BlockSpec((HEAD_DIM // 2, size), lambda f, info: (0, f)),
            ],
            out_specs=[
                pl.BlockSpec((depth, size), lambda f, info: (0, f)),
                pl.BlockSpec((4, 8, 2 * HEAD_DIM, size), lambda f, info: (0, 0, 0, 0)),
            ],
            scratch_shapes=[
                pltpu.VMEM((HEAD_DIM, span), jnp.bfloat16),
                pltpu.VMEM((HEAD_DIM, span), jnp.bfloat16),
                pltpu.VMEM((1, span), jnp.float32),
                pltpu.VMEM((HEAD_DIM, span), jnp.float32),
                pltpu.VMEM((4, 8, 2 * HEAD_DIM, size), jnp.float32),
            ],
        ),
        out_shape=[
            jax.ShapeDtypeStruct((depth, slots), jnp.bfloat16),
            jax.ShapeDtypeStruct((4, 8, 2 * HEAD_DIM, size), jnp.bfloat16),
        ],
        compiler_params=pltpu.CompilerParams(vmem_limit_bytes=VMEM_MOST),
        cost_estimate=lasting(65),
        name="attend_back",
    )(info, begins, queries, pair, outputs, grads, totals, cosine, sine_table)


def segment_begins(slots, lengths):
    seq_index = jnp.arange(lengths.shape[0], dtype=jnp.int32)
    ends = jnp.sum(jnp.where(seq_index[:, None] >= seq_index[None, :], lengths[None, :], 0), axis=1)
    passed = slots[:, None] >= ends[None, :]
    begins = jnp.sum(jnp.where(passed, lengths[None, :], 0), axis=1)
    return begins, slots < ends[-1]


def local_plane(
    tokens,
    attn_gain,
    query_weight,
    key_weight,
    value_weight,
    output_weight,
    mlp_gain,
    gate_weight,
    up_weight,
    down_weight,
    out_grad,
    lengths,
):
    size, width = tokens.shape
    f = lax.axis_index("fsdp")
    t = lax.axis_index("tp")
    block = query_weight.shape[0]
    head_rows = query_weight.shape[1] // 2
    units = gate_weight.shape[1] // 8
    bf16, f32 = jnp.bfloat16, jnp.float32

    def across_plane(parts):
        return lax.all_to_all(parts, "fsdp", 0, 0, tiled=False)

    def planes_together(part):
        flat = part.reshape(-1, block)
        return lax.all_gather(flat, "tp", axis=0, tiled=True).reshape(4, *part.shape)

    gate_up, inner_own = first_forms(
        gate_weight, up_weight, query_weight, key_weight.T, value_weight.T
    )
    inner_all = planes_together(inner_own)
    down_all = across_plane(down_weight.reshape(8, units, block))
    gate_up = across_plane(gate_up)
    gains_own = jnp.stack([attn_gain, mlp_gain]).astype(f32)

    my_slots = (f * 4 + t) * size + jnp.arange(size, dtype=jnp.int32)
    _, my_valid = segment_begins(my_slots, lengths)
    valid_rows = my_valid[:, None]
    chunk_index = jnp.arange(8, dtype=jnp.int32) * 4 + t
    plane_slots = (chunk_index[:, None] * size + jnp.arange(size, dtype=jnp.int32)[None, :]).reshape(-1)
    begins, plane_valid = segment_begins(plane_slots, lengths)
    positions = jnp.where(plane_valid, plane_slots - begins, 0)
    begins = begins.reshape(8, 1, size)
    info = jnp.stack(
        [
            begins[:, 0, 0] // size,
            jnp.minimum((begins[:, 0, size - 1] + size - 1) // size, chunk_index),
            chunk_index,
        ],
        axis=1,
    ).astype(jnp.int32)
    ladder = jnp.arange(HEAD_DIM // 2).astype(f32)
    frequency = 10000.0 ** (-2.0 * ladder / HEAD_DIM)
    angles = positions.astype(f32)[None, :] * frequency[:, None]
    cosine, sine_table = jnp.cos(angles), jnp.sin(angles)

    valid_rows = valid_rows.astype(f32)
    cosine, gate_up, down_all = lax.optimization_barrier((cosine, gate_up, down_all))
    down_all, gate_up = planes_together(down_all), planes_together(gate_up)
    rows_first, queries, pair, inner_rows_w, output_all, grad_rows, gains_all = first_rows(
        tokens, gains_own, inner_all, output_weight, cosine, sine_table, out_grad, valid_rows, 2
    )
    output_rows = across_plane(output_all.reshape(8, head_rows, block))
    gains = jnp.moveaxis(gains_all, 0, 1).reshape(2, width)
    gain_first, gain_second = gains[0:1], gains[1:2]
    attended, totals = attend(info, begins, queries, pair)
    middle, row_second, grad_hidden = forward_output(
        attended, output_rows, tokens, gain_second, grad_rows, down_all, 4
    )
    rows_second, hidden, grad_gate_low, grad_up_low, down_grads = forward_hidden(
        row_second, grad_rows, grad_hidden, gate_up, 5
    )
    (
        grad_middle,
        gain_second_part,
        grad_output_w,
        grad_attended,
        gate_grads,
        up_grads,
    ) = backward_middle(
        grad_gate_low,
        grad_up_low,
        gate_up,
        rows_second,
        grad_rows,
        output_rows,
        attended,
        middle,
        gain_second,
        6,
    )
    def own_plane(parts, *shape):
        flat = parts.reshape(-1, block)
        return lax.psum_scatter(flat, "tp", scatter_dimension=0, tiled=True).reshape(*shape)

    down_grads = own_plane(down_grads, 8, units, block)
    gate_grads, down_grads = lax.optimization_barrier((gate_grads, down_grads))
    gate_grads = own_plane(gate_grads, 8, units, block)
    output_parts = across_plane(grad_output_w)
    output_parts, gate_grads = lax.optimization_barrier((output_parts, gate_grads))
    output_own = own_plane(output_parts, 2 * head_rows, block)
    grad_query, grad_pair_parts = attend_back(
        info, begins, queries, pair, attended, grad_attended, totals, cosine, sine_table
    )
    single, layer_out, query_parts = backward_pairs(
        grad_pair_parts,
        hidden,
        down_all,
        middle,
        valid_rows,
        grad_query,
        rows_first,
        cosine,
        sine_table,
        7,
    )
    up_grads, query_parts, output_own = lax.optimization_barrier((up_grads, query_parts, output_own))
    up_grads = own_plane(up_grads, 8, units, block)
    tokens_grad, gain_first_part, single_parts, own_down, own_gate = backward_first(
        grad_query,
        single,
        inner_rows_w,
        rows_first,
        tokens,
        grad_middle,
        gain_first,
        down_grads,
        gate_grads,
        8,
    )
    query_own = own_plane(query_parts, 2 * head_rows, block)
    gain_sums, pair_own, own_up = last_sums(
        gain_first_part, gain_second_part, single_parts, up_grads, 9
    )
    layer_out, tokens_grad, query, output, gate, up, down = last_forms(
        layer_out, tokens_grad, query_own, output_own, own_down, own_gate, own_up
    )
    return (
        layer_out,
        tokens_grad,
        gain_sums[0],
        query,
        pair_own[0].T,
        pair_own[1].T,
        output,
        gain_sums[1],
        gate,
        up,
        down,
    )


def solution(mesh):
    plane = dict(mesh.shape) == {"fsdp": 8, "tp": 4}
    body = local_plane if plane else local
    in_specs = (
        P(("fsdp", "tp"), None),
        P("fsdp"),
        P("fsdp", "tp"),
        P("fsdp", "tp"),
        P("fsdp", "tp"),
        P("tp", "fsdp"),
        P("fsdp"),
        P("fsdp", "tp"),
        P("fsdp", "tp"),
        P("tp", "fsdp"),
        P(("fsdp", "tp"), None),
        P(),
    )
    out_specs = (
        P(("fsdp", "tp"), None),
        P(("fsdp", "tp"), None),
        P("fsdp"),
        P("fsdp", "tp"),
        P("fsdp", "tp"),
        P("fsdp", "tp"),
        P("tp", "fsdp"),
        P("fsdp"),
        P("fsdp", "tp"),
        P("fsdp", "tp"),
        P("tp", "fsdp"),
    )
    return jax.shard_map(body, mesh=mesh, in_specs=in_specs, out_specs=out_specs, check_vma=False)
```
